32 devices in a mesh: groups: 2 (over x), rows: 16 (over z, y, core).
Axes of the slice: x: 2, y: 2, z: 4, core: 2. Of those that a mesh axis runs over, the one named last changes fastest.
Arguments:
- latents: bfloat16 [2, 64, 256, 128], P('groups', 'rows'), parts along dimension 0, may hold values from -60 to 60
- gain_one: float32 [128], replicated, may hold values from 0.25 to 1.75
- shift_one: float32 [128], replicated, may hold values from -3 to 3
- weight_one: bfloat16 [3, 3, 3, 128, 128], replicated, may hold values from -0.109375 to 0.109375
- bias_one: float32 [128], replicated, may hold values from -3 to 3
- gain_two: float32 [128], replicated, may hold values from 0.25 to 1.75
- shift_two: float32 [128], replicated, may hold values from -3 to 3
- weight_two: bfloat16 [3, 3, 3, 128, 128], replicated, may hold values from -0.109375 to 0.109375
- bias_two: float32 [128], replicated, may hold values from -3 to 3
Outputs:
- decoded: bfloat16 [2, 64, 256, 128], P('groups', 'rows'), parts along dimension 0
The draws below stay inside these ranges and needn't reach their ends.
There are 2 independent parts, one for each index of `groups`. The reference program is written for one: setup_inputs(seed, part) draws one part's arguments, and reference() takes and returns one part's arrays. A program takes and returns all parts, laid end to end along the dimension named above; an argument that names none is the same for every part. Nothing has to cross between parts.
All inputs are finite; a program needn't handle non-finite values.
Results may differ from the reference program's by a relative error of at most 0.004.
Values may be sent and summed in bfloat16 or wider, within the bound.
No kernel may reach another device: no remote copies, remote signals or barrier semaphores. Data moves between devices by JAX's collectives and lax.ppermute only.
A program may use at most 64 MiB of HBM per device.

```python
import jax
import jax.numpy as jnp
from jax import lax

C = 128
GROUPS = 32
FRAMES = 1
ROWS_DEV = 4
W = 256
H = 64


def draw_latents(key, part):
    key_base = jax.random.fold_in(key, 11)
    key_chan = jax.random.fold_in(key, 12)
    key_band = jax.random.fold_in(key, 14)
    key_bandshift = jax.random.fold_in(key, 15)
    shape = (FRAMES, H, W, C)
    band_count = H // ROWS_DEV
    positions = jnp.arange(H, dtype=jnp.float32) / max(H - 1, 1)
    band_level = jnp.exp(jax.random.uniform(key_band, (band_count,), jnp.float32, jnp.log(0.25), jnp.log(2.5)))
    band_offset = jax.random.normal(key_bandshift, (band_count, C), jnp.float32)
    row_level = jnp.repeat(band_level, ROWS_DEV)
    row_offset = jnp.repeat(band_offset, ROWS_DEV, axis=0)
    base = jnp.clip(jax.random.normal(key_base, shape, jnp.float32), -6.0, 6.0)
    row_scale = jnp.exp(jnp.log(3.0) * positions)
    chan_scale = jnp.exp(jax.random.uniform(key_chan, (C,), jnp.float32, jnp.log(0.3), jnp.log(3.0)))
    shifted = base + row_offset[None, :, None, :]
    values = shifted * chan_scale * (row_scale * row_level)[None, :, None, None]
    return jnp.clip(values, -60.0, 60.0).astype(jnp.bfloat16)


def scatter_about(own_key, shape, spread, reach, kind=jnp.bfloat16):
    array = spread * jax.random.normal(own_key, shape, jnp.float32)
    return jnp.clip(array, min=-reach, max=reach).astype(kind)


def setup_inputs(seed: int = 0, part: int = 0) -> dict:
    keys = jax.random.split(jax.random.key(seed), 10)
    part_keys = jax.random.split(jax.random.fold_in(keys[9], part), 10)
    return {
        "latents": draw_latents(jax.random.fold_in(jax.random.fold_in(keys[9], part), 71), part),
        "gain_one": jnp.clip(1.0 + 0.15 * jax.random.normal(keys[1], (C,), jnp.float32), 0.25, 1.75),
        "shift_one": scatter_about(keys[2], (C,), 0.5, 3.0, jnp.float32),
        "weight_one": scatter_about(keys[3], (3, 3, 3, C, C), (27 * C) ** -0.5, 0.109375),
        "bias_one": scatter_about(keys[4], (C,), 0.5, 3.0, jnp.float32),
        "gain_two": jnp.clip(1.0 + 0.15 * jax.random.normal(keys[5], (C,), jnp.float32), 0.25, 1.75),
        "shift_two": scatter_about(keys[6], (C,), 0.5, 3.0, jnp.float32),
        "weight_two": scatter_about(keys[7], (3, 3, 3, C, C), (27 * C) ** -0.5, 0.109375),
        "bias_two": scatter_about(keys[8], (C,), 0.5, 3.0, jnp.float32),
    }


def group_norm_silu(values, gain, shift):
    frame_count, row_count, col_count, channels = values.shape
    per_group = channels // GROUPS
    grouped = values.reshape(frame_count, row_count, col_count, GROUPS, per_group)
    mean = lax.optimization_barrier(jnp.mean(grouped, axis=(0, 1, 2, 4)))
    centered = grouped - mean[:, None]
    var = lax.optimization_barrier(jnp.mean(centered * centered, axis=(0, 1, 2, 4)))
    inv = 1.0 / jnp.sqrt(var + 1e-06)
    normed = (centered * inv[:, None]).reshape(frame_count, row_count, col_count, channels)
    normed = normed * gain + shift
    return jax.nn.silu(normed).astype(jnp.bfloat16)

def causal_conv(acts, weight, bias):
    timed = jnp.concatenate([acts[:1], acts[:1], acts], axis=0)
    padded = jnp.pad(timed, ((0, 0), (1, 1), (1, 1), (0, 0)), mode='edge')
    result = lax.conv_general_dilated(padded[None].astype(jnp.float32), weight.astype(jnp.float32), (1, 1, 1), 'VALID', dimension_numbers=('NDHWC', 'DHWIO', 'NDHWC'), precision=lax.Precision.HIGHEST)
    return result[0] + bias

def reference(latents, gain_one, shift_one, weight_one, bias_one, gain_two, shift_two, weight_two, bias_two):
    act_one = group_norm_silu(latents.astype(jnp.float32), gain_one, shift_one)
    hidden = causal_conv(act_one, weight_one, bias_one).astype(jnp.bfloat16)
    act_two = group_norm_silu(hidden.astype(jnp.float32), gain_two, shift_two)
    branch = causal_conv(act_two, weight_two, bias_two)
    return (latents.astype(jnp.float32) + branch).astype(jnp.bfloat16)
```

```python
import jax
import jax.numpy as jnp
from jax import lax
from jax.sharding import PartitionSpec as P

GROUPS = 32


def sum_over_rows(values):
    count = lax.axis_size("rows")
    if count & (count - 1):
        return lax.psum(values, "rows")
    step = 1
    while step < count:
        pairs = [(i, i ^ step) for i in range(count)]
        values = values + lax.ppermute(values, "rows", pairs)
        step *= 2
    return values


def halo_rows(block, depth):
    count = lax.axis_size("rows")
    forward = [(i, i + 1) for i in range(count - 1)]
    backward = [(i + 1, i) for i in range(count - 1)]
    upper = lax.ppermute(block[-depth:], "rows", forward)
    lower = lax.ppermute(block[:depth], "rows", backward)
    return upper, lower


def channel_sums(values):
    return jnp.stack([jnp.sum(values, axis=(0, 1)), jnp.sum(values * values, axis=(0, 1))])


def scale_offset(sums, gain, shift, entries):
    channels = sums.shape[1]
    per_group = channels // GROUPS
    group = jnp.arange(channels) // per_group
    same = (group[:, None] == group[None, :]).astype(jnp.float32)
    totals = jnp.sum(sums[:, :, None] * same[None], axis=1) / (entries * per_group)
    mean = totals[0]
    var = totals[1] - mean * mean
    inverse = 1.0 / jnp.sqrt(var + 1e-06)
    scale = inverse * gain
    return mean, scale, shift


def normalize(values, mean, scale, shift):
    return jax.nn.silu((values - mean) * scale + shift).astype(jnp.bfloat16)


def summed_weight(weight):
    total = jnp.sum(weight.astype(jnp.float32), axis=0)
    high = total.astype(jnp.bfloat16)
    low = (total - high.astype(jnp.float32)).astype(jnp.bfloat16)
    both = jnp.concatenate([high, low], axis=-1)
    return both.reshape(-1, both.shape[-1])


def conv(acts, weight, bias):
    rows, width, channels = acts.shape
    out_rows = rows - 2
    widened = jnp.concatenate([acts[:, :1], acts, acts[:, -1:]], axis=1)
    taps = [
        widened[di : di + out_rows, dj : dj + width] for di in range(3) for dj in range(3)
    ]
    stacked = jnp.concatenate(taps, axis=2).reshape(out_rows * width, 9 * channels)
    both = jnp.dot(stacked, weight, preferred_element_type=jnp.float32)
    half = both.shape[1] // 2
    return (both[:, :half] + both[:, half:] + bias).reshape(out_rows, width, half)


def body(
    latents, gain_one, shift_one, weight_one, bias_one, gain_two, shift_two, weight_two, bias_two
):
    index = lax.axis_index("rows")
    first = index == 0
    last = index == lax.axis_size("rows") - 1
    own = latents[0]
    rows, width, _ = own.shape
    entries = rows * width * lax.axis_size("rows")
    upper, lower = halo_rows(own, 2)
    upper = jnp.where(first, own[:1], upper)
    lower = jnp.where(last, own[-1:], lower)
    extended = jnp.concatenate([upper, own, lower], axis=0).astype(jnp.float32)

    sums = sum_over_rows(channel_sums(own.astype(jnp.float32)))
    act_one = normalize(extended, *scale_offset(sums, gain_one, shift_one, entries))
    hidden = conv(act_one, summed_weight(weight_one), bias_one).astype(jnp.bfloat16)
    hidden = hidden.astype(jnp.float32)
    upper = jnp.where(first, hidden[1:2], hidden[:1])
    lower = jnp.where(last, hidden[-2:-1], hidden[-1:])
    sums = sum_over_rows(channel_sums(hidden[1:-1]))
    hidden = jnp.concatenate([upper, hidden[1:-1], lower], axis=0)
    act_two = normalize(hidden, *scale_offset(sums, gain_two, shift_two, entries))
    branch = conv(act_two, summed_weight(weight_two), bias_two)
    return (own.astype(jnp.float32) + branch).astype(jnp.bfloat16)[None]


def solution(mesh):
    return jax.shard_map(
        body,
        mesh=mesh,
        in_specs=(P("groups", "rows", None, None), P(), P(), P(), P(), P(), P(), P(), P()),
        out_specs=P("groups", "rows", None, None),
        check_vma=False,
    )
```

```python
import jax
import jax.numpy as jnp
from jax import lax
from jax.sharding import PartitionSpec as P

GROUPS = 32


def sum_over_rows(values):
    count = lax.axis_size("rows")
    copies = jnp.broadcast_to(values[None], (count,) + values.shape)
    return jnp.sum(lax.all_to_all(copies, "rows", 0, 0), axis=0)


def halo_rows(block, depth):
    count = lax.axis_size("rows")
    forward = [(i, i + 1) for i in range(count - 1)]
    backward = [(i + 1, i) for i in range(count - 1)]
    upper = lax.ppermute(block[-depth:], "rows", forward)
    lower = lax.ppermute(block[:depth], "rows", backward)
    return upper, lower


def channel_sums(values):
    return jnp.stack([jnp.sum(values, axis=(0, 1)), jnp.sum(values * values, axis=(0, 1))])


def scale_offset(sums, gain, shift, entries):
    channels = sums.shape[1]
    per_group = channels // GROUPS
    group = jnp.arange(channels) // per_group
    same = (group[:, None] == group[None, :]).astype(jnp.float32)
    totals = jnp.sum(sums[:, :, None] * same[None], axis=1) / (entries * per_group)
    mean = totals[0]
    var = totals[1] - mean * mean
    inverse = 1.0 / jnp.sqrt(var + 1e-06)
    scale = inverse * gain
    return mean, scale, shift


def normalize(values, mean, scale, shift):
    return jax.nn.silu((values - mean) * scale + shift).astype(jnp.bfloat16)


def summed_weight(weight):
    total = jnp.sum(weight.astype(jnp.float32), axis=0)
    high = total.astype(jnp.bfloat16)
    low = (total - high.astype(jnp.float32)).astype(jnp.bfloat16)
    both = jnp.concatenate([high, low], axis=-1)
    return both.reshape(-1, both.shape[-1])


def conv(acts, weight, bias):
    rows, width, channels = acts.shape
    out_rows = rows - 2
    widened = jnp.concatenate([acts[:, :1], acts, acts[:, -1:]], axis=1)
    taps = [
        widened[di : di + out_rows, dj : dj + width] for di in range(3) for dj in range(3)
    ]
    stacked = jnp.concatenate(taps, axis=2).reshape(out_rows * width, 9 * channels)
    both = jnp.dot(stacked, weight, preferred_element_type=jnp.float32)
    half = both.shape[1] // 2
    return (both[:, :half] + both[:, half:] + bias).reshape(out_rows, width, half)


def body(
    latents, gain_one, shift_one, weight_one, bias_one, gain_two, shift_two, weight_two, bias_two
):
    index = lax.axis_index("rows")
    first = index == 0
    last = index == lax.axis_size("rows") - 1
    own = latents[0]
    rows, width, _ = own.shape
    entries = rows * width * lax.axis_size("rows")
    upper, lower = halo_rows(own, 2)
    upper = jnp.where(first, own[:1], upper)
    lower = jnp.where(last, own[-1:], lower)
    extended = jnp.concatenate([upper, own, lower], axis=0).astype(jnp.float32)

    sums = sum_over_rows(channel_sums(own.astype(jnp.float32)))
    act_one = normalize(extended, *scale_offset(sums, gain_one, shift_one, entries))
    hidden = conv(act_one, summed_weight(weight_one), bias_one).astype(jnp.bfloat16)
    hidden = hidden.astype(jnp.float32)
    upper = jnp.where(first, hidden[1:2], hidden[:1])
    lower = jnp.where(last, hidden[-2:-1], hidden[-1:])
    sums = sum_over_rows(channel_sums(hidden[1:-1]))
    hidden = jnp.concatenate([upper, hidden[1:-1], lower], axis=0)
    act_two = normalize(hidden, *scale_offset(sums, gain_two, shift_two, entries))
    branch = conv(act_two, summed_weight(weight_two), bias_two)
    return (own.astype(jnp.float32) + branch).astype(jnp.bfloat16)[None]


def solution(mesh):
    return jax.shard_map(
        body,
        mesh=mesh,
        in_specs=(P("groups", "rows", None, None), P(), P(), P(), P(), P(), P(), P(), P()),
        out_specs=P("groups", "rows", None, None),
        check_vma=False,
    )
```

```python
import jax
import jax.numpy as jnp
from jax import lax
from jax.sharding import PartitionSpec as P

GROUPS = 32


def sum_over_rows(values):
    return jnp.sum(lax.all_gather(values, "rows"), axis=0)


def halo_rows(block, depth):
    count = lax.axis_size("rows")
    forward = [(i, i + 1) for i in range(count - 1)]
    backward = [(i + 1, i) for i in range(count - 1)]
    upper = lax.ppermute(block[-depth:], "rows", forward)
    lower = lax.ppermute(block[:depth], "rows", backward)
    return upper, lower


def channel_sums(values):
    return jnp.stack([jnp.sum(values, axis=(0, 1)), jnp.sum(values * values, axis=(0, 1))])


def scale_offset(sums, gain, shift, entries):
    channels = sums.shape[1]
    per_group = channels // GROUPS
    group = jnp.arange(channels) // per_group
    same = (group[:, None] == group[None, :]).astype(jnp.float32)
    totals = jnp.sum(sums[:, :, None] * same[None], axis=1) / (entries * per_group)
    mean = totals[0]
    var = totals[1] - mean * mean
    inverse = 1.0 / jnp.sqrt(var + 1e-06)
    scale = inverse * gain
    return mean, scale, shift


def normalize(values, mean, scale, shift):
    return jax.nn.silu((values - mean) * scale + shift).astype(jnp.bfloat16)


def summed_weight(weight):
    total = jnp.sum(weight.astype(jnp.float32), axis=0)
    high = total.astype(jnp.bfloat16)
    low = (total - high.astype(jnp.float32)).astype(jnp.bfloat16)
    both = jnp.concatenate([high, low], axis=-1)
    return both.reshape(-1, both.shape[-1])


def conv(acts, weight, bias):
    rows, width, channels = acts.shape
    out_rows = rows - 2
    widened = jnp.concatenate([acts[:, :1], acts, acts[:, -1:]], axis=1)
    taps = [
        widened[di : di + out_rows, dj : dj + width] for di in range(3) for dj in range(3)
    ]
    stacked = jnp.concatenate(taps, axis=2).reshape(out_rows * width, 9 * channels)
    both = jnp.dot(stacked, weight, preferred_element_type=jnp.float32)
    half = both.shape[1] // 2
    return (both[:, :half] + both[:, half:] + bias).reshape(out_rows, width, half)


def body(
    latents, gain_one, shift_one, weight_one, bias_one, gain_two, shift_two, weight_two, bias_two
):
    index = lax.axis_index("rows")
    first = index == 0
    last = index == lax.axis_size("rows") - 1
    own = latents[0]
    rows, width, _ = own.shape
    entries = rows * width * lax.axis_size("rows")
    upper, lower = halo_rows(own, 2)
    upper = jnp.where(first, own[:1], upper)
    lower = jnp.where(last, own[-1:], lower)
    extended = jnp.concatenate([upper, own, lower], axis=0).astype(jnp.float32)

    sums = sum_over_rows(channel_sums(own.astype(jnp.float32)))
    act_one = normalize(extended, *scale_offset(sums, gain_one, shift_one, entries))
    hidden = conv(act_one, summed_weight(weight_one), bias_one).astype(jnp.bfloat16)
    hidden = hidden.astype(jnp.float32)
    upper = jnp.where(first, hidden[1:2], hidden[:1])
    lower = jnp.where(last, hidden[-2:-1], hidden[-1:])
    sums = sum_over_rows(channel_sums(hidden[1:-1]))
    hidden = jnp.concatenate([upper, hidden[1:-1], lower], axis=0)
    act_two = normalize(hidden, *scale_offset(sums, gain_two, shift_two, entries))
    branch = conv(act_two, summed_weight(weight_two), bias_two)
    return (own.astype(jnp.float32) + branch).astype(jnp.bfloat16)[None]


def solution(mesh):
    return jax.shard_map(
        body,
        mesh=mesh,
        in_specs=(P("groups", "rows", None, None), P(), P(), P(), P(), P(), P(), P(), P()),
        out_specs=P("groups", "rows", None, None),
        check_vma=False,
    )
```

```python
import functools

import jax
import jax.numpy as jnp
from jax import lax
from jax.experimental import pallas as pl
from jax.experimental.pallas import tpu as pltpu
from jax.sharding import PartitionSpec as P

GROUPS = 32
VMEM = pl.BlockSpec(memory_space=pltpu.VMEM)
PARAMS = pltpu.CompilerParams(vmem_limit_bytes=24 * 1024 * 1024)


def store_sums(total, square, out_ref):
    pair = jnp.concatenate([total, square], axis=0)
    out_ref[...] = jnp.broadcast_to(pair[None], out_ref.shape)


def sums_kernel(own_ref, out_ref):
    rows, width, channels = own_ref.shape
    total = jnp.zeros((8, channels), jnp.float32)
    square = jnp.zeros((8, channels), jnp.float32)
    for row in range(rows):
        values = own_ref[row].astype(jnp.float32)
        total += jnp.sum(values.reshape(width // 8, 8, channels), axis=0)
        square += jnp.sum((values * values).reshape(width // 8, 8, channels), axis=0)
    store_sums(
        jnp.sum(total, axis=0, keepdims=True), jnp.sum(square, axis=0, keepdims=True), out_ref
    )


def weights_kernel(one_ref, two_ref, out_one_ref, out_two_ref):
    for source, target in ((one_ref, out_one_ref), (two_ref, out_two_ref)):
        taps, channels = source.shape[0] // 3, source.shape[1]
        for tap in range(taps):
            total = source[tap].astype(jnp.float32)
            total += source[taps + tap].astype(jnp.float32)
            total += source[2 * taps + tap].astype(jnp.float32)
            high = total.astype(jnp.bfloat16)
            low = (total - high.astype(jnp.float32)).astype(jnp.bfloat16)
            rows = pl.ds(tap * channels, channels)
            target[rows, :] = jnp.concatenate([high, low], axis=1)


def scale_offset(sums_ref, gain_ref, shift_ref, entries):
    sums = jnp.sum(sums_ref[...], axis=0)
    channels = sums.shape[1]
    per_group = channels // GROUPS
    sums = jnp.concatenate([sums, jnp.zeros((6, channels), jnp.float32)], axis=0)
    step = 1
    while step < per_group:
        sums += pltpu.roll(sums, channels - step, 1)
        step *= 2
    lane = lax.broadcasted_iota(jnp.int32, sums.shape, 1)
    sums = jnp.where(lane % per_group == 0, sums, 0.0)
    step = 1
    while step < per_group:
        sums += pltpu.roll(sums, step, 1)
        step *= 2
    sums = sums * (1.0 / (entries * per_group))
    mean = sums[0:1]
    var = sums[1:2] - mean * mean
    scale = gain_ref[...] / jnp.sqrt(var + 1e-06)
    return scale, shift_ref[...] - mean * scale


def store_taps(values, scale, offset, target, row):
    width, channels = values.shape
    normed = values.astype(jnp.float32) * scale + offset
    act = normed * (0.5 * jnp.tanh(0.5 * normed) + 0.5)
    column = lax.broadcasted_iota(jnp.int32, act.shape, 0)
    left = jnp.where(column == 0, act, pltpu.roll(act, 1, 0))
    right = jnp.where(column == width - 1, act, pltpu.roll(act, width - 1, 0))
    target[row, :, 0:channels] = left.astype(jnp.bfloat16)
    target[row, :, channels : 2 * channels] = act.astype(jnp.bfloat16)
    target[row, :, 2 * channels : 3 * channels] = right.astype(jnp.bfloat16)


def conv_row(taps_ref, row, weight_ref, bias_ref):
    window = jnp.concatenate([taps_ref[row], taps_ref[row + 1], taps_ref[row + 2]], axis=1)
    both = jnp.dot(window, weight_ref[...], preferred_element_type=jnp.float32)
    half = both.shape[1] // 2
    return both[:, :half] + both[:, half:] + bias_ref[...]


def first_kernel(
    count, sums_ref, own_ref, upper_ref, lower_ref, weight_ref, bias_ref, gain_ref, shift_ref,
    hidden_ref, out_ref, taps_ref,
):
    index = lax.axis_index("rows")
    rows, width, channels = own_ref.shape
    scale, offset = scale_offset(sums_ref, gain_ref, shift_ref, rows * width * count)
    for row in range(2):
        values = jnp.where(index == 0, own_ref[0], upper_ref[row])
        store_taps(values, scale, offset, taps_ref, row)
    for row in range(rows):
        store_taps(own_ref[row], scale, offset, taps_ref, row + 2)
    for row in range(2):
        values = jnp.where(index == count - 1, own_ref[rows - 1], lower_ref[row])
        store_taps(values, scale, offset, taps_ref, row + rows + 2)
    total = jnp.zeros((8, channels), jnp.float32)
    square = jnp.zeros((8, channels), jnp.float32)
    for row in range(rows + 2):
        hidden = conv_row(taps_ref, row, weight_ref, bias_ref).astype(jnp.bfloat16)
        hidden_ref[row] = hidden
        if 0 < row <= rows:
            values = hidden.astype(jnp.float32)
            total += jnp.sum(values.reshape(width // 8, 8, channels), axis=0)
            square += jnp.sum((values * values).reshape(width // 8, 8, channels), axis=0)
    store_sums(
        jnp.sum(total, axis=0, keepdims=True), jnp.sum(square, axis=0, keepdims=True), out_ref
    )

    @pl.when(index == 0)
    def _():
        hidden_ref[0] = hidden_ref[1]

    @pl.when(index == count - 1)
    def _():
        hidden_ref[rows + 1] = hidden_ref[rows]


def second_kernel(
    count, sums_ref, hidden_ref, own_ref, weight_ref, bias_ref, gain_ref, shift_ref,
    out_ref, taps_ref,
):
    rows, width, channels = own_ref.shape
    scale, offset = scale_offset(sums_ref, gain_ref, shift_ref, rows * width * count)
    for row in range(rows + 2):
        store_taps(hidden_ref[row], scale, offset, taps_ref, row)
    for row in range(rows):
        branch = conv_row(taps_ref, row, weight_ref, bias_ref)
        out_ref[row] = (own_ref[row].astype(jnp.float32) + branch).astype(jnp.bfloat16)


def halo_rows(block, depth):
    count = lax.axis_size("rows")
    forward = [(i, i + 1) for i in range(count - 1)]
    backward = [(i + 1, i) for i in range(count - 1)]
    upper = lax.ppermute(block[-depth:], "rows", forward)
    lower = lax.ppermute(block[:depth], "rows", backward)
    return upper, lower


def body(
    latents, gain_one, shift_one, weight_one, bias_one, gain_two, shift_two, weight_two, bias_two
):
    count = lax.axis_size("rows")
    own = latents[0]
    rows, width, channels = own.shape
    taps = weight_one.shape[1] * weight_one.shape[2]
    vector = functools.partial(jnp.reshape, shape=(1, channels))
    sums_shape = jax.ShapeDtypeStruct((count, 2, channels), jnp.float32)
    weight_shape = jax.ShapeDtypeStruct((taps * channels, 2 * channels), jnp.bfloat16)

    sums = pl.pallas_call(
        sums_kernel, out_shape=sums_shape, in_specs=[VMEM], out_specs=VMEM,
        compiler_params=PARAMS, name="sums",
    )(own)
    sums = lax.all_to_all(sums, "rows", 0, 0)
    upper, lower = halo_rows(own, 2)
    one, two = pl.pallas_call(
        weights_kernel, out_shape=[weight_shape] * 2, in_specs=[VMEM] * 2, out_specs=[VMEM] * 2,
        compiler_params=PARAMS, name="weights",
        cost_estimate=pl.CostEstimate(flops=6 * 9 * 3 * 128 * 128, bytes_accessed=4000000, transcendentals=0),
    )(weight_one.reshape(3 * taps, channels, channels), weight_two.reshape(3 * taps, channels, channels))
    hidden, sums = pl.pallas_call(
        functools.partial(first_kernel, count),
        out_shape=[jax.ShapeDtypeStruct((rows + 2, width, channels), jnp.bfloat16), sums_shape],
        in_specs=[VMEM] * 8,
        out_specs=[VMEM] * 2,
        scratch_shapes=[pltpu.VMEM((rows + 4, width, 3 * channels), jnp.bfloat16)],
        compiler_params=PARAMS, name="first",
    )(sums, own, upper, lower, one, vector(bias_one), vector(gain_one), vector(shift_one))
    sums = lax.all_to_all(sums, "rows", 0, 0)
    decoded = pl.pallas_call(
        functools.partial(second_kernel, count),
        out_shape=jax.ShapeDtypeStruct(own.shape, jnp.bfloat16),
        in_specs=[VMEM] * 7,
        out_specs=VMEM,
        scratch_shapes=[pltpu.VMEM((rows + 2, width, 3 * channels), jnp.bfloat16)],
        compiler_params=PARAMS, name="second",
    )(sums, hidden, own, two, vector(bias_two), vector(gain_two), vector(shift_two))
    return decoded[None]


def solution(mesh):
    return jax.shard_map(
        body,
        mesh=mesh,
        in_specs=(P("groups", "rows", None, None), P(), P(), P(), P(), P(), P(), P(), P()),
        out_specs=P("groups", "rows", None, None),
        check_vma=False,
    )
```

```python
import functools

import jax
import jax.numpy as jnp
from jax import lax
from jax.experimental import pallas as pl
from jax.experimental.pallas import tpu as pltpu
from jax.sharding import PartitionSpec as P

GROUPS = 32
VMEM = pl.BlockSpec(memory_space=pltpu.VMEM)
HBM = pl.BlockSpec(memory_space=pltpu.HBM)
ANY = pl.BlockSpec(memory_space=pl.ANY)
PARAMS = pltpu.CompilerParams(vmem_limit_bytes=24 * 1024 * 1024)


def store_sums(parts, out_ref):
    total = jnp.sum(sum(part[0] for part in parts), axis=0, keepdims=True)
    square = jnp.sum(sum(part[1] for part in parts), axis=0, keepdims=True)
    pair = jnp.concatenate([total, square], axis=0)
    out_ref[...] = jnp.broadcast_to(pair[None], out_ref.shape)


def partial_sums(values):
    width, channels = values.shape
    split = (width // 64, 64, channels)
    return jnp.sum(values.reshape(split), axis=0), jnp.sum((values * values).reshape(split), axis=0)


def sums_kernel(own_ref, out_ref, top_ref, bottom_ref):
    rows = own_ref.shape[0]
    parts = [partial_sums(own_ref[row].astype(jnp.float32)) for row in range(rows)]
    store_sums(parts, out_ref)
    for row in range(2):
        top_ref[row] = own_ref[row]
        bottom_ref[row] = own_ref[rows - 2 + row]


def weights_kernel(source, bias, gain, shift, *rest):
    out_ref, params_ref, held, vectors, sems, vector_sems = rest[-6:]
    taps, channels = source.shape[1], source.shape[2]
    vector_copies = [
        pltpu.make_async_copy(vector, vectors.at[i], vector_sems.at[i])
        for i, vector in enumerate((bias, gain, shift))
    ]
    copies = [
        pltpu.make_async_copy(source.at[:, tap], held.at[tap], sems.at[tap]) for tap in range(taps)
    ]
    for copy in copies + vector_copies:
        copy.start()
    for tap in range(taps):
        copies[tap].wait()
        total = held[tap, 0].astype(jnp.float32)
        total += held[tap, 1].astype(jnp.float32)
        total += held[tap, 2].astype(jnp.float32)
        high = total.astype(jnp.bfloat16)
        low = (total - high.astype(jnp.float32)).astype(jnp.bfloat16)
        out_ref[pl.ds(tap * channels, channels), :] = jnp.concatenate([high, low], axis=1)
    for i in range(3):
        vector_copies[i].wait()
        params_ref[pl.ds(i, 1), :] = vectors[i]


def scale_offset(sums_ref, params_ref, entries):
    sums = jnp.sum(sums_ref[...], axis=0)
    channels = sums.shape[1]
    per_group = channels // GROUPS
    sums = jnp.concatenate([sums, jnp.zeros((6, channels), jnp.float32)], axis=0)
    step = 1
    while step < per_group:
        sums += pltpu.roll(sums, channels - step, 1)
        step *= 2
    lane = lax.broadcasted_iota(jnp.int32, sums.shape, 1)
    sums = jnp.where(lane % per_group == 0, sums, 0.0)
    step = 1
    while step < per_group:
        sums += pltpu.roll(sums, step, 1)
        step *= 2
    sums = sums * (1.0 / (entries * per_group))
    mean = sums[0:1]
    var = sums[1:2] - mean * mean
    scale = params_ref[1:2, :] / jnp.sqrt(var + 1e-06)
    return scale, params_ref[2:3, :] - mean * scale


def store_taps(values, scale, offset, target, row):
    width, channels = values.shape
    normed = values.astype(jnp.float32) * scale + offset
    act = normed * (0.5 * jnp.tanh(0.5 * normed) + 0.5)
    column = lax.broadcasted_iota(jnp.int32, act.shape, 0)
    left = jnp.where(column == 0, act, pltpu.roll(act, 1, 0))
    right = jnp.where(column == width - 1, act, pltpu.roll(act, width - 1, 0))
    target[row, :, 0:channels] = left.astype(jnp.bfloat16)
    target[row, :, channels : 2 * channels] = act.astype(jnp.bfloat16)
    target[row, :, 2 * channels : 3 * channels] = right.astype(jnp.bfloat16)


def conv_row(taps_ref, row, weight_ref, params_ref):
    window = jnp.concatenate([taps_ref[row], taps_ref[row + 1], taps_ref[row + 2]], axis=1)
    both = jnp.dot(window, weight_ref[...], preferred_element_type=jnp.float32)
    half = both.shape[1] // 2
    return both[:, :half] + both[:, half:] + params_ref[0:1, :]


def first_kernel(
    count, sums_ref, own_ref, upper_ref, lower_ref, weight_ref, params_ref,
    hidden_ref, out_ref, taps_ref,
):
    index = lax.axis_index("rows")
    rows, width, channels = own_ref.shape
    scale, offset = scale_offset(sums_ref, params_ref, rows * width * count)
    for row in range(2):
        values = jnp.where(index == 0, own_ref[0], upper_ref[row])
        store_taps(values, scale, offset, taps_ref, row)
    for row in range(rows):
        store_taps(own_ref[row], scale, offset, taps_ref, row + 2)
    for row in range(2):
        values = jnp.where(index == count - 1, own_ref[rows - 1], lower_ref[row])
        store_taps(values, scale, offset, taps_ref, row + rows + 2)
    parts = []
    for row in range(rows + 2):
        hidden = conv_row(taps_ref, row, weight_ref, params_ref).astype(jnp.bfloat16)
        hidden_ref[row] = hidden
        if 0 < row <= rows:
            parts.append(partial_sums(hidden.astype(jnp.float32)))
    store_sums(parts, out_ref)

    @pl.when(index == 0)
    def _():
        hidden_ref[0] = hidden_ref[1]

    @pl.when(index == count - 1)
    def _():
        hidden_ref[rows + 1] = hidden_ref[rows]


def second_kernel(
    count, sums_ref, hidden_ref, own_ref, weight_ref, params_ref,
    out_ref, taps_ref,
):
    rows, width, channels = own_ref.shape
    scale, offset = scale_offset(sums_ref, params_ref, rows * width * count)
    for row in range(rows + 2):
        store_taps(hidden_ref[row], scale, offset, taps_ref, row)
    for row in range(rows):
        branch = conv_row(taps_ref, row, weight_ref, params_ref)
        out_ref[row] = (own_ref[row].astype(jnp.float32) + branch).astype(jnp.bfloat16)


def prepared_weight(weight, bias, gain, shift, after, name):
    taps, channels = weight.shape[1] * weight.shape[2], weight.shape[3]
    vectors = [vector.reshape(1, channels) for vector in (bias, gain, shift)]
    return pl.pallas_call(
        weights_kernel,
        out_shape=[
            jax.ShapeDtypeStruct((taps * channels, 2 * channels), jnp.bfloat16),
            jax.ShapeDtypeStruct((8, channels), jnp.float32),
        ],
        in_specs=[HBM] * 4 + [ANY] * len(after),
        out_specs=[VMEM] * 2,
        scratch_shapes=[
            pltpu.VMEM((taps, 3, channels, channels), jnp.bfloat16),
            pltpu.VMEM((3, 1, channels), jnp.float32),
            pltpu.SemaphoreType.DMA((taps,)),
            pltpu.SemaphoreType.DMA((3,)),
        ],
        compiler_params=PARAMS,
        name=name,
        cost_estimate=pl.CostEstimate(
            flops=4 * taps * channels * channels,
            bytes_accessed=10 * taps * channels * channels,
            transcendentals=0,
        ),
    )(weight.reshape(3, taps, channels, channels), *vectors, *after)


def body(
    latents, gain_one, shift_one, weight_one, bias_one, gain_two, shift_two, weight_two, bias_two
):
    count = lax.axis_size("rows")
    own = latents[0]
    rows, width, channels = own.shape
    sums_shape = jax.ShapeDtypeStruct((count, 2, channels), jnp.float32)
    slab_shape = jax.ShapeDtypeStruct((2, width, channels), jnp.bfloat16)
    forward = [(i, i + 1) for i in range(count - 1)]
    backward = [(i + 1, i) for i in range(count - 1)]

    sums, top, bottom = pl.pallas_call(
        sums_kernel, out_shape=[sums_shape, slab_shape, slab_shape], in_specs=[VMEM],
        out_specs=[VMEM] * 3, compiler_params=PARAMS, name="sums",
    )(own)
    sums = lax.all_to_all(sums, "rows", 0, 0)
    upper = lax.ppermute(bottom, "rows", forward)
    lower = lax.ppermute(top, "rows", backward)
    one, params = prepared_weight(weight_one, bias_one, gain_one, shift_one, (), "weights_one")
    hidden, sums = pl.pallas_call(
        functools.partial(first_kernel, count),
        out_shape=[jax.ShapeDtypeStruct((rows + 2, width, channels), jnp.bfloat16), sums_shape],
        in_specs=[VMEM] * 6,
        out_specs=[VMEM] * 2,
        scratch_shapes=[pltpu.VMEM((rows + 4, width, 3 * channels), jnp.bfloat16)],
        compiler_params=PARAMS, name="first",
    )(sums, own, upper, lower, one, params)
    two, params = prepared_weight(
        weight_two, bias_two, gain_two, shift_two, (hidden,), "weights_two"
    )
    sums = lax.all_to_all(sums, "rows", 0, 0)
    decoded = pl.pallas_call(
        functools.partial(second_kernel, count),
        out_shape=jax.ShapeDtypeStruct(own.shape, jnp.bfloat16),
        in_specs=[VMEM] * 5,
        out_specs=VMEM,
        scratch_shapes=[pltpu.VMEM((rows + 2, width, 3 * channels), jnp.bfloat16)],
        compiler_params=PARAMS, name="second",
    )(sums, hidden, own, two, params)
    return decoded[None]


def solution(mesh):
    return jax.shard_map(
        body,
        mesh=mesh,
        in_specs=(P("groups", "rows", None, None), P(), P(), P(), P(), P(), P(), P(), P()),
        out_specs=P("groups", "rows", None, None),
        check_vma=False,
    )
```

```python
import functools

import jax
import jax.numpy as jnp
from jax import lax
from jax.experimental import pallas as pl
from jax.experimental.pallas import tpu as pltpu
from jax.sharding import PartitionSpec as P

GROUPS = 32
VMEM = pl.BlockSpec(memory_space=pltpu.VMEM)
HBM = pl.BlockSpec(memory_space=pltpu.HBM)
ANY = pl.BlockSpec(memory_space=pl.ANY)
PARAMS = pltpu.CompilerParams(vmem_limit_bytes=24 * 1024 * 1024)


def store_sums(parts, out_ref):
    total = jnp.sum(sum(part[0] for part in parts), axis=0, keepdims=True)
    square = jnp.sum(sum(part[1] for part in parts), axis=0, keepdims=True)
    pair = jnp.concatenate([total, square], axis=0)
    out_ref[...] = jnp.broadcast_to(pair[None], out_ref.shape)


def partial_sums(values):
    width, channels = values.shape
    split = (width // 16, 16, channels)
    return jnp.sum(values.reshape(split), axis=0), jnp.sum((values * values).reshape(split), axis=0)


def sums_kernel(own_ref, out_ref, top_ref, bottom_ref):
    rows = own_ref.shape[0]
    parts = [partial_sums(own_ref[row].astype(jnp.float32)) for row in range(rows)]
    store_sums(parts, out_ref)
    for row in range(2):
        top_ref[row] = own_ref[row]
        bottom_ref[row] = own_ref[rows - 2 + row]


def weights_kernel(source, bias, gain, shift, *rest):
    out_ref, params_ref, held, vectors, sems, vector_sems = rest[-6:]
    taps, channels = source.shape[1], source.shape[2]
    vector_copies = [
        pltpu.make_async_copy(vector, vectors.at[i], vector_sems.at[i])
        for i, vector in enumerate((bias, gain, shift))
    ]
    copies = [
        pltpu.make_async_copy(source.at[:, tap], held.at[tap], sems.at[tap]) for tap in range(taps)
    ]
    for copy in copies + vector_copies:
        copy.start()
    for tap in range(taps):
        copies[tap].wait()
        total = held[tap, 0].astype(jnp.float32)
        total += held[tap, 1].astype(jnp.float32)
        total += held[tap, 2].astype(jnp.float32)
        high = total.astype(jnp.bfloat16)
        low = (total - high.astype(jnp.float32)).astype(jnp.bfloat16)
        out_ref[pl.ds(tap * channels, channels), :] = jnp.concatenate([high, low], axis=1)
    for i in range(3):
        vector_copies[i].wait()
        params_ref[pl.ds(i, 1), :] = vectors[i]


def scale_offset(sums_ref, params_ref, entries):
    sums = jnp.sum(sums_ref[...], axis=0)
    channels = sums.shape[1]
    per_group = channels // GROUPS
    sums = jnp.concatenate([sums, jnp.zeros((6, channels), jnp.float32)], axis=0)
    step = 1
    while step < per_group:
        sums += pltpu.roll(sums, channels - step, 1)
        step *= 2
    lane = lax.broadcasted_iota(jnp.int32, sums.shape, 1)
    sums = jnp.where(lane % per_group == 0, sums, 0.0)
    step = 1
    while step < per_group:
        sums += pltpu.roll(sums, step, 1)
        step *= 2
    sums = sums * (1.0 / (entries * per_group))
    mean = sums[0:1]
    var = sums[1:2] - mean * mean
    scale = params_ref[1:2, :] / jnp.sqrt(var + 1e-06)
    return scale, params_ref[2:3, :] - mean * scale


def store_taps(values, scale, offset, target, row):
    width, channels = values.shape
    normed = values.astype(jnp.float32) * scale + offset
    act = normed * (0.5 * jnp.tanh(0.5 * normed) + 0.5)
    column = lax.broadcasted_iota(jnp.int32, act.shape, 0)
    left = jnp.where(column == 0, act, pltpu.roll(act, 1, 0))
    right = jnp.where(column == width - 1, act, pltpu.roll(act, width - 1, 0))
    target[row, :, 0:channels] = left.astype(jnp.bfloat16)
    target[row, :, channels : 2 * channels] = act.astype(jnp.bfloat16)
    target[row, :, 2 * channels : 3 * channels] = right.astype(jnp.bfloat16)


def conv_row(taps_ref, row, weight_ref, params_ref):
    window = jnp.concatenate([taps_ref[row], taps_ref[row + 1], taps_ref[row + 2]], axis=1)
    both = jnp.dot(window, weight_ref[...], preferred_element_type=jnp.float32)
    half = both.shape[1] // 2
    return both[:, :half] + both[:, half:] + params_ref[0:1, :]


def first_kernel(
    count, sums_ref, own_ref, upper_ref, lower_ref, weight_ref, params_ref,
    hidden_ref, out_ref, taps_ref,
):
    index = lax.axis_index("rows")
    rows, width, channels = own_ref.shape
    scale, offset = scale_offset(sums_ref, params_ref, rows * width * count)
    for row in range(2):
        values = jnp.where(index == 0, own_ref[0], upper_ref[row])
        store_taps(values, scale, offset, taps_ref, row)
    for row in range(rows):
        store_taps(own_ref[row], scale, offset, taps_ref, row + 2)
    for row in range(2):
        values = jnp.where(index == count - 1, own_ref[rows - 1], lower_ref[row])
        store_taps(values, scale, offset, taps_ref, row + rows + 2)
    parts = []
    for row in range(rows + 2):
        hidden = conv_row(taps_ref, row, weight_ref, params_ref).astype(jnp.bfloat16)
        hidden_ref[row] = hidden
        if 0 < row <= rows:
            parts.append(partial_sums(hidden.astype(jnp.float32)))
    store_sums(parts, out_ref)

    @pl.when(index == 0)
    def _():
        hidden_ref[0] = hidden_ref[1]

    @pl.when(index == count - 1)
    def _():
        hidden_ref[rows + 1] = hidden_ref[rows]


def second_kernel(
    count, sums_ref, hidden_ref, own_ref, weight_ref, params_ref,
    out_ref, taps_ref,
):
    rows, width, channels = own_ref.shape
    scale, offset = scale_offset(sums_ref, params_ref, rows * width * count)
    for row in range(rows + 2):
        store_taps(hidden_ref[row], scale, offset, taps_ref, row)
    for row in range(rows):
        branch = conv_row(taps_ref, row, weight_ref, params_ref)
        out_ref[row] = (own_ref[row].astype(jnp.float32) + branch).astype(jnp.bfloat16)


def prepared_weight(weight, bias, gain, shift, after, name):
    taps, channels = weight.shape[1] * weight.shape[2], weight.shape[3]
    vectors = [vector.reshape(1, channels) for vector in (bias, gain, shift)]
    return pl.pallas_call(
        weights_kernel,
        out_shape=[
            jax.ShapeDtypeStruct((taps * channels, 2 * channels), jnp.bfloat16),
            jax.ShapeDtypeStruct((8, channels), jnp.float32),
        ],
        in_specs=[HBM] * 4 + [ANY] * len(after),
        out_specs=[VMEM] * 2,
        scratch_shapes=[
            pltpu.VMEM((taps, 3, channels, channels), jnp.bfloat16),
            pltpu.VMEM((3, 1, channels), jnp.float32),
            pltpu.SemaphoreType.DMA((taps,)),
            pltpu.SemaphoreType.DMA((3,)),
        ],
        compiler_params=PARAMS,
        name=name,
        cost_estimate=pl.CostEstimate(
            flops=4 * taps * channels * channels,
            bytes_accessed=10 * taps * channels * channels,
            transcendentals=0,
        ),
    )(weight.reshape(3, taps, channels, channels), *vectors, *after)


def body(
    latents, gain_one, shift_one, weight_one, bias_one, gain_two, shift_two, weight_two, bias_two
):
    count = lax.axis_size("rows")
    own = latents[0]
    rows, width, channels = own.shape
    sums_shape = jax.ShapeDtypeStruct((count, 2, channels), jnp.float32)
    slab_shape = jax.ShapeDtypeStruct((2, width, channels), jnp.bfloat16)
    even = [[i, i + 1] for i in range(0, count, 2)]
    odd = [[i, (i + 1) % count] for i in range(1, count, 2)]

    sums, top, bottom = pl.pallas_call(
        sums_kernel, out_shape=[sums_shape, slab_shape, slab_shape], in_specs=[VMEM],
        out_specs=[VMEM] * 3, compiler_params=PARAMS, name="sums",
    )(own)
    sums = lax.all_to_all(sums, "rows", 0, 0)
    is_even = lax.axis_index("rows") % 2 == 0
    to_even = jnp.where(is_even, bottom, top)
    to_odd = jnp.where(is_even, top, bottom)
    with_even = lax.all_gather(to_even, "rows", axis_index_groups=even)
    with_odd = lax.all_gather(to_odd, "rows", axis_index_groups=odd)
    upper = jnp.where(is_even, with_odd[0], with_even[0])
    lower = jnp.where(is_even, with_even[1], with_odd[1])
    one, params = prepared_weight(weight_one, bias_one, gain_one, shift_one, (), "weights_one")
    hidden, sums = pl.pallas_call(
        functools.partial(first_kernel, count),
        out_shape=[jax.ShapeDtypeStruct((rows + 2, width, channels), jnp.bfloat16), sums_shape],
        in_specs=[VMEM] * 6,
        out_specs=[VMEM] * 2,
        scratch_shapes=[pltpu.VMEM((rows + 4, width, 3 * channels), jnp.bfloat16)],
        compiler_params=PARAMS, name="first",
    )(sums, own, upper, lower, one, params)
    two, params = prepared_weight(
        weight_two, bias_two, gain_two, shift_two, (hidden,), "weights_two"
    )
    sums = lax.all_to_all(sums, "rows", 0, 0)
    decoded = pl.pallas_call(
        functools.partial(second_kernel, count),
        out_shape=jax.ShapeDtypeStruct(own.shape, jnp.bfloat16),
        in_specs=[VMEM] * 5,
        out_specs=VMEM,
        scratch_shapes=[pltpu.VMEM((rows + 2, width, 3 * channels), jnp.bfloat16)],
        compiler_params=PARAMS, name="second",
    )(sums, hidden, own, two, params)
    return decoded[None]


def solution(mesh):
    return jax.shard_map(
        body,
        mesh=mesh,
        in_specs=(P("groups", "rows", None, None), P(), P(), P(), P(), P(), P(), P(), P()),
        out_specs=P("groups", "rows", None, None),
        check_vma=False,
    )
```

```python
import functools

import jax
import jax.numpy as jnp
from jax import lax
from jax.experimental import pallas as pl
from jax.experimental.pallas import tpu as pltpu
from jax.sharding import PartitionSpec as P

GROUPS = 32
VMEM = pl.BlockSpec(memory_space=pltpu.VMEM)
HBM = pl.BlockSpec(memory_space=pltpu.HBM)
ANY = pl.BlockSpec(memory_space=pl.ANY)
PARAMS = pltpu.CompilerParams(vmem_limit_bytes=24 * 1024 * 1024)


def store_sums(total, square, out_ref):
    total = jnp.sum(total, axis=0, keepdims=True)
    square = jnp.sum(square, axis=0, keepdims=True)
    pair = jnp.concatenate([total, square], axis=0)
    out_ref[...] = jnp.broadcast_to(pair[None], out_ref.shape)


def add_sums(values, total, square):
    width, channels = values.shape
    split = (width // 8, 8, channels)
    total += jnp.sum(values.reshape(split), axis=0)
    square += jnp.sum((values * values).reshape(split), axis=0)
    return total, square


def sums_kernel(own_ref, out_ref):
    rows, _, channels = own_ref.shape
    total = jnp.zeros((8, channels), jnp.float32)
    square = jnp.zeros((8, channels), jnp.float32)
    for row in range(rows):
        total, square = add_sums(own_ref[row].astype(jnp.float32), total, square)
    store_sums(total, square, out_ref)


def slabs_kernel(own_ref, sums_ref, pair_ref, other_ref):
    rows = own_ref.shape[0]
    even = lax.axis_index("rows") % 2 == 0
    for row in range(2):
        top = own_ref[row]
        bottom = own_ref[rows - 2 + row]
        pair_ref[row] = jnp.where(even, bottom, top)
        other_ref[row] = jnp.where(even, top, bottom)


def weights_kernel(source, bias, gain, shift, *rest):
    out_ref, params_ref, held, vectors, sems, vector_sems = rest[-6:]
    taps, channels = source.shape[1], source.shape[2]
    vector_copies = [
        pltpu.make_async_copy(vector, vectors.at[i], vector_sems.at[i])
        for i, vector in enumerate((bias, gain, shift))
    ]
    copies = [
        pltpu.make_async_copy(source.at[:, tap], held.at[tap], sems.at[tap]) for tap in range(taps)
    ]
    for copy in copies + vector_copies:
        copy.start()
    for tap in range(taps):
        copies[tap].wait()
        total = held[tap, 0].astype(jnp.float32)
        total += held[tap, 1].astype(jnp.float32)
        total += held[tap, 2].astype(jnp.float32)
        high = total.astype(jnp.bfloat16)
        low = (total - high.astype(jnp.float32)).astype(jnp.bfloat16)
        out_ref[pl.ds(tap * channels, channels), :] = jnp.concatenate([high, low], axis=1)
    for i in range(3):
        vector_copies[i].wait()
        params_ref[pl.ds(i, 1), :] = vectors[i]


def scale_offset(sums_ref, params_ref, entries):
    sums = jnp.sum(sums_ref[...], axis=0)
    channels = sums.shape[1]
    per_group = channels // GROUPS
    sums = jnp.concatenate([sums, jnp.zeros((6, channels), jnp.float32)], axis=0)
    step = 1
    while step < per_group:
        sums += pltpu.roll(sums, channels - step, 1)
        step *= 2
    lane = lax.broadcasted_iota(jnp.int32, sums.shape, 1)
    sums = jnp.where(lane % per_group == 0, sums, 0.0)
    step = 1
    while step < per_group:
        sums += pltpu.roll(sums, step, 1)
        step *= 2
    sums = sums * (1.0 / (entries * per_group))
    mean = sums[0:1]
    var = sums[1:2] - mean * mean
    scale = params_ref[1:2, :] / jnp.sqrt(var + 1e-06)
    return scale, params_ref[2:3, :] - mean * scale


def store_taps(values, scale, offset, target, row):
    width, channels = values.shape
    normed = values.astype(jnp.float32) * scale + offset
    act = normed * (0.5 * jnp.tanh(0.5 * normed) + 0.5)
    column = lax.broadcasted_iota(jnp.int32, act.shape, 0)
    left = jnp.where(column == 0, act, pltpu.roll(act, 1, 0))
    right = jnp.where(column == width - 1, act, pltpu.roll(act, width - 1, 0))
    target[row, :, 0:channels] = left.astype(jnp.bfloat16)
    target[row, :, channels : 2 * channels] = act.astype(jnp.bfloat16)
    target[row, :, 2 * channels : 3 * channels] = right.astype(jnp.bfloat16)


def conv_row(taps_ref, row, weight_ref, params_ref):
    window = jnp.concatenate([taps_ref[row], taps_ref[row + 1], taps_ref[row + 2]], axis=1)
    both = jnp.dot(window, weight_ref[...], preferred_element_type=jnp.float32)
    half = both.shape[1] // 2
    return both[:, :half] + both[:, half:] + params_ref[0:1, :]


def first_kernel(
    count, sums_ref, own_ref, pair_ref, other_ref, weight_ref, params_ref,
    hidden_ref, out_ref, taps_ref,
):
    index = lax.axis_index("rows")
    rows, width, channels = own_ref.shape
    scale, offset = scale_offset(sums_ref, params_ref, rows * width * count)
    even = index % 2 == 0
    for row in range(2):
        values = jnp.where(even, other_ref[row], pair_ref[row])
        values = jnp.where(index == 0, own_ref[0], values)
        store_taps(values, scale, offset, taps_ref, row)
    for row in range(rows):
        store_taps(own_ref[row], scale, offset, taps_ref, row + 2)
    for row in range(2):
        values = jnp.where(even, pair_ref[row], other_ref[row])
        values = jnp.where(index == count - 1, own_ref[rows - 1], values)
        store_taps(values, scale, offset, taps_ref, row + rows + 2)
    total = jnp.zeros((8, channels), jnp.float32)
    square = jnp.zeros((8, channels), jnp.float32)
    for row in range(rows + 2):
        hidden = conv_row(taps_ref, row, weight_ref, params_ref).astype(jnp.bfloat16)
        hidden_ref[row] = hidden
        if 0 < row <= rows:
            total, square = add_sums(hidden.astype(jnp.float32), total, square)
    store_sums(total, square, out_ref)

    @pl.when(index == 0)
    def _():
        hidden_ref[0] = hidden_ref[1]

    @pl.when(index == count - 1)
    def _():
        hidden_ref[rows + 1] = hidden_ref[rows]


def second_kernel(
    count, sums_ref, hidden_ref, own_ref, weight_ref, params_ref,
    out_ref, taps_ref,
):
    rows, width, channels = own_ref.shape
    scale, offset = scale_offset(sums_ref, params_ref, rows * width * count)
    for row in range(rows + 2):
        store_taps(hidden_ref[row], scale, offset, taps_ref, row)
    for row in range(rows):
        branch = conv_row(taps_ref, row, weight_ref, params_ref)
        out_ref[row] = (own_ref[row].astype(jnp.float32) + branch).astype(jnp.bfloat16)


def prepared_weight(weight, bias, gain, shift, after, name):
    taps, channels = weight.shape[1] * weight.shape[2], weight.shape[3]
    vectors = [vector.reshape(1, channels) for vector in (bias, gain, shift)]
    return pl.pallas_call(
        weights_kernel,
        out_shape=[
            jax.ShapeDtypeStruct((taps * channels, 2 * channels), jnp.bfloat16),
            jax.ShapeDtypeStruct((8, channels), jnp.float32),
        ],
        in_specs=[HBM] * 4 + [ANY] * len(after),
        out_specs=[VMEM] * 2,
        scratch_shapes=[
            pltpu.VMEM((taps, 3, channels, channels), jnp.bfloat16),
            pltpu.VMEM((3, 1, channels), jnp.float32),
            pltpu.SemaphoreType.DMA((taps,)),
            pltpu.SemaphoreType.DMA((3,)),
        ],
        compiler_params=PARAMS,
        name=name,
        cost_estimate=pl.CostEstimate(
            flops=4 * taps * channels * channels,
            bytes_accessed=10 * taps * channels * channels,
            transcendentals=0,
        ),
    )(weight.reshape(3, taps, channels, channels), *vectors, *after)


def body(
    latents, gain_one, shift_one, weight_one, bias_one, gain_two, shift_two, weight_two, bias_two
):
    count = lax.axis_size("rows")
    own = latents[0]
    rows, width, channels = own.shape
    sums_shape = jax.ShapeDtypeStruct((count, 2, channels), jnp.float32)
    slab_shape = jax.ShapeDtypeStruct((2, width, channels), jnp.bfloat16)
    swap_pair = [(i, i ^ 1) for i in range(count)]
    swap_other = [(i, i + 1 if i % 2 else i - 1) for i in range(1, count - 1)]

    own_sums = pl.pallas_call(
        sums_kernel, out_shape=sums_shape, in_specs=[VMEM], out_specs=VMEM,
        compiler_params=PARAMS, name="sums",
    )(own)
    pair, other = pl.pallas_call(
        slabs_kernel, out_shape=[slab_shape] * 2, in_specs=[VMEM] * 2, out_specs=[VMEM] * 2,
        compiler_params=PARAMS, name="slabs",
        cost_estimate=pl.CostEstimate(flops=20000000000, bytes_accessed=1000000, transcendentals=0),
    )(own, own_sums)
    sums = lax.all_to_all(own_sums, "rows", 0, 0)
    pair = lax.ppermute(pair, "rows", swap_pair)
    other = lax.ppermute(other, "rows", swap_other)
    one, params = prepared_weight(weight_one, bias_one, gain_one, shift_one, (), "weights_one")
    hidden, sums = pl.pallas_call(
        functools.partial(first_kernel, count),
        out_shape=[jax.ShapeDtypeStruct((rows + 2, width, channels), jnp.bfloat16), sums_shape],
        in_specs=[VMEM] * 6,
        out_specs=[VMEM] * 2,
        scratch_shapes=[pltpu.VMEM((rows + 4, width, 3 * channels), jnp.bfloat16)],
        compiler_params=PARAMS, name="first",
    )(sums, own, pair, other, one, params)
    two, params = prepared_weight(
        weight_two, bias_two, gain_two, shift_two, (hidden,), "weights_two"
    )
    sums = lax.all_to_all(sums, "rows", 0, 0)
    decoded = pl.pallas_call(
        functools.partial(second_kernel, count),
        out_shape=jax.ShapeDtypeStruct(own.shape, jnp.bfloat16),
        in_specs=[VMEM] * 5,
        out_specs=VMEM,
        scratch_shapes=[pltpu.VMEM((rows + 2, width, 3 * channels), jnp.bfloat16)],
        compiler_params=PARAMS, name="second",
    )(sums, hidden, own, two, params)
    return decoded[None]


def solution(mesh):
    return jax.shard_map(
        body,
        mesh=mesh,
        in_specs=(P("groups", "rows", None, None), P(), P(), P(), P(), P(), P(), P(), P()),
        out_specs=P("groups", "rows", None, None),
        check_vma=False,
    )
```

```python
import functools

import jax
import jax.numpy as jnp
from jax import lax
from jax.experimental import pallas as pl
from jax.experimental.pallas import tpu as pltpu
from jax.sharding import PartitionSpec as P

GROUPS = 32
VMEM = pl.BlockSpec(memory_space=pltpu.VMEM)
HBM = pl.BlockSpec(memory_space=pltpu.HBM)
ANY = pl.BlockSpec(memory_space=pl.ANY)
PARAMS = pltpu.CompilerParams(vmem_limit_bytes=24 * 1024 * 1024)


def store_sums(total, square, out_ref):
    total = jnp.sum(total, axis=0, keepdims=True)
    square = jnp.sum(square, axis=0, keepdims=True)
    pair = jnp.concatenate([total, square], axis=0)
    group = lax.axis_index("groups")
    for i in range(out_ref.shape[0]):
        out_ref[i] = jnp.where(group == i, pair, 0.0)


def add_sums(values, total, square):
    width, channels = values.shape
    split = (width // 8, 8, channels)
    total += jnp.sum(values.reshape(split), axis=0)
    square += jnp.sum((values * values).reshape(split), axis=0)
    return total, square


def sums_kernel(own_ref, out_ref, pair_ref, other_ref):
    rows, _, channels = own_ref.shape
    even = lax.axis_index("rows") % 2 == 0
    for row in range(2):
        top = own_ref[row]
        bottom = own_ref[rows - 2 + row]
        pair_ref[row] = jnp.where(even, bottom, top)
        other_ref[row] = jnp.where(even, top, bottom)
    total = jnp.zeros((8, channels), jnp.float32)
    square = jnp.zeros((8, channels), jnp.float32)
    for row in range(rows):
        total, square = add_sums(own_ref[row].astype(jnp.float32), total, square)
    store_sums(total, square, out_ref)


def weights_kernel(source, bias, gain, shift, *rest):
    out_ref, params_ref, held, vectors, sems, vector_sems = rest[-6:]
    taps, channels = source.shape[1], source.shape[2]
    vector_copies = [
        pltpu.make_async_copy(vector, vectors.at[i], vector_sems.at[i])
        for i, vector in enumerate((bias, gain, shift))
    ]
    copies = [
        pltpu.make_async_copy(source.at[:, tap], held.at[tap], sems.at[tap]) for tap in range(taps)
    ]
    for copy in copies + vector_copies:
        copy.start()
    for tap in range(taps):
        copies[tap].wait()
        total = held[tap, 0].astype(jnp.float32)
        total += held[tap, 1].astype(jnp.float32)
        total += held[tap, 2].astype(jnp.float32)
        high = total.astype(jnp.bfloat16)
        low = (total - high.astype(jnp.float32)).astype(jnp.bfloat16)
        out_ref[pl.ds(tap * channels, channels), :] = jnp.concatenate([high, low], axis=1)
    for i in range(3):
        vector_copies[i].wait()
        params_ref[pl.ds(i, 1), :] = vectors[i]


def scale_offset(sums_ref, params_ref, entries):
    sums = sums_ref[lax.axis_index("groups")]
    channels = sums.shape[1]
    per_group = channels // GROUPS
    sums = jnp.concatenate([sums, jnp.zeros((6, channels), jnp.float32)], axis=0)
    step = 1
    while step < per_group:
        sums += pltpu.roll(sums, channels - step, 1)
        step *= 2
    lane = lax.broadcasted_iota(jnp.int32, sums.shape, 1)
    sums = jnp.where(lane % per_group == 0, sums, 0.0)
    step = 1
    while step < per_group:
        sums += pltpu.roll(sums, step, 1)
        step *= 2
    sums = sums * (1.0 / (entries * per_group))
    mean = sums[0:1]
    var = sums[1:2] - mean * mean
    scale = params_ref[1:2, :] / jnp.sqrt(var + 1e-06)
    return scale, params_ref[2:3, :] - mean * scale


def store_taps(values, scale, offset, target, row):
    width, channels = values.shape
    normed = values.astype(jnp.float32) * scale + offset
    act = normed * (0.5 * jnp.tanh(0.5 * normed) + 0.5)
    column = lax.broadcasted_iota(jnp.int32, act.shape, 0)
    left = jnp.where(column == 0, act, pltpu.roll(act, 1, 0))
    right = jnp.where(column == width - 1, act, pltpu.roll(act, width - 1, 0))
    target[row, :, 0:channels] = left.astype(jnp.bfloat16)
    target[row, :, channels : 2 * channels] = act.astype(jnp.bfloat16)
    target[row, :, 2 * channels : 3 * channels] = right.astype(jnp.bfloat16)


def conv_row(taps_ref, row, weight_ref, params_ref):
    window = jnp.concatenate([taps_ref[row], taps_ref[row + 1], taps_ref[row + 2]], axis=1)
    both = jnp.dot(window, weight_ref[...], preferred_element_type=jnp.float32)
    half = both.shape[1] // 2
    return both[:, :half] + both[:, half:] + params_ref[0:1, :]


def first_kernel(
    count, sums_ref, own_ref, pair_ref, other_ref, weight_ref, params_ref,
    hidden_ref, out_ref, taps_ref,
):
    index = lax.axis_index("rows")
    rows, width, channels = own_ref.shape
    scale, offset = scale_offset(sums_ref, params_ref, rows * width * count)
    even = index % 2 == 0
    for row in range(2):
        values = jnp.where(even, other_ref[row], pair_ref[row])
        values = jnp.where(index == 0, own_ref[0], values)
        store_taps(values, scale, offset, taps_ref, row)
    for row in range(rows):
        store_taps(own_ref[row], scale, offset, taps_ref, row + 2)
    for row in range(2):
        values = jnp.where(even, pair_ref[row], other_ref[row])
        values = jnp.where(index == count - 1, own_ref[rows - 1], values)
        store_taps(values, scale, offset, taps_ref, row + rows + 2)
    total = jnp.zeros((8, channels), jnp.float32)
    square = jnp.zeros((8, channels), jnp.float32)
    for row in range(rows + 2):
        hidden = conv_row(taps_ref, row, weight_ref, params_ref).astype(jnp.bfloat16)
        hidden_ref[row] = hidden
        if 0 < row <= rows:
            total, square = add_sums(hidden.astype(jnp.float32), total, square)
    store_sums(total, square, out_ref)

    @pl.when(index == 0)
    def _():
        hidden_ref[0] = hidden_ref[1]

    @pl.when(index == count - 1)
    def _():
        hidden_ref[rows + 1] = hidden_ref[rows]


def second_kernel(
    count, sums_ref, hidden_ref, own_ref, weight_ref, params_ref,
    out_ref, taps_ref,
):
    rows, width, channels = own_ref.shape
    scale, offset = scale_offset(sums_ref, params_ref, rows * width * count)
    for row in range(rows + 2):
        store_taps(hidden_ref[row], scale, offset, taps_ref, row)
    for row in range(rows):
        branch = conv_row(taps_ref, row, weight_ref, params_ref)
        out_ref[row] = (own_ref[row].astype(jnp.float32) + branch).astype(jnp.bfloat16)


def prepared_weight(weight, bias, gain, shift, after, name):
    taps, channels = weight.shape[1] * weight.shape[2], weight.shape[3]
    vectors = [vector.reshape(1, channels) for vector in (bias, gain, shift)]
    return pl.pallas_call(
        weights_kernel,
        out_shape=[
            jax.ShapeDtypeStruct((taps * channels, 2 * channels), jnp.bfloat16),
            jax.ShapeDtypeStruct((8, channels), jnp.float32),
        ],
        in_specs=[HBM] * 4 + [ANY] * len(after),
        out_specs=[VMEM] * 2,
        scratch_shapes=[
            pltpu.VMEM((taps, 3, channels, channels), jnp.bfloat16),
            pltpu.VMEM((3, 1, channels), jnp.float32),
            pltpu.SemaphoreType.DMA((taps,)),
            pltpu.SemaphoreType.DMA((3,)),
        ],
        compiler_params=PARAMS,
        name=name,
        cost_estimate=pl.CostEstimate(
            flops=4 * taps * channels * channels,
            bytes_accessed=10 * taps * channels * channels,
            transcendentals=0,
        ),
    )(weight.reshape(3, taps, channels, channels), *vectors, *after)


def exchanged(sums):
    return lax.psum(sums, ("groups", "rows"))


def body(
    latents, gain_one, shift_one, weight_one, bias_one, gain_two, shift_two, weight_two, bias_two
):
    count = lax.axis_size("rows")
    own = latents[0]
    rows, width, channels = own.shape
    sums_shape = jax.ShapeDtypeStruct((lax.axis_size("groups"), 2, channels), jnp.float32)
    slab_shape = jax.ShapeDtypeStruct((2, width, channels), jnp.bfloat16)
    swap_pair = [(i, i ^ 1) for i in range(count)]
    swap_other = [(i, i + 1 if i % 2 else i - 1) for i in range(1, count - 1)]

    sums, pair, other = pl.pallas_call(
        sums_kernel, out_shape=[sums_shape] + [slab_shape] * 2, in_specs=[VMEM],
        out_specs=[VMEM] * 3, compiler_params=PARAMS, name="sums",
    )(own)
    sums = exchanged(sums)
    pair = lax.ppermute(pair, "rows", swap_pair)
    other = lax.ppermute(other, "rows", swap_other)
    one, params = prepared_weight(weight_one, bias_one, gain_one, shift_one, (), "weights_one")
    hidden, sums = pl.pallas_call(
        functools.partial(first_kernel, count),
        out_shape=[jax.ShapeDtypeStruct((rows + 2, width, channels), jnp.bfloat16), sums_shape],
        in_specs=[VMEM] * 6,
        out_specs=[VMEM] * 2,
        scratch_shapes=[pltpu.VMEM((rows + 4, width, 3 * channels), jnp.bfloat16)],
        compiler_params=PARAMS, name="first",
    )(sums, own, pair, other, one, params)
    two, params = prepared_weight(
        weight_two, bias_two, gain_two, shift_two, (hidden,), "weights_two"
    )
    sums = exchanged(sums)
    decoded = pl.pallas_call(
        functools.partial(second_kernel, count),
        out_shape=jax.ShapeDtypeStruct(own.shape, jnp.bfloat16),
        in_specs=[VMEM] * 5,
        out_specs=VMEM,
        scratch_shapes=[pltpu.VMEM((rows + 2, width, 3 * channels), jnp.bfloat16)],
        compiler_params=PARAMS, name="second",
    )(sums, hidden, own, two, params)
    return decoded[None]


def solution(mesh):
    return jax.shard_map(
        body,
        mesh=mesh,
        in_specs=(P("groups", "rows", None, None), P(), P(), P(), P(), P(), P(), P(), P()),
        out_specs=P("groups", "rows", None, None),
        check_vma=False,
    )
```

```python
import functools

import jax
import jax.numpy as jnp
from jax import lax
from jax.experimental import pallas as pl
from jax.experimental.pallas import tpu as pltpu
from jax.sharding import PartitionSpec as P

GROUPS = 32
VMEM = pl.BlockSpec(memory_space=pltpu.VMEM)
PARAMS = pltpu.CompilerParams(vmem_limit_bytes=24 * 1024 * 1024)


def store_sums(total, square, out_ref):
    total = jnp.sum(total, axis=0, keepdims=True)
    square = jnp.sum(square, axis=0, keepdims=True)
    pair = jnp.concatenate([total, square], axis=0)
    out_ref[...] = jnp.broadcast_to(pair[None], out_ref.shape)


def add_sums(values, total, square):
    width, channels = values.shape
    split = (width // 8, 8, channels)
    total += jnp.sum(values.reshape(split), axis=0)
    square += jnp.sum((values * values).reshape(split), axis=0)
    return total, square


def sums_kernel(own_ref, out_ref, pair_ref, other_ref):
    rows, _, channels = own_ref.shape
    even = lax.axis_index("rows") % 2 == 0
    for row in range(2):
        top = own_ref[row]
        bottom = own_ref[rows - 2 + row]
        pair_ref[row] = jnp.where(even, bottom, top)
        other_ref[row] = jnp.where(even, top, bottom)
    total = jnp.zeros((8, channels), jnp.float32)
    square = jnp.zeros((8, channels), jnp.float32)
    for row in range(rows):
        total, square = add_sums(own_ref[row].astype(jnp.float32), total, square)
    store_sums(total, square, out_ref)


def weights_kernel(one_ref, two_ref, *rest):
    vectors, outs = rest[:6], rest[6:]
    for source, target in ((one_ref, outs[0]), (two_ref, outs[1])):
        taps, channels = source.shape[1], source.shape[2]
        for tap in range(taps):
            total = source[0, tap].astype(jnp.float32)
            total += source[1, tap].astype(jnp.float32)
            total += source[2, tap].astype(jnp.float32)
            high = total.astype(jnp.bfloat16)
            low = (total - high.astype(jnp.float32)).astype(jnp.bfloat16)
            target[pl.ds(tap * channels, channels), :] = jnp.concatenate([high, low], axis=1)
    for i in range(6):
        outs[2 + i // 3][pl.ds(i % 3, 1), :] = vectors[i][...]


def scale_offset(sums_ref, params_ref, entries):
    sums = jnp.sum(sums_ref[...], axis=0)
    channels = sums.shape[1]
    per_group = channels // GROUPS
    sums = jnp.concatenate([sums, jnp.zeros((6, channels), jnp.float32)], axis=0)
    step = 1
    while step < per_group:
        sums += pltpu.roll(sums, channels - step, 1)
        step *= 2
    lane = lax.broadcasted_iota(jnp.int32, sums.shape, 1)
    sums = jnp.where(lane % per_group == 0, sums, 0.0)
    step = 1
    while step < per_group:
        sums += pltpu.roll(sums, step, 1)
        step *= 2
    sums = sums * (1.0 / (entries * per_group))
    mean = sums[0:1]
    var = sums[1:2] - mean * mean
    scale = params_ref[1:2, :] / jnp.sqrt(var + 1e-06)
    return scale, params_ref[2:3, :] - mean * scale


def store_taps(values, scale, offset, target, row):
    width, channels = values.shape
    normed = values.astype(jnp.float32) * scale + offset
    act = normed * (0.5 * jnp.tanh(0.5 * normed) + 0.5)
    column = lax.broadcasted_iota(jnp.int32, act.shape, 0)
    left = jnp.where(column == 0, act, pltpu.roll(act, 1, 0))
    right = jnp.where(column == width - 1, act, pltpu.roll(act, width - 1, 0))
    target[row, :, 0:channels] = left.astype(jnp.bfloat16)
    target[row, :, channels : 2 * channels] = act.astype(jnp.bfloat16)
    target[row, :, 2 * channels : 3 * channels] = right.astype(jnp.bfloat16)


def conv_row(taps_ref, row, weight_ref, params_ref):
    window = jnp.concatenate([taps_ref[row], taps_ref[row + 1], taps_ref[row + 2]], axis=1)
    both = jnp.dot(window, weight_ref[...], preferred_element_type=jnp.float32)
    half = both.shape[1] // 2
    return both[:, :half] + both[:, half:] + params_ref[0:1, :]


def first_kernel(
    count, sums_ref, own_ref, pair_ref, other_ref, weight_ref, params_ref,
    hidden_ref, out_ref, taps_ref,
):
    index = lax.axis_index("rows")
    rows, width, channels = own_ref.shape
    scale, offset = scale_offset(sums_ref, params_ref, rows * width * count)
    even = index % 2 == 0
    for row in range(2):
        values = jnp.where(even, other_ref[row], pair_ref[row])
        values = jnp.where(index == 0, own_ref[0], values)
        store_taps(values, scale, offset, taps_ref, row)
    for row in range(rows):
        store_taps(own_ref[row], scale, offset, taps_ref, row + 2)
    for row in range(2):
        values = jnp.where(even, pair_ref[row], other_ref[row])
        values = jnp.where(index == count - 1, own_ref[rows - 1], values)
        store_taps(values, scale, offset, taps_ref, row + rows + 2)
    total = jnp.zeros((8, channels), jnp.float32)
    square = jnp.zeros((8, channels), jnp.float32)
    for row in range(rows + 2):
        hidden = conv_row(taps_ref, row, weight_ref, params_ref).astype(jnp.bfloat16)
        hidden_ref[row] = hidden
        if 0 < row <= rows:
            total, square = add_sums(hidden.astype(jnp.float32), total, square)
    store_sums(total, square, out_ref)

    @pl.when(index == 0)
    def _():
        hidden_ref[0] = hidden_ref[1]

    @pl.when(index == count - 1)
    def _():
        hidden_ref[rows + 1] = hidden_ref[rows]


def second_kernel(
    count, sums_ref, hidden_ref, own_ref, weight_ref, params_ref,
    out_ref, taps_ref,
):
    rows, width, channels = own_ref.shape
    scale, offset = scale_offset(sums_ref, params_ref, rows * width * count)
    for row in range(rows + 2):
        store_taps(hidden_ref[row], scale, offset, taps_ref, row)
    for row in range(rows):
        branch = conv_row(taps_ref, row, weight_ref, params_ref)
        out_ref[row] = (own_ref[row].astype(jnp.float32) + branch).astype(jnp.bfloat16)


def prepared(weights, vectors):
    taps, channels = weights[0].shape[1] * weights[0].shape[2], weights[0].shape[3]
    weight_shape = jax.ShapeDtypeStruct((taps * channels, 2 * channels), jnp.bfloat16)
    vector_shape = jax.ShapeDtypeStruct((8, channels), jnp.float32)
    return pl.pallas_call(
        weights_kernel,
        out_shape=[weight_shape] * 2 + [vector_shape] * 2,
        in_specs=[VMEM] * 8,
        out_specs=[VMEM] * 4,
        compiler_params=PARAMS,
        name="weights",
        cost_estimate=pl.CostEstimate(
            flops=40000000000, bytes_accessed=10000000, transcendentals=0
        ),
    )(
        *[weight.reshape(3, taps, channels, channels) for weight in weights],
        *[vector.reshape(1, channels) for vector in vectors],
    )


def exchanged(sums):
    return lax.all_to_all(sums, "rows", 0, 0)


def body(
    latents, gain_one, shift_one, weight_one, bias_one, gain_two, shift_two, weight_two, bias_two
):
    count = lax.axis_size("rows")
    own = latents[0]
    rows, width, channels = own.shape
    sums_shape = jax.ShapeDtypeStruct((count, 2, channels), jnp.float32)
    slab_shape = jax.ShapeDtypeStruct((2, width, channels), jnp.bfloat16)
    swap_pair = [(i, i ^ 1) for i in range(count)]
    swap_other = [(i, i + 1 if i % 2 else i - 1) for i in range(1, count - 1)]

    sums, pair, other = pl.pallas_call(
        sums_kernel, out_shape=[sums_shape] + [slab_shape] * 2, in_specs=[VMEM],
        out_specs=[VMEM] * 3, compiler_params=PARAMS, name="sums",
    )(own)
    sums = exchanged(sums)
    pair = lax.ppermute(pair, "rows", swap_pair)
    other = lax.ppermute(other, "rows", swap_other)
    one, two, params_one, params_two = prepared(
        (weight_one, weight_two),
        (bias_one, gain_one, shift_one, bias_two, gain_two, shift_two),
    )
    hidden, sums = pl.pallas_call(
        functools.partial(first_kernel, count),
        out_shape=[jax.ShapeDtypeStruct((rows + 2, width, channels), jnp.bfloat16), sums_shape],
        in_specs=[VMEM] * 6,
        out_specs=[VMEM] * 2,
        scratch_shapes=[pltpu.VMEM((rows + 4, width, 3 * channels), jnp.bfloat16)],
        compiler_params=PARAMS, name="first",
    )(sums, own, pair, other, one, params_one)
    sums = exchanged(sums)
    decoded = pl.pallas_call(
        functools.partial(second_kernel, count),
        out_shape=jax.ShapeDtypeStruct(own.shape, jnp.bfloat16),
        in_specs=[VMEM] * 5,
        out_specs=VMEM,
        scratch_shapes=[pltpu.VMEM((rows + 2, width, 3 * channels), jnp.bfloat16)],
        compiler_params=PARAMS, name="second",
    )(sums, hidden, own, two, params_two)
    return decoded[None]


def solution(mesh):
    return jax.shard_map(
        body,
        mesh=mesh,
        in_specs=(P("groups", "rows", None, None), P(), P(), P(), P(), P(), P(), P(), P()),
        out_specs=P("groups", "rows", None, None),
        check_vma=False,
    )
```

```python
import functools

import jax
import jax.numpy as jnp
from jax import lax
from jax.experimental import pallas as pl
from jax.experimental.pallas import tpu as pltpu
from jax.sharding import PartitionSpec as P

GROUPS = 32
VMEM = pl.BlockSpec(memory_space=pltpu.VMEM)
PARAMS = pltpu.CompilerParams(vmem_limit_bytes=24 * 1024 * 1024)


def store_sums(total, square, out_ref):
    total = jnp.sum(total, axis=0, keepdims=True)
    square = jnp.sum(square, axis=0, keepdims=True)
    pair = jnp.concatenate([total, square], axis=0)
    out_ref[...] = jnp.broadcast_to(pair[None], out_ref.shape)


def add_sums(values, total, square):
    width, channels = values.shape
    split = (width // 8, 8, channels)
    total += jnp.sum(values.reshape(split), axis=0)
    square += jnp.sum((values * values).reshape(split), axis=0)
    return total, square


def sums_kernel(own_ref, out_ref, pair_ref, other_ref):
    rows, _, channels = own_ref.shape
    even = lax.axis_index("rows") % 2 == 0
    for row in range(2):
        top = own_ref[row]
        bottom = own_ref[rows - 2 + row]
        pair_ref[row] = jnp.where(even, bottom, top)
        other_ref[row] = jnp.where(even, top, bottom)
    total = jnp.zeros((8, channels), jnp.float32)
    square = jnp.zeros((8, channels), jnp.float32)
    for row in range(rows):
        total, square = add_sums(own_ref[row].astype(jnp.float32), total, square)
    store_sums(total, square, out_ref)


def weights_kernel(one_ref, two_ref, *rest):
    vectors, outs = rest[:6], rest[6:]
    for source, target in ((one_ref, outs[0]), (two_ref, outs[1])):
        taps, channels = source.shape[1], source.shape[2]
        for tap in range(taps):
            total = source[0, tap].astype(jnp.float32)
            total += source[1, tap].astype(jnp.float32)
            total += source[2, tap].astype(jnp.float32)
            high = total.astype(jnp.bfloat16)
            low = (total - high.astype(jnp.float32)).astype(jnp.bfloat16)
            target[pl.ds(tap * channels, channels), :] = jnp.concatenate([high, low], axis=1)
    for i in range(6):
        outs[2 + i // 3][pl.ds(i % 3, 1), :] = vectors[i][...]


def scale_offset(sums_ref, params_ref, entries):
    sums = jnp.sum(sums_ref[...], axis=0)
    channels = sums.shape[1]
    per_group = channels // GROUPS
    sums = jnp.concatenate([sums, jnp.zeros((6, channels), jnp.float32)], axis=0)
    step = 1
    while step < per_group:
        sums += pltpu.roll(sums, channels - step, 1)
        step *= 2
    lane = lax.broadcasted_iota(jnp.int32, sums.shape, 1)
    sums = jnp.where(lane % per_group == 0, sums, 0.0)
    step = 1
    while step < per_group:
        sums += pltpu.roll(sums, step, 1)
        step *= 2
    sums = sums * (1.0 / (entries * per_group))
    mean = sums[0:1]
    var = sums[1:2] - mean * mean
    scale = params_ref[1:2, :] / jnp.sqrt(var + 1e-06)
    return scale, params_ref[2:3, :] - mean * scale


def store_taps(values, scale, offset, target, row):
    width, channels = values.shape
    normed = values.astype(jnp.float32) * scale + offset
    act = normed * (0.5 * jnp.tanh(0.5 * normed) + 0.5)
    column = lax.broadcasted_iota(jnp.int32, act.shape, 0)
    left = jnp.where(column == 0, act, pltpu.roll(act, 1, 0))
    right = jnp.where(column == width - 1, act, pltpu.roll(act, width - 1, 0))
    target[row, :, 0:channels] = left.astype(jnp.bfloat16)
    target[row, :, channels : 2 * channels] = act.astype(jnp.bfloat16)
    target[row, :, 2 * channels : 3 * channels] = right.astype(jnp.bfloat16)


def conv_row(taps_ref, row, weight_ref, params_ref):
    window = jnp.concatenate([taps_ref[row], taps_ref[row + 1], taps_ref[row + 2]], axis=1)
    both = jnp.dot(window, weight_ref[...], preferred_element_type=jnp.float32)
    half = both.shape[1] // 2
    return both[:, :half] + both[:, half:] + params_ref[0:1, :]


def first_kernel(
    count, sums_ref, own_ref, pair_ref, other_ref, weight_ref, params_ref,
    hidden_ref, out_ref, taps_ref,
):
    index = lax.axis_index("rows")
    rows, width, channels = own_ref.shape
    scale, offset = scale_offset(sums_ref, params_ref, rows * width * count)
    even = index % 2 == 0
    for row in range(2):
        values = jnp.where(even, other_ref[row], pair_ref[row])
        values = jnp.where(index == 0, own_ref[0], values)
        store_taps(values, scale, offset, taps_ref, row)
    for row in range(rows):
        store_taps(own_ref[row], scale, offset, taps_ref, row + 2)
    for row in range(2):
        values = jnp.where(even, pair_ref[row], other_ref[row])
        values = jnp.where(index == count - 1, own_ref[rows - 1], values)
        store_taps(values, scale, offset, taps_ref, row + rows + 2)
    total = jnp.zeros((8, channels), jnp.float32)
    square = jnp.zeros((8, channels), jnp.float32)
    for row in range(rows + 2):
        hidden = conv_row(taps_ref, row, weight_ref, params_ref).astype(jnp.bfloat16)
        hidden_ref[row] = hidden
        if 0 < row <= rows:
            total, square = add_sums(hidden.astype(jnp.float32), total, square)
    store_sums(total, square, out_ref)

    @pl.when(index == 0)
    def _():
        hidden_ref[0] = hidden_ref[1]

    @pl.when(index == count - 1)
    def _():
        hidden_ref[rows + 1] = hidden_ref[rows]


def second_kernel(
    count, sums_ref, hidden_ref, own_ref, weight_ref, params_ref,
    out_ref, taps_ref,
):
    rows, width, channels = own_ref.shape
    scale, offset = scale_offset(sums_ref, params_ref, rows * width * count)
    for row in range(rows + 2):
        store_taps(hidden_ref[row], scale, offset, taps_ref, row)
    for row in range(rows):
        branch = conv_row(taps_ref, row, weight_ref, params_ref)
        out_ref[row] = (own_ref[row].astype(jnp.float32) + branch).astype(jnp.bfloat16)


def prepared(weights, vectors):
    taps, channels = weights[0].shape[1] * weights[0].shape[2], weights[0].shape[3]
    weight_shape = jax.ShapeDtypeStruct((taps * channels, 2 * channels), jnp.bfloat16)
    vector_shape = jax.ShapeDtypeStruct((8, channels), jnp.float32)
    return pl.pallas_call(
        weights_kernel,
        out_shape=[weight_shape] * 2 + [vector_shape] * 2,
        in_specs=[VMEM] * 8,
        out_specs=[VMEM] * 4,
        compiler_params=PARAMS,
        name="weights",
        cost_estimate=pl.CostEstimate(
            flops=40000000000, bytes_accessed=10000000, transcendentals=0
        ),
    )(
        *[weight.reshape(3, taps, channels, channels) for weight in weights],
        *[vector.reshape(1, channels) for vector in vectors],
    )


def exchanged(sums):
    return lax.all_to_all(sums, "rows", 0, 0)


def body(
    latents, gain_one, shift_one, weight_one, bias_one, gain_two, shift_two, weight_two, bias_two
):
    count = lax.axis_size("rows")
    own = latents[0]
    rows, width, channels = own.shape
    sums_shape = jax.ShapeDtypeStruct((count, 2, channels), jnp.float32)
    slab_shape = jax.ShapeDtypeStruct((2, width, channels), jnp.bfloat16)
    swap_pair = [(i, i ^ 1) for i in range(count)]
    swap_other = [(i, i + 1 if i % 2 else i - 1) for i in range(1, count - 1)]

    sums, pair, other = pl.pallas_call(
        sums_kernel, out_shape=[sums_shape] + [slab_shape] * 2, in_specs=[VMEM],
        out_specs=[VMEM] * 3, compiler_params=PARAMS, name="sums",
        cost_estimate=pl.CostEstimate(
            flops=40000000000, bytes_accessed=10000000, transcendentals=0
        ),
    )(own)
    sums = exchanged(sums)
    other = lax.ppermute(other, "rows", swap_other)
    pair = lax.ppermute(pair, "rows", swap_pair)
    one, two, params_one, params_two = prepared(
        (weight_one, weight_two),
        (bias_one, gain_one, shift_one, bias_two, gain_two, shift_two),
    )
    hidden, sums = pl.pallas_call(
        functools.partial(first_kernel, count),
        out_shape=[jax.ShapeDtypeStruct((rows + 2, width, channels), jnp.bfloat16), sums_shape],
        in_specs=[VMEM] * 6,
        out_specs=[VMEM] * 2,
        scratch_shapes=[pltpu.VMEM((rows + 4, width, 3 * channels), jnp.bfloat16)],
        compiler_params=PARAMS, name="first",
    )(sums, own, pair, other, one, params_one)
    sums = exchanged(sums)
    decoded = pl.pallas_call(
        functools.partial(second_kernel, count),
        out_shape=jax.ShapeDtypeStruct(own.shape, jnp.bfloat16),
        in_specs=[VMEM] * 5,
        out_specs=VMEM,
        scratch_shapes=[pltpu.VMEM((rows + 2, width, 3 * channels), jnp.bfloat16)],
        compiler_params=PARAMS, name="second",
    )(sums, hidden, own, two, params_two)
    return decoded[None]


def solution(mesh):
    return jax.shard_map(
        body,
        mesh=mesh,
        in_specs=(P("groups", "rows", None, None), P(), P(), P(), P(), P(), P(), P(), P()),
        out_specs=P("groups", "rows", None, None),
        check_vma=False,
    )
```

```python
import functools

import jax
import jax.numpy as jnp
from jax import lax
from jax.experimental import pallas as pl
from jax.experimental.pallas import tpu as pltpu
from jax.sharding import PartitionSpec as P

GROUPS = 32
VMEM = pl.BlockSpec(memory_space=pltpu.VMEM)
PARAMS = pltpu.CompilerParams(vmem_limit_bytes=24 * 1024 * 1024)


def store_sums(total, square, out_ref):
    total = jnp.sum(total, axis=0, keepdims=True)
    square = jnp.sum(square, axis=0, keepdims=True)
    pair = jnp.concatenate([total, square], axis=0)
    out_ref[...] = jnp.broadcast_to(pair[None], out_ref.shape)


def add_sums(values, total, square):
    width, channels = values.shape
    split = (width // 8, 8, channels)
    total += jnp.sum(values.reshape(split), axis=0)
    square += jnp.sum((values * values).reshape(split), axis=0)
    return total, square


def sums_kernel(own_ref, out_ref, pair_ref, other_ref):
    rows, _, channels = own_ref.shape
    even = lax.axis_index("rows") % 2 == 0
    for row in range(2):
        top = own_ref[row]
        bottom = own_ref[rows - 2 + row]
        pair_ref[row] = jnp.where(even, bottom, top)
        other_ref[row] = jnp.where(even, top, bottom)
    total = jnp.zeros((8, channels), jnp.float32)
    square = jnp.zeros((8, channels), jnp.float32)
    for row in range(rows):
        total, square = add_sums(own_ref[row].astype(jnp.float32), total, square)
    store_sums(total, square, out_ref)


def weights_kernel(one_ref, two_ref, *rest):
    vectors, outs = rest[:6], rest[6:]
    for source, target in ((one_ref, outs[0]), (two_ref, outs[1])):
        taps, channels = source.shape[1], source.shape[2]
        for tap in range(taps):
            total = source[0, tap].astype(jnp.float32)
            total += source[1, tap].astype(jnp.float32)
            total += source[2, tap].astype(jnp.float32)
            high = total.astype(jnp.bfloat16)
            low = (total - high.astype(jnp.float32)).astype(jnp.bfloat16)
            target[pl.ds(tap * channels, channels), :] = jnp.concatenate([high, low], axis=1)
    for i in range(6):
        outs[2 + i // 3][pl.ds(i % 3, 1), :] = vectors[i][...]


def scale_offset(sums, params_ref, entries):
    channels = sums.shape[1]
    per_group = channels // GROUPS
    sums = jnp.concatenate([sums, jnp.zeros((6, channels), jnp.float32)], axis=0)
    step = 1
    while step < per_group:
        sums += pltpu.roll(sums, channels - step, 1)
        step *= 2
    lane = lax.broadcasted_iota(jnp.int32, sums.shape, 1)
    sums = jnp.where(lane % per_group == 0, sums, 0.0)
    step = 1
    while step < per_group:
        sums += pltpu.roll(sums, step, 1)
        step *= 2
    sums = sums * (1.0 / (entries * per_group))
    mean = sums[0:1]
    var = sums[1:2] - mean * mean
    scale = params_ref[1:2, :] / jnp.sqrt(var + 1e-06)
    return scale, params_ref[2:3, :] - mean * scale


def store_taps(values, scale, offset, target, row):
    width, channels = values.shape
    normed = values.astype(jnp.float32) * scale + offset
    act = normed * (0.5 * jnp.tanh(0.5 * normed) + 0.5)
    column = lax.broadcasted_iota(jnp.int32, act.shape, 0)
    left = jnp.where(column == 0, act, pltpu.roll(act, 1, 0))
    right = jnp.where(column == width - 1, act, pltpu.roll(act, width - 1, 0))
    target[row, :, 0:channels] = left.astype(jnp.bfloat16)
    target[row, :, channels : 2 * channels] = act.astype(jnp.bfloat16)
    target[row, :, 2 * channels : 3 * channels] = right.astype(jnp.bfloat16)


def conv_row(taps_ref, row, weight_ref, params_ref):
    window = jnp.concatenate([taps_ref[row], taps_ref[row + 1], taps_ref[row + 2]], axis=1)
    both = jnp.dot(window, weight_ref[...], preferred_element_type=jnp.float32)
    half = both.shape[1] // 2
    return both[:, :half] + both[:, half:] + params_ref[0:1, :]


def first_kernel(
    count, sums_ref, own_ref, pair_ref, other_ref, weight_ref, params_ref,
    hidden_ref, out_ref, taps_ref,
):
    index = lax.axis_index("rows")
    rows, width, channels = own_ref.shape
    scale, offset = scale_offset(jnp.sum(sums_ref[...], axis=0), params_ref, rows * width * count)
    even = index % 2 == 0
    for row in range(2):
        values = jnp.where(even, other_ref[row], pair_ref[row])
        values = jnp.where(index == 0, own_ref[0], values)
        store_taps(values, scale, offset, taps_ref, row)
    for row in range(rows):
        store_taps(own_ref[row], scale, offset, taps_ref, row + 2)
    for row in range(2):
        values = jnp.where(even, pair_ref[row], other_ref[row])
        values = jnp.where(index == count - 1, own_ref[rows - 1], values)
        store_taps(values, scale, offset, taps_ref, row + rows + 2)
    total = jnp.zeros((8, channels), jnp.float32)
    square = jnp.zeros((8, channels), jnp.float32)
    for row in range(rows + 2):
        hidden = conv_row(taps_ref, row, weight_ref, params_ref).astype(jnp.bfloat16)
        hidden_ref[row] = hidden
        if 0 < row <= rows:
            total, square = add_sums(hidden.astype(jnp.float32), total, square)
    store_sums(total, square, out_ref)

    @pl.when(index == 0)
    def _():
        hidden_ref[0] = hidden_ref[1]

    @pl.when(index == count - 1)
    def _():
        hidden_ref[rows + 1] = hidden_ref[rows]


def second_kernel(
    count, sums_ref, partner_ref, hidden_ref, own_ref, weight_ref, params_ref,
    out_ref, taps_ref,
):
    rows, width, channels = own_ref.shape
    sums = jnp.sum(sums_ref[...] + partner_ref[...], axis=0)
    scale, offset = scale_offset(sums, params_ref, rows * width * count)
    for row in range(rows + 2):
        store_taps(hidden_ref[row], scale, offset, taps_ref, row)
    for row in range(rows):
        branch = conv_row(taps_ref, row, weight_ref, params_ref)
        out_ref[row] = (own_ref[row].astype(jnp.float32) + branch).astype(jnp.bfloat16)


def prepared(weights, vectors):
    taps, channels = weights[0].shape[1] * weights[0].shape[2], weights[0].shape[3]
    weight_shape = jax.ShapeDtypeStruct((taps * channels, 2 * channels), jnp.bfloat16)
    vector_shape = jax.ShapeDtypeStruct((8, channels), jnp.float32)
    return pl.pallas_call(
        weights_kernel,
        out_shape=[weight_shape] * 2 + [vector_shape] * 2,
        in_specs=[VMEM] * 8,
        out_specs=[VMEM] * 4,
        compiler_params=PARAMS,
        name="weights",
        cost_estimate=pl.CostEstimate(
            flops=40000000000, bytes_accessed=10000000, transcendentals=0
        ),
    )(
        *[weight.reshape(3, taps, channels, channels) for weight in weights],
        *[vector.reshape(1, channels) for vector in vectors],
    )


def exchanged(sums):
    return lax.all_to_all(sums, "rows", 0, 0)


def body(
    latents, gain_one, shift_one, weight_one, bias_one, gain_two, shift_two, weight_two, bias_two
):
    count = lax.axis_size("rows")
    own = latents[0]
    rows, width, channels = own.shape
    sums_shape = jax.ShapeDtypeStruct((count, 2, channels), jnp.float32)
    slab_shape = jax.ShapeDtypeStruct((2, width, channels), jnp.bfloat16)
    swap_pair = [(i, i ^ 1) for i in range(count)]
    swap_other = [(i, i + 1 if i % 2 else i - 1) for i in range(1, count - 1)]

    sums, pair, other = pl.pallas_call(
        sums_kernel, out_shape=[sums_shape] + [slab_shape] * 2, in_specs=[VMEM],
        out_specs=[VMEM] * 3, compiler_params=PARAMS, name="sums",
        cost_estimate=pl.CostEstimate(
            flops=40000000000, bytes_accessed=10000000, transcendentals=0
        ),
    )(own)
    sums = exchanged(sums)
    other = lax.ppermute(other, "rows", swap_other)
    pair = lax.ppermute(pair, "rows", swap_pair)
    one, two, params_one, params_two = prepared(
        (weight_one, weight_two),
        (bias_one, gain_one, shift_one, bias_two, gain_two, shift_two),
    )
    hidden, sums = pl.pallas_call(
        functools.partial(first_kernel, count),
        out_shape=[
            jax.ShapeDtypeStruct((rows + 2, width, channels), jnp.bfloat16),
            jax.ShapeDtypeStruct((count // 2, 2, channels), jnp.float32),
        ],
        in_specs=[VMEM] * 6,
        out_specs=[VMEM] * 2,
        scratch_shapes=[pltpu.VMEM((rows + 4, width, 3 * channels), jnp.bfloat16)],
        compiler_params=PARAMS, name="first",
    )(sums, own, pair, other, one, params_one)
    by_core = [list(range(core, count, 2)) for core in range(2)]
    sums = lax.all_to_all(sums, "rows", 0, 0, axis_index_groups=by_core)
    partner = lax.ppermute(sums, "rows", swap_pair)
    decoded = pl.pallas_call(
        functools.partial(second_kernel, count),
        out_shape=jax.ShapeDtypeStruct(own.shape, jnp.bfloat16),
        in_specs=[VMEM] * 6,
        out_specs=VMEM,
        scratch_shapes=[pltpu.VMEM((rows + 2, width, 3 * channels), jnp.bfloat16)],
        compiler_params=PARAMS, name="second",
    )(sums, partner, hidden, own, two, params_two)
    return decoded[None]


def solution(mesh):
    return jax.shard_map(
        body,
        mesh=mesh,
        in_specs=(P("groups", "rows", None, None), P(), P(), P(), P(), P(), P(), P(), P()),
        out_specs=P("groups", "rows", None, None),
        check_vma=False,
    )
```

```python
import functools

import jax
import jax.numpy as jnp
from jax import lax
from jax.experimental import pallas as pl
from jax.experimental.pallas import tpu as pltpu
from jax.sharding import PartitionSpec as P

GROUPS = 32
VMEM = pl.BlockSpec(memory_space=pltpu.VMEM)
PARAMS = pltpu.CompilerParams(vmem_limit_bytes=24 * 1024 * 1024)


def store_sums(total, square, out_ref):
    total = jnp.sum(total, axis=0, keepdims=True)
    square = jnp.sum(square, axis=0, keepdims=True)
    pair = jnp.concatenate([total, square], axis=0)
    out_ref[...] = jnp.broadcast_to(pair[None], out_ref.shape)


def add_sums(values, total, square):
    width, channels = values.shape
    split = (width // 8, 8, channels)
    total += jnp.sum(values.reshape(split), axis=0)
    square += jnp.sum((values * values).reshape(split), axis=0)
    return total, square


def sums_kernel(own_ref, out_ref, pair_ref, other_ref):
    rows, _, channels = own_ref.shape
    even = lax.axis_index("rows") % 2 == 0
    for row in range(2):
        top = own_ref[row]
        bottom = own_ref[rows - 2 + row]
        pair_ref[row] = jnp.where(even, bottom, top)
        other_ref[row] = jnp.where(even, top, bottom)
    total = jnp.zeros((8, channels), jnp.float32)
    square = jnp.zeros((8, channels), jnp.float32)
    for row in range(rows):
        total, square = add_sums(own_ref[row].astype(jnp.float32), total, square)
    store_sums(total, square, out_ref)


def weights_kernel(one_ref, two_ref, *rest):
    vectors, outs = rest[:6], rest[6:]
    for source, target in ((one_ref, outs[0]), (two_ref, outs[1])):
        taps, channels = source.shape[1], source.shape[2]
        for tap in range(taps):
            total = source[0, tap].astype(jnp.float32)
            total += source[1, tap].astype(jnp.float32)
            total += source[2, tap].astype(jnp.float32)
            high = total.astype(jnp.bfloat16)
            low = (total - high.astype(jnp.float32)).astype(jnp.bfloat16)
            target[pl.ds(tap * channels, channels), :] = jnp.concatenate([high, low], axis=1)
    for i in range(6):
        outs[2 + i // 3][pl.ds(i % 3, 1), :] = vectors[i][...]


def scale_offset(sums_ref, params_ref, entries):
    sums = jnp.sum(sums_ref[...], axis=0)
    channels = sums.shape[1]
    per_group = channels // GROUPS
    sums = jnp.concatenate([sums, jnp.zeros((6, channels), jnp.float32)], axis=0)
    step = 1
    while step < per_group:
        sums += pltpu.roll(sums, channels - step, 1)
        step *= 2
    lane = lax.broadcasted_iota(jnp.int32, sums.shape, 1)
    sums = jnp.where(lane % per_group == 0, sums, 0.0)
    step = 1
    while step < per_group:
        sums += pltpu.roll(sums, step, 1)
        step *= 2
    sums = sums * (1.0 / (entries * per_group))
    mean = sums[0:1]
    var = sums[1:2] - mean * mean
    scale = params_ref[1:2, :] / jnp.sqrt(var + 1e-06)
    return scale, params_ref[2:3, :] - mean * scale


def store_taps(values, scale, offset, target, row):
    width, channels = values.shape
    normed = values.astype(jnp.float32) * scale + offset
    act = normed * (0.5 * jnp.tanh(0.5 * normed) + 0.5)
    column = lax.broadcasted_iota(jnp.int32, act.shape, 0)
    left = jnp.where(column == 0, act, pltpu.roll(act, 1, 0))
    right = jnp.where(column == width - 1, act, pltpu.roll(act, width - 1, 0))
    target[row, :, 0:channels] = left.astype(jnp.bfloat16)
    target[row, :, channels : 2 * channels] = act.astype(jnp.bfloat16)
    target[row, :, 2 * channels : 3 * channels] = right.astype(jnp.bfloat16)


def conv_row(taps_ref, row, weight_ref, params_ref):
    window = jnp.concatenate([taps_ref[row], taps_ref[row + 1], taps_ref[row + 2]], axis=1)
    both = jnp.dot(window, weight_ref[...], preferred_element_type=jnp.float32)
    half = both.shape[1] // 2
    return both[:, :half] + both[:, half:] + params_ref[0:1, :]


def first_kernel(
    count, sums_ref, own_ref, pair_ref, other_ref, weight_ref, params_ref,
    hidden_ref, out_ref, taps_ref,
):
    index = lax.axis_index("rows")
    rows, width, channels = own_ref.shape
    scale, offset = scale_offset(sums_ref, params_ref, rows * width * count)
    even = index % 2 == 0
    for row in range(2):
        values = jnp.where(even, other_ref[row], pair_ref[row])
        values = jnp.where(index == 0, own_ref[0], values)
        store_taps(values, scale, offset, taps_ref, row)
    for row in range(rows):
        store_taps(own_ref[row], scale, offset, taps_ref, row + 2)
    for row in range(2):
        values = jnp.where(even, pair_ref[row], other_ref[row])
        values = jnp.where(index == count - 1, own_ref[rows - 1], values)
        store_taps(values, scale, offset, taps_ref, row + rows + 2)
    total = jnp.zeros((8, channels), jnp.float32)
    square = jnp.zeros((8, channels), jnp.float32)
    for row in range(rows + 2):
        hidden = conv_row(taps_ref, row, weight_ref, params_ref).astype(jnp.bfloat16)
        hidden_ref[row] = hidden
        if 0 < row <= rows:
            total, square = add_sums(hidden.astype(jnp.float32), total, square)
    store_sums(total, square, out_ref)

    @pl.when(index == 0)
    def _():
        hidden_ref[0] = hidden_ref[1]

    @pl.when(index == count - 1)
    def _():
        hidden_ref[rows + 1] = hidden_ref[rows]


def second_kernel(
    count, sums_ref, hidden_ref, own_ref, weight_ref, params_ref,
    out_ref, taps_ref,
):
    rows, width, channels = own_ref.shape
    scale, offset = scale_offset(sums_ref, params_ref, rows * width * count)
    for row in range(rows + 2):
        store_taps(hidden_ref[row], scale, offset, taps_ref, row)
    for row in range(rows):
        branch = conv_row(taps_ref, row, weight_ref, params_ref)
        out_ref[row] = (own_ref[row].astype(jnp.float32) + branch).astype(jnp.bfloat16)


def prepared(weights, vectors):
    taps, channels = weights[0].shape[1] * weights[0].shape[2], weights[0].shape[3]
    weight_shape = jax.ShapeDtypeStruct((taps * channels, 2 * channels), jnp.bfloat16)
    vector_shape = jax.ShapeDtypeStruct((8, channels), jnp.float32)
    return pl.pallas_call(
        weights_kernel,
        out_shape=[weight_shape] * 2 + [vector_shape] * 2,
        in_specs=[VMEM] * 8,
        out_specs=[VMEM] * 4,
        compiler_params=PARAMS,
        name="weights",
        cost_estimate=pl.CostEstimate(flops=2000000, bytes_accessed=3000000, transcendentals=0),
    )(
        *[weight.reshape(3, taps, channels, channels) for weight in weights],
        *[vector.reshape(1, channels) for vector in vectors],
    )


def exchanged(sums):
    return lax.all_to_all(sums, "rows", 0, 0)


def body(
    latents, gain_one, shift_one, weight_one, bias_one, gain_two, shift_two, weight_two, bias_two
):
    count = lax.axis_size("rows")
    own = latents[0]
    rows, width, channels = own.shape
    sums_shape = jax.ShapeDtypeStruct((count, 2, channels), jnp.float32)
    slab_shape = jax.ShapeDtypeStruct((2, width, channels), jnp.bfloat16)
    swap_pair = [(i, i ^ 1) for i in range(count)]
    swap_other = [(i, i + 1 if i % 2 else i - 1) for i in range(1, count - 1)]

    sums, pair, other = pl.pallas_call(
        sums_kernel, out_shape=[sums_shape] + [slab_shape] * 2, in_specs=[VMEM],
        out_specs=[VMEM] * 3, compiler_params=PARAMS, name="sums",
        cost_estimate=pl.CostEstimate(
            flops=40000000000, bytes_accessed=10000000, transcendentals=0
        ),
    )(own)
    sums = exchanged(sums)
    other = lax.ppermute(other, "rows", swap_other)
    pair = lax.ppermute(pair, "rows", swap_pair)
    one, two, params_one, params_two = prepared(
        (weight_one, weight_two),
        (bias_one, gain_one, shift_one, bias_two, gain_two, shift_two),
    )
    hidden, sums = pl.pallas_call(
        functools.partial(first_kernel, count),
        out_shape=[jax.ShapeDtypeStruct((rows + 2, width, channels), jnp.bfloat16), sums_shape],
        in_specs=[VMEM] * 6,
        out_specs=[VMEM] * 2,
        scratch_shapes=[pltpu.VMEM((rows + 4, width, 3 * channels), jnp.bfloat16)],
        compiler_params=PARAMS, name="first",
    )(sums, own, pair, other, one, params_one)
    sums = exchanged(sums)
    decoded = pl.pallas_call(
        functools.partial(second_kernel, count),
        out_shape=jax.ShapeDtypeStruct(own.shape, jnp.bfloat16),
        in_specs=[VMEM] * 5,
        out_specs=VMEM,
        scratch_shapes=[pltpu.VMEM((rows + 2, width, 3 * channels), jnp.bfloat16)],
        compiler_params=PARAMS, name="second",
    )(sums, hidden, own, two, params_two)
    return decoded[None]


def solution(mesh):
    return jax.shard_map(
        body,
        mesh=mesh,
        in_specs=(P("groups", "rows", None, None), P(), P(), P(), P(), P(), P(), P(), P()),
        out_specs=P("groups", "rows", None, None),
        check_vma=False,
    )
```

```python
import functools

import jax
import jax.numpy as jnp
from jax import lax
from jax.experimental import pallas as pl
from jax.experimental.pallas import tpu as pltpu
from jax.sharding import PartitionSpec as P

GROUPS = 32
ANY = pl.BlockSpec(memory_space=pl.ANY)
VMEM = pl.BlockSpec(memory_space=pltpu.VMEM)
PARAMS = pltpu.CompilerParams(vmem_limit_bytes=24 * 1024 * 1024)


def store_sums(total, square, out_ref):
    total = jnp.sum(total, axis=0, keepdims=True)
    square = jnp.sum(square, axis=0, keepdims=True)
    pair = jnp.concatenate([total, square], axis=0)
    out_ref[...] = jnp.broadcast_to(pair[None], out_ref.shape)


def add_sums(values, total, square):
    width, channels = values.shape
    split = (width // 8, 8, channels)
    total += jnp.sum(values.reshape(split), axis=0)
    square += jnp.sum((values * values).reshape(split), axis=0)
    return total, square


def sums_kernel(own_ref, out_ref, pair_ref, other_ref):
    rows, _, channels = own_ref.shape
    even = lax.axis_index("rows") % 2 == 0
    for row in range(2):
        top = own_ref[row]
        bottom = own_ref[rows - 2 + row]
        pair_ref[row] = jnp.where(even, bottom, top)
        other_ref[row] = jnp.where(even, top, bottom)
    total = jnp.zeros((8, channels), jnp.float32)
    square = jnp.zeros((8, channels), jnp.float32)
    for row in range(rows):
        total, square = add_sums(own_ref[row].astype(jnp.float32), total, square)
    store_sums(total, square, out_ref)


def weights_kernel(one_ref, two_ref, *rest):
    vectors, outs = rest[:6], rest[6:]
    for source, target in ((one_ref, outs[0]), (two_ref, outs[1])):
        taps, channels = source.shape[1], source.shape[2]
        for tap in range(taps):
            total = source[0, tap].astype(jnp.float32)
            total += source[1, tap].astype(jnp.float32)
            total += source[2, tap].astype(jnp.float32)
            high = total.astype(jnp.bfloat16)
            low = (total - high.astype(jnp.float32)).astype(jnp.bfloat16)
            target[pl.ds(tap * channels, channels), :] = jnp.concatenate([high, low], axis=1)
    for i in range(6):
        outs[2 + i // 3][pl.ds(i % 3, 1), :] = vectors[i][...]


def scale_offset(sums_ref, params_ref, entries):
    sums = jnp.sum(sums_ref[...], axis=0)
    channels = sums.shape[1]
    per_group = channels // GROUPS
    sums = jnp.concatenate([sums, jnp.zeros((6, channels), jnp.float32)], axis=0)
    member = lax.broadcasted_iota(jnp.int32, sums.shape, 1) % per_group
    total = sums
    for step in range(1, per_group):
        total += jnp.where(member >= step, pltpu.roll(sums, step, 1), 0.0)
        total += jnp.where(member < per_group - step, pltpu.roll(sums, channels - step, 1), 0.0)
    total = total * (1.0 / (entries * per_group))
    mean = total[0:1]
    var = total[1:2] - mean * mean
    scale = params_ref[1:2, :] * lax.rsqrt(var + 1e-06)
    return 0.5 * scale, 0.5 * (params_ref[2:3, :] - mean * scale)


def store_taps(values, scale, offset, wide_ref, taps_ref, row):
    width, channels = values.shape
    half = values.astype(jnp.float32) * scale + offset
    act = half * jnp.tanh(half) + half
    wide_ref[row, 8 : 8 + width, :] = act
    wide_ref[row, 7:8, :] = act[0:1]
    wide_ref[row, 8 + width : 9 + width, :] = act[width - 1 : width]
    for tap in range(3):
        shifted = wide_ref[row, 7 + tap : 7 + tap + width, :]
        taps_ref[row, :, tap * channels : (tap + 1) * channels] = shifted.astype(jnp.bfloat16)


def conv_rows(taps_ref, row, count, weight_ref, params_ref):
    _, width, lanes = taps_ref.shape
    window = jnp.concatenate(
        [taps_ref[row + tap : row + tap + count].reshape(count * width, lanes) for tap in range(3)],
        axis=1,
    )
    both = jnp.dot(window, weight_ref[...], preferred_element_type=jnp.float32)
    half = both.shape[1] // 2
    return both[:, :half] + both[:, half:] + params_ref[0:1, :]


def first_kernel(
    count, sums_ref, own_ref, pair_ref, other_ref, weight_ref, params_ref,
    hidden_ref, out_ref, wide_ref, taps_ref,
):
    index = lax.axis_index("rows")
    rows, width, channels = own_ref.shape
    even = index % 2 == 0
    scale, offset = scale_offset(sums_ref, params_ref, rows * width * count)

    def make(row):
        if row < 2:
            values = jnp.where(even, other_ref[row], pair_ref[row])
            values = jnp.where(index == 0, own_ref[0], values)
        elif row < rows + 2:
            values = own_ref[row - 2]
        else:
            values = jnp.where(even, pair_ref[row - rows - 2], other_ref[row - rows - 2])
            values = jnp.where(index == count - 1, own_ref[rows - 1], values)
        store_taps(values, scale, offset, wide_ref, taps_ref, row)

    total = jnp.zeros((8, channels), jnp.float32)
    square = jnp.zeros((8, channels), jnp.float32)
    make(0)
    make(1)
    for row in range(0, rows + 2, 2):
        make(row + 2)
        make(row + 3)
        hidden = conv_rows(taps_ref, row, 2, weight_ref, params_ref).astype(jnp.bfloat16)
        for i in range(2):
            values = hidden[i * width : (i + 1) * width]
            hidden_ref[row + i] = values
            if 0 < row + i <= rows:
                total, square = add_sums(values.astype(jnp.float32), total, square)
    store_sums(total, square, out_ref)

    @pl.when(index == 0)
    def _():
        hidden_ref[0] = hidden_ref[1]

    @pl.when(index == count - 1)
    def _():
        hidden_ref[rows + 1] = hidden_ref[rows]


def second_kernel(
    count, sums_ref, hidden_ref, own_ref, weight_ref, params_ref,
    out_ref, wide_ref, taps_ref, done_ref, sems,
):
    rows, width, channels = own_ref.shape
    scale, offset = scale_offset(sums_ref, params_ref, rows * width * count)
    copies = [
        pltpu.make_async_copy(done_ref.at[row], out_ref.at[row], sems.at[row])
        for row in range(rows)
    ]
    for row in range(2):
        store_taps(hidden_ref[row], scale, offset, wide_ref, taps_ref, row)
    for row in range(0, rows, 2):
        for i in range(2):
            store_taps(hidden_ref[row + 2 + i], scale, offset, wide_ref, taps_ref, row + 2 + i)
        branch = conv_rows(taps_ref, row, 2, weight_ref, params_ref)
        for i in range(2):
            values = own_ref[row + i].astype(jnp.float32) + branch[i * width : (i + 1) * width]
            done_ref[row + i] = values.astype(jnp.bfloat16)
            copies[row + i].start()
    for copy in copies:
        copy.wait()


def prepared(weights, vectors):
    taps, channels = weights[0].shape[1] * weights[0].shape[2], weights[0].shape[3]
    weight_shape = jax.ShapeDtypeStruct((taps * channels, 2 * channels), jnp.bfloat16)
    vector_shape = jax.ShapeDtypeStruct((8, channels), jnp.float32)
    return pl.pallas_call(
        weights_kernel,
        out_shape=[weight_shape] * 2 + [vector_shape] * 2,
        in_specs=[VMEM] * 8,
        out_specs=[VMEM] * 4,
        compiler_params=PARAMS,
        name="weights",
        cost_estimate=pl.CostEstimate(flops=2000000, bytes_accessed=3000000, transcendentals=0),
    )(
        *[weight.reshape(3, taps, channels, channels) for weight in weights],
        *[vector.reshape(1, channels) for vector in vectors],
    )


def exchanged(sums):
    return lax.all_to_all(sums, "rows", 0, 0)


def body(
    latents, gain_one, shift_one, weight_one, bias_one, gain_two, shift_two, weight_two, bias_two
):
    count = lax.axis_size("rows")
    own = latents[0]
    rows, width, channels = own.shape
    sums_shape = jax.ShapeDtypeStruct((count, 2, channels), jnp.float32)
    slab_shape = jax.ShapeDtypeStruct((2, width, channels), jnp.bfloat16)
    swap_pair = [(i, i ^ 1) for i in range(count)]
    swap_other = [(i, i + 1 if i % 2 else i - 1) for i in range(1, count - 1)]

    sums, pair, other = pl.pallas_call(
        sums_kernel, out_shape=[sums_shape] + [slab_shape] * 2, in_specs=[VMEM],
        out_specs=[VMEM] * 3, compiler_params=PARAMS, name="sums",
        cost_estimate=pl.CostEstimate(
            flops=40000000000, bytes_accessed=10000000, transcendentals=0
        ),
    )(own)
    sums = exchanged(sums)
    other = lax.ppermute(other, "rows", swap_other)
    pair = lax.ppermute(pair, "rows", swap_pair)
    one, two, params_one, params_two = prepared(
        (weight_one, weight_two),
        (bias_one, gain_one, shift_one, bias_two, gain_two, shift_two),
    )
    hidden, sums = pl.pallas_call(
        functools.partial(first_kernel, count),
        out_shape=[jax.ShapeDtypeStruct((rows + 2, width, channels), jnp.bfloat16), sums_shape],
        in_specs=[VMEM] * 6,
        out_specs=[VMEM] * 2,
        scratch_shapes=[
            pltpu.VMEM((rows + 4, width + 16, channels), jnp.float32),
            pltpu.VMEM((rows + 4, width, 3 * channels), jnp.bfloat16),
        ],
        compiler_params=PARAMS, name="first",
    )(sums, own, pair, other, one, params_one)
    sums = exchanged(sums)
    decoded = pl.pallas_call(
        functools.partial(second_kernel, count),
        out_shape=jax.ShapeDtypeStruct(own.shape, jnp.bfloat16),
        in_specs=[VMEM] * 5,
        out_specs=ANY,
        scratch_shapes=[
            pltpu.VMEM((rows + 2, width + 16, channels), jnp.float32),
            pltpu.VMEM((rows + 2, width, 3 * channels), jnp.bfloat16),
            pltpu.VMEM(own.shape, jnp.bfloat16),
            pltpu.SemaphoreType.DMA((rows,)),
        ],
        compiler_params=PARAMS, name="second",
    )(sums, hidden, own, two, params_two)
    return decoded[None]


def solution(mesh):
    return jax.shard_map(
        body,
        mesh=mesh,
        in_specs=(P("groups", "rows", None, None), P(), P(), P(), P(), P(), P(), P(), P()),
        out_specs=P("groups", "rows", None, None),
        check_vma=False,
    )
```

```python
import functools

import jax
import jax.numpy as jnp
from jax import lax
from jax.experimental import pallas as pl
from jax.experimental.pallas import tpu as pltpu
from jax.sharding import PartitionSpec as P

GROUPS = 32
ANY = pl.BlockSpec(memory_space=pl.ANY)
VMEM = pl.BlockSpec(memory_space=pltpu.VMEM)
PARAMS = pltpu.CompilerParams(vmem_limit_bytes=24 * 1024 * 1024)


def store_sums(total, square, out_ref):
    total = jnp.sum(total, axis=0, keepdims=True)
    square = jnp.sum(square, axis=0, keepdims=True)
    pair = jnp.concatenate([total, square], axis=0)
    out_ref[...] = jnp.broadcast_to(pair[None], out_ref.shape)


def add_sums(values, total, square):
    width, channels = values.shape
    split = (width // 8, 8, channels)
    total += jnp.sum(values.reshape(split), axis=0)
    square += jnp.sum((values * values).reshape(split), axis=0)
    return total, square


def sums_kernel(own_ref, out_ref, pair_ref, other_ref):
    rows, _, channels = own_ref.shape
    even = lax.axis_index("rows") % 2 == 0
    for row in range(2):
        top = own_ref[row]
        bottom = own_ref[rows - 2 + row]
        pair_ref[row] = jnp.where(even, bottom, top)
        other_ref[row] = jnp.where(even, top, bottom)
    total = jnp.zeros((8, channels), jnp.float32)
    square = jnp.zeros((8, channels), jnp.float32)
    for row in range(rows):
        total, square = add_sums(own_ref[row].astype(jnp.float32), total, square)
    store_sums(total, square, out_ref)


def weights_kernel(one_ref, two_ref, *rest):
    vectors, outs = rest[:6], rest[6:]
    for source, target in ((one_ref, outs[0]), (two_ref, outs[1])):
        taps, channels = source.shape[1], source.shape[2]
        for tap in range(taps):
            total = source[0, tap].astype(jnp.float32)
            total += source[1, tap].astype(jnp.float32)
            total += source[2, tap].astype(jnp.float32)
            high = total.astype(jnp.bfloat16)
            low = (total - high.astype(jnp.float32)).astype(jnp.bfloat16)
            target[pl.ds(tap * channels, channels), :] = jnp.concatenate([high, low], axis=1)
    for i in range(6):
        outs[2 + i // 3][pl.ds(i % 3, 1), :] = vectors[i][...]


def scale_offset(sums_ref, params_ref, entries):
    sums = jnp.sum(sums_ref[...], axis=0)
    channels = sums.shape[1]
    per_group = channels // GROUPS
    sums = jnp.concatenate([sums, jnp.zeros((6, channels), jnp.float32)], axis=0)
    member = lax.broadcasted_iota(jnp.int32, sums.shape, 1) % per_group
    total = sums
    for step in range(1, per_group):
        total += jnp.where(member >= step, pltpu.roll(sums, step, 1), 0.0)
        total += jnp.where(member < per_group - step, pltpu.roll(sums, channels - step, 1), 0.0)
    total = total * (1.0 / (entries * per_group))
    mean = total[0:1]
    var = total[1:2] - mean * mean
    scale = params_ref[1:2, :] * lax.rsqrt(var + 1e-06)
    return 0.5 * scale, 0.5 * (params_ref[2:3, :] - mean * scale)


def store_taps(values, scale, offset, wide_ref, taps_ref, row):
    width, channels = values.shape
    half = values.astype(jnp.float32) * scale + offset
    act = half * jnp.tanh(half) + half
    wide_ref[row, 8 : 8 + width, :] = act
    wide_ref[row, 7:8, :] = act[0:1]
    wide_ref[row, 8 + width : 9 + width, :] = act[width - 1 : width]
    for tap in range(3):
        shifted = wide_ref[row, 7 + tap : 7 + tap + width, :]
        taps_ref[row, :, tap * channels : (tap + 1) * channels] = shifted.astype(jnp.bfloat16)


def conv_rows(taps_ref, row, count, weight_ref, params_ref):
    _, width, lanes = taps_ref.shape
    window = jnp.concatenate(
        [taps_ref[row + tap : row + tap + count].reshape(count * width, lanes) for tap in range(3)],
        axis=1,
    )
    both = jnp.dot(window, weight_ref[...], preferred_element_type=jnp.float32)
    half = both.shape[1] // 2
    return both[:, :half] + both[:, half:] + params_ref[0:1, :]


def first_kernel(
    count, sums_ref, own_ref, pair_ref, other_ref, weight_ref, params_ref,
    hidden_ref, out_ref, wide_ref, taps_ref,
):
    index = lax.axis_index("rows")
    rows, width, channels = own_ref.shape
    even = index % 2 == 0
    scale, offset = scale_offset(sums_ref, params_ref, rows * width * count)

    def make(row):
        if row < 2:
            values = jnp.where(even, other_ref[row], pair_ref[row])
            values = jnp.where(index == 0, own_ref[0], values)
        elif row < rows + 2:
            values = own_ref[row - 2]
        else:
            values = jnp.where(even, pair_ref[row - rows - 2], other_ref[row - rows - 2])
            values = jnp.where(index == count - 1, own_ref[rows - 1], values)
        store_taps(values, scale, offset, wide_ref, taps_ref, row)

    total = jnp.zeros((8, channels), jnp.float32)
    square = jnp.zeros((8, channels), jnp.float32)
    make(0)
    make(1)
    for row in range(0, rows + 2, 2):
        make(row + 2)
        make(row + 3)
        hidden = conv_rows(taps_ref, row, 2, weight_ref, params_ref).astype(jnp.bfloat16)
        for i in range(2):
            values = hidden[i * width : (i + 1) * width]
            hidden_ref[row + i] = values
            if 0 < row + i <= rows:
                total, square = add_sums(values.astype(jnp.float32), total, square)
    store_sums(total, square, out_ref)

    @pl.when(index == 0)
    def _():
        hidden_ref[0] = hidden_ref[1]

    @pl.when(index == count - 1)
    def _():
        hidden_ref[rows + 1] = hidden_ref[rows]


def second_kernel(
    count, sums_ref, hidden_ref, own_ref, weight_ref, params_ref,
    out_ref, wide_ref, taps_ref, done_ref, sems,
):
    rows, width, channels = own_ref.shape
    scale, offset = scale_offset(sums_ref, params_ref, rows * width * count)
    copies = [
        pltpu.make_async_copy(done_ref.at[row], out_ref.at[row], sems.at[row])
        for row in range(rows)
    ]
    for row in range(2):
        store_taps(hidden_ref[row], scale, offset, wide_ref, taps_ref, row)
    for row in range(0, rows, 2):
        for i in range(2):
            store_taps(hidden_ref[row + 2 + i], scale, offset, wide_ref, taps_ref, row + 2 + i)
        branch = conv_rows(taps_ref, row, 2, weight_ref, params_ref)
        for i in range(2):
            values = own_ref[row + i].astype(jnp.float32) + branch[i * width : (i + 1) * width]
            done_ref[row + i] = values.astype(jnp.bfloat16)
            copies[row + i].start()
    for copy in copies:
        copy.wait()


def prepared(weights, vectors):
    taps, channels = weights[0].shape[1] * weights[0].shape[2], weights[0].shape[3]
    weight_shape = jax.ShapeDtypeStruct((taps * channels, 2 * channels), jnp.bfloat16)
    vector_shape = jax.ShapeDtypeStruct((8, channels), jnp.float32)
    return pl.pallas_call(
        weights_kernel,
        out_shape=[weight_shape] * 2 + [vector_shape] * 2,
        in_specs=[VMEM] * 8,
        out_specs=[VMEM] * 4,
        compiler_params=PARAMS,
        name="weights",
        cost_estimate=pl.CostEstimate(flops=2000000, bytes_accessed=3000000, transcendentals=0),
    )(
        *[weight.reshape(3, taps, channels, channels) for weight in weights],
        *[vector.reshape(1, channels) for vector in vectors],
    )


def exchanged(sums):
    return lax.all_to_all(sums, "rows", 0, 0)


def body(
    latents, gain_one, shift_one, weight_one, bias_one, gain_two, shift_two, weight_two, bias_two
):
    count = lax.axis_size("rows")
    inner = 4 if count % 4 == 0 else count
    own = latents[0]
    rows, width, channels = own.shape
    sums_shape = jax.ShapeDtypeStruct((count, 2, channels), jnp.float32)
    slab_shape = jax.ShapeDtypeStruct((2, width, channels), jnp.bfloat16)
    swap_pair = [(i, i ^ 1) for i in range(count)]
    swap_other = [(i, i + 1 if i % 2 else i - 1) for i in range(1, count - 1)]

    sums, pair, other = pl.pallas_call(
        sums_kernel, out_shape=[sums_shape] + [slab_shape] * 2, in_specs=[VMEM],
        out_specs=[VMEM] * 3, compiler_params=PARAMS, name="sums",
        cost_estimate=pl.CostEstimate(
            flops=40000000000, bytes_accessed=10000000, transcendentals=0
        ),
    )(own)
    sums = exchanged(sums)
    other = lax.ppermute(other, "rows", swap_other)
    pair = lax.ppermute(pair, "rows", swap_pair)
    one, two, params_one, params_two = prepared(
        (weight_one, weight_two),
        (bias_one, gain_one, shift_one, bias_two, gain_two, shift_two),
    )
    hidden, sums = pl.pallas_call(
        functools.partial(first_kernel, count),
        out_shape=[
            jax.ShapeDtypeStruct((rows + 2, width, channels), jnp.bfloat16),
            jax.ShapeDtypeStruct((inner, 2, channels), jnp.float32),
        ],
        in_specs=[VMEM] * 6,
        out_specs=[VMEM] * 2,
        scratch_shapes=[
            pltpu.VMEM((rows + 4, width + 16, channels), jnp.float32),
            pltpu.VMEM((rows + 4, width, 3 * channels), jnp.bfloat16),
        ],
        compiler_params=PARAMS, name="first",
    )(sums, own, pair, other, one, params_one)
    near = [list(range(i, i + inner)) for i in range(0, count, inner)]
    far = [list(range(i, count, inner)) for i in range(inner)]
    sums = lax.all_to_all(sums, "rows", 0, 0, axis_index_groups=near)
    sums = jnp.broadcast_to(jnp.sum(sums, axis=0)[None], (count // inner, 2, channels))
    sums = lax.all_to_all(sums, "rows", 0, 0, axis_index_groups=far)
    decoded = pl.pallas_call(
        functools.partial(second_kernel, count),
        out_shape=jax.ShapeDtypeStruct(own.shape, jnp.bfloat16),
        in_specs=[VMEM] * 5,
        out_specs=ANY,
        scratch_shapes=[
            pltpu.VMEM((rows + 2, width + 16, channels), jnp.float32),
            pltpu.VMEM((rows + 2, width, 3 * channels), jnp.bfloat16),
            pltpu.VMEM(own.shape, jnp.bfloat16),
            pltpu.SemaphoreType.DMA((rows,)),
        ],
        compiler_params=PARAMS, name="second",
    )(sums, hidden, own, two, params_two)
    return decoded[None]


def solution(mesh):
    return jax.shard_map(
        body,
        mesh=mesh,
        in_specs=(P("groups", "rows", None, None), P(), P(), P(), P(), P(), P(), P(), P()),
        out_specs=P("groups", "rows", None, None),
        check_vma=False,
    )
```

```python
import functools

import jax
import jax.numpy as jnp
from jax import lax
from jax.experimental import pallas as pl
from jax.experimental.pallas import tpu as pltpu
from jax.sharding import PartitionSpec as P

GROUPS = 32
ANY = pl.BlockSpec(memory_space=pl.ANY)
VMEM = pl.BlockSpec(memory_space=pltpu.VMEM)
PARAMS = pltpu.CompilerParams(vmem_limit_bytes=24 * 1024 * 1024)


def store_sums(total, square, out_ref):
    total = jnp.sum(total, axis=0, keepdims=True)
    square = jnp.sum(square, axis=0, keepdims=True)
    pair = jnp.concatenate([total, square], axis=0)
    out_ref[...] = jnp.broadcast_to(pair[None], out_ref.shape)


def add_sums(values, total, square):
    width, channels = values.shape
    split = (width // 8, 8, channels)
    total += jnp.sum(values.reshape(split), axis=0)
    square += jnp.sum((values * values).reshape(split), axis=0)
    return total, square


def sums_kernel(own_ref, out_ref, other_ref, pair_ref):
    rows, _, channels = own_ref.shape
    even = lax.axis_index("rows") % 2 == 0
    for row in range(2):
        top = own_ref[row]
        bottom = own_ref[rows - 2 + row]
        pair_ref[row] = jnp.where(even, bottom, top)
        other_ref[row] = jnp.where(even, top, bottom)
    total = jnp.zeros((8, channels), jnp.float32)
    square = jnp.zeros((8, channels), jnp.float32)
    for row in range(rows):
        total, square = add_sums(own_ref[row].astype(jnp.float32), total, square)
    store_sums(total, square, out_ref)


def weights_kernel(one_ref, two_ref, *rest):
    vectors, outs = rest[:6], rest[6:]
    for source, target in ((one_ref, outs[0]), (two_ref, outs[1])):
        taps, channels = source.shape[1], source.shape[2]
        for tap in range(taps):
            total = source[0, tap].astype(jnp.float32)
            total += source[1, tap].astype(jnp.float32)
            total += source[2, tap].astype(jnp.float32)
            high = total.astype(jnp.bfloat16)
            low = (total - high.astype(jnp.float32)).astype(jnp.bfloat16)
            target[pl.ds(tap * channels, channels), :] = jnp.concatenate([high, low], axis=1)
    for i in range(6):
        outs[2 + i // 3][pl.ds(i % 3, 1), :] = vectors[i][...]


def scale_offset(sums_ref, params_ref, entries):
    sums = jnp.sum(sums_ref[...], axis=0)
    channels = sums.shape[1]
    per_group = channels // GROUPS
    sums = jnp.concatenate([sums, jnp.zeros((6, channels), jnp.float32)], axis=0)
    member = lax.broadcasted_iota(jnp.int32, sums.shape, 1) % per_group
    total = sums
    for step in range(1, per_group):
        total += jnp.where(member >= step, pltpu.roll(sums, step, 1), 0.0)
        total += jnp.where(member < per_group - step, pltpu.roll(sums, channels - step, 1), 0.0)
    total = total * (1.0 / (entries * per_group))
    mean = total[0:1]
    var = total[1:2] - mean * mean
    scale = params_ref[1:2, :] * lax.rsqrt(var + 1e-06)
    return 0.5 * scale, 0.5 * (params_ref[2:3, :] - mean * scale)


def store_taps(values, scale, offset, wide_ref, taps_ref, row):
    width, channels = values.shape
    half = values.astype(jnp.float32) * scale + offset
    act = half * jnp.tanh(half) + half
    wide_ref[row, 8 : 8 + width, :] = act
    wide_ref[row, 7:8, :] = act[0:1]
    wide_ref[row, 8 + width : 9 + width, :] = act[width - 1 : width]
    for tap in range(3):
        shifted = wide_ref[row, 7 + tap : 7 + tap + width, :]
        taps_ref[row, :, tap * channels : (tap + 1) * channels] = shifted.astype(jnp.bfloat16)


def conv_rows(taps_ref, row, count, weight_ref, params_ref):
    _, width, lanes = taps_ref.shape
    window = jnp.concatenate(
        [taps_ref[row + tap : row + tap + count].reshape(count * width, lanes) for tap in range(3)],
        axis=1,
    )
    both = jnp.dot(window, weight_ref[...], preferred_element_type=jnp.float32)
    half = both.shape[1] // 2
    return both[:, :half] + both[:, half:] + params_ref[0:1, :]


def first_kernel(
    count, sums_ref, own_ref, other_ref, pair_ref, weight_ref, params_ref,
    hidden_ref, out_ref, wide_ref, taps_ref,
):
    index = lax.axis_index("rows")
    rows, width, channels = own_ref.shape
    even = index % 2 == 0
    scale, offset = scale_offset(sums_ref, params_ref, rows * width * count)

    def make(row):
        if row < 2:
            values = jnp.where(even, other_ref[row], pair_ref[row])
            values = jnp.where(index == 0, own_ref[0], values)
        elif row < rows + 2:
            values = own_ref[row - 2]
        else:
            values = jnp.where(even, pair_ref[row - rows - 2], other_ref[row - rows - 2])
            values = jnp.where(index == count - 1, own_ref[rows - 1], values)
        store_taps(values, scale, offset, wide_ref, taps_ref, row)

    total = jnp.zeros((8, channels), jnp.float32)
    square = jnp.zeros((8, channels), jnp.float32)
    make(0)
    make(1)
    for row in range(0, rows + 2, 2):
        make(row + 2)
        make(row + 3)
        hidden = conv_rows(taps_ref, row, 2, weight_ref, params_ref).astype(jnp.bfloat16)
        for i in range(2):
            values = hidden[i * width : (i + 1) * width]
            hidden_ref[row + i] = values
            if 0 < row + i <= rows:
                total, square = add_sums(values.astype(jnp.float32), total, square)
    store_sums(total, square, out_ref)

    @pl.when(index == 0)
    def _():
        hidden_ref[0] = hidden_ref[1]

    @pl.when(index == count - 1)
    def _():
        hidden_ref[rows + 1] = hidden_ref[rows]


def second_kernel(
    count, sums_ref, hidden_ref, own_ref, weight_ref, params_ref,
    out_ref, wide_ref, taps_ref, done_ref, sems,
):
    rows, width, channels = own_ref.shape
    scale, offset = scale_offset(sums_ref, params_ref, rows * width * count)
    copies = [
        pltpu.make_async_copy(done_ref.at[row], out_ref.at[row], sems.at[row])
        for row in range(rows)
    ]
    for row in range(2):
        store_taps(hidden_ref[row], scale, offset, wide_ref, taps_ref, row)
    for row in range(0, rows, 2):
        for i in range(2):
            store_taps(hidden_ref[row + 2 + i], scale, offset, wide_ref, taps_ref, row + 2 + i)
        branch = conv_rows(taps_ref, row, 2, weight_ref, params_ref)
        for i in range(2):
            values = own_ref[row + i].astype(jnp.float32) + branch[i * width : (i + 1) * width]
            done_ref[row + i] = values.astype(jnp.bfloat16)
            copies[row + i].start()
    for copy in copies:
        copy.wait()


def prepared(weights, vectors):
    taps, channels = weights[0].shape[1] * weights[0].shape[2], weights[0].shape[3]
    weight_shape = jax.ShapeDtypeStruct((taps * channels, 2 * channels), jnp.bfloat16)
    vector_shape = jax.ShapeDtypeStruct((8, channels), jnp.float32)
    return pl.pallas_call(
        weights_kernel,
        out_shape=[weight_shape] * 2 + [vector_shape] * 2,
        in_specs=[VMEM] * 8,
        out_specs=[VMEM] * 4,
        compiler_params=PARAMS,
        name="weights",
        cost_estimate=pl.CostEstimate(flops=2000000, bytes_accessed=3000000, transcendentals=0),
    )(
        *[weight.reshape(3, taps, channels, channels) for weight in weights],
        *[vector.reshape(1, channels) for vector in vectors],
    )


def exchanged(sums):
    return lax.all_to_all(sums, "rows", 0, 0)


def body(
    latents, gain_one, shift_one, weight_one, bias_one, gain_two, shift_two, weight_two, bias_two
):
    count = lax.axis_size("rows")
    own = latents[0]
    rows, width, channels = own.shape
    sums_shape = jax.ShapeDtypeStruct((count, 2, channels), jnp.float32)
    slab_shape = jax.ShapeDtypeStruct((2, width, channels), jnp.bfloat16)
    swap_pair = [(i, i ^ 1) for i in range(count)]
    swap_other = [(i, i + 1 if i % 2 else i - 1) for i in range(1, count - 1)]

    sums, other, pair = pl.pallas_call(
        sums_kernel, out_shape=[sums_shape] + [slab_shape] * 2, in_specs=[VMEM],
        out_specs=[VMEM] * 3, compiler_params=PARAMS, name="sums",
        cost_estimate=pl.CostEstimate(
            flops=40000000000, bytes_accessed=10000000, transcendentals=0
        ),
    )(own)
    sums = exchanged(sums)
    other = lax.ppermute(other, "rows", swap_other)
    pair = lax.ppermute(pair, "rows", swap_pair)
    one, two, params_one, params_two = prepared(
        (weight_one, weight_two),
        (bias_one, gain_one, shift_one, bias_two, gain_two, shift_two),
    )
    hidden, sums = pl.pallas_call(
        functools.partial(first_kernel, count),
        out_shape=[jax.ShapeDtypeStruct((rows + 2, width, channels), jnp.bfloat16), sums_shape],
        in_specs=[VMEM] * 6,
        out_specs=[VMEM] * 2,
        scratch_shapes=[
            pltpu.VMEM((rows + 4, width + 16, channels), jnp.float32),
            pltpu.VMEM((rows + 4, width, 3 * channels), jnp.bfloat16),
        ],
        compiler_params=PARAMS, name="first",
    )(sums, own, other, pair, one, params_one)
    sums = exchanged(sums)
    decoded = pl.pallas_call(
        functools.partial(second_kernel, count),
        out_shape=jax.ShapeDtypeStruct(own.shape, jnp.bfloat16),
        in_specs=[VMEM] * 5,
        out_specs=ANY,
        scratch_shapes=[
            pltpu.VMEM((rows + 2, width + 16, channels), jnp.float32),
            pltpu.VMEM((rows + 2, width, 3 * channels), jnp.bfloat16),
            pltpu.VMEM(own.shape, jnp.bfloat16),
            pltpu.SemaphoreType.DMA((rows,)),
        ],
        compiler_params=PARAMS, name="second",
    )(sums, hidden, own, two, params_two)
    return decoded[None]


def solution(mesh):
    return jax.shard_map(
        body,
        mesh=mesh,
        in_specs=(P("groups", "rows", None, None), P(), P(), P(), P(), P(), P(), P(), P()),
        out_specs=P("groups", "rows", None, None),
        check_vma=False,
    )
```

```python
import functools

import jax
import jax.numpy as jnp
from jax import lax
from jax.experimental import pallas as pl
from jax.experimental.pallas import tpu as pltpu
from jax.sharding import PartitionSpec as P

GROUPS = 32
ANY = pl.BlockSpec(memory_space=pl.ANY)
VMEM = pl.BlockSpec(memory_space=pltpu.VMEM)
PARAMS = pltpu.CompilerParams(vmem_limit_bytes=24 * 1024 * 1024)


def store_sums(total, square, out_ref):
    total = jnp.sum(total, axis=0, keepdims=True)
    square = jnp.sum(square, axis=0, keepdims=True)
    both = jnp.concatenate([total, square], axis=0)
    out_ref[...] = jnp.broadcast_to(both[None], out_ref.shape)


def add_sums(values, total, square):
    width, channels = values.shape
    split = (width // 8, 8, channels)
    total += jnp.sum(values.reshape(split), axis=0)
    square += jnp.sum((values * values).reshape(split), axis=0)
    return total, square


def sums_kernel(own_ref, out_ref, pair_ref, other_ref):
    rows, _, channels = own_ref.shape
    even = lax.axis_index("rows") % 2 == 0
    for row in range(2):
        top = own_ref[row]
        bottom = own_ref[rows - 2 + row]
        pair_ref[row] = jnp.where(even, bottom, top)
        other_ref[row] = jnp.where(even, top, bottom)
    total = jnp.zeros((8, channels), jnp.float32)
    square = jnp.zeros((8, channels), jnp.float32)
    for row in range(rows):
        total, square = add_sums(own_ref[row].astype(jnp.float32), total, square)
    store_sums(total, square, out_ref)


def weights_kernel(sums_ref, one_ref, two_ref, *rest):
    vectors, outs, copies_ref = rest[:6], rest[6:10], rest[10]
    copies_ref[...] = jnp.broadcast_to(sums_ref[...], copies_ref.shape)
    for source, target in ((one_ref, outs[0]), (two_ref, outs[1])):
        taps, channels = source.shape[1], source.shape[2]
        for tap in range(taps):
            total = source[0, tap].astype(jnp.float32)
            total += source[1, tap].astype(jnp.float32)
            total += source[2, tap].astype(jnp.float32)
            high = total.astype(jnp.bfloat16)
            low = (total - high.astype(jnp.float32)).astype(jnp.bfloat16)
            target[pl.ds(tap * channels, channels), :] = jnp.concatenate([high, low], axis=1)
    for i in range(6):
        outs[2 + i // 3][pl.ds(i % 3, 1), :] = vectors[i][...]


def scale_offset(sums_ref, params_ref, entries):
    sums = jnp.sum(sums_ref[...], axis=0)
    channels = sums.shape[1]
    per_group = channels // GROUPS
    sums = jnp.concatenate([sums, jnp.zeros((6, channels), jnp.float32)], axis=0)
    member = lax.broadcasted_iota(jnp.int32, sums.shape, 1) % per_group
    total = sums
    for step in range(1, per_group):
        total += jnp.where(member >= step, pltpu.roll(sums, step, 1), 0.0)
        total += jnp.where(member < per_group - step, pltpu.roll(sums, channels - step, 1), 0.0)
    total = total * (1.0 / (entries * per_group))
    mean = total[0:1]
    var = total[1:2] - mean * mean
    scale = params_ref[1:2, :] * lax.rsqrt(var + 1e-06)
    return 0.5 * scale, 0.5 * (params_ref[2:3, :] - mean * scale)


def store_taps(values, scale, offset, wide_ref, taps_ref, row):
    width, channels = values.shape
    half = values.astype(jnp.float32) * scale + offset
    act = half * jnp.tanh(half) + half
    wide_ref[row, 8 : 8 + width, :] = act
    wide_ref[row, 7:8, :] = act[0:1]
    wide_ref[row, 8 + width : 9 + width, :] = act[width - 1 : width]
    for tap in range(3):
        shifted = wide_ref[row, 7 + tap : 7 + tap + width, :]
        taps_ref[row, :, tap * channels : (tap + 1) * channels] = shifted.astype(jnp.bfloat16)


def conv_rows(taps_ref, row, count, weight_ref, params_ref):
    _, width, lanes = taps_ref.shape
    window = jnp.concatenate(
        [taps_ref[row + tap : row + tap + count].reshape(count * width, lanes) for tap in range(3)],
        axis=1,
    )
    both = jnp.dot(window, weight_ref[...], preferred_element_type=jnp.float32)
    half = both.shape[1] // 2
    return both[:, :half] + both[:, half:] + params_ref[0:1, :]


def first_kernel(
    count, sums_ref, own_ref, pair_ref, other_ref, weight_ref, params_ref,
    hidden_ref, out_ref, wide_ref, taps_ref,
):
    index = lax.axis_index("rows")
    rows, width, channels = own_ref.shape
    even = index % 2 == 0
    scale, offset = scale_offset(sums_ref, params_ref, rows * width * count)

    def make(row):
        if row < 2:
            values = jnp.where(even, other_ref[row], pair_ref[row])
            values = jnp.where(index == 0, own_ref[0], values)
        elif row < rows + 2:
            values = own_ref[row - 2]
        else:
            values = jnp.where(even, pair_ref[row - rows - 2], other_ref[row - rows - 2])
            values = jnp.where(index == count - 1, own_ref[rows - 1], values)
        store_taps(values, scale, offset, wide_ref, taps_ref, row)

    total = jnp.zeros((8, channels), jnp.float32)
    square = jnp.zeros((8, channels), jnp.float32)
    make(0)
    make(1)
    for row in range(0, rows + 2, 2):
        make(row + 2)
        make(row + 3)
        hidden = conv_rows(taps_ref, row, 2, weight_ref, params_ref).astype(jnp.bfloat16)
        for i in range(2):
            values = hidden[i * width : (i + 1) * width]
            hidden_ref[row + i] = values
            if 0 < row + i <= rows:
                total, square = add_sums(values.astype(jnp.float32), total, square)
    store_sums(total, square, out_ref)

    @pl.when(index == 0)
    def _():
        hidden_ref[0] = hidden_ref[1]

    @pl.when(index == count - 1)
    def _():
        hidden_ref[rows + 1] = hidden_ref[rows]


def second_kernel(
    count, sums_ref, hidden_ref, own_ref, weight_ref, params_ref,
    out_ref, wide_ref, taps_ref, done_ref, sems,
):
    rows, width, channels = own_ref.shape
    scale, offset = scale_offset(sums_ref, params_ref, rows * width * count)
    copies = [
        pltpu.make_async_copy(done_ref.at[row], out_ref.at[row], sems.at[row])
        for row in range(rows)
    ]
    for row in range(2):
        store_taps(hidden_ref[row], scale, offset, wide_ref, taps_ref, row)
    for row in range(0, rows, 2):
        for i in range(2):
            store_taps(hidden_ref[row + 2 + i], scale, offset, wide_ref, taps_ref, row + 2 + i)
        branch = conv_rows(taps_ref, row, 2, weight_ref, params_ref)
        for i in range(2):
            values = own_ref[row + i].astype(jnp.float32) + branch[i * width : (i + 1) * width]
            done_ref[row + i] = values.astype(jnp.bfloat16)
            copies[row + i].start()
    for copy in copies:
        copy.wait()


def prepared(sums, count, weights, vectors):
    taps, channels = weights[0].shape[1] * weights[0].shape[2], weights[0].shape[3]
    weight_shape = jax.ShapeDtypeStruct((taps * channels, 2 * channels), jnp.bfloat16)
    vector_shape = jax.ShapeDtypeStruct((8, channels), jnp.float32)
    return pl.pallas_call(
        weights_kernel,
        out_shape=[weight_shape] * 2
        + [vector_shape] * 2
        + [jax.ShapeDtypeStruct((count, 2, channels), jnp.float32)],
        in_specs=[VMEM] * 9,
        out_specs=[VMEM] * 5,
        compiler_params=PARAMS,
        name="weights",
        cost_estimate=pl.CostEstimate(flops=2000000, bytes_accessed=3000000, transcendentals=0),
    )(
        sums,
        *[weight.reshape(3, taps, channels, channels) for weight in weights],
        *[vector.reshape(1, channels) for vector in vectors],
    )


def exchanged(sums):
    return lax.all_to_all(sums, "rows", 0, 0)


def body(
    latents, gain_one, shift_one, weight_one, bias_one, gain_two, shift_two, weight_two, bias_two
):
    count = lax.axis_size("rows")
    own = latents[0]
    rows, width, channels = own.shape
    sums_shape = jax.ShapeDtypeStruct((count, 2, channels), jnp.float32)
    slab_shape = jax.ShapeDtypeStruct((2, width, channels), jnp.bfloat16)
    swap_pair = [(i, i ^ 1) for i in range(count)]
    swap_other = [(i, i + 1 if i % 2 else i - 1) for i in range(1, count - 1)]

    sums, pair, other = pl.pallas_call(
        sums_kernel,
        out_shape=[jax.ShapeDtypeStruct((1, 2, channels), jnp.float32)] + [slab_shape] * 2, in_specs=[VMEM],
        out_specs=[VMEM] * 3, compiler_params=PARAMS, name="sums",
        cost_estimate=pl.CostEstimate(
            flops=40000000000, bytes_accessed=10000000, transcendentals=0
        ),
    )(own)
    other = lax.ppermute(other, "rows", swap_other)
    pair = lax.ppermute(pair, "rows", swap_pair)
    one, two, params_one, params_two, sums = prepared(
        sums,
        count,
        (weight_one, weight_two),
        (bias_one, gain_one, shift_one, bias_two, gain_two, shift_two),
    )
    sums = exchanged(sums)
    hidden, sums = pl.pallas_call(
        functools.partial(first_kernel, count),
        out_shape=[jax.ShapeDtypeStruct((rows + 2, width, channels), jnp.bfloat16), sums_shape],
        in_specs=[VMEM] * 6,
        out_specs=[VMEM] * 2,
        scratch_shapes=[
            pltpu.VMEM((rows + 4, width + 16, channels), jnp.float32),
            pltpu.VMEM((rows + 4, width, 3 * channels), jnp.bfloat16),
        ],
        compiler_params=PARAMS, name="first",
    )(sums, own, pair, other, one, params_one)
    sums = exchanged(sums)
    decoded = pl.pallas_call(
        functools.partial(second_kernel, count),
        out_shape=jax.ShapeDtypeStruct(own.shape, jnp.bfloat16),
        in_specs=[VMEM] * 5,
        out_specs=ANY,
        scratch_shapes=[
            pltpu.VMEM((rows + 2, width + 16, channels), jnp.float32),
            pltpu.VMEM((rows + 2, width, 3 * channels), jnp.bfloat16),
            pltpu.VMEM(own.shape, jnp.bfloat16),
            pltpu.SemaphoreType.DMA((rows,)),
        ],
        compiler_params=PARAMS, name="second",
    )(sums, hidden, own, two, params_two)
    return decoded[None]


def solution(mesh):
    return jax.shard_map(
        body,
        mesh=mesh,
        in_specs=(P("groups", "rows", None, None), P(), P(), P(), P(), P(), P(), P(), P()),
        out_specs=P("groups", "rows", None, None),
        check_vma=False,
    )
```

```python
import functools

import jax
import jax.numpy as jnp
from jax import lax
from jax.experimental import pallas as pl
from jax.experimental.pallas import tpu as pltpu
from jax.sharding import PartitionSpec as P

GROUPS = 32
ANY = pl.BlockSpec(memory_space=pl.ANY)
VMEM = pl.BlockSpec(memory_space=pltpu.VMEM)
PARAMS = pltpu.CompilerParams(vmem_limit_bytes=24 * 1024 * 1024)


def store_sums(total, square, out_ref):
    total = jnp.sum(total, axis=0, keepdims=True)
    square = jnp.sum(square, axis=0, keepdims=True)
    both = jnp.concatenate([total, square], axis=0)
    out_ref[...] = jnp.broadcast_to(both[None], out_ref.shape)


def add_sums(values, total, square):
    width, channels = values.shape
    split = (width // 8, 8, channels)
    total += jnp.sum(values.reshape(split), axis=0)
    square += jnp.sum((values * values).reshape(split), axis=0)
    return total, square


def sums_kernel(own_ref, *rest):
    vectors, (out_ref, pair_ref, other_ref, one_ref, two_ref) = rest[:6], rest[6:]
    for i in range(3):
        one_ref[pl.ds(i, 1), :] = vectors[i][...]
        two_ref[pl.ds(i, 1), :] = vectors[3 + i][...]
    rows, _, channels = own_ref.shape
    even = lax.axis_index("rows") % 2 == 0
    for row in range(2):
        top = own_ref[row]
        bottom = own_ref[rows - 2 + row]
        pair_ref[row] = jnp.where(even, bottom, top)
        other_ref[row] = jnp.where(even, top, bottom)
    total = jnp.zeros((8, channels), jnp.float32)
    square = jnp.zeros((8, channels), jnp.float32)
    for row in range(rows):
        total, square = add_sums(own_ref[row].astype(jnp.float32), total, square)
    store_sums(total, square, out_ref)


def sum_weight(source, target):
    taps, channels = source.shape[1], source.shape[2]
    for tap in range(taps):
        total = source[0, tap].astype(jnp.float32)
        total += source[1, tap].astype(jnp.float32)
        total += source[2, tap].astype(jnp.float32)
        high = total.astype(jnp.bfloat16)
        low = (total - high.astype(jnp.float32)).astype(jnp.bfloat16)
        target[pl.ds(tap * channels, channels), :] = jnp.concatenate([high, low], axis=1)


def scale_offset(sums_ref, params_ref, entries):
    sums = jnp.sum(sums_ref[...], axis=0)
    channels = sums.shape[1]
    per_group = channels // GROUPS
    sums = jnp.concatenate([sums, jnp.zeros((6, channels), jnp.float32)], axis=0)
    member = lax.broadcasted_iota(jnp.int32, sums.shape, 1) % per_group
    total = sums
    for step in range(1, per_group):
        total += jnp.where(member >= step, pltpu.roll(sums, step, 1), 0.0)
        total += jnp.where(member < per_group - step, pltpu.roll(sums, channels - step, 1), 0.0)
    total = total * (1.0 / (entries * per_group))
    mean = total[0:1]
    var = total[1:2] - mean * mean
    scale = params_ref[1:2, :] * lax.rsqrt(var + 1e-06)
    return 0.5 * scale, 0.5 * (params_ref[2:3, :] - mean * scale)


def store_taps(values, scale, offset, wide_ref, taps_ref, row):
    width, channels = values.shape
    half = values.astype(jnp.float32) * scale + offset
    act = half * jnp.tanh(half) + half
    wide_ref[row, 8 : 8 + width, :] = act
    wide_ref[row, 7:8, :] = act[0:1]
    wide_ref[row, 8 + width : 9 + width, :] = act[width - 1 : width]
    for tap in range(3):
        shifted = wide_ref[row, 7 + tap : 7 + tap + width, :]
        taps_ref[row, :, tap * channels : (tap + 1) * channels] = shifted.astype(jnp.bfloat16)


def conv_rows(taps_ref, row, count, weight_ref, params_ref):
    _, width, lanes = taps_ref.shape
    window = jnp.concatenate(
        [taps_ref[row + tap : row + tap + count].reshape(count * width, lanes) for tap in range(3)],
        axis=1,
    )
    both = jnp.dot(window, weight_ref[...], preferred_element_type=jnp.float32)
    half = both.shape[1] // 2
    return both[:, :half] + both[:, half:] + params_ref[0:1, :]


def first_kernel(
    count, sums_ref, own_ref, pair_ref, other_ref, weight_ref, params_ref,
    hidden_ref, out_ref, wide_ref, taps_ref, summed_ref,
):
    index = lax.axis_index("rows")
    rows, width, channels = own_ref.shape
    even = index % 2 == 0
    scale, offset = scale_offset(sums_ref, params_ref, rows * width * count)
    sum_weight(weight_ref, summed_ref)

    def make(row):
        if row < 2:
            values = jnp.where(even, other_ref[row], pair_ref[row])
            values = jnp.where(index == 0, own_ref[0], values)
        elif row < rows + 2:
            values = own_ref[row - 2]
        else:
            values = jnp.where(even, pair_ref[row - rows - 2], other_ref[row - rows - 2])
            values = jnp.where(index == count - 1, own_ref[rows - 1], values)
        store_taps(values, scale, offset, wide_ref, taps_ref, row)

    total = jnp.zeros((8, channels), jnp.float32)
    square = jnp.zeros((8, channels), jnp.float32)
    make(0)
    make(1)
    for row in range(0, rows + 2, 2):
        make(row + 2)
        make(row + 3)
        hidden = conv_rows(taps_ref, row, 2, summed_ref, params_ref).astype(jnp.bfloat16)
        for i in range(2):
            values = hidden[i * width : (i + 1) * width]
            hidden_ref[row + i] = values
            if 0 < row + i <= rows:
                total, square = add_sums(values.astype(jnp.float32), total, square)
    store_sums(total, square, out_ref)

    @pl.when(index == 0)
    def _():
        hidden_ref[0] = hidden_ref[1]

    @pl.when(index == count - 1)
    def _():
        hidden_ref[rows + 1] = hidden_ref[rows]


def second_kernel(
    count, sums_ref, hidden_ref, own_ref, weight_ref, params_ref,
    out_ref, wide_ref, taps_ref, summed_ref, done_ref, sems,
):
    rows, width, channels = own_ref.shape
    scale, offset = scale_offset(sums_ref, params_ref, rows * width * count)
    sum_weight(weight_ref, summed_ref)
    copies = [
        pltpu.make_async_copy(done_ref.at[row], out_ref.at[row], sems.at[row])
        for row in range(rows)
    ]
    for row in range(2):
        store_taps(hidden_ref[row], scale, offset, wide_ref, taps_ref, row)
    for row in range(0, rows, 2):
        for i in range(2):
            store_taps(hidden_ref[row + 2 + i], scale, offset, wide_ref, taps_ref, row + 2 + i)
        branch = conv_rows(taps_ref, row, 2, summed_ref, params_ref)
        for i in range(2):
            values = own_ref[row + i].astype(jnp.float32) + branch[i * width : (i + 1) * width]
            done_ref[row + i] = values.astype(jnp.bfloat16)
            copies[row + i].start()
    for copy in copies:
        copy.wait()


def exchanged(sums):
    return lax.all_to_all(sums, "rows", 0, 0)


def body(
    latents, gain_one, shift_one, weight_one, bias_one, gain_two, shift_two, weight_two, bias_two
):
    count = lax.axis_size("rows")
    own = latents[0]
    rows, width, channels = own.shape
    sums_shape = jax.ShapeDtypeStruct((count, 2, channels), jnp.float32)
    taps = weight_one.shape[1] * weight_one.shape[2]
    summed = pltpu.VMEM((taps * channels, 2 * channels), jnp.bfloat16)
    slab_shape = jax.ShapeDtypeStruct((2, width, channels), jnp.bfloat16)

    def raw(weight):
        return weight.reshape(3, taps, channels, channels)

    swap_pair = [(i, i ^ 1) for i in range(count)]
    swap_other = [(i, i + 1 if i % 2 else i - 1) for i in range(1, count - 1)]

    vectors = (bias_one, gain_one, shift_one, bias_two, gain_two, shift_two)
    sums, pair, other, params_one, params_two = pl.pallas_call(
        sums_kernel,
        out_shape=[sums_shape]
        + [slab_shape] * 2
        + [jax.ShapeDtypeStruct((8, channels), jnp.float32)] * 2,
        in_specs=[VMEM] * 7,
        out_specs=[VMEM] * 5,
        compiler_params=PARAMS,
        name="sums",
        cost_estimate=pl.CostEstimate(
            flops=40000000000, bytes_accessed=10000000, transcendentals=0
        ),
    )(own, *[vector.reshape(1, channels) for vector in vectors])
    other = lax.ppermute(other, "rows", swap_other)
    pair = lax.ppermute(pair, "rows", swap_pair)
    sums = exchanged(sums)
    hidden, sums = pl.pallas_call(
        functools.partial(first_kernel, count),
        out_shape=[jax.ShapeDtypeStruct((rows + 2, width, channels), jnp.bfloat16), sums_shape],
        in_specs=[VMEM] * 6,
        out_specs=[VMEM] * 2,
        scratch_shapes=[
            pltpu.VMEM((rows + 4, width + 16, channels), jnp.float32),
            pltpu.VMEM((rows + 4, width, 3 * channels), jnp.bfloat16),
            summed,
        ],
        compiler_params=PARAMS, name="first",
    )(sums, own, pair, other, raw(weight_one), params_one)
    sums = exchanged(sums)
    decoded = pl.pallas_call(
        functools.partial(second_kernel, count),
        out_shape=jax.ShapeDtypeStruct(own.shape, jnp.bfloat16),
        in_specs=[VMEM] * 5,
        out_specs=ANY,
        scratch_shapes=[
            pltpu.VMEM((rows + 2, width + 16, channels), jnp.float32),
            pltpu.VMEM((rows + 2, width, 3 * channels), jnp.bfloat16),
            summed,
            pltpu.VMEM(own.shape, jnp.bfloat16),
            pltpu.SemaphoreType.DMA((rows,)),
        ],
        compiler_params=PARAMS, name="second",
    )(sums, hidden, own, raw(weight_two), params_two)
    return decoded[None]


def solution(mesh):
    return jax.shard_map(
        body,
        mesh=mesh,
        in_specs=(P("groups", "rows", None, None), P(), P(), P(), P(), P(), P(), P(), P()),
        out_specs=P("groups", "rows", None, None),
        check_vma=False,
    )
```

```python
import functools

import jax
import jax.numpy as jnp
from jax import lax
from jax.experimental import pallas as pl
from jax.experimental.pallas import tpu as pltpu
from jax.sharding import PartitionSpec as P

GROUPS = 32
HBM = pl.BlockSpec(memory_space=pltpu.HBM)
ANY = pl.BlockSpec(memory_space=pl.ANY)
VMEM = pl.BlockSpec(memory_space=pltpu.VMEM)
PARAMS = pltpu.CompilerParams(vmem_limit_bytes=24 * 1024 * 1024)


def store_sums(total, square, out_ref):
    total = jnp.sum(total, axis=0, keepdims=True)
    square = jnp.sum(square, axis=0, keepdims=True)
    both = jnp.concatenate([total, square], axis=0)
    out_ref[...] = jnp.broadcast_to(both[None], out_ref.shape)


def add_sums(values, total, square):
    width, channels = values.shape
    split = (width // 8, 8, channels)
    total += jnp.sum(values.reshape(split), axis=0)
    square += jnp.sum((values * values).reshape(split), axis=0)
    return total, square


def sums_kernel(latents_ref, *rest):
    sources, (out_ref, own_ref, pair_ref, other_ref, one_ref, two_ref) = rest[:6], rest[6:12]
    vectors_ref, sems, vector_sems = rest[12:]
    rows, _, channels = own_ref.shape
    copies = [
        pltpu.make_async_copy(latents_ref.at[row], own_ref.at[row], sems.at[row])
        for row in range(rows)
    ]
    vector_copies = [
        pltpu.make_async_copy(source, vectors_ref.at[i], vector_sems.at[i])
        for i, source in enumerate(sources)
    ]
    for copy in copies + vector_copies:
        copy.start()
    total = jnp.zeros((8, channels), jnp.float32)
    square = jnp.zeros((8, channels), jnp.float32)
    for row in range(rows):
        copies[row].wait()
        total, square = add_sums(own_ref[row].astype(jnp.float32), total, square)
    store_sums(total, square, out_ref)
    even = lax.axis_index("rows") % 2 == 0
    for row in range(2):
        top = own_ref[row]
        bottom = own_ref[rows - 2 + row]
        pair_ref[row] = jnp.where(even, bottom, top)
        other_ref[row] = jnp.where(even, top, bottom)
    for copy in vector_copies:
        copy.wait()
    for i in range(3):
        one_ref[pl.ds(i, 1), :] = vectors_ref[i]
        two_ref[pl.ds(i, 1), :] = vectors_ref[3 + i]


def sum_weight(source, target):
    taps, channels = source.shape[1], source.shape[2]
    for tap in range(taps):
        total = source[0, tap].astype(jnp.float32)
        total += source[1, tap].astype(jnp.float32)
        total += source[2, tap].astype(jnp.float32)
        high = total.astype(jnp.bfloat16)
        low = (total - high.astype(jnp.float32)).astype(jnp.bfloat16)
        target[pl.ds(tap * channels, channels), :] = jnp.concatenate([high, low], axis=1)


def scale_offset(sums_ref, params_ref, entries):
    sums = jnp.sum(sums_ref[...], axis=0)
    channels = sums.shape[1]
    per_group = channels // GROUPS
    sums = jnp.concatenate([sums, jnp.zeros((6, channels), jnp.float32)], axis=0)
    member = lax.broadcasted_iota(jnp.int32, sums.shape, 1) % per_group
    total = sums
    for step in range(1, per_group):
        total += jnp.where(member >= step, pltpu.roll(sums, step, 1), 0.0)
        total += jnp.where(member < per_group - step, pltpu.roll(sums, channels - step, 1), 0.0)
    total = total * (1.0 / (entries * per_group))
    mean = total[0:1]
    var = total[1:2] - mean * mean
    scale = params_ref[1:2, :] * lax.rsqrt(var + 1e-06)
    return 0.5 * scale, 0.5 * (params_ref[2:3, :] - mean * scale)


def store_taps(values, scale, offset, wide_ref, taps_ref, row):
    width, channels = values.shape
    half = values.astype(jnp.float32) * scale + offset
    act = half * jnp.tanh(half) + half
    wide_ref[row, 8 : 8 + width, :] = act
    wide_ref[row, 7:8, :] = act[0:1]
    wide_ref[row, 8 + width : 9 + width, :] = act[width - 1 : width]
    for tap in range(3):
        shifted = wide_ref[row, 7 + tap : 7 + tap + width, :]
        taps_ref[row, :, tap * channels : (tap + 1) * channels] = shifted.astype(jnp.bfloat16)


def conv_rows(taps_ref, row, count, weight_ref, params_ref):
    _, width, lanes = taps_ref.shape
    window = jnp.concatenate(
        [taps_ref[row + tap : row + tap + count].reshape(count * width, lanes) for tap in range(3)],
        axis=1,
    )
    both = jnp.dot(window, weight_ref[...], preferred_element_type=jnp.float32)
    half = both.shape[1] // 2
    return both[:, :half] + both[:, half:] + params_ref[0:1, :]


def first_kernel(
    count, sums_ref, own_ref, pair_ref, other_ref, weight_ref, params_ref,
    hidden_ref, out_ref, wide_ref, taps_ref, summed_ref,
):
    index = lax.axis_index("rows")
    rows, width, channels = own_ref.shape
    even = index % 2 == 0
    scale, offset = scale_offset(sums_ref, params_ref, rows * width * count)
    sum_weight(weight_ref, summed_ref)

    def make(row):
        if row < 2:
            values = jnp.where(even, other_ref[row], pair_ref[row])
            values = jnp.where(index == 0, own_ref[0], values)
        elif row < rows + 2:
            values = own_ref[row - 2]
        else:
            values = jnp.where(even, pair_ref[row - rows - 2], other_ref[row - rows - 2])
            values = jnp.where(index == count - 1, own_ref[rows - 1], values)
        store_taps(values, scale, offset, wide_ref, taps_ref, row)

    total = jnp.zeros((8, channels), jnp.float32)
    square = jnp.zeros((8, channels), jnp.float32)
    make(0)
    make(1)
    for row in range(0, rows + 2, 2):
        make(row + 2)
        make(row + 3)
        hidden = conv_rows(taps_ref, row, 2, summed_ref, params_ref).astype(jnp.bfloat16)
        for i in range(2):
            values = hidden[i * width : (i + 1) * width]
            hidden_ref[row + i] = values
            if 0 < row + i <= rows:
                total, square = add_sums(values.astype(jnp.float32), total, square)
    store_sums(total, square, out_ref)

    @pl.when(index == 0)
    def _():
        hidden_ref[0] = hidden_ref[1]

    @pl.when(index == count - 1)
    def _():
        hidden_ref[rows + 1] = hidden_ref[rows]


def second_kernel(
    count, sums_ref, hidden_ref, own_ref, weight_ref, params_ref,
    out_ref, wide_ref, taps_ref, summed_ref, done_ref, sems,
):
    rows, width, channels = own_ref.shape
    scale, offset = scale_offset(sums_ref, params_ref, rows * width * count)
    sum_weight(weight_ref, summed_ref)
    copies = [
        pltpu.make_async_copy(done_ref.at[row], out_ref.at[row], sems.at[row])
        for row in range(rows)
    ]
    for row in range(2):
        store_taps(hidden_ref[row], scale, offset, wide_ref, taps_ref, row)
    for row in range(0, rows, 2):
        for i in range(2):
            store_taps(hidden_ref[row + 2 + i], scale, offset, wide_ref, taps_ref, row + 2 + i)
        branch = conv_rows(taps_ref, row, 2, summed_ref, params_ref)
        for i in range(2):
            values = own_ref[row + i].astype(jnp.float32) + branch[i * width : (i + 1) * width]
            done_ref[row + i] = values.astype(jnp.bfloat16)
            copies[row + i].start()
    for copy in copies:
        copy.wait()


def exchanged(sums):
    return lax.all_to_all(sums, "rows", 0, 0)


def body(
    latents, gain_one, shift_one, weight_one, bias_one, gain_two, shift_two, weight_two, bias_two
):
    count = lax.axis_size("rows")
    own = latents[0]
    rows, width, channels = own.shape
    sums_shape = jax.ShapeDtypeStruct((count, 2, channels), jnp.float32)
    taps = weight_one.shape[1] * weight_one.shape[2]
    summed = pltpu.VMEM((taps * channels, 2 * channels), jnp.bfloat16)
    slab_shape = jax.ShapeDtypeStruct((2, width, channels), jnp.bfloat16)

    def raw(weight):
        return weight.reshape(3, taps, channels, channels)

    swap_pair = [(i, i ^ 1) for i in range(count)]
    swap_other = [(i, i + 1 if i % 2 else i - 1) for i in range(1, count - 1)]

    vectors = (bias_one, gain_one, shift_one, bias_two, gain_two, shift_two)
    vector_shape = jax.ShapeDtypeStruct((8, channels), jnp.float32)
    sums, own, pair, other, params_one, params_two = pl.pallas_call(
        sums_kernel,
        out_shape=[sums_shape, jax.ShapeDtypeStruct(own.shape, own.dtype)]
        + [slab_shape] * 2
        + [vector_shape] * 2,
        in_specs=[HBM] * 7,
        out_specs=[VMEM] * 6,
        scratch_shapes=[
            pltpu.VMEM((6, 1, channels), jnp.float32),
            pltpu.SemaphoreType.DMA((rows,)),
            pltpu.SemaphoreType.DMA((6,)),
        ],
        compiler_params=PARAMS,
        name="sums",
        cost_estimate=pl.CostEstimate(
            flops=40000000000, bytes_accessed=10000000, transcendentals=0
        ),
    )(
        pltpu.with_memory_space_constraint(own, pltpu.HBM),
        *[
            pltpu.with_memory_space_constraint(vector.reshape(1, channels), pltpu.HBM)
            for vector in vectors
        ],
    )
    other = lax.ppermute(other, "rows", swap_other)
    pair = lax.ppermute(pair, "rows", swap_pair)
    sums = exchanged(sums)
    hidden, sums = pl.pallas_call(
        functools.partial(first_kernel, count),
        out_shape=[jax.ShapeDtypeStruct((rows + 2, width, channels), jnp.bfloat16), sums_shape],
        in_specs=[VMEM] * 6,
        out_specs=[VMEM] * 2,
        scratch_shapes=[
            pltpu.VMEM((rows + 4, width + 16, channels), jnp.float32),
            pltpu.VMEM((rows + 4, width, 3 * channels), jnp.bfloat16),
            summed,
        ],
        compiler_params=PARAMS, name="first",
    )(sums, own, pair, other, raw(weight_one), params_one)
    sums = exchanged(sums)
    decoded = pl.pallas_call(
        functools.partial(second_kernel, count),
        out_shape=jax.ShapeDtypeStruct(own.shape, jnp.bfloat16),
        in_specs=[VMEM] * 5,
        out_specs=ANY,
        scratch_shapes=[
            pltpu.VMEM((rows + 2, width + 16, channels), jnp.float32),
            pltpu.VMEM((rows + 2, width, 3 * channels), jnp.bfloat16),
            summed,
            pltpu.VMEM(own.shape, jnp.bfloat16),
            pltpu.SemaphoreType.DMA((rows,)),
        ],
        compiler_params=PARAMS, name="second",
    )(sums, hidden, own, raw(weight_two), params_two)
    return decoded[None]


def solution(mesh):
    return jax.shard_map(
        body,
        mesh=mesh,
        in_specs=(P("groups", "rows", None, None), P(), P(), P(), P(), P(), P(), P(), P()),
        out_specs=P("groups", "rows", None, None),
        check_vma=False,
    )
```

```python
import functools

import jax
import jax.numpy as jnp
from jax import lax
from jax.experimental import pallas as pl
from jax.experimental.pallas import tpu as pltpu
from jax.sharding import PartitionSpec as P

GROUPS = 32
HBM = pl.BlockSpec(memory_space=pltpu.HBM)
ANY = pl.BlockSpec(memory_space=pl.ANY)
VMEM = pl.BlockSpec(memory_space=pltpu.VMEM)
PARAMS = pltpu.CompilerParams(vmem_limit_bytes=24 * 1024 * 1024)


def store_sums(total, square, out_ref):
    total = jnp.sum(total, axis=0, keepdims=True)
    square = jnp.sum(square, axis=0, keepdims=True)
    both = jnp.concatenate([total, square], axis=0)
    out_ref[...] = jnp.broadcast_to(both[None], out_ref.shape)


def add_sums(values, total, square):
    width, channels = values.shape
    split = (width // 8, 8, channels)
    total += jnp.sum(values.reshape(split), axis=0)
    square += jnp.sum((values * values).reshape(split), axis=0)
    return total, square


def sums_kernel(latents_ref, *rest):
    sources, (out_ref, own_ref, pair_ref, other_ref, one_ref, two_ref) = rest[:6], rest[6:12]
    vectors_ref, sems, vector_sems = rest[12:]
    rows, _, channels = own_ref.shape
    copies = [
        pltpu.make_async_copy(latents_ref.at[row], own_ref.at[row], sems.at[row])
        for row in range(rows)
    ]
    vector_copies = [
        pltpu.make_async_copy(source, vectors_ref.at[i], vector_sems.at[i])
        for i, source in enumerate(sources)
    ]
    for copy in copies + vector_copies:
        copy.start()
    total = jnp.zeros((8, channels), jnp.float32)
    square = jnp.zeros((8, channels), jnp.float32)
    for row in range(rows):
        copies[row].wait()
        total, square = add_sums(own_ref[row].astype(jnp.float32), total, square)
    store_sums(total, square, out_ref)
    even = lax.axis_index("rows") % 2 == 0
    for row in range(2):
        top = own_ref[row]
        bottom = own_ref[rows - 2 + row]
        pair_ref[row] = jnp.where(even, bottom, top)
        other_ref[row] = jnp.where(even, top, bottom)
    for copy in vector_copies:
        copy.wait()
    for i in range(3):
        one_ref[pl.ds(i, 1), :] = vectors_ref[i]
        two_ref[pl.ds(i, 1), :] = vectors_ref[3 + i]


def sum_weight(source, target):
    taps, channels = source.shape[1], source.shape[2]
    for tap in range(taps):
        total = source[0, tap].astype(jnp.float32)
        total += source[1, tap].astype(jnp.float32)
        total += source[2, tap].astype(jnp.float32)
        high = total.astype(jnp.bfloat16)
        low = (total - high.astype(jnp.float32)).astype(jnp.bfloat16)
        target[pl.ds(tap * channels, channels), :] = jnp.concatenate([high, low], axis=1)


def scale_offset(sums_ref, params_ref, entries):
    sums = jnp.sum(sums_ref[...], axis=0)
    channels = sums.shape[1]
    per_group = channels // GROUPS
    sums = jnp.concatenate([sums, jnp.zeros((6, channels), jnp.float32)], axis=0)
    member = lax.broadcasted_iota(jnp.int32, sums.shape, 1) % per_group
    total = sums
    for step in range(1, per_group):
        total += jnp.where(member >= step, pltpu.roll(sums, step, 1), 0.0)
        total += jnp.where(member < per_group - step, pltpu.roll(sums, channels - step, 1), 0.0)
    total = total * (1.0 / (entries * per_group))
    mean = total[0:1]
    var = total[1:2] - mean * mean
    scale = params_ref[1:2, :] * lax.rsqrt(var + 1e-06)
    return 0.5 * scale, 0.5 * (params_ref[2:3, :] - mean * scale)


def store_taps(values, scale, offset, wide_ref, taps_ref, row):
    width, channels = values.shape
    half = values.astype(jnp.float32) * scale + offset
    act = half * jnp.tanh(half) + half
    wide_ref[row, 8 : 8 + width, :] = act
    wide_ref[row, 7:8, :] = act[0:1]
    wide_ref[row, 8 + width : 9 + width, :] = act[width - 1 : width]
    for tap in range(3):
        shifted = wide_ref[row, 7 + tap : 7 + tap + width, :]
        taps_ref[row, :, tap * channels : (tap + 1) * channels] = shifted.astype(jnp.bfloat16)


def conv_rows(taps_ref, row, count, weight_ref, params_ref):
    _, width, lanes = taps_ref.shape
    window = jnp.concatenate(
        [taps_ref[row + tap : row + tap + count].reshape(count * width, lanes) for tap in range(3)],
        axis=1,
    )
    both = jnp.dot(window, weight_ref[...], preferred_element_type=jnp.float32)
    half = both.shape[1] // 2
    return both[:, :half] + both[:, half:] + params_ref[0:1, :]


def first_kernel(
    count, sums_ref, own_ref, pair_ref, other_ref, weight_ref, params_ref,
    hidden_ref, out_ref, wide_ref, taps_ref, summed_ref,
):
    index = lax.axis_index("rows")
    rows, width, channels = own_ref.shape
    even = index % 2 == 0
    scale, offset = scale_offset(sums_ref, params_ref, rows * width * count)
    sum_weight(weight_ref, summed_ref)

    def make(row):
        if row < 2:
            values = jnp.where(even, other_ref[row], pair_ref[row])
            values = jnp.where(index == 0, own_ref[0], values)
        elif row < rows + 2:
            values = own_ref[row - 2]
        else:
            values = jnp.where(even, pair_ref[row - rows - 2], other_ref[row - rows - 2])
            values = jnp.where(index == count - 1, own_ref[rows - 1], values)
        store_taps(values, scale, offset, wide_ref, taps_ref, row)

    total = jnp.zeros((8, channels), jnp.float32)
    square = jnp.zeros((8, channels), jnp.float32)
    make(0)
    make(1)
    for row in range(0, rows + 2, 2):
        make(row + 2)
        make(row + 3)
        hidden = conv_rows(taps_ref, row, 2, summed_ref, params_ref).astype(jnp.bfloat16)
        for i in range(2):
            values = hidden[i * width : (i + 1) * width]
            hidden_ref[row + i] = values
            if 0 < row + i <= rows:
                total, square = add_sums(values.astype(jnp.float32), total, square)
    store_sums(total, square, out_ref)

    @pl.when(index == 0)
    def _():
        hidden_ref[0] = hidden_ref[1]

    @pl.when(index == count - 1)
    def _():
        hidden_ref[rows + 1] = hidden_ref[rows]


def second_kernel(
    count, sums_ref, hidden_ref, own_ref, weight_ref, params_ref,
    out_ref, wide_ref, taps_ref, summed_ref, done_ref, sems,
):
    rows, width, channels = own_ref.shape
    scale, offset = scale_offset(sums_ref, params_ref, rows * width * count)
    sum_weight(weight_ref, summed_ref)
    copies = [
        pltpu.make_async_copy(done_ref.at[row], out_ref.at[row], sems.at[row])
        for row in range(rows)
    ]
    for row in range(2):
        store_taps(hidden_ref[row], scale, offset, wide_ref, taps_ref, row)
    for row in range(0, rows, 2):
        for i in range(2):
            store_taps(hidden_ref[row + 2 + i], scale, offset, wide_ref, taps_ref, row + 2 + i)
        branch = conv_rows(taps_ref, row, 2, summed_ref, params_ref)
        for i in range(2):
            values = own_ref[row + i].astype(jnp.float32) + branch[i * width : (i + 1) * width]
            done_ref[row + i] = values.astype(jnp.bfloat16)
            copies[row + i].start()
    for copy in copies:
        copy.wait()


def exchanged(sums):
    return lax.all_to_all(sums, "rows", 0, 0)


def body(
    latents, gain_one, shift_one, weight_one, bias_one, gain_two, shift_two, weight_two, bias_two
):
    count = lax.axis_size("rows")
    own = latents[0]
    rows, width, channels = own.shape
    sums_shape = jax.ShapeDtypeStruct((count, 2, channels), jnp.float32)
    taps = weight_one.shape[1] * weight_one.shape[2]
    summed = pltpu.VMEM((taps * channels, 2 * channels), jnp.bfloat16)
    slab_shape = jax.ShapeDtypeStruct((2, width, channels), jnp.bfloat16)

    def raw(weight):
        return weight.reshape(3, taps, channels, channels)

    swap_pair = [(i, i ^ 1) for i in range(count)]
    swap_other = [(i, i + 1 if i % 2 else i - 1) for i in range(1, count - 1)]

    vectors = (bias_one, gain_one, shift_one, bias_two, gain_two, shift_two)
    vector_shape = jax.ShapeDtypeStruct((8, channels), jnp.float32)
    sums, own, pair, other, params_one, params_two = pl.pallas_call(
        sums_kernel,
        out_shape=[sums_shape, jax.ShapeDtypeStruct(own.shape, own.dtype)]
        + [slab_shape] * 2
        + [vector_shape] * 2,
        in_specs=[HBM] * 7,
        out_specs=[VMEM] * 6,
        scratch_shapes=[
            pltpu.VMEM((6, 1, channels), jnp.float32),
            pltpu.SemaphoreType.DMA((rows,)),
            pltpu.SemaphoreType.DMA((6,)),
        ],
        compiler_params=PARAMS,
        name="sums",
    )(
        pltpu.with_memory_space_constraint(own, pltpu.HBM),
        *[
            pltpu.with_memory_space_constraint(vector.reshape(1, channels), pltpu.HBM)
            for vector in vectors
        ],
    )
    other = lax.ppermute(other, "rows", swap_other)
    pair = lax.ppermute(pair, "rows", swap_pair)
    sums = exchanged(sums)
    hidden, sums = pl.pallas_call(
        functools.partial(first_kernel, count),
        out_shape=[jax.ShapeDtypeStruct((rows + 2, width, channels), jnp.bfloat16), sums_shape],
        in_specs=[VMEM] * 6,
        out_specs=[VMEM] * 2,
        scratch_shapes=[
            pltpu.VMEM((rows + 4, width + 16, channels), jnp.float32),
            pltpu.VMEM((rows + 4, width, 3 * channels), jnp.bfloat16),
            summed,
        ],
        compiler_params=PARAMS, name="first",
    )(sums, own, pair, other, raw(weight_one), params_one)
    sums = exchanged(sums)
    decoded = pl.pallas_call(
        functools.partial(second_kernel, count),
        out_shape=jax.ShapeDtypeStruct(own.shape, jnp.bfloat16),
        in_specs=[VMEM] * 5,
        out_specs=ANY,
        scratch_shapes=[
            pltpu.VMEM((rows + 2, width + 16, channels), jnp.float32),
            pltpu.VMEM((rows + 2, width, 3 * channels), jnp.bfloat16),
            summed,
            pltpu.VMEM(own.shape, jnp.bfloat16),
            pltpu.SemaphoreType.DMA((rows,)),
        ],
        compiler_params=PARAMS, name="second",
    )(sums, hidden, own, raw(weight_two), params_two)
    return decoded[None]


def solution(mesh):
    return jax.shard_map(
        body,
        mesh=mesh,
        in_specs=(P("groups", "rows", None, None), P(), P(), P(), P(), P(), P(), P(), P()),
        out_specs=P("groups", "rows", None, None),
        check_vma=False,
    )
```

```python
import functools

import jax
import jax.numpy as jnp
from jax import lax
from jax.experimental import pallas as pl
from jax.experimental.pallas import tpu as pltpu
from jax.sharding import PartitionSpec as P

GROUPS = 32
HBM = pl.BlockSpec(memory_space=pltpu.HBM)
ANY = pl.BlockSpec(memory_space=pl.ANY)
VMEM = pl.BlockSpec(memory_space=pltpu.VMEM)
PARAMS = pltpu.CompilerParams(vmem_limit_bytes=24 * 1024 * 1024)


def store_sums(total, square, out_ref):
    total = jnp.sum(total, axis=0, keepdims=True)
    square = jnp.sum(square, axis=0, keepdims=True)
    both = jnp.concatenate([total, square], axis=0)
    out_ref[...] = jnp.broadcast_to(both[None], out_ref.shape)


def add_sums(values, total, square):
    width, channels = values.shape
    split = (width // 8, 8, channels)
    total += jnp.sum(values.reshape(split), axis=0)
    square += jnp.sum((values * values).reshape(split), axis=0)
    return total, square


def sums_kernel(own_ref, out_ref):
    rows, _, channels = own_ref.shape
    total = jnp.zeros((8, channels), jnp.float32)
    square = jnp.zeros((8, channels), jnp.float32)
    for row in range(rows):
        total, square = add_sums(own_ref[row].astype(jnp.float32), total, square)
    store_sums(total, square, out_ref)


def load_kernel(latents_ref, *rest):
    sources, (own_ref, pair_ref, other_ref, one_ref, two_ref) = rest[:6], rest[6:11]
    vectors_ref, sems, vector_sems = rest[11:]
    rows, _, channels = own_ref.shape
    copies = [
        pltpu.make_async_copy(latents_ref.at[row], own_ref.at[row], sems.at[row])
        for row in range(rows)
    ]
    vector_copies = [
        pltpu.make_async_copy(source, vectors_ref.at[i], vector_sems.at[i])
        for i, source in enumerate(sources)
    ]
    for copy in copies + vector_copies:
        copy.start()
    for copy in copies:
        copy.wait()
    even = lax.axis_index("rows") % 2 == 0
    for row in range(2):
        top = own_ref[row]
        bottom = own_ref[rows - 2 + row]
        pair_ref[row] = jnp.where(even, bottom, top)
        other_ref[row] = jnp.where(even, top, bottom)
    for copy in vector_copies:
        copy.wait()
    for i in range(3):
        one_ref[pl.ds(i, 1), :] = vectors_ref[i]
        two_ref[pl.ds(i, 1), :] = vectors_ref[3 + i]


def sum_weight(source, target):
    taps, channels = source.shape[1], source.shape[2]
    for tap in range(taps):
        total = source[0, tap].astype(jnp.float32)
        total += source[1, tap].astype(jnp.float32)
        total += source[2, tap].astype(jnp.float32)
        high = total.astype(jnp.bfloat16)
        low = (total - high.astype(jnp.float32)).astype(jnp.bfloat16)
        target[pl.ds(tap * channels, channels), :] = jnp.concatenate([high, low], axis=1)


def scale_offset(sums_ref, params_ref, entries):
    sums = jnp.sum(sums_ref[...], axis=0)
    channels = sums.shape[1]
    per_group = channels // GROUPS
    sums = jnp.concatenate([sums, jnp.zeros((6, channels), jnp.float32)], axis=0)
    member = lax.broadcasted_iota(jnp.int32, sums.shape, 1) % per_group
    total = sums
    for step in range(1, per_group):
        total += jnp.where(member >= step, pltpu.roll(sums, step, 1), 0.0)
        total += jnp.where(member < per_group - step, pltpu.roll(sums, channels - step, 1), 0.0)
    total = total * (1.0 / (entries * per_group))
    mean = total[0:1]
    var = total[1:2] - mean * mean
    scale = params_ref[1:2, :] * lax.rsqrt(var + 1e-06)
    return 0.5 * scale, 0.5 * (params_ref[2:3, :] - mean * scale)


def store_taps(values, scale, offset, wide_ref, taps_ref, row):
    width, channels = values.shape
    half = values.astype(jnp.float32) * scale + offset
    act = half * jnp.tanh(half) + half
    wide_ref[row, 8 : 8 + width, :] = act
    wide_ref[row, 7:8, :] = act[0:1]
    wide_ref[row, 8 + width : 9 + width, :] = act[width - 1 : width]
    for tap in range(3):
        shifted = wide_ref[row, 7 + tap : 7 + tap + width, :]
        taps_ref[row, :, tap * channels : (tap + 1) * channels] = shifted.astype(jnp.bfloat16)


def conv_rows(taps_ref, row, count, weight_ref, params_ref):
    _, width, lanes = taps_ref.shape
    window = jnp.concatenate(
        [taps_ref[row + tap : row + tap + count].reshape(count * width, lanes) for tap in range(3)],
        axis=1,
    )
    both = jnp.dot(window, weight_ref[...], preferred_element_type=jnp.float32)
    half = both.shape[1] // 2
    return both[:, :half] + both[:, half:] + params_ref[0:1, :]


def first_kernel(
    count, sums_ref, own_ref, pair_ref, other_ref, weight_ref, params_ref,
    hidden_ref, out_ref, wide_ref, taps_ref, summed_ref,
):
    index = lax.axis_index("rows")
    rows, width, channels = own_ref.shape
    even = index % 2 == 0
    scale, offset = scale_offset(sums_ref, params_ref, rows * width * count)
    sum_weight(weight_ref, summed_ref)

    def make(row):
        if row < 2:
            values = jnp.where(even, other_ref[row], pair_ref[row])
            values = jnp.where(index == 0, own_ref[0], values)
        elif row < rows + 2:
            values = own_ref[row - 2]
        else:
            values = jnp.where(even, pair_ref[row - rows - 2], other_ref[row - rows - 2])
            values = jnp.where(index == count - 1, own_ref[rows - 1], values)
        store_taps(values, scale, offset, wide_ref, taps_ref, row)

    total = jnp.zeros((8, channels), jnp.float32)
    square = jnp.zeros((8, channels), jnp.float32)
    for row in range(rows + 4):
        make(row)
    hidden = conv_rows(taps_ref, 0, rows + 2, summed_ref, params_ref).astype(jnp.bfloat16)
    for row in range(rows + 2):
        values = hidden[row * width : (row + 1) * width]
        hidden_ref[row] = values
        if 0 < row <= rows:
            total, square = add_sums(values.astype(jnp.float32), total, square)
    store_sums(total, square, out_ref)

    @pl.when(index == 0)
    def _():
        hidden_ref[0] = hidden_ref[1]

    @pl.when(index == count - 1)
    def _():
        hidden_ref[rows + 1] = hidden_ref[rows]


def second_kernel(
    count, sums_ref, hidden_ref, own_ref, weight_ref, params_ref,
    out_ref, wide_ref, taps_ref, summed_ref, done_ref, sems,
):
    rows, width, channels = own_ref.shape
    scale, offset = scale_offset(sums_ref, params_ref, rows * width * count)
    sum_weight(weight_ref, summed_ref)
    copies = [
        pltpu.make_async_copy(done_ref.at[row], out_ref.at[row], sems.at[row])
        for row in range(rows)
    ]
    for row in range(rows + 2):
        store_taps(hidden_ref[row], scale, offset, wide_ref, taps_ref, row)
    branch = conv_rows(taps_ref, 0, rows, summed_ref, params_ref)
    for row in range(rows):
        values = own_ref[row].astype(jnp.float32) + branch[row * width : (row + 1) * width]
        done_ref[row] = values.astype(jnp.bfloat16)
        copies[row].start()
    for copy in copies:
        copy.wait()


def exchanged(sums):
    return lax.all_to_all(sums, "rows", 0, 0)


def body(
    latents, gain_one, shift_one, weight_one, bias_one, gain_two, shift_two, weight_two, bias_two
):
    count = lax.axis_size("rows")
    own = latents[0]
    rows, width, channels = own.shape
    sums_shape = jax.ShapeDtypeStruct((count, 2, channels), jnp.float32)
    taps = weight_one.shape[1] * weight_one.shape[2]
    summed = pltpu.VMEM((taps * channels, 2 * channels), jnp.bfloat16)
    slab_shape = jax.ShapeDtypeStruct((2, width, channels), jnp.bfloat16)

    def raw(weight):
        return weight.reshape(3, taps, channels, channels)

    swap_pair = [(i, i ^ 1) for i in range(count)]
    swap_other = [(i, i + 1 if i % 2 else i - 1) for i in range(1, count - 1)]

    vectors = (bias_one, gain_one, shift_one, bias_two, gain_two, shift_two)
    vector_shape = jax.ShapeDtypeStruct((8, channels), jnp.float32)
    own, pair, other, params_one, params_two = pl.pallas_call(
        load_kernel,
        out_shape=[jax.ShapeDtypeStruct(own.shape, own.dtype)]
        + [slab_shape] * 2
        + [vector_shape] * 2,
        in_specs=[HBM] * 7,
        out_specs=[VMEM] * 5,
        scratch_shapes=[
            pltpu.VMEM((6, 1, channels), jnp.float32),
            pltpu.SemaphoreType.DMA((rows,)),
            pltpu.SemaphoreType.DMA((6,)),
        ],
        compiler_params=PARAMS,
        name="load",
    )(
        pltpu.with_memory_space_constraint(own, pltpu.HBM),
        *[
            pltpu.with_memory_space_constraint(vector.reshape(1, channels), pltpu.HBM)
            for vector in vectors
        ],
    )
    sums = pl.pallas_call(
        sums_kernel,
        out_shape=sums_shape,
        in_specs=[VMEM],
        out_specs=VMEM,
        compiler_params=PARAMS,
        name="sums",
        cost_estimate=pl.CostEstimate(
            flops=40000000000, bytes_accessed=10000000, transcendentals=0
        ),
    )(own)
    other = lax.ppermute(other, "rows", swap_other)
    pair = lax.ppermute(pair, "rows", swap_pair)
    sums = exchanged(sums)
    hidden, sums = pl.pallas_call(
        functools.partial(first_kernel, count),
        out_shape=[jax.ShapeDtypeStruct((rows + 2, width, channels), jnp.bfloat16), sums_shape],
        in_specs=[VMEM] * 6,
        out_specs=[VMEM] * 2,
        scratch_shapes=[
            pltpu.VMEM((rows + 4, width + 16, channels), jnp.float32),
            pltpu.VMEM((rows + 4, width, 3 * channels), jnp.bfloat16),
            summed,
        ],
        compiler_params=PARAMS, name="first",
    )(sums, own, pair, other, raw(weight_one), params_one)
    sums = exchanged(sums)
    decoded = pl.pallas_call(
        functools.partial(second_kernel, count),
        out_shape=jax.ShapeDtypeStruct(own.shape, jnp.bfloat16),
        in_specs=[VMEM] * 5,
        out_specs=ANY,
        scratch_shapes=[
            pltpu.VMEM((rows + 2, width + 16, channels), jnp.float32),
            pltpu.VMEM((rows + 2, width, 3 * channels), jnp.bfloat16),
            summed,
            pltpu.VMEM(own.shape, jnp.bfloat16),
            pltpu.SemaphoreType.DMA((rows,)),
        ],
        compiler_params=PARAMS, name="second",
    )(sums, hidden, own, raw(weight_two), params_two)
    return decoded[None]


def solution(mesh):
    return jax.shard_map(
        body,
        mesh=mesh,
        in_specs=(P("groups", "rows", None, None), P(), P(), P(), P(), P(), P(), P(), P()),
        out_specs=P("groups", "rows", None, None),
        check_vma=False,
    )
```

```python
import functools

import jax
import jax.numpy as jnp
from jax import lax
from jax.experimental import pallas as pl
from jax.experimental.pallas import tpu as pltpu
from jax.sharding import PartitionSpec as P

GROUPS = 32
ANY = pl.BlockSpec(memory_space=pl.ANY)
VMEM = pl.BlockSpec(memory_space=pltpu.VMEM)
PARAMS = pltpu.CompilerParams(vmem_limit_bytes=24 * 1024 * 1024)


def store_sums(total, square, out_ref):
    total = jnp.sum(total, axis=0, keepdims=True)
    square = jnp.sum(square, axis=0, keepdims=True)
    both = jnp.concatenate([total, square], axis=0)
    out_ref[...] = jnp.broadcast_to(both[None], out_ref.shape)


def add_sums(values, total, square):
    width, channels = values.shape
    split = (width // 8, 8, channels)
    total += jnp.sum(values.reshape(split), axis=0)
    square += jnp.sum((values * values).reshape(split), axis=0)
    return total, square


def sums_kernel(own_ref, out_ref, pair_ref, other_ref):
    rows, _, channels = own_ref.shape
    even = lax.axis_index("rows") % 2 == 0
    for row in range(2):
        top = own_ref[row]
        bottom = own_ref[rows - 2 + row]
        pair_ref[row] = jnp.where(even, bottom, top)
        other_ref[row] = jnp.where(even, top, bottom)
    total = jnp.zeros((8, channels), jnp.float32)
    square = jnp.zeros((8, channels), jnp.float32)
    for row in range(rows):
        total, square = add_sums(own_ref[row].astype(jnp.float32), total, square)
    store_sums(total, square, out_ref)


def sum_weight(source, target):
    taps, channels = source.shape[1], source.shape[2]
    for tap in range(taps):
        total = source[0, tap].astype(jnp.float32)
        total += source[1, tap].astype(jnp.float32)
        total += source[2, tap].astype(jnp.float32)
        high = total.astype(jnp.bfloat16)
        low = (total - high.astype(jnp.float32)).astype(jnp.bfloat16)
        target[pl.ds(tap * channels, channels), :] = jnp.concatenate([high, low], axis=1)


def sum_paired(source, target):
    taps, channels = source.shape[1], source.shape[2]
    columns = taps // 3
    zeros = jnp.zeros((columns * channels, channels), jnp.bfloat16)
    for tap in range(taps):
        total = source[0, tap].astype(jnp.float32)
        total += source[1, tap].astype(jnp.float32)
        total += source[2, tap].astype(jnp.float32)
        total = total.astype(jnp.bfloat16)
        target[pl.ds(tap * channels, channels), 0:channels] = total
        target[pl.ds((tap + columns) * channels, channels), channels : 2 * channels] = total
    target[pl.ds(taps * channels, columns * channels), 0:channels] = zeros
    target[pl.ds(0, columns * channels), channels : 2 * channels] = zeros


def scale_offset(sums_ref, gain_ref, shift_ref, entries):
    sums = jnp.sum(sums_ref[...], axis=0)
    channels = sums.shape[1]
    per_group = channels // GROUPS
    sums = jnp.concatenate([sums, jnp.zeros((6, channels), jnp.float32)], axis=0)
    member = lax.broadcasted_iota(jnp.int32, sums.shape, 1) % per_group
    total = sums
    for step in range(1, per_group):
        total += jnp.where(member >= step, pltpu.roll(sums, step, 1), 0.0)
        total += jnp.where(member < per_group - step, pltpu.roll(sums, channels - step, 1), 0.0)
    total = total * (1.0 / (entries * per_group))
    mean = total[0:1]
    var = total[1:2] - mean * mean
    scale = gain_ref[...] * lax.rsqrt(var + 1e-06)
    return 0.5 * scale, 0.5 * (shift_ref[...] - mean * scale)


def store_taps(values, scale, offset, wide_ref, taps_ref, row):
    width, channels = values.shape
    half = values.astype(jnp.float32) * scale + offset
    act = half * jnp.tanh(half) + half
    wide_ref[row, 8 : 8 + width, :] = act
    wide_ref[row, 7:8, :] = act[0:1]
    wide_ref[row, 8 + width : 9 + width, :] = act[width - 1 : width]
    for tap in range(3):
        shifted = wide_ref[row, 7 + tap : 7 + tap + width, :]
        taps_ref[row, :, tap * channels : (tap + 1) * channels] = shifted.astype(jnp.bfloat16)


def conv_rows(taps_ref, row, count, weight_ref):
    _, width, lanes = taps_ref.shape
    window = jnp.concatenate(
        [taps_ref[row + tap : row + tap + count].reshape(count * width, lanes) for tap in range(3)],
        axis=1,
    )
    both = jnp.dot(window, weight_ref[...], preferred_element_type=jnp.float32)
    half = both.shape[1] // 2
    return both[:, :half] + both[:, half:]


def first_kernel(
    count, sums_ref, own_ref, pair_ref, other_ref, weight_ref, bias_ref, gain_ref, shift_ref,
    hidden_ref, out_ref, wide_ref, taps_ref, summed_ref,
):
    index = lax.axis_index("rows")
    rows, width, channels = own_ref.shape
    even = index % 2 == 0
    scale, offset = scale_offset(sums_ref, gain_ref, shift_ref, rows * width * count)
    sum_weight(weight_ref, summed_ref)

    def make(row):
        if row < 2:
            values = jnp.where(even, other_ref[row], pair_ref[row])
            values = jnp.where(index == 0, own_ref[0], values)
        elif row < rows + 2:
            values = own_ref[row - 2]
        else:
            values = jnp.where(even, pair_ref[row - rows - 2], other_ref[row - rows - 2])
            values = jnp.where(index == count - 1, own_ref[rows - 1], values)
        store_taps(values, scale, offset, wide_ref, taps_ref, row)

    total = jnp.zeros((8, channels), jnp.float32)
    square = jnp.zeros((8, channels), jnp.float32)
    for row in range(rows + 4):
        make(row)
    hidden = conv_rows(taps_ref, 0, rows + 2, summed_ref) + bias_ref[...]
    hidden = hidden.astype(jnp.bfloat16)
    for row in range(rows + 2):
        values = hidden[row * width : (row + 1) * width]
        hidden_ref[row] = values
        if 0 < row <= rows:
            total, square = add_sums(values.astype(jnp.float32), total, square)
    store_sums(total, square, out_ref)

    @pl.when(index == 0)
    def _():
        hidden_ref[0] = hidden_ref[1]

    @pl.when(index == count - 1)
    def _():
        hidden_ref[rows + 1] = hidden_ref[rows]


def second_kernel(
    count, sums_ref, hidden_ref, own_ref, weight_ref, bias_ref, gain_ref, shift_ref,
    out_ref, wide_ref, taps_ref, summed_ref, done_ref, sems,
):
    rows, width, channels = own_ref.shape
    scale, offset = scale_offset(sums_ref, gain_ref, shift_ref, rows * width * count)
    sum_paired(weight_ref, summed_ref)
    copies = [
        pltpu.make_async_copy(done_ref.at[row], out_ref.at[row], sems.at[row])
        for row in range(rows)
    ]
    for row in range(2):
        store_taps(hidden_ref[row], scale, offset, wide_ref, taps_ref, row)
    for row in range(0, rows, 2):
        for i in range(2, 4):
            store_taps(hidden_ref[row + i], scale, offset, wide_ref, taps_ref, row + i)
        window = jnp.concatenate([taps_ref[row + tap] for tap in range(4)], axis=1)
        both = jnp.dot(window, summed_ref[...], preferred_element_type=jnp.float32)
        for i in range(2):
            branch = both[:, i * channels : (i + 1) * channels] + bias_ref[...]
            values = own_ref[row + i].astype(jnp.float32) + branch
            done_ref[row + i] = values.astype(jnp.bfloat16)
            copies[row + i].start()
    for copy in copies:
        copy.wait()


def exchanged(sums):
    return lax.all_to_all(sums, "rows", 0, 0)


def body(
    latents, gain_one, shift_one, weight_one, bias_one, gain_two, shift_two, weight_two, bias_two
):
    count = lax.axis_size("rows")
    own = latents[0]
    rows, width, channels = own.shape
    sums_shape = jax.ShapeDtypeStruct((count, 2, channels), jnp.float32)
    taps = weight_one.shape[1] * weight_one.shape[2]
    slab_shape = jax.ShapeDtypeStruct((2, width, channels), jnp.bfloat16)

    def operands(weight, *vectors):
        vectors = [vector.reshape(1, channels) for vector in vectors]
        return weight.reshape(3, taps, channels, channels), *vectors

    swap_pair = [(i, i ^ 1) for i in range(count)]
    swap_other = [(i, i + 1 if i % 2 else i - 1) for i in range(1, count - 1)]

    sums, pair, other = pl.pallas_call(
        sums_kernel,
        out_shape=[sums_shape, slab_shape, slab_shape],
        in_specs=[VMEM],
        out_specs=[VMEM] * 3,
        compiler_params=PARAMS,
        name="sums",
        cost_estimate=pl.CostEstimate(
            flops=40000000000, bytes_accessed=10000000, transcendentals=0
        ),
    )(own)
    other = lax.ppermute(other, "rows", swap_other)
    pair = lax.ppermute(pair, "rows", swap_pair)
    sums = exchanged(sums)
    hidden, sums = pl.pallas_call(
        functools.partial(first_kernel, count),
        out_shape=[jax.ShapeDtypeStruct((rows + 2, width, channels), jnp.bfloat16), sums_shape],
        in_specs=[VMEM] * 8,
        out_specs=[VMEM] * 2,
        scratch_shapes=[
            pltpu.VMEM((rows + 4, width + 16, channels), jnp.float32),
            pltpu.VMEM((rows + 4, width, 3 * channels), jnp.bfloat16),
            pltpu.VMEM((taps * channels, 2 * channels), jnp.bfloat16),
        ],
        compiler_params=PARAMS, name="first",
    )(sums, own, pair, other, *operands(weight_one, bias_one, gain_one, shift_one))
    sums = exchanged(sums)
    decoded = pl.pallas_call(
        functools.partial(second_kernel, count),
        out_shape=jax.ShapeDtypeStruct(own.shape, jnp.bfloat16),
        in_specs=[VMEM] * 7,
        out_specs=ANY,
        scratch_shapes=[
            pltpu.VMEM((rows + 2, width + 16, channels), jnp.float32),
            pltpu.VMEM((rows + 2, width, 3 * channels), jnp.bfloat16),
            pltpu.VMEM((taps // 3 * 4 * channels, 2 * channels), jnp.bfloat16),
            pltpu.VMEM(own.shape, jnp.bfloat16),
            pltpu.SemaphoreType.DMA((rows,)),
        ],
        compiler_params=PARAMS, name="second",
    )(sums, hidden, own, *operands(weight_two, bias_two, gain_two, shift_two))
    return decoded[None]


def solution(mesh):
    return jax.shard_map(
        body,
        mesh=mesh,
        in_specs=(P("groups", "rows", None, None), P(), P(), P(), P(), P(), P(), P(), P()),
        out_specs=P("groups", "rows", None, None),
        check_vma=False,
    )
```

```python
import functools

import jax
import jax.numpy as jnp
from jax import lax
from jax.experimental import pallas as pl
from jax.experimental.pallas import tpu as pltpu
from jax.sharding import PartitionSpec as P

GROUPS = 32
ANY = pl.BlockSpec(memory_space=pl.ANY)
VMEM = pl.BlockSpec(memory_space=pltpu.VMEM)
LONG = pl.CostEstimate(flops=40000000000, bytes_accessed=10000000, transcendentals=0)
PARAMS = pltpu.CompilerParams(vmem_limit_bytes=24 * 1024 * 1024)


def store_sums(total, square, out_ref):
    total = jnp.sum(total, axis=0, keepdims=True)
    square = jnp.sum(square, axis=0, keepdims=True)
    both = jnp.concatenate([total, square], axis=0)
    out_ref[...] = jnp.broadcast_to(both[None], out_ref.shape)


def add_sums(values, total, square):
    width, channels = values.shape
    split = (width // 8, 8, channels)
    total += jnp.sum(values.reshape(split), axis=0)
    square += jnp.sum((values * values).reshape(split), axis=0)
    return total, square


def sums_kernel(own_ref, out_ref, pair_ref, other_ref):
    rows, _, channels = own_ref.shape
    even = lax.axis_index("rows") % 2 == 0
    for row in range(2):
        top = own_ref[row]
        bottom = own_ref[rows - 2 + row]
        pair_ref[row] = jnp.where(even, bottom, top)
        other_ref[row] = jnp.where(even, top, bottom)
    total = jnp.zeros((8, channels), jnp.float32)
    square = jnp.zeros((8, channels), jnp.float32)
    for row in range(rows):
        total, square = add_sums(own_ref[row].astype(jnp.float32), total, square)
    store_sums(total, square, out_ref)


def sum_weight(source, target):
    taps, channels = source.shape[1], source.shape[2]
    for tap in range(taps):
        total = source[0, tap].astype(jnp.float32)
        total += source[1, tap].astype(jnp.float32)
        total += source[2, tap].astype(jnp.float32)
        high = total.astype(jnp.bfloat16)
        low = (total - high.astype(jnp.float32)).astype(jnp.bfloat16)
        target[pl.ds(tap * channels, channels), :] = jnp.concatenate([high, low], axis=1)


def sum_paired(source, target):
    taps, channels = source.shape[1], source.shape[2]
    columns = taps // 3
    zeros = jnp.zeros((columns * channels, channels), jnp.bfloat16)
    for tap in range(taps):
        total = source[0, tap].astype(jnp.float32)
        total += source[1, tap].astype(jnp.float32)
        total += source[2, tap].astype(jnp.float32)
        total = total.astype(jnp.bfloat16)
        target[pl.ds(tap * channels, channels), 0:channels] = total
        target[pl.ds((tap + columns) * channels, channels), channels : 2 * channels] = total
    target[pl.ds(taps * channels, columns * channels), 0:channels] = zeros
    target[pl.ds(0, columns * channels), channels : 2 * channels] = zeros


def scale_offset(sums_ref, gain_ref, shift_ref, entries):
    sums = jnp.sum(sums_ref[...], axis=0)
    channels = sums.shape[1]
    per_group = channels // GROUPS
    sums = jnp.concatenate([sums, jnp.zeros((6, channels), jnp.float32)], axis=0)
    member = lax.broadcasted_iota(jnp.int32, sums.shape, 1) % per_group
    total = sums
    for step in range(1, per_group):
        total += jnp.where(member >= step, pltpu.roll(sums, step, 1), 0.0)
        total += jnp.where(member < per_group - step, pltpu.roll(sums, channels - step, 1), 0.0)
    total = total * (1.0 / (entries * per_group))
    mean = total[0:1]
    var = total[1:2] - mean * mean
    scale = gain_ref[...] * lax.rsqrt(var + 1e-06)
    return 0.5 * scale, 0.5 * (shift_ref[...] - mean * scale)


def store_taps(values, scale, offset, wide_ref, taps_ref, row):
    width, channels = values.shape
    half = values.astype(jnp.float32) * scale + offset
    act = half * jnp.tanh(half) + half
    wide_ref[row, 8 : 8 + width, :] = act
    wide_ref[row, 7:8, :] = act[0:1]
    wide_ref[row, 8 + width : 9 + width, :] = act[width - 1 : width]
    for tap in range(3):
        shifted = wide_ref[row, 7 + tap : 7 + tap + width, :]
        taps_ref[row, :, tap * channels : (tap + 1) * channels] = shifted.astype(jnp.bfloat16)


def conv_rows(taps_ref, row, count, weight_ref):
    _, width, lanes = taps_ref.shape
    window = jnp.concatenate(
        [taps_ref[row + tap : row + tap + count].reshape(count * width, lanes) for tap in range(3)],
        axis=1,
    )
    both = jnp.dot(window, weight_ref[...], preferred_element_type=jnp.float32)
    half = both.shape[1] // 2
    return both[:, :half] + both[:, half:]


def first_kernel(
    count, sums_ref, own_ref, pair_ref, other_ref, weight_ref, bias_ref, gain_ref, shift_ref,
    hidden_ref, out_ref, wide_ref, taps_ref, summed_ref,
):
    index = lax.axis_index("rows")
    rows, width, channels = own_ref.shape
    even = index % 2 == 0
    scale, offset = scale_offset(sums_ref, gain_ref, shift_ref, rows * width * count)
    sum_weight(weight_ref, summed_ref)

    def make(row):
        if row < 2:
            values = jnp.where(even, other_ref[row], pair_ref[row])
            values = jnp.where(index == 0, own_ref[0], values)
        elif row < rows + 2:
            values = own_ref[row - 2]
        else:
            values = jnp.where(even, pair_ref[row - rows - 2], other_ref[row - rows - 2])
            values = jnp.where(index == count - 1, own_ref[rows - 1], values)
        store_taps(values, scale, offset, wide_ref, taps_ref, row)

    total = jnp.zeros((8, channels), jnp.float32)
    square = jnp.zeros((8, channels), jnp.float32)
    for row in range(rows + 4):
        make(row)
    hidden = conv_rows(taps_ref, 0, rows + 2, summed_ref) + bias_ref[...]
    hidden = hidden.astype(jnp.bfloat16)
    for row in range(rows + 2):
        values = hidden[row * width : (row + 1) * width]
        hidden_ref[row] = values
        if 0 < row <= rows:
            total, square = add_sums(values.astype(jnp.float32), total, square)
    store_sums(total, square, out_ref)

    @pl.when(index == 0)
    def _():
        hidden_ref[0] = hidden_ref[1]

    @pl.when(index == count - 1)
    def _():
        hidden_ref[rows + 1] = hidden_ref[rows]


def second_kernel(
    count, sums_ref, hidden_ref, own_ref, weight_ref, bias_ref, gain_ref, shift_ref,
    out_ref, wide_ref, taps_ref, summed_ref, done_ref, sems,
):
    rows, width, channels = own_ref.shape
    scale, offset = scale_offset(sums_ref, gain_ref, shift_ref, rows * width * count)
    sum_paired(weight_ref, summed_ref)
    copies = [
        pltpu.make_async_copy(done_ref.at[row], out_ref.at[row], sems.at[row])
        for row in range(rows)
    ]
    for row in range(2):
        store_taps(hidden_ref[row], scale, offset, wide_ref, taps_ref, row)
    for row in range(0, rows, 2):
        for i in range(2, 4):
            store_taps(hidden_ref[row + i], scale, offset, wide_ref, taps_ref, row + i)
        window = jnp.concatenate([taps_ref[row + tap] for tap in range(4)], axis=1)
        both = jnp.dot(window, summed_ref[...], preferred_element_type=jnp.float32)
        for i in range(2):
            branch = both[:, i * channels : (i + 1) * channels] + bias_ref[...]
            values = own_ref[row + i].astype(jnp.float32) + branch
            done_ref[row + i] = values.astype(jnp.bfloat16)
            copies[row + i].start()
    for copy in copies:
        copy.wait()


def exchanged(sums):
    return lax.all_to_all(sums, "rows", 0, 0)


def body(
    latents, gain_one, shift_one, weight_one, bias_one, gain_two, shift_two, weight_two, bias_two
):
    count = lax.axis_size("rows")
    own = latents[0]
    rows, width, channels = own.shape
    sums_shape = jax.ShapeDtypeStruct((count, 2, channels), jnp.float32)
    taps = weight_one.shape[1] * weight_one.shape[2]
    slab_shape = jax.ShapeDtypeStruct((2, width, channels), jnp.bfloat16)

    def operands(weight, *vectors):
        vectors = [vector.reshape(1, channels) for vector in vectors]
        return weight.reshape(3, taps, channels, channels), *vectors

    swap_pair = [(i, i ^ 1) for i in range(count)]
    swap_other = [(i, i + 1 if i % 2 else i - 1) for i in range(1, count - 1)]

    sums, pair, other = pl.pallas_call(
        sums_kernel,
        out_shape=[sums_shape, slab_shape, slab_shape],
        in_specs=[VMEM],
        out_specs=[VMEM] * 3,
        compiler_params=PARAMS,
        name="sums",
        cost_estimate=LONG,
    )(own)
    other = lax.ppermute(other, "rows", swap_other)
    pair = lax.ppermute(pair, "rows", swap_pair)
    sums = exchanged(sums)
    hidden, sums = pl.pallas_call(
        functools.partial(first_kernel, count),
        out_shape=[jax.ShapeDtypeStruct((rows + 2, width, channels), jnp.bfloat16), sums_shape],
        in_specs=[VMEM] * 8,
        out_specs=[VMEM] * 2,
        scratch_shapes=[
            pltpu.VMEM((rows + 4, width + 16, channels), jnp.float32),
            pltpu.VMEM((rows + 4, width, 3 * channels), jnp.bfloat16),
            pltpu.VMEM((taps * channels, 2 * channels), jnp.bfloat16),
        ],
        compiler_params=PARAMS, name="first", cost_estimate=LONG,
    )(sums, own, pair, other, *operands(weight_one, bias_one, gain_one, shift_one))
    sums = exchanged(sums)
    decoded = pl.pallas_call(
        functools.partial(second_kernel, count),
        out_shape=jax.ShapeDtypeStruct(own.shape, jnp.bfloat16),
        in_specs=[VMEM] * 7,
        out_specs=ANY,
        scratch_shapes=[
            pltpu.VMEM((rows + 2, width + 16, channels), jnp.float32),
            pltpu.VMEM((rows + 2, width, 3 * channels), jnp.bfloat16),
            pltpu.VMEM((taps // 3 * 4 * channels, 2 * channels), jnp.bfloat16),
            pltpu.VMEM(own.shape, jnp.bfloat16),
            pltpu.SemaphoreType.DMA((rows,)),
        ],
        compiler_params=PARAMS, name="second",
    )(sums, hidden, own, *operands(weight_two, bias_two, gain_two, shift_two))
    return decoded[None]


def solution(mesh):
    return jax.shard_map(
        body,
        mesh=mesh,
        in_specs=(P("groups", "rows", None, None), P(), P(), P(), P(), P(), P(), P(), P()),
        out_specs=P("groups", "rows", None, None),
        check_vma=False,
    )
```

```python
import functools

import jax
import jax.numpy as jnp
from jax import lax
from jax.experimental import pallas as pl
from jax.experimental.pallas import tpu as pltpu
from jax.sharding import PartitionSpec as P

GROUPS = 32
LONG = pl.CostEstimate(flops=40000000000, bytes_accessed=10000000, transcendentals=0)
HBM = pl.BlockSpec(memory_space=pltpu.HBM)
ANY = pl.BlockSpec(memory_space=pl.ANY)
VMEM = pl.BlockSpec(memory_space=pltpu.VMEM)
PARAMS = pltpu.CompilerParams(vmem_limit_bytes=24 * 1024 * 1024)


def store_sums(total, square, out_ref):
    total = jnp.sum(total, axis=0, keepdims=True)
    square = jnp.sum(square, axis=0, keepdims=True)
    both = jnp.concatenate([total, square], axis=0)
    out_ref[...] = jnp.broadcast_to(both[None], out_ref.shape)


def add_sums(values, total, square):
    width, channels = values.shape
    split = (width // 8, 8, channels)
    total += jnp.sum(values.reshape(split), axis=0)
    square += jnp.sum((values * values).reshape(split), axis=0)
    return total, square


def sums_kernel(latents_ref, *rest):
    sources, (out_ref, own_ref, pair_ref, other_ref) = rest[:6], rest[6:10]
    outs, (vectors_ref, sems, vector_sems) = rest[10:12], rest[12:]
    rows, _, channels = own_ref.shape
    half = rows // 2
    copies = [
        pltpu.make_async_copy(
            latents_ref.at[pl.ds(i * half, half)], own_ref.at[pl.ds(i * half, half)], sems.at[i]
        )
        for i in range(2)
    ]
    vector_copies = [
        pltpu.make_async_copy(source, vectors_ref.at[i], vector_sems.at[i])
        for i, source in enumerate(sources)
    ]
    for copy in copies + vector_copies:
        copy.start()
    total = jnp.zeros((8, channels), jnp.float32)
    square = jnp.zeros((8, channels), jnp.float32)
    for row in range(rows):
        if row % half == 0:
            copies[row // half].wait()
        total, square = add_sums(own_ref[row].astype(jnp.float32), total, square)
    store_sums(total, square, out_ref)
    even = lax.axis_index("rows") % 2 == 0
    for row in range(2):
        top = own_ref[row]
        bottom = own_ref[rows - 2 + row]
        pair_ref[row] = jnp.where(even, bottom, top)
        other_ref[row] = jnp.where(even, top, bottom)
    for copy in vector_copies:
        copy.wait()
    for i in range(6):
        outs[i // 3][pl.ds(i % 3, 1), :] = vectors_ref[i]


def sum_weight(source, target):
    taps, channels = source.shape[1], source.shape[2]
    for tap in range(taps):
        total = source[0, tap].astype(jnp.float32)
        total += source[1, tap].astype(jnp.float32)
        total += source[2, tap].astype(jnp.float32)
        high = total.astype(jnp.bfloat16)
        low = (total - high.astype(jnp.float32)).astype(jnp.bfloat16)
        target[pl.ds(tap * channels, channels), :] = jnp.concatenate([high, low], axis=1)


def sum_paired(source, target):
    taps, channels = source.shape[1], source.shape[2]
    columns = taps // 3
    zeros = jnp.zeros((columns * channels, channels), jnp.bfloat16)
    for tap in range(taps):
        total = source[0, tap].astype(jnp.float32)
        total += source[1, tap].astype(jnp.float32)
        total += source[2, tap].astype(jnp.float32)
        total = total.astype(jnp.bfloat16)
        target[pl.ds(tap * channels, channels), 0:channels] = total
        target[pl.ds((tap + columns) * channels, channels), channels : 2 * channels] = total
    target[pl.ds(taps * channels, columns * channels), 0:channels] = zeros
    target[pl.ds(0, columns * channels), channels : 2 * channels] = zeros


def scale_offset(sums_ref, params_ref, entries):
    sums = jnp.sum(sums_ref[...], axis=0)
    channels = sums.shape[1]
    per_group = channels // GROUPS
    sums = jnp.concatenate([sums, jnp.zeros((6, channels), jnp.float32)], axis=0)
    member = lax.broadcasted_iota(jnp.int32, sums.shape, 1) % per_group
    total = sums
    for step in range(1, per_group):
        total += jnp.where(member >= step, pltpu.roll(sums, step, 1), 0.0)
        total += jnp.where(member < per_group - step, pltpu.roll(sums, channels - step, 1), 0.0)
    total = total * (1.0 / (entries * per_group))
    mean = total[0:1]
    var = total[1:2] - mean * mean
    scale = params_ref[1:2, :] * lax.rsqrt(var + 1e-06)
    return 0.5 * scale, 0.5 * (params_ref[2:3, :] - mean * scale)


def store_taps(values, scale, offset, wide_ref, taps_ref, row):
    width, channels = values.shape
    half = values.astype(jnp.float32) * scale + offset
    act = half * jnp.tanh(half) + half
    wide_ref[row, 8 : 8 + width, :] = act
    wide_ref[row, 7:8, :] = act[0:1]
    wide_ref[row, 8 + width : 9 + width, :] = act[width - 1 : width]
    for tap in range(3):
        shifted = wide_ref[row, 7 + tap : 7 + tap + width, :]
        taps_ref[row, :, tap * channels : (tap + 1) * channels] = shifted.astype(jnp.bfloat16)


def conv_rows(taps_ref, row, count, weight_ref):
    _, width, lanes = taps_ref.shape
    window = jnp.concatenate(
        [taps_ref[row + tap : row + tap + count].reshape(count * width, lanes) for tap in range(3)],
        axis=1,
    )
    both = jnp.dot(window, weight_ref[...], preferred_element_type=jnp.float32)
    half = both.shape[1] // 2
    return both[:, :half] + both[:, half:]


def first_kernel(
    count, sums_ref, own_ref, pair_ref, other_ref, weight_ref, params_ref,
    hidden_ref, out_ref, wide_ref, taps_ref, summed_ref,
):
    index = lax.axis_index("rows")
    rows, width, channels = own_ref.shape
    even = index % 2 == 0
    scale, offset = scale_offset(sums_ref, params_ref, rows * width * count)
    sum_weight(weight_ref, summed_ref)

    def make(row):
        if row < 2:
            values = jnp.where(even, other_ref[row], pair_ref[row])
            values = jnp.where(index == 0, own_ref[0], values)
        elif row < rows + 2:
            values = own_ref[row - 2]
        else:
            values = jnp.where(even, pair_ref[row - rows - 2], other_ref[row - rows - 2])
            values = jnp.where(index == count - 1, own_ref[rows - 1], values)
        store_taps(values, scale, offset, wide_ref, taps_ref, row)

    total = jnp.zeros((8, channels), jnp.float32)
    square = jnp.zeros((8, channels), jnp.float32)
    for row in range(rows + 4):
        make(row)
    hidden = conv_rows(taps_ref, 0, rows + 2, summed_ref) + params_ref[0:1, :]
    hidden = hidden.astype(jnp.bfloat16)
    for row in range(rows + 2):
        values = hidden[row * width : (row + 1) * width]
        hidden_ref[row] = values
        if 0 < row <= rows:
            total, square = add_sums(values.astype(jnp.float32), total, square)
    store_sums(total, square, out_ref)

    @pl.when(index == 0)
    def _():
        hidden_ref[0] = hidden_ref[1]

    @pl.when(index == count - 1)
    def _():
        hidden_ref[rows + 1] = hidden_ref[rows]


def second_kernel(
    count, sums_ref, hidden_ref, own_ref, weight_ref, params_ref,
    out_ref, wide_ref, taps_ref, summed_ref, done_ref, sems,
):
    rows, width, channels = own_ref.shape
    scale, offset = scale_offset(sums_ref, params_ref, rows * width * count)
    sum_paired(weight_ref, summed_ref)
    copies = [
        pltpu.make_async_copy(done_ref.at[row], out_ref.at[row], sems.at[row])
        for row in range(rows)
    ]
    for row in range(2):
        store_taps(hidden_ref[row], scale, offset, wide_ref, taps_ref, row)
    for row in range(0, rows, 2):
        for i in range(2, 4):
            store_taps(hidden_ref[row + i], scale, offset, wide_ref, taps_ref, row + i)
        window = jnp.concatenate([taps_ref[row + tap] for tap in range(4)], axis=1)
        both = jnp.dot(window, summed_ref[...], preferred_element_type=jnp.float32)
        for i in range(2):
            branch = both[:, i * channels : (i + 1) * channels] + params_ref[0:1, :]
            values = own_ref[row + i].astype(jnp.float32) + branch
            done_ref[row + i] = values.astype(jnp.bfloat16)
            copies[row + i].start()
    for copy in copies:
        copy.wait()


def exchanged(sums):
    return lax.all_to_all(sums, "rows", 0, 0)


def body(
    latents, gain_one, shift_one, weight_one, bias_one, gain_two, shift_two, weight_two, bias_two
):
    count = lax.axis_size("rows")
    own = latents[0]
    rows, width, channels = own.shape
    sums_shape = jax.ShapeDtypeStruct((count, 2, channels), jnp.float32)
    taps = weight_one.shape[1] * weight_one.shape[2]
    slab_shape = jax.ShapeDtypeStruct((2, width, channels), jnp.bfloat16)

    def raw(weight):
        return weight.reshape(3, taps, channels, channels)

    swap_pair = [(i, i ^ 1) for i in range(count)]
    swap_other = [(i, i + 1 if i % 2 else i - 1) for i in range(1, count - 1)]

    vectors = (bias_one, gain_one, shift_one, bias_two, gain_two, shift_two)
    vector_shape = jax.ShapeDtypeStruct((8, channels), jnp.float32)
    sums, own, pair, other, params_one, params_two = pl.pallas_call(
        sums_kernel,
        out_shape=[sums_shape, jax.ShapeDtypeStruct(own.shape, own.dtype)]
        + [slab_shape] * 2
        + [vector_shape] * 2,
        in_specs=[HBM] * 7,
        out_specs=[VMEM] * 6,
        scratch_shapes=[
            pltpu.VMEM((6, 1, channels), jnp.float32),
            pltpu.SemaphoreType.DMA((2,)),
            pltpu.SemaphoreType.DMA((6,)),
        ],
        compiler_params=PARAMS,
        name="sums",
        cost_estimate=LONG,
    )(
        pltpu.with_memory_space_constraint(own, pltpu.HBM),
        *[
            pltpu.with_memory_space_constraint(vector.reshape(1, channels), pltpu.HBM)
            for vector in vectors
        ],
    )
    other = lax.ppermute(other, "rows", swap_other)
    pair = lax.ppermute(pair, "rows", swap_pair)
    sums = exchanged(sums)
    hidden, sums = pl.pallas_call(
        functools.partial(first_kernel, count),
        out_shape=[jax.ShapeDtypeStruct((rows + 2, width, channels), jnp.bfloat16), sums_shape],
        in_specs=[VMEM] * 6,
        out_specs=[VMEM] * 2,
        scratch_shapes=[
            pltpu.VMEM((rows + 4, width + 16, channels), jnp.float32),
            pltpu.VMEM((rows + 4, width, 3 * channels), jnp.bfloat16),
            pltpu.VMEM((taps * channels, 2 * channels), jnp.bfloat16),
        ],
        compiler_params=PARAMS, name="first",
    )(sums, own, pair, other, raw(weight_one), params_one)
    sums = exchanged(sums)
    decoded = pl.pallas_call(
        functools.partial(second_kernel, count),
        out_shape=jax.ShapeDtypeStruct(own.shape, jnp.bfloat16),
        in_specs=[VMEM] * 5,
        out_specs=ANY,
        scratch_shapes=[
            pltpu.VMEM((rows + 2, width + 16, channels), jnp.float32),
            pltpu.VMEM((rows + 2, width, 3 * channels), jnp.bfloat16),
            pltpu.VMEM((taps // 3 * 4 * channels, 2 * channels), jnp.bfloat16),
            pltpu.VMEM(own.shape, jnp.bfloat16),
            pltpu.SemaphoreType.DMA((rows,)),
        ],
        compiler_params=PARAMS, name="second",
    )(sums, hidden, own, raw(weight_two), params_two)
    return decoded[None]


def solution(mesh):
    return jax.shard_map(
        body,
        mesh=mesh,
        in_specs=(P("groups", "rows", None, None), P(), P(), P(), P(), P(), P(), P(), P()),
        out_specs=P("groups", "rows", None, None),
        check_vma=False,
    )
```

```python
import functools

import jax
import jax.numpy as jnp
from jax import lax
from jax.experimental import pallas as pl
from jax.experimental.pallas import tpu as pltpu
from jax.sharding import PartitionSpec as P

GROUPS = 32
HBM = pl.BlockSpec(memory_space=pltpu.HBM)
ANY = pl.BlockSpec(memory_space=pl.ANY)
VMEM = pl.BlockSpec(memory_space=pltpu.VMEM)
PARAMS = pltpu.CompilerParams(vmem_limit_bytes=24 * 1024 * 1024)


def store_sums(total, square, out_ref):
    total = jnp.sum(total, axis=0, keepdims=True)
    square = jnp.sum(square, axis=0, keepdims=True)
    both = jnp.concatenate([total, square], axis=0)
    out_ref[...] = jnp.broadcast_to(both[None], out_ref.shape)


def add_sums(values, total, square):
    width, channels = values.shape
    split = (width // 8, 8, channels)
    total += jnp.sum(values.reshape(split), axis=0)
    square += jnp.sum((values * values).reshape(split), axis=0)
    return total, square


def sums_kernel(own_ref, out_ref, pair_ref, other_ref):
    rows, _, channels = own_ref.shape
    even = lax.axis_index("rows") % 2 == 0
    for row in range(2):
        top = own_ref[row]
        bottom = own_ref[rows - 2 + row]
        pair_ref[row] = jnp.where(even, bottom, top)
        other_ref[row] = jnp.where(even, top, bottom)
    total = jnp.zeros((8, channels), jnp.float32)
    square = jnp.zeros((8, channels), jnp.float32)
    for row in range(rows):
        total, square = add_sums(own_ref[row].astype(jnp.float32), total, square)
    store_sums(total, square, out_ref)


def sum_weight(source, target):
    taps, channels = source.shape[1], source.shape[2]
    for tap in range(taps):
        total = source[0, tap].astype(jnp.float32)
        total += source[1, tap].astype(jnp.float32)
        total += source[2, tap].astype(jnp.float32)
        high = total.astype(jnp.bfloat16)
        low = (total - high.astype(jnp.float32)).astype(jnp.bfloat16)
        target[pl.ds(tap * channels, channels), :] = jnp.concatenate([high, low], axis=1)


def sum_paired(source, target):
    taps, channels = source.shape[1], source.shape[2]
    columns = taps // 3
    zeros = jnp.zeros((columns * channels, channels), jnp.bfloat16)
    for tap in range(taps):
        total = source[0, tap].astype(jnp.float32)
        total += source[1, tap].astype(jnp.float32)
        total += source[2, tap].astype(jnp.float32)
        total = total.astype(jnp.bfloat16)
        target[pl.ds(tap * channels, channels), 0:channels] = total
        target[pl.ds((tap + columns) * channels, channels), channels : 2 * channels] = total
    target[pl.ds(taps * channels, columns * channels), 0:channels] = zeros
    target[pl.ds(0, columns * channels), channels : 2 * channels] = zeros


def scale_offset(sums_ref, gain_ref, shift_ref, entries):
    sums = jnp.sum(sums_ref[...], axis=0)
    channels = sums.shape[1]
    per_group = channels // GROUPS
    sums = jnp.concatenate([sums, jnp.zeros((6, channels), jnp.float32)], axis=0)
    member = lax.broadcasted_iota(jnp.int32, sums.shape, 1) % per_group
    total = sums
    for step in range(1, per_group):
        total += jnp.where(member >= step, pltpu.roll(sums, step, 1), 0.0)
        total += jnp.where(member < per_group - step, pltpu.roll(sums, channels - step, 1), 0.0)
    total = total * (1.0 / (entries * per_group))
    mean = total[0:1]
    var = total[1:2] - mean * mean
    scale = gain_ref[...] * lax.rsqrt(var + 1e-06)
    return 0.5 * scale, 0.5 * (shift_ref[...] - mean * scale)


def store_taps(values, scale, offset, wide_ref, taps_ref, row):
    width, channels = values.shape
    half = values.astype(jnp.float32) * scale + offset
    act = half * jnp.tanh(half) + half
    wide_ref[row, 8 : 8 + width, :] = act
    wide_ref[row, 7:8, :] = act[0:1]
    wide_ref[row, 8 + width : 9 + width, :] = act[width - 1 : width]
    for tap in range(3):
        shifted = wide_ref[row, 7 + tap : 7 + tap + width, :]
        taps_ref[row, :, tap * channels : (tap + 1) * channels] = shifted.astype(jnp.bfloat16)


def conv_rows(taps_ref, row, count, weight_ref):
    _, width, lanes = taps_ref.shape
    window = jnp.concatenate(
        [taps_ref[row + tap : row + tap + count].reshape(count * width, lanes) for tap in range(3)],
        axis=1,
    )
    both = jnp.dot(window, weight_ref[...], preferred_element_type=jnp.float32)
    half = both.shape[1] // 2
    return both[:, :half] + both[:, half:]


def first_kernel(
    count, sums_ref, own_ref, pair_ref, other_ref, weight_ref, bias_ref, gain_ref, shift_ref,
    bias_two_ref, gain_two_ref, shift_two_ref,
    hidden_ref, out_ref, next_ref, wide_ref, taps_ref, summed_ref, vectors_ref, sems,
):
    copies = [
        pltpu.make_async_copy(source, vectors_ref.at[i], sems.at[i])
        for i, source in enumerate((bias_two_ref, gain_two_ref, shift_two_ref))
    ]
    for copy in copies:
        copy.start()
    index = lax.axis_index("rows")
    rows, width, channels = own_ref.shape
    even = index % 2 == 0
    scale, offset = scale_offset(sums_ref, gain_ref, shift_ref, rows * width * count)
    sum_weight(weight_ref, summed_ref)

    def make(row):
        if row < 2:
            values = jnp.where(even, other_ref[row], pair_ref[row])
            values = jnp.where(index == 0, own_ref[0], values)
        elif row < rows + 2:
            values = own_ref[row - 2]
        else:
            values = jnp.where(even, pair_ref[row - rows - 2], other_ref[row - rows - 2])
            values = jnp.where(index == count - 1, own_ref[rows - 1], values)
        store_taps(values, scale, offset, wide_ref, taps_ref, row)

    total = jnp.zeros((8, channels), jnp.float32)
    square = jnp.zeros((8, channels), jnp.float32)
    for row in range(rows + 4):
        make(row)
    hidden = conv_rows(taps_ref, 0, rows + 2, summed_ref) + bias_ref[...]
    hidden = hidden.astype(jnp.bfloat16)
    for row in range(rows + 2):
        values = hidden[row * width : (row + 1) * width]
        hidden_ref[row] = values
        if 0 < row <= rows:
            total, square = add_sums(values.astype(jnp.float32), total, square)
    store_sums(total, square, out_ref)
    for i in range(3):
        copies[i].wait()
        next_ref[pl.ds(i, 1), :] = vectors_ref[i]

    @pl.when(index == 0)
    def _():
        hidden_ref[0] = hidden_ref[1]

    @pl.when(index == count - 1)
    def _():
        hidden_ref[rows + 1] = hidden_ref[rows]


def second_kernel(
    count, sums_ref, hidden_ref, own_ref, weight_ref, params_ref,
    out_ref, wide_ref, taps_ref, summed_ref, done_ref, sems,
):
    rows, width, channels = own_ref.shape
    scale, offset = scale_offset(
        sums_ref, params_ref.at[1:2], params_ref.at[2:3], rows * width * count
    )
    sum_paired(weight_ref, summed_ref)
    copies = [
        pltpu.make_async_copy(done_ref.at[row], out_ref.at[row], sems.at[row])
        for row in range(rows)
    ]
    for row in range(2):
        store_taps(hidden_ref[row], scale, offset, wide_ref, taps_ref, row)
    for row in range(0, rows, 2):
        for i in range(2, 4):
            store_taps(hidden_ref[row + i], scale, offset, wide_ref, taps_ref, row + i)
        window = jnp.concatenate([taps_ref[row + tap] for tap in range(4)], axis=1)
        both = jnp.dot(window, summed_ref[...], preferred_element_type=jnp.float32)
        for i in range(2):
            branch = both[:, i * channels : (i + 1) * channels] + params_ref[0:1, :]
            values = own_ref[row + i].astype(jnp.float32) + branch
            done_ref[row + i] = values.astype(jnp.bfloat16)
            copies[row + i].start()
    for copy in copies:
        copy.wait()


def exchanged(sums):
    return lax.all_to_all(sums, "rows", 0, 0)


def body(
    latents, gain_one, shift_one, weight_one, bias_one, gain_two, shift_two, weight_two, bias_two
):
    count = lax.axis_size("rows")
    own = latents[0]
    rows, width, channels = own.shape
    sums_shape = jax.ShapeDtypeStruct((count, 2, channels), jnp.float32)
    taps = weight_one.shape[1] * weight_one.shape[2]
    slab_shape = jax.ShapeDtypeStruct((2, width, channels), jnp.bfloat16)

    def raw(weight):
        return weight.reshape(3, taps, channels, channels)

    swap_pair = [(i, i ^ 1) for i in range(count)]
    swap_other = [(i, i + 1 if i % 2 else i - 1) for i in range(1, count - 1)]

    sums, pair, other = pl.pallas_call(
        sums_kernel,
        out_shape=[sums_shape, slab_shape, slab_shape],
        in_specs=[VMEM],
        out_specs=[VMEM] * 3,
        compiler_params=PARAMS,
        name="sums",
        cost_estimate=pl.CostEstimate(
            flops=40000000000, bytes_accessed=10000000, transcendentals=0
        ),
    )(own)
    other = lax.ppermute(other, "rows", swap_other)
    pair = lax.ppermute(pair, "rows", swap_pair)
    sums = exchanged(sums)
    hidden, sums, params = pl.pallas_call(
        functools.partial(first_kernel, count),
        out_shape=[
            jax.ShapeDtypeStruct((rows + 2, width, channels), jnp.bfloat16),
            sums_shape,
            jax.ShapeDtypeStruct((8, channels), jnp.float32),
        ],
        in_specs=[VMEM] * 8 + [HBM] * 3,
        out_specs=[VMEM] * 3,
        scratch_shapes=[
            pltpu.VMEM((rows + 4, width + 16, channels), jnp.float32),
            pltpu.VMEM((rows + 4, width, 3 * channels), jnp.bfloat16),
            pltpu.VMEM((taps * channels, 2 * channels), jnp.bfloat16),
            pltpu.VMEM((3, 1, channels), jnp.float32),
            pltpu.SemaphoreType.DMA((3,)),
        ],
        compiler_params=PARAMS, name="first",
    )(
        sums,
        own,
        pair,
        other,
        raw(weight_one),
        *[vector.reshape(1, channels) for vector in (bias_one, gain_one, shift_one)],
        *[
            pltpu.with_memory_space_constraint(vector.reshape(1, channels), pltpu.HBM)
            for vector in (bias_two, gain_two, shift_two)
        ],
    )
    sums = exchanged(sums)
    decoded = pl.pallas_call(
        functools.partial(second_kernel, count),
        out_shape=jax.ShapeDtypeStruct(own.shape, jnp.bfloat16),
        in_specs=[VMEM] * 5,
        out_specs=ANY,
        scratch_shapes=[
            pltpu.VMEM((rows + 2, width + 16, channels), jnp.float32),
            pltpu.VMEM((rows + 2, width, 3 * channels), jnp.bfloat16),
            pltpu.VMEM((taps // 3 * 4 * channels, 2 * channels), jnp.bfloat16),
            pltpu.VMEM(own.shape, jnp.bfloat16),
            pltpu.SemaphoreType.DMA((rows,)),
        ],
        compiler_params=PARAMS, name="second",
    )(sums, hidden, own, raw(weight_two), params)
    return decoded[None]


def solution(mesh):
    return jax.shard_map(
        body,
        mesh=mesh,
        in_specs=(P("groups", "rows", None, None), P(), P(), P(), P(), P(), P(), P(), P()),
        out_specs=P("groups", "rows", None, None),
        check_vma=False,
    )
```

```python
import functools

import jax
import jax.numpy as jnp
from jax import lax
from jax.experimental import pallas as pl
from jax.experimental.pallas import tpu as pltpu
from jax.sharding import PartitionSpec as P

GROUPS = 32
HBM = pl.BlockSpec(memory_space=pltpu.HBM)
ANY = pl.BlockSpec(memory_space=pl.ANY)
VMEM = pl.BlockSpec(memory_space=pltpu.VMEM)
PARAMS = pltpu.CompilerParams(vmem_limit_bytes=24 * 1024 * 1024)


def store_sums(total, square, out_ref):
    total = jnp.sum(total, axis=0, keepdims=True)
    square = jnp.sum(square, axis=0, keepdims=True)
    both = jnp.concatenate([total, square], axis=0)
    out_ref[...] = jnp.broadcast_to(both[None], out_ref.shape)


def add_sums(values, total, square):
    width, channels = values.shape
    split = (width // 8, 8, channels)
    total += jnp.sum(values.reshape(split), axis=0)
    square += jnp.sum((values * values).reshape(split), axis=0)
    return total, square


def sums_kernel(own_ref, out_ref, pair_ref, other_ref):
    rows, _, channels = own_ref.shape
    even = lax.axis_index("rows") % 2 == 0
    for row in range(2):
        top = own_ref[row]
        bottom = own_ref[rows - 2 + row]
        pair_ref[row] = jnp.where(even, bottom, top)
        other_ref[row] = jnp.where(even, top, bottom)
    total = jnp.zeros((8, channels), jnp.float32)
    square = jnp.zeros((8, channels), jnp.float32)
    for row in range(rows):
        total, square = add_sums(own_ref[row].astype(jnp.float32), total, square)
    store_sums(total, square, out_ref)


def tap_total(source, tap):
    total = source[0, tap].astype(jnp.float32)
    total += source[1, tap].astype(jnp.float32)
    return total + source[2, tap].astype(jnp.float32)


def sum_weight(source, target):
    taps, channels = source.shape[1], source.shape[2]

    @pl.loop(0, taps)
    def _(tap):
        total = tap_total(source, tap)
        high = total.astype(jnp.bfloat16)
        low = (total - high.astype(jnp.float32)).astype(jnp.bfloat16)
        rows = pl.ds(pl.multiple_of(tap * channels, channels), channels)
        target[rows, 0:channels] = high
        target[rows, channels : 2 * channels] = low


def sum_paired(source, target):
    taps, channels = source.shape[1], source.shape[2]
    columns = taps // 3
    zeros = jnp.zeros((columns * channels, channels), jnp.bfloat16)
    target[pl.ds(taps * channels, columns * channels), 0:channels] = zeros
    target[pl.ds(0, columns * channels), channels : 2 * channels] = zeros

    @pl.loop(0, taps)
    def _(tap):
        total = tap_total(source, tap).astype(jnp.bfloat16)
        rows = pl.ds(pl.multiple_of(tap * channels, channels), channels)
        target[rows, 0:channels] = total
        rows = pl.ds(pl.multiple_of((tap + columns) * channels, channels), channels)
        target[rows, channels : 2 * channels] = total


def scale_offset(sums_ref, gain_ref, shift_ref, entries):
    sums = jnp.sum(sums_ref[...], axis=0)
    channels = sums.shape[1]
    per_group = channels // GROUPS
    sums = jnp.concatenate([sums, jnp.zeros((6, channels), jnp.float32)], axis=0)
    member = lax.broadcasted_iota(jnp.int32, sums.shape, 1) % per_group
    total = sums
    for step in range(1, per_group):
        total += jnp.where(member >= step, pltpu.roll(sums, step, 1), 0.0)
        total += jnp.where(member < per_group - step, pltpu.roll(sums, channels - step, 1), 0.0)
    total = total * (1.0 / (entries * per_group))
    mean = total[0:1]
    var = total[1:2] - mean * mean
    scale = gain_ref[...] * lax.rsqrt(var + 1e-06)
    return 0.5 * scale, 0.5 * (shift_ref[...] - mean * scale)


def store_taps(values, scale, offset, wide_ref, taps_ref, row):
    width, channels = values.shape
    half = values.astype(jnp.float32) * scale + offset
    act = half * jnp.tanh(half) + half
    wide_ref[row, 8 : 8 + width, :] = act
    wide_ref[row, 7:8, :] = act[0:1]
    wide_ref[row, 8 + width : 9 + width, :] = act[width - 1 : width]
    for tap in range(3):
        shifted = wide_ref[row, 7 + tap : 7 + tap + width, :]
        taps_ref[row, :, tap * channels : (tap + 1) * channels] = shifted.astype(jnp.bfloat16)


def window(taps_ref, row, count, taps):
    _, width, lanes = taps_ref.shape
    parts = [
        taps_ref[pl.ds(row + tap, count)].reshape(count * width, lanes) for tap in range(taps)
    ]
    return jnp.concatenate(parts, axis=1)


def first_kernel(
    count, sums_ref, own_ref, pair_ref, other_ref, weight_ref, bias_ref, gain_ref, shift_ref,
    bias_two_ref, gain_two_ref, shift_two_ref,
    hidden_ref, out_ref, next_ref, wide_ref, taps_ref, summed_ref, vectors_ref, sems,
):
    copies = [
        pltpu.make_async_copy(source, vectors_ref.at[i], sems.at[i])
        for i, source in enumerate((bias_two_ref, gain_two_ref, shift_two_ref))
    ]
    for copy in copies:
        copy.start()
    index = lax.axis_index("rows")
    rows, width, channels = own_ref.shape
    even = index % 2 == 0
    scale, offset = scale_offset(sums_ref, gain_ref, shift_ref, rows * width * count)
    sum_weight(weight_ref, summed_ref)

    def make(values, row):
        store_taps(values, scale, offset, wide_ref, taps_ref, row)

    @pl.loop(0, 2)
    def _(row):
        values = jnp.where(even, other_ref[row], pair_ref[row])
        make(jnp.where(index == 0, own_ref[0], values), row)

    @pl.loop(0, rows)
    def _(row):
        make(own_ref[row], row + 2)

    @pl.loop(0, 2)
    def _(row):
        values = jnp.where(even, pair_ref[row], other_ref[row])
        make(jnp.where(index == count - 1, own_ref[rows - 1], values), row + rows + 2)

    def conv(step, carry):
        total, square = carry
        row = 2 * step
        both = jnp.dot(
            window(taps_ref, row, 2, 3), summed_ref[...], preferred_element_type=jnp.float32
        )
        hidden = both[:, :channels] + both[:, channels:] + bias_ref[...]
        hidden = hidden.astype(jnp.bfloat16)
        for i in range(2):
            values = hidden[i * width : (i + 1) * width]
            hidden_ref[row + i] = values
            inside = jnp.logical_and(row + i > 0, row + i <= rows)
            zero = jnp.zeros((8, channels), jnp.float32)
            added, added_square = add_sums(values.astype(jnp.float32), zero, zero)
            total += jnp.where(inside, added, 0.0)
            square += jnp.where(inside, added_square, 0.0)
        return total, square

    zero = jnp.zeros((8, channels), jnp.float32)
    total, square = lax.fori_loop(0, (rows + 2) // 2, conv, (zero, zero))
    store_sums(total, square, out_ref)
    for i in range(3):
        copies[i].wait()
        next_ref[pl.ds(i, 1), :] = vectors_ref[i]

    @pl.when(index == 0)
    def _():
        hidden_ref[0] = hidden_ref[1]

    @pl.when(index == count - 1)
    def _():
        hidden_ref[rows + 1] = hidden_ref[rows]


def second_kernel(
    count, sums_ref, hidden_ref, own_ref, weight_ref, params_ref,
    out_ref, wide_ref, taps_ref, summed_ref, done_ref, sems,
):
    rows, width, channels = own_ref.shape
    scale, offset = scale_offset(
        sums_ref, params_ref.at[1:2], params_ref.at[2:3], rows * width * count
    )
    sum_paired(weight_ref, summed_ref)
    def copy_out(row):
        return pltpu.make_async_copy(done_ref.at[row], out_ref.at[row], sems.at[row])

    @pl.loop(0, rows + 2)
    def _(row):
        store_taps(hidden_ref[row], scale, offset, wide_ref, taps_ref, row)

    @pl.loop(0, rows // 2)
    def _(step):
        row = 2 * step
        both = jnp.dot(
            window(taps_ref, row, 1, 4), summed_ref[...], preferred_element_type=jnp.float32
        )
        for i in range(2):
            branch = both[:, i * channels : (i + 1) * channels] + params_ref[0:1, :]
            values = own_ref[row + i].astype(jnp.float32) + branch
            done_ref[row + i] = values.astype(jnp.bfloat16)
            copy_out(row + i).start()

    for row in range(rows):
        copy_out(row).wait()


def exchanged(sums):
    return lax.all_to_all(sums, "rows", 0, 0)


def body(
    latents, gain_one, shift_one, weight_one, bias_one, gain_two, shift_two, weight_two, bias_two
):
    count = lax.axis_size("rows")
    own = latents[0]
    rows, width, channels = own.shape
    sums_shape = jax.ShapeDtypeStruct((count, 2, channels), jnp.float32)
    taps = weight_one.shape[1] * weight_one.shape[2]
    slab_shape = jax.ShapeDtypeStruct((2, width, channels), jnp.bfloat16)

    def raw(weight):
        return weight.reshape(3, taps, channels, channels)

    swap_pair = [(i, i ^ 1) for i in range(count)]
    swap_other = [(i, i + 1 if i % 2 else i - 1) for i in range(1, count - 1)]

    sums, pair, other = pl.pallas_call(
        sums_kernel,
        out_shape=[sums_shape, slab_shape, slab_shape],
        in_specs=[VMEM],
        out_specs=[VMEM] * 3,
        compiler_params=PARAMS,
        name="sums",
        cost_estimate=pl.CostEstimate(
            flops=40000000000, bytes_accessed=10000000, transcendentals=0
        ),
    )(own)
    other = lax.ppermute(other, "rows", swap_other)
    pair = lax.ppermute(pair, "rows", swap_pair)
    sums = exchanged(sums)
    hidden, sums, params = pl.pallas_call(
        functools.partial(first_kernel, count),
        out_shape=[
            jax.ShapeDtypeStruct((rows + 2, width, channels), jnp.bfloat16),
            sums_shape,
            jax.ShapeDtypeStruct((8, channels), jnp.float32),
        ],
        in_specs=[VMEM] * 8 + [HBM] * 3,
        out_specs=[VMEM] * 3,
        scratch_shapes=[
            pltpu.VMEM((rows + 4, width + 16, channels), jnp.float32),
            pltpu.VMEM((rows + 4, width, 3 * channels), jnp.bfloat16),
            pltpu.VMEM((taps * channels, 2 * channels), jnp.bfloat16),
            pltpu.VMEM((3, 1, channels), jnp.float32),
            pltpu.SemaphoreType.DMA((3,)),
        ],
        compiler_params=PARAMS, name="first",
    )(
        sums,
        own,
        pair,
        other,
        raw(weight_one),
        *[vector.reshape(1, channels) for vector in (bias_one, gain_one, shift_one)],
        *[
            pltpu.with_memory_space_constraint(vector.reshape(1, channels), pltpu.HBM)
            for vector in (bias_two, gain_two, shift_two)
        ],
    )
    sums = exchanged(sums)
    decoded = pl.pallas_call(
        functools.partial(second_kernel, count),
        out_shape=jax.ShapeDtypeStruct(own.shape, jnp.bfloat16),
        in_specs=[VMEM] * 5,
        out_specs=ANY,
        scratch_shapes=[
            pltpu.VMEM((rows + 2, width + 16, channels), jnp.float32),
            pltpu.VMEM((rows + 2, width, 3 * channels), jnp.bfloat16),
            pltpu.VMEM((taps // 3 * 4 * channels, 2 * channels), jnp.bfloat16),
            pltpu.VMEM(own.shape, jnp.bfloat16),
            pltpu.SemaphoreType.DMA((rows,)),
        ],
        compiler_params=PARAMS, name="second",
    )(sums, hidden, own, raw(weight_two), params)
    return decoded[None]


def solution(mesh):
    return jax.shard_map(
        body,
        mesh=mesh,
        in_specs=(P("groups", "rows", None, None), P(), P(), P(), P(), P(), P(), P(), P()),
        out_specs=P("groups", "rows", None, None),
        check_vma=False,
    )
```

```python
import functools

import jax
import jax.numpy as jnp
from jax import lax
from jax.experimental import pallas as pl
from jax.experimental.pallas import tpu as pltpu
from jax.sharding import PartitionSpec as P

GROUPS = 32
HBM = pl.BlockSpec(memory_space=pltpu.HBM)
ANY = pl.BlockSpec(memory_space=pl.ANY)
VMEM = pl.BlockSpec(memory_space=pltpu.VMEM)
LONG = pl.CostEstimate(flops=40000000000, bytes_accessed=10000000, transcendentals=0)
PARAMS = pltpu.CompilerParams(vmem_limit_bytes=24 * 1024 * 1024)


def store_sums(total, square, out_ref):
    total = jnp.sum(total, axis=0, keepdims=True)
    square = jnp.sum(square, axis=0, keepdims=True)
    both = jnp.concatenate([total, square], axis=0)
    out_ref[...] = jnp.broadcast_to(both[None], out_ref.shape)


def add_sums(values, total, square):
    width, channels = values.shape
    split = (width // 8, 8, channels)
    total += jnp.sum(values.reshape(split), axis=0)
    square += jnp.sum((values * values).reshape(split), axis=0)
    return total, square


def slabs_kernel(latents_ref, pair_ref, other_ref, sems):
    even = 1 - lax.axis_index("rows") % 2
    last = latents_ref.shape[0] - 2
    copies = [
        pltpu.make_async_copy(latents_ref.at[pl.ds(start, 2)], target, sems.at[i])
        for i, (start, target) in enumerate(
            ((last * even, pair_ref), (last * (1 - even), other_ref))
        )
    ]
    for copy in copies:
        copy.start()
    for copy in copies:
        copy.wait()


def sums_kernel(own_ref, out_ref):
    rows, _, channels = own_ref.shape
    total = jnp.zeros((8, channels), jnp.float32)
    square = jnp.zeros((8, channels), jnp.float32)
    for row in range(rows):
        total, square = add_sums(own_ref[row].astype(jnp.float32), total, square)
    store_sums(total, square, out_ref)


def sum_weight(source, target):
    taps, channels = source.shape[1], source.shape[2]
    for tap in range(taps):
        total = source[0, tap].astype(jnp.float32)
        total += source[1, tap].astype(jnp.float32)
        total += source[2, tap].astype(jnp.float32)
        high = total.astype(jnp.bfloat16)
        low = (total - high.astype(jnp.float32)).astype(jnp.bfloat16)
        target[pl.ds(tap * channels, channels), :] = jnp.concatenate([high, low], axis=1)


def sum_paired(source, target):
    taps, channels = source.shape[1], source.shape[2]
    columns = taps // 3
    zeros = jnp.zeros((columns * channels, channels), jnp.bfloat16)
    for tap in range(taps):
        total = source[0, tap].astype(jnp.float32)
        total += source[1, tap].astype(jnp.float32)
        total += source[2, tap].astype(jnp.float32)
        total = total.astype(jnp.bfloat16)
        target[pl.ds(tap * channels, channels), 0:channels] = total
        target[pl.ds((tap + columns) * channels, channels), channels : 2 * channels] = total
    target[pl.ds(taps * channels, columns * channels), 0:channels] = zeros
    target[pl.ds(0, columns * channels), channels : 2 * channels] = zeros


def scale_offset(sums_ref, gain_ref, shift_ref, entries):
    sums = jnp.sum(sums_ref[...], axis=0)
    channels = sums.shape[1]
    per_group = channels // GROUPS
    sums = jnp.concatenate([sums, jnp.zeros((6, channels), jnp.float32)], axis=0)
    member = lax.broadcasted_iota(jnp.int32, sums.shape, 1) % per_group
    total = sums
    for step in range(1, per_group):
        total += jnp.where(member >= step, pltpu.roll(sums, step, 1), 0.0)
        total += jnp.where(member < per_group - step, pltpu.roll(sums, channels - step, 1), 0.0)
    total = total * (1.0 / (entries * per_group))
    mean = total[0:1]
    var = total[1:2] - mean * mean
    scale = gain_ref[...] * lax.rsqrt(var + 1e-06)
    return 0.5 * scale, 0.5 * (shift_ref[...] - mean * scale)


def store_taps(values, scale, offset, wide_ref, taps_ref, row):
    width, channels = values.shape
    half = values.astype(jnp.float32) * scale + offset
    act = half * jnp.tanh(half) + half
    wide_ref[row, 8 : 8 + width, :] = act
    wide_ref[row, 7:8, :] = act[0:1]
    wide_ref[row, 8 + width : 9 + width, :] = act[width - 1 : width]
    for tap in range(3):
        shifted = wide_ref[row, 7 + tap : 7 + tap + width, :]
        taps_ref[row, :, tap * channels : (tap + 1) * channels] = shifted.astype(jnp.bfloat16)


def conv_rows(taps_ref, row, count, weight_ref):
    _, width, lanes = taps_ref.shape
    window = jnp.concatenate(
        [taps_ref[row + tap : row + tap + count].reshape(count * width, lanes) for tap in range(3)],
        axis=1,
    )
    both = jnp.dot(window, weight_ref[...], preferred_element_type=jnp.float32)
    half = both.shape[1] // 2
    return both[:, :half] + both[:, half:]


def first_kernel(
    count, sums_ref, own_ref, pair_ref, other_ref, weight_ref, bias_ref, gain_ref, shift_ref,
    bias_two_ref, gain_two_ref, shift_two_ref,
    hidden_ref, out_ref, next_ref, wide_ref, taps_ref, summed_ref, vectors_ref, sems,
):
    copies = [
        pltpu.make_async_copy(source, vectors_ref.at[i], sems.at[i])
        for i, source in enumerate((bias_two_ref, gain_two_ref, shift_two_ref))
    ]
    for copy in copies:
        copy.start()
    index = lax.axis_index("rows")
    rows, width, channels = own_ref.shape
    even = index % 2 == 0
    scale, offset = scale_offset(sums_ref, gain_ref, shift_ref, rows * width * count)
    sum_weight(weight_ref, summed_ref)

    def make(row):
        if row < 2:
            values = jnp.where(even, other_ref[row], pair_ref[row])
            values = jnp.where(index == 0, own_ref[0], values)
        elif row < rows + 2:
            values = own_ref[row - 2]
        else:
            values = jnp.where(even, pair_ref[row - rows - 2], other_ref[row - rows - 2])
            values = jnp.where(index == count - 1, own_ref[rows - 1], values)
        store_taps(values, scale, offset, wide_ref, taps_ref, row)

    total = jnp.zeros((8, channels), jnp.float32)
    square = jnp.zeros((8, channels), jnp.float32)
    for row in range(rows + 4):
        make(row)
    hidden = conv_rows(taps_ref, 0, rows + 2, summed_ref) + bias_ref[...]
    hidden = hidden.astype(jnp.bfloat16)
    for row in range(rows + 2):
        values = hidden[row * width : (row + 1) * width]
        hidden_ref[row] = values
        if 0 < row <= rows:
            total, square = add_sums(values.astype(jnp.float32), total, square)
    store_sums(total, square, out_ref)
    for i in range(3):
        copies[i].wait()
        next_ref[pl.ds(i, 1), :] = vectors_ref[i]

    @pl.when(index == 0)
    def _():
        hidden_ref[0] = hidden_ref[1]

    @pl.when(index == count - 1)
    def _():
        hidden_ref[rows + 1] = hidden_ref[rows]


def second_kernel(
    count, sums_ref, hidden_ref, own_ref, weight_ref, params_ref,
    out_ref, wide_ref, taps_ref, summed_ref, done_ref, sems,
):
    rows, width, channels = own_ref.shape
    scale, offset = scale_offset(
        sums_ref, params_ref.at[1:2], params_ref.at[2:3], rows * width * count
    )
    sum_paired(weight_ref, summed_ref)
    copies = [
        pltpu.make_async_copy(done_ref.at[row], out_ref.at[row], sems.at[row])
        for row in range(rows)
    ]
    for row in range(2):
        store_taps(hidden_ref[row], scale, offset, wide_ref, taps_ref, row)
    for row in range(0, rows, 2):
        for i in range(2, 4):
            store_taps(hidden_ref[row + i], scale, offset, wide_ref, taps_ref, row + i)
        window = jnp.concatenate([taps_ref[row + tap] for tap in range(4)], axis=1)
        both = jnp.dot(window, summed_ref[...], preferred_element_type=jnp.float32)
        for i in range(2):
            branch = both[:, i * channels : (i + 1) * channels] + params_ref[0:1, :]
            values = own_ref[row + i].astype(jnp.float32) + branch
            done_ref[row + i] = values.astype(jnp.bfloat16)
            copies[row + i].start()
    for copy in copies:
        copy.wait()


def exchanged(sums):
    return lax.all_to_all(sums, "rows", 0, 0)


def body(
    latents, gain_one, shift_one, weight_one, bias_one, gain_two, shift_two, weight_two, bias_two
):
    count = lax.axis_size("rows")
    own = latents[0]
    rows, width, channels = own.shape
    sums_shape = jax.ShapeDtypeStruct((count, 2, channels), jnp.float32)
    taps = weight_one.shape[1] * weight_one.shape[2]
    slab_shape = jax.ShapeDtypeStruct((2, width, channels), jnp.bfloat16)

    def raw(weight):
        return weight.reshape(3, taps, channels, channels)

    swap_pair = [(i, i ^ 1) for i in range(count)]
    swap_other = [(i, i + 1 if i % 2 else i - 1) for i in range(1, count - 1)]

    pair, other = pl.pallas_call(
        slabs_kernel,
        out_shape=[slab_shape] * 2,
        in_specs=[HBM],
        out_specs=[VMEM] * 2,
        scratch_shapes=[pltpu.SemaphoreType.DMA((2,))],
        compiler_params=PARAMS,
        name="slabs",
        cost_estimate=LONG,
    )(pltpu.with_memory_space_constraint(own, pltpu.HBM))
    sums = pl.pallas_call(
        sums_kernel,
        out_shape=sums_shape,
        in_specs=[VMEM],
        out_specs=VMEM,
        compiler_params=PARAMS,
        name="sums",
        cost_estimate=LONG,
    )(own)
    other = lax.ppermute(other, "rows", swap_other)
    pair = lax.ppermute(pair, "rows", swap_pair)
    sums = exchanged(sums)
    hidden, sums, params = pl.pallas_call(
        functools.partial(first_kernel, count),
        out_shape=[
            jax.ShapeDtypeStruct((rows + 2, width, channels), jnp.bfloat16),
            sums_shape,
            jax.ShapeDtypeStruct((8, channels), jnp.float32),
        ],
        in_specs=[VMEM] * 8 + [HBM] * 3,
        out_specs=[VMEM] * 3,
        scratch_shapes=[
            pltpu.VMEM((rows + 4, width + 16, channels), jnp.float32),
            pltpu.VMEM((rows + 4, width, 3 * channels), jnp.bfloat16),
            pltpu.VMEM((taps * channels, 2 * channels), jnp.bfloat16),
            pltpu.VMEM((3, 1, channels), jnp.float32),
            pltpu.SemaphoreType.DMA((3,)),
        ],
        compiler_params=PARAMS, name="first",
    )(
        sums,
        own,
        pair,
        other,
        raw(weight_one),
        *[vector.reshape(1, channels) for vector in (bias_one, gain_one, shift_one)],
        *[
            pltpu.with_memory_space_constraint(vector.reshape(1, channels), pltpu.HBM)
            for vector in (bias_two, gain_two, shift_two)
        ],
    )
    sums = exchanged(sums)
    decoded = pl.pallas_call(
        functools.partial(second_kernel, count),
        out_shape=jax.ShapeDtypeStruct(own.shape, jnp.bfloat16),
        in_specs=[VMEM] * 5,
        out_specs=ANY,
        scratch_shapes=[
            pltpu.VMEM((rows + 2, width + 16, channels), jnp.float32),
            pltpu.VMEM((rows + 2, width, 3 * channels), jnp.bfloat16),
            pltpu.VMEM((taps // 3 * 4 * channels, 2 * channels), jnp.bfloat16),
            pltpu.VMEM(own.shape, jnp.bfloat16),
            pltpu.SemaphoreType.DMA((rows,)),
        ],
        compiler_params=PARAMS, name="second",
    )(sums, hidden, own, raw(weight_two), params)
    return decoded[None]


def solution(mesh):
    return jax.shard_map(
        body,
        mesh=mesh,
        in_specs=(P("groups", "rows", None, None), P(), P(), P(), P(), P(), P(), P(), P()),
        out_specs=P("groups", "rows", None, None),
        check_vma=False,
    )
```

```python
import functools

import jax
import jax.numpy as jnp
from jax import lax
from jax.experimental import pallas as pl
from jax.experimental.pallas import tpu as pltpu
from jax.sharding import PartitionSpec as P

GROUPS = 32
HBM = pl.BlockSpec(memory_space=pltpu.HBM)
ANY = pl.BlockSpec(memory_space=pl.ANY)
VMEM = pl.BlockSpec(memory_space=pltpu.VMEM)
PARAMS = pltpu.CompilerParams(vmem_limit_bytes=24 * 1024 * 1024)


def store_sums(total, square, out_ref):
    total = jnp.sum(total, axis=0, keepdims=True)
    square = jnp.sum(square, axis=0, keepdims=True)
    both = jnp.concatenate([total, square], axis=0)
    out_ref[...] = jnp.broadcast_to(both[None], out_ref.shape)


def add_sums(values, total, square):
    width, channels = values.shape
    split = (width // 8, 8, channels)
    total += jnp.sum(values.reshape(split), axis=0)
    square += jnp.sum((values * values).reshape(split), axis=0)
    return total, square


def sums_kernel(own_ref, out_ref, pair_ref, other_ref):
    rows, _, channels = own_ref.shape
    even = lax.axis_index("rows") % 2 == 0
    for row in range(2):
        top = own_ref[row]
        bottom = own_ref[rows - 2 + row]
        pair_ref[row] = jnp.where(even, bottom, top)
        other_ref[row] = jnp.where(even, top, bottom)
    total = jnp.zeros((8, channels), jnp.float32)
    square = jnp.zeros((8, channels), jnp.float32)
    for row in range(rows):
        total, square = add_sums(own_ref[row].astype(jnp.float32), total, square)
    store_sums(total, square, out_ref)


def sum_weight(source, target):
    taps, channels = source.shape[1], source.shape[2]
    for tap in range(taps):
        total = source[0, tap].astype(jnp.float32)
        total += source[1, tap].astype(jnp.float32)
        total += source[2, tap].astype(jnp.float32)
        high = total.astype(jnp.bfloat16)
        low = (total - high.astype(jnp.float32)).astype(jnp.bfloat16)
        target[pl.ds(tap * channels, channels), :] = jnp.concatenate([high, low], axis=1)


def sum_paired(source, target):
    taps, channels = source.shape[1], source.shape[2]
    columns = taps // 3
    zeros = jnp.zeros((columns * channels, channels), jnp.bfloat16)
    for tap in range(taps):
        total = source[0, tap].astype(jnp.float32)
        total += source[1, tap].astype(jnp.float32)
        total += source[2, tap].astype(jnp.float32)
        total = total.astype(jnp.bfloat16)
        target[pl.ds(tap * channels, channels), 0:channels] = total
        target[pl.ds((tap + columns) * channels, channels), channels : 2 * channels] = total
    target[pl.ds(taps * channels, columns * channels), 0:channels] = zeros
    target[pl.ds(0, columns * channels), channels : 2 * channels] = zeros


def scale_offset(sums_ref, gain_ref, shift_ref, entries):
    sums = jnp.sum(sums_ref[...], axis=0)
    channels = sums.shape[1]
    per_group = channels // GROUPS
    sums = jnp.concatenate([sums, jnp.zeros((6, channels), jnp.float32)], axis=0)
    member = lax.broadcasted_iota(jnp.int32, sums.shape, 1) % per_group
    total = sums
    for step in range(1, per_group):
        total += jnp.where(member >= step, pltpu.roll(sums, step, 1), 0.0)
        total += jnp.where(member < per_group - step, pltpu.roll(sums, channels - step, 1), 0.0)
    total = total * (1.0 / (entries * per_group))
    mean = total[0:1]
    var = total[1:2] - mean * mean
    scale = gain_ref[...] * lax.rsqrt(var + 1e-06)
    return 0.5 * scale, 0.5 * (shift_ref[...] - mean * scale)


def activated(values, scale, offset):
    half = values.astype(jnp.float32) * scale + offset
    return half * jnp.tanh(half) + half


def store_blocks(blocks, taps_ref, row):
    leads = len(blocks)
    first, final = blocks[0], blocks[-1]
    sublane = lax.broadcasted_iota(jnp.int32, first.shape, 0)
    before = jnp.where(sublane == 0, first, pltpu.roll(final, 1, 0))
    after = jnp.where(sublane == 15, final, pltpu.roll(first, 15, 0))
    for lead, block in enumerate([before] + blocks + [after]):
        taps_ref[row, lead * 16 : (lead + 1) * 16, :] = block.astype(jnp.bfloat16)


def store_natural(values, scale, offset, wide_ref, taps_ref, row):
    leads = values.shape[0] // 16
    wide_ref[row] = activated(values, scale, offset)
    blocks = [wide_ref[row, pl.ds(lead, 16, stride=leads), :] for lead in range(leads)]
    store_blocks(blocks, taps_ref, row)


def store_permuted(values, scale, offset, taps_ref, row):
    leads = values.shape[0] // 16
    act = activated(values, scale, offset)
    blocks = [act[lead * 16 : (lead + 1) * 16] for lead in range(leads)]
    store_blocks(blocks, taps_ref, row)


def window(taps_ref, row, count, taps):
    width, lanes = taps_ref.shape[1] - 32, taps_ref.shape[2]
    parts = [
        taps_ref[row + tap : row + tap + count, 16 * column : 16 * column + width, :]
        for tap in range(taps)
        for column in range(3)
    ]
    return jnp.concatenate([part.reshape(count * width, lanes) for part in parts], axis=1)


def conv_rows(taps_ref, row, count, weight_ref):
    both = jnp.dot(
        window(taps_ref, row, count, 3), weight_ref[...], preferred_element_type=jnp.float32
    )
    half = both.shape[1] // 2
    return both[:, :half] + both[:, half:]


def first_kernel(
    count, sums_ref, own_ref, pair_ref, other_ref, weight_ref, bias_ref, gain_ref, shift_ref,
    bias_two_ref, gain_two_ref, shift_two_ref,
    hidden_ref, out_ref, next_ref, wide_ref, taps_ref, summed_ref, vectors_ref, sems,
):
    copies = [
        pltpu.make_async_copy(source, vectors_ref.at[i], sems.at[i])
        for i, source in enumerate((bias_two_ref, gain_two_ref, shift_two_ref))
    ]
    for copy in copies:
        copy.start()
    index = lax.axis_index("rows")
    rows, width, channels = own_ref.shape
    even = index % 2 == 0
    scale, offset = scale_offset(sums_ref, gain_ref, shift_ref, rows * width * count)
    sum_weight(weight_ref, summed_ref)

    def make(row):
        if row < 2:
            values = jnp.where(even, other_ref[row], pair_ref[row])
            values = jnp.where(index == 0, own_ref[0], values)
        elif row < rows + 2:
            values = own_ref[row - 2]
        else:
            values = jnp.where(even, pair_ref[row - rows - 2], other_ref[row - rows - 2])
            values = jnp.where(index == count - 1, own_ref[rows - 1], values)
        store_natural(values, scale, offset, wide_ref, taps_ref, row)

    total = jnp.zeros((8, channels), jnp.float32)
    square = jnp.zeros((8, channels), jnp.float32)
    for row in range(rows + 4):
        make(row)
    hidden = conv_rows(taps_ref, 0, rows + 2, summed_ref) + bias_ref[...]
    hidden = hidden.astype(jnp.bfloat16)
    for row in range(rows + 2):
        values = hidden[row * width : (row + 1) * width]
        hidden_ref[row] = values
        if 0 < row <= rows:
            total, square = add_sums(values.astype(jnp.float32), total, square)
    store_sums(total, square, out_ref)
    for i in range(3):
        copies[i].wait()
        next_ref[pl.ds(i, 1), :] = vectors_ref[i]

    @pl.when(index == 0)
    def _():
        hidden_ref[0] = hidden_ref[1]

    @pl.when(index == count - 1)
    def _():
        hidden_ref[rows + 1] = hidden_ref[rows]


def second_kernel(
    count, sums_ref, hidden_ref, own_ref, weight_ref, params_ref,
    out_ref, wide_ref, taps_ref, summed_ref, done_ref, sems,
):
    rows, width, channels = own_ref.shape
    scale, offset = scale_offset(
        sums_ref, params_ref.at[1:2], params_ref.at[2:3], rows * width * count
    )
    sum_paired(weight_ref, summed_ref)
    copies = [
        pltpu.make_async_copy(done_ref.at[row], out_ref.at[row], sems.at[row])
        for row in range(rows)
    ]
    for row in range(2):
        store_permuted(hidden_ref[row], scale, offset, taps_ref, row)
    for row in range(0, rows, 2):
        for i in range(2, 4):
            store_permuted(hidden_ref[row + i], scale, offset, taps_ref, row + i)
        both = jnp.dot(
            window(taps_ref, row, 1, 4), summed_ref[...], preferred_element_type=jnp.float32
        )
        leads = width // 16
        for i in range(2):
            branch = both[:, i * channels : (i + 1) * channels] + params_ref[0:1, :]
            for lead in range(leads):
                block = branch[lead * 16 : (lead + 1) * 16]
                wide_ref[row + i, pl.ds(lead, 16, stride=leads), :] = block
            values = own_ref[row + i].astype(jnp.float32) + wide_ref[row + i]
            done_ref[row + i] = values.astype(jnp.bfloat16)
            copies[row + i].start()
    for copy in copies:
        copy.wait()


def exchanged(sums):
    return lax.all_to_all(sums, "rows", 0, 0)


def body(
    latents, gain_one, shift_one, weight_one, bias_one, gain_two, shift_two, weight_two, bias_two
):
    count = lax.axis_size("rows")
    own = latents[0]
    rows, width, channels = own.shape
    sums_shape = jax.ShapeDtypeStruct((count, 2, channels), jnp.float32)
    taps = weight_one.shape[1] * weight_one.shape[2]
    slab_shape = jax.ShapeDtypeStruct((2, width, channels), jnp.bfloat16)

    def raw(weight):
        return weight.reshape(3, taps, channels, channels)

    swap_pair = [(i, i ^ 1) for i in range(count)]
    swap_other = [(i, i + 1 if i % 2 else i - 1) for i in range(1, count - 1)]

    sums, pair, other = pl.pallas_call(
        sums_kernel,
        out_shape=[sums_shape, slab_shape, slab_shape],
        in_specs=[VMEM],
        out_specs=[VMEM] * 3,
        compiler_params=PARAMS,
        name="sums",
        cost_estimate=pl.CostEstimate(
            flops=40000000000, bytes_accessed=10000000, transcendentals=0
        ),
    )(own)
    other = lax.ppermute(other, "rows", swap_other)
    pair = lax.ppermute(pair, "rows", swap_pair)
    sums = exchanged(sums)
    hidden, sums, params = pl.pallas_call(
        functools.partial(first_kernel, count),
        out_shape=[
            jax.ShapeDtypeStruct((rows + 2, width, channels), jnp.bfloat16),
            sums_shape,
            jax.ShapeDtypeStruct((8, channels), jnp.float32),
        ],
        in_specs=[VMEM] * 8 + [HBM] * 3,
        out_specs=[VMEM] * 3,
        scratch_shapes=[
            pltpu.VMEM((rows + 4, width, channels), jnp.float32),
            pltpu.VMEM((rows + 4, width + 32, channels), jnp.bfloat16),
            pltpu.VMEM((taps * channels, 2 * channels), jnp.bfloat16),
            pltpu.VMEM((3, 1, channels), jnp.float32),
            pltpu.SemaphoreType.DMA((3,)),
        ],
        compiler_params=PARAMS, name="first",
    )(
        sums,
        own,
        pair,
        other,
        raw(weight_one),
        *[vector.reshape(1, channels) for vector in (bias_one, gain_one, shift_one)],
        *[
            pltpu.with_memory_space_constraint(vector.reshape(1, channels), pltpu.HBM)
            for vector in (bias_two, gain_two, shift_two)
        ],
    )
    sums = exchanged(sums)
    decoded = pl.pallas_call(
        functools.partial(second_kernel, count),
        out_shape=jax.ShapeDtypeStruct(own.shape, jnp.bfloat16),
        in_specs=[VMEM] * 5,
        out_specs=ANY,
        scratch_shapes=[
            pltpu.VMEM((rows, width, channels), jnp.float32),
            pltpu.VMEM((rows + 2, width + 32, channels), jnp.bfloat16),
            pltpu.VMEM((taps // 3 * 4 * channels, 2 * channels), jnp.bfloat16),
            pltpu.VMEM(own.shape, jnp.bfloat16),
            pltpu.SemaphoreType.DMA((rows,)),
        ],
        compiler_params=PARAMS, name="second",
    )(sums, hidden, own, raw(weight_two), params)
    return decoded[None]


def solution(mesh):
    return jax.shard_map(
        body,
        mesh=mesh,
        in_specs=(P("groups", "rows", None, None), P(), P(), P(), P(), P(), P(), P(), P()),
        out_specs=P("groups", "rows", None, None),
        check_vma=False,
    )
```

```python
import functools

import jax
import jax.numpy as jnp
from jax import lax
from jax.experimental import pallas as pl
from jax.experimental.pallas import tpu as pltpu
from jax.sharding import PartitionSpec as P

GROUPS = 32
HBM = pl.BlockSpec(memory_space=pltpu.HBM)
ANY = pl.BlockSpec(memory_space=pl.ANY)
VMEM = pl.BlockSpec(memory_space=pltpu.VMEM)
LONG = pl.CostEstimate(flops=40000000000, bytes_accessed=10000000, transcendentals=0)
PARAMS = pltpu.CompilerParams(vmem_limit_bytes=24 * 1024 * 1024)


def store_sums(total, square, out_ref):
    total = jnp.sum(total, axis=0, keepdims=True)
    square = jnp.sum(square, axis=0, keepdims=True)
    both = jnp.concatenate([total, square], axis=0)
    out_ref[...] = jnp.broadcast_to(both[None], out_ref.shape)


def add_sums(values, total, square):
    width, channels = values.shape
    split = (width // 8, 8, channels)
    total += jnp.sum(values.reshape(split), axis=0)
    square += jnp.sum((values * values).reshape(split), axis=0)
    return total, square


def slabs_kernel(latents_ref, pair_ref, other_ref, sems):
    even = 1 - lax.axis_index("rows") % 2
    last = latents_ref.shape[0] - 2
    copies = [
        pltpu.make_async_copy(latents_ref.at[pl.ds(start, 2)], target, sems.at[i])
        for i, (start, target) in enumerate(
            ((last * even, pair_ref), (last * (1 - even), other_ref))
        )
    ]
    for copy in copies:
        copy.start()
    for copy in copies:
        copy.wait()


def sums_kernel(own_ref, out_ref):
    rows, _, channels = own_ref.shape
    total = jnp.zeros((8, channels), jnp.float32)
    square = jnp.zeros((8, channels), jnp.float32)
    for row in range(rows):
        total, square = add_sums(own_ref[row].astype(jnp.float32), total, square)
    store_sums(total, square, out_ref)


def sum_weight(source, target):
    taps, channels = source.shape[1], source.shape[2]
    for tap in range(taps):
        total = source[0, tap].astype(jnp.float32)
        total += source[1, tap].astype(jnp.float32)
        total += source[2, tap].astype(jnp.float32)
        high = total.astype(jnp.bfloat16)
        low = (total - high.astype(jnp.float32)).astype(jnp.bfloat16)
        target[pl.ds(tap * channels, channels), :] = jnp.concatenate([high, low], axis=1)


def sum_paired(source, target):
    taps, channels = source.shape[1], source.shape[2]
    columns = taps // 3
    zeros = jnp.zeros((columns * channels, channels), jnp.bfloat16)
    for tap in range(taps):
        total = source[0, tap].astype(jnp.float32)
        total += source[1, tap].astype(jnp.float32)
        total += source[2, tap].astype(jnp.float32)
        total = total.astype(jnp.bfloat16)
        target[pl.ds(tap * channels, channels), 0:channels] = total
        target[pl.ds((tap + columns) * channels, channels), channels : 2 * channels] = total
    target[pl.ds(taps * channels, columns * channels), 0:channels] = zeros
    target[pl.ds(0, columns * channels), channels : 2 * channels] = zeros


def scale_offset(sums_ref, gain_ref, shift_ref, entries):
    sums = jnp.sum(sums_ref[...], axis=0)
    channels = sums.shape[1]
    per_group = channels // GROUPS
    sums = jnp.concatenate([sums, jnp.zeros((6, channels), jnp.float32)], axis=0)
    member = lax.broadcasted_iota(jnp.int32, sums.shape, 1) % per_group
    total = sums
    for step in range(1, per_group):
        total += jnp.where(member >= step, pltpu.roll(sums, step, 1), 0.0)
        total += jnp.where(member < per_group - step, pltpu.roll(sums, channels - step, 1), 0.0)
    total = total * (1.0 / (entries * per_group))
    mean = total[0:1]
    var = total[1:2] - mean * mean
    scale = gain_ref[...] * lax.rsqrt(var + 1e-06)
    return 0.5 * scale, 0.5 * (shift_ref[...] - mean * scale)


def store_taps(values, scale, offset, wide_ref, taps_ref, row):
    width, channels = values.shape
    half = values.astype(jnp.float32) * scale + offset
    act = half * jnp.tanh(half) + half
    wide_ref[row, 8 : 8 + width, :] = act
    wide_ref[row, 7:8, :] = act[0:1]
    wide_ref[row, 8 + width : 9 + width, :] = act[width - 1 : width]
    for tap in range(3):
        shifted = wide_ref[row, 7 + tap : 7 + tap + width, :]
        taps_ref[row, :, tap * channels : (tap + 1) * channels] = shifted.astype(jnp.bfloat16)


def conv_rows(taps_ref, row, count, weight_ref):
    _, width, lanes = taps_ref.shape
    window = jnp.concatenate(
        [taps_ref[row + tap : row + tap + count].reshape(count * width, lanes) for tap in range(3)],
        axis=1,
    )
    both = jnp.dot(window, weight_ref[...], preferred_element_type=jnp.float32)
    half = both.shape[1] // 2
    return both[:, :half] + both[:, half:]


def first_kernel(
    count, sums_ref, own_ref, pair_ref, other_ref, weight_ref, bias_ref, gain_ref, shift_ref,
    bias_two_ref, gain_two_ref, shift_two_ref,
    hidden_ref, out_ref, next_ref, wide_ref, taps_ref, summed_ref, vectors_ref, sems,
):
    copies = [
        pltpu.make_async_copy(source, vectors_ref.at[i], sems.at[i])
        for i, source in enumerate((bias_two_ref, gain_two_ref, shift_two_ref))
    ]
    for copy in copies:
        copy.start()
    index = lax.axis_index("rows")
    rows, width, channels = own_ref.shape
    even = index % 2 == 0
    scale, offset = scale_offset(sums_ref, gain_ref, shift_ref, rows * width * count)
    sum_weight(weight_ref, summed_ref)

    def make(row):
        if row < 2:
            values = jnp.where(even, other_ref[row], pair_ref[row])
            values = jnp.where(index == 0, own_ref[0], values)
        elif row < rows + 2:
            values = own_ref[row - 2]
        else:
            values = jnp.where(even, pair_ref[row - rows - 2], other_ref[row - rows - 2])
            values = jnp.where(index == count - 1, own_ref[rows - 1], values)
        store_taps(values, scale, offset, wide_ref, taps_ref, row)

    total = jnp.zeros((8, channels), jnp.float32)
    square = jnp.zeros((8, channels), jnp.float32)
    for row in range(rows + 4):
        make(row)
    hidden = conv_rows(taps_ref, 0, rows + 2, summed_ref) + bias_ref[...]
    hidden = hidden.astype(jnp.bfloat16)
    for row in range(rows + 2):
        values = hidden[row * width : (row + 1) * width]
        hidden_ref[row] = values
        if 0 < row <= rows:
            total, square = add_sums(values.astype(jnp.float32), total, square)
    store_sums(total, square, out_ref)
    for i in range(3):
        copies[i].wait()
        next_ref[pl.ds(i, 1), :] = vectors_ref[i]

    @pl.when(index == 0)
    def _():
        hidden_ref[0] = hidden_ref[1]

    @pl.when(index == count - 1)
    def _():
        hidden_ref[rows + 1] = hidden_ref[rows]


def second_kernel(
    count, sums_ref, hidden_ref, own_ref, weight_ref, params_ref,
    out_ref, wide_ref, taps_ref, summed_ref, done_ref, sems,
):
    rows, width, channels = own_ref.shape
    scale, offset = scale_offset(
        sums_ref, params_ref.at[1:2], params_ref.at[2:3], rows * width * count
    )
    sum_paired(weight_ref, summed_ref)
    copies = [
        pltpu.make_async_copy(done_ref.at[row], out_ref.at[row], sems.at[row])
        for row in range(rows)
    ]
    for row in range(2):
        store_taps(hidden_ref[row], scale, offset, wide_ref, taps_ref, row)
    for row in range(0, rows, 2):
        for i in range(2, 4):
            store_taps(hidden_ref[row + i], scale, offset, wide_ref, taps_ref, row + i)
        window = jnp.concatenate([taps_ref[row + tap] for tap in range(4)], axis=1)
        both = jnp.dot(window, summed_ref[...], preferred_element_type=jnp.float32)
        for i in range(2):
            branch = both[:, i * channels : (i + 1) * channels] + params_ref[0:1, :]
            values = own_ref[row + i].astype(jnp.float32) + branch
            done_ref[row + i] = values.astype(jnp.bfloat16)
            copies[row + i].start()
    for copy in copies:
        copy.wait()


def exchanged(sums):
    return lax.all_to_all(sums, "rows", 0, 0)


def body(
    latents, gain_one, shift_one, weight_one, bias_one, gain_two, shift_two, weight_two, bias_two
):
    count = lax.axis_size("rows")
    own = latents[0]
    rows, width, channels = own.shape
    sums_shape = jax.ShapeDtypeStruct((count, 2, channels), jnp.float32)
    taps = weight_one.shape[1] * weight_one.shape[2]

    def raw(weight):
        return weight.reshape(3, taps, channels, channels)

    swap_pair = [(i, i ^ 1) for i in range(count)]
    swap_other = [(i, i + 1 if i % 2 else i - 1) for i in range(1, count - 1)]

    pair, other = pl.pallas_call(
        slabs_kernel,
        out_shape=[pltpu.HBM((2, width, channels), jnp.bfloat16)] * 2,
        in_specs=[HBM],
        out_specs=[HBM] * 2,
        scratch_shapes=[pltpu.SemaphoreType.DMA((2,))],
        compiler_params=PARAMS,
        name="slabs",
        cost_estimate=LONG,
    )(pltpu.with_memory_space_constraint(own, pltpu.HBM))
    sums = pl.pallas_call(
        sums_kernel,
        out_shape=sums_shape,
        in_specs=[VMEM],
        out_specs=VMEM,
        compiler_params=PARAMS,
        name="sums",
        cost_estimate=LONG,
    )(own)
    other = lax.ppermute(other, "rows", swap_other)
    pair = lax.ppermute(pair, "rows", swap_pair)
    sums = exchanged(sums)
    hidden, sums, params = pl.pallas_call(
        functools.partial(first_kernel, count),
        out_shape=[
            jax.ShapeDtypeStruct((rows + 2, width, channels), jnp.bfloat16),
            sums_shape,
            jax.ShapeDtypeStruct((8, channels), jnp.float32),
        ],
        in_specs=[VMEM] * 8 + [HBM] * 3,
        out_specs=[VMEM] * 3,
        scratch_shapes=[
            pltpu.VMEM((rows + 4, width + 16, channels), jnp.float32),
            pltpu.VMEM((rows + 4, width, 3 * channels), jnp.bfloat16),
            pltpu.VMEM((taps * channels, 2 * channels), jnp.bfloat16),
            pltpu.VMEM((3, 1, channels), jnp.float32),
            pltpu.SemaphoreType.DMA((3,)),
        ],
        compiler_params=PARAMS, name="first",
    )(
        sums,
        own,
        pair,
        other,
        raw(weight_one),
        *[vector.reshape(1, channels) for vector in (bias_one, gain_one, shift_one)],
        *[
            pltpu.with_memory_space_constraint(vector.reshape(1, channels), pltpu.HBM)
            for vector in (bias_two, gain_two, shift_two)
        ],
    )
    sums = exchanged(sums)
    decoded = pl.pallas_call(
        functools.partial(second_kernel, count),
        out_shape=jax.ShapeDtypeStruct(own.shape, jnp.bfloat16),
        in_specs=[VMEM] * 5,
        out_specs=ANY,
        scratch_shapes=[
            pltpu.VMEM((rows + 2, width + 16, channels), jnp.float32),
            pltpu.VMEM((rows + 2, width, 3 * channels), jnp.bfloat16),
            pltpu.VMEM((taps // 3 * 4 * channels, 2 * channels), jnp.bfloat16),
            pltpu.VMEM(own.shape, jnp.bfloat16),
            pltpu.SemaphoreType.DMA((rows,)),
        ],
        compiler_params=PARAMS, name="second",
    )(sums, hidden, own, raw(weight_two), params)
    return decoded[None]


def solution(mesh):
    return jax.shard_map(
        body,
        mesh=mesh,
        in_specs=(P("groups", "rows", None, None), P(), P(), P(), P(), P(), P(), P(), P()),
        out_specs=P("groups", "rows", None, None),
        check_vma=False,
    )
```

```python
import functools

import jax
import jax.numpy as jnp
from jax import lax
from jax.experimental import pallas as pl
from jax.experimental.pallas import tpu as pltpu
from jax.sharding import PartitionSpec as P

GROUPS = 32
HBM = pl.BlockSpec(memory_space=pltpu.HBM)
ANY = pl.BlockSpec(memory_space=pl.ANY)
VMEM = pl.BlockSpec(memory_space=pltpu.VMEM)
PARAMS = pltpu.CompilerParams(vmem_limit_bytes=24 * 1024 * 1024)


def store_sums(total, square, out_ref):
    total = jnp.sum(total, axis=0, keepdims=True)
    square = jnp.sum(square, axis=0, keepdims=True)
    both = jnp.concatenate([total, square], axis=0)
    out_ref[...] = jnp.broadcast_to(both[None], out_ref.shape)


def add_sums(values, total, square):
    width, channels = values.shape
    split = (width // 8, 8, channels)
    total += jnp.sum(values.reshape(split), axis=0)
    square += jnp.sum((values * values).reshape(split), axis=0)
    return total, square


def sums_kernel(own_ref, out_ref, pair_ref, other_ref):
    rows, _, channels = own_ref.shape
    even = lax.axis_index("rows") % 2 == 0
    for row in range(2):
        top = own_ref[row]
        bottom = own_ref[rows - 2 + row]
        pair_ref[row] = jnp.where(even, bottom, top)
        other_ref[row] = jnp.where(even, top, bottom)
    total = jnp.zeros((8, channels), jnp.float32)
    square = jnp.zeros((8, channels), jnp.float32)
    for row in range(rows):
        total, square = add_sums(own_ref[row].astype(jnp.float32), total, square)
    store_sums(total, square, out_ref)


def sum_weight(source, target):
    taps, channels = source.shape[1], source.shape[2]
    for tap in range(taps):
        total = source[0, tap].astype(jnp.float32)
        total += source[1, tap].astype(jnp.float32)
        total += source[2, tap].astype(jnp.float32)
        high = total.astype(jnp.bfloat16)
        low = (total - high.astype(jnp.float32)).astype(jnp.bfloat16)
        target[pl.ds(tap * channels, channels), :] = jnp.concatenate([high, low], axis=1)


def sum_paired(source, target):
    taps, channels = source.shape[1], source.shape[2]
    columns = taps // 3
    zeros = jnp.zeros((columns * channels, channels), jnp.bfloat16)
    for tap in range(taps):
        total = source[0, tap].astype(jnp.float32)
        total += source[1, tap].astype(jnp.float32)
        total += source[2, tap].astype(jnp.float32)
        total = total.astype(jnp.bfloat16)
        target[pl.ds(tap * channels, channels), 0:channels] = total
        target[pl.ds((tap + columns) * channels, channels), channels : 2 * channels] = total
    target[pl.ds(taps * channels, columns * channels), 0:channels] = zeros
    target[pl.ds(0, columns * channels), channels : 2 * channels] = zeros


def scale_offset(sums_ref, gain_ref, shift_ref, entries):
    sums = jnp.sum(sums_ref[...], axis=0)
    channels = sums.shape[1]
    per_group = channels // GROUPS
    sums = jnp.concatenate([sums, jnp.zeros((6, channels), jnp.float32)], axis=0)
    member = lax.broadcasted_iota(jnp.int32, sums.shape, 1) % per_group
    total = sums
    for step in range(1, per_group):
        total += jnp.where(member >= step, pltpu.roll(sums, step, 1), 0.0)
        total += jnp.where(member < per_group - step, pltpu.roll(sums, channels - step, 1), 0.0)
    total = total * (1.0 / (entries * per_group))
    mean = total[0:1]
    var = total[1:2] - mean * mean
    scale = gain_ref[...] * lax.rsqrt(var + 1e-06)
    return 0.5 * scale, 0.5 * (shift_ref[...] - mean * scale)


def store_taps(values, scale, offset, wide_ref, taps_ref, row):
    width, channels = values.shape
    half = values.astype(jnp.float32) * scale + offset
    act = half * jnp.tanh(half) + half
    wide_ref[row, 8 : 8 + width, :] = act
    wide_ref[row, 7:8, :] = act[0:1]
    wide_ref[row, 8 + width : 9 + width, :] = act[width - 1 : width]
    for tap in range(3):
        shifted = wide_ref[row, 7 + tap : 7 + tap + width, :]
        taps_ref[row, :, tap * channels : (tap + 1) * channels] = shifted.astype(jnp.bfloat16)


def conv_rows(taps_ref, row, count, weight_ref):
    _, width, lanes = taps_ref.shape
    window = jnp.concatenate(
        [taps_ref[row + tap : row + tap + count].reshape(count * width, lanes) for tap in range(3)],
        axis=1,
    )
    both = jnp.dot(window, weight_ref[...], preferred_element_type=jnp.float32)
    half = both.shape[1] // 2
    return both[:, :half] + both[:, half:]


def first_kernel(
    count, sums_ref, own_ref, pair_ref, other_ref, weight_ref, bias_ref, gain_ref, shift_ref,
    bias_two_ref, gain_two_ref, shift_two_ref,
    hidden_ref, out_ref, next_ref, wide_ref, taps_ref, summed_ref, vectors_ref, sems,
):
    copies = [
        pltpu.make_async_copy(source, vectors_ref.at[i], sems.at[i])
        for i, source in enumerate((bias_two_ref, gain_two_ref, shift_two_ref))
    ]
    for copy in copies:
        copy.start()
    index = lax.axis_index("rows")
    rows, width, channels = own_ref.shape
    even = index % 2 == 0
    scale, offset = scale_offset(sums_ref, gain_ref, shift_ref, rows * width * count)
    sum_weight(weight_ref, summed_ref)

    def make(row):
        if row < 2:
            values = jnp.where(even, other_ref[row], pair_ref[row])
            values = jnp.where(index == 0, own_ref[0], values)
        elif row < rows + 2:
            values = own_ref[row - 2]
        else:
            values = jnp.where(even, pair_ref[row - rows - 2], other_ref[row - rows - 2])
            values = jnp.where(index == count - 1, own_ref[rows - 1], values)
        store_taps(values, scale, offset, wide_ref, taps_ref, row)

    total = jnp.zeros((8, channels), jnp.float32)
    square = jnp.zeros((8, channels), jnp.float32)
    for row in range(rows + 4):
        make(row)
    hidden = conv_rows(taps_ref, 0, rows + 2, summed_ref) + bias_ref[...]
    hidden = hidden.astype(jnp.bfloat16)
    for row in range(rows + 2):
        values = hidden[row * width : (row + 1) * width]
        hidden_ref[row] = values
        if 0 < row <= rows:
            total, square = add_sums(values.astype(jnp.float32), total, square)
    store_sums(total, square, out_ref)
    for i in range(3):
        copies[i].wait()
        next_ref[pl.ds(i, 1), :] = vectors_ref[i]

    @pl.when(index == 0)
    def _():
        hidden_ref[0] = hidden_ref[1]

    @pl.when(index == count - 1)
    def _():
        hidden_ref[rows + 1] = hidden_ref[rows]


def second_kernel(
    count, sums_ref, hidden_ref, own_ref, weight_ref, params_ref,
    out_ref, wide_ref, taps_ref, summed_ref, done_ref, sems,
):
    rows, width, channels = own_ref.shape
    scale, offset = scale_offset(
        sums_ref, params_ref.at[1:2], params_ref.at[2:3], rows * width * count
    )
    sum_paired(weight_ref, summed_ref)
    copies = [
        pltpu.make_async_copy(done_ref.at[row], out_ref.at[row], sems.at[row])
        for row in range(rows)
    ]
    for row in range(2):
        store_taps(hidden_ref[row], scale, offset, wide_ref, taps_ref, row)
    for row in range(0, rows, 2):
        for i in range(2, 4):
            store_taps(hidden_ref[row + i], scale, offset, wide_ref, taps_ref, row + i)
        window = jnp.concatenate([taps_ref[row + tap] for tap in range(4)], axis=1)
        both = jnp.dot(window, summed_ref[...], preferred_element_type=jnp.float32)
        for i in range(2):
            branch = both[:, i * channels : (i + 1) * channels] + params_ref[0:1, :]
            values = own_ref[row + i].astype(jnp.float32) + branch
            done_ref[row + i] = values.astype(jnp.bfloat16)
            copies[row + i].start()
    for copy in copies:
        copy.wait()


def exchanged(sums):
    count = lax.axis_size("rows")
    ends_first = [i // 2 if i % 2 == 0 else count - 1 - i // 2 for i in range(count)]
    return lax.all_to_all(sums, "rows", 0, 0, axis_index_groups=[ends_first])


def body(
    latents, gain_one, shift_one, weight_one, bias_one, gain_two, shift_two, weight_two, bias_two
):
    count = lax.axis_size("rows")
    own = latents[0]
    rows, width, channels = own.shape
    sums_shape = jax.ShapeDtypeStruct((count, 2, channels), jnp.float32)
    taps = weight_one.shape[1] * weight_one.shape[2]
    slab_shape = jax.ShapeDtypeStruct((2, width, channels), jnp.bfloat16)

    def raw(weight):
        return weight.reshape(3, taps, channels, channels)

    swap_pair = [(i, i ^ 1) for i in range(count)]
    swap_other = [(i, i + 1 if i % 2 else i - 1) for i in range(1, count - 1)]

    sums, pair, other = pl.pallas_call(
        sums_kernel,
        out_shape=[sums_shape, slab_shape, slab_shape],
        in_specs=[VMEM],
        out_specs=[VMEM] * 3,
        compiler_params=PARAMS,
        name="sums",
        cost_estimate=pl.CostEstimate(
            flops=40000000000, bytes_accessed=10000000, transcendentals=0
        ),
    )(own)
    other = lax.ppermute(other, "rows", swap_other)
    pair = lax.ppermute(pair, "rows", swap_pair)
    sums = exchanged(sums)
    hidden, sums, params = pl.pallas_call(
        functools.partial(first_kernel, count),
        out_shape=[
            jax.ShapeDtypeStruct((rows + 2, width, channels), jnp.bfloat16),
            sums_shape,
            jax.ShapeDtypeStruct((8, channels), jnp.float32),
        ],
        in_specs=[VMEM] * 8 + [HBM] * 3,
        out_specs=[VMEM] * 3,
        scratch_shapes=[
            pltpu.VMEM((rows + 4, width + 16, channels), jnp.float32),
            pltpu.VMEM((rows + 4, width, 3 * channels), jnp.bfloat16),
            pltpu.VMEM((taps * channels, 2 * channels), jnp.bfloat16),
            pltpu.VMEM((3, 1, channels), jnp.float32),
            pltpu.SemaphoreType.DMA((3,)),
        ],
        compiler_params=PARAMS, name="first",
    )(
        sums,
        own,
        pair,
        other,
        raw(weight_one),
        *[vector.reshape(1, channels) for vector in (bias_one, gain_one, shift_one)],
        *[
            pltpu.with_memory_space_constraint(vector.reshape(1, channels), pltpu.HBM)
            for vector in (bias_two, gain_two, shift_two)
        ],
    )
    sums = exchanged(sums)
    decoded = pl.pallas_call(
        functools.partial(second_kernel, count),
        out_shape=jax.ShapeDtypeStruct(own.shape, jnp.bfloat16),
        in_specs=[VMEM] * 5,
        out_specs=ANY,
        scratch_shapes=[
            pltpu.VMEM((rows + 2, width + 16, channels), jnp.float32),
            pltpu.VMEM((rows + 2, width, 3 * channels), jnp.bfloat16),
            pltpu.VMEM((taps // 3 * 4 * channels, 2 * channels), jnp.bfloat16),
            pltpu.VMEM(own.shape, jnp.bfloat16),
            pltpu.SemaphoreType.DMA((rows,)),
        ],
        compiler_params=PARAMS, name="second",
    )(sums, hidden, own, raw(weight_two), params)
    return decoded[None]


def solution(mesh):
    return jax.shard_map(
        body,
        mesh=mesh,
        in_specs=(P("groups", "rows", None, None), P(), P(), P(), P(), P(), P(), P(), P()),
        out_specs=P("groups", "rows", None, None),
        check_vma=False,
    )
```

```python
import functools

import jax
import jax.numpy as jnp
from jax import lax
from jax.experimental import pallas as pl
from jax.experimental.pallas import tpu as pltpu
from jax.sharding import PartitionSpec as P

GROUPS = 32
HBM = pl.BlockSpec(memory_space=pltpu.HBM)
ANY = pl.BlockSpec(memory_space=pl.ANY)
VMEM = pl.BlockSpec(memory_space=pltpu.VMEM)
PARAMS = pltpu.CompilerParams(vmem_limit_bytes=24 * 1024 * 1024)


def store_sums(total, square, out_ref):
    total = jnp.sum(total, axis=0, keepdims=True)
    square = jnp.sum(square, axis=0, keepdims=True)
    both = jnp.concatenate([total, square], axis=0)
    out_ref[...] = jnp.broadcast_to(both[None], out_ref.shape)


def add_sums(values, total, square):
    width, channels = values.shape
    split = (width // 8, 8, channels)
    total += jnp.sum(values.reshape(split), axis=0)
    square += jnp.sum((values * values).reshape(split), axis=0)
    return total, square


def sums_kernel(own_ref, out_ref, pair_ref, other_ref):
    rows, _, channels = own_ref.shape
    even = lax.axis_index("rows") % 2 == 0
    for row in range(2):
        top = own_ref[row]
        bottom = own_ref[rows - 2 + row]
        pair_ref[row] = jnp.where(even, bottom, top)
        other_ref[row] = jnp.where(even, top, bottom)
    total = jnp.zeros((8, channels), jnp.float32)
    square = jnp.zeros((8, channels), jnp.float32)
    for row in range(rows):
        total, square = add_sums(own_ref[row].astype(jnp.float32), total, square)
    store_sums(total, square, out_ref)


def sum_weight(source, target):
    taps, channels = source.shape[1], source.shape[2]
    for tap in range(taps):
        total = source[0, tap].astype(jnp.float32)
        total += source[1, tap].astype(jnp.float32)
        total += source[2, tap].astype(jnp.float32)
        high = total.astype(jnp.bfloat16)
        low = (total - high.astype(jnp.float32)).astype(jnp.bfloat16)
        target[pl.ds(tap * channels, channels), :] = jnp.concatenate([high, low], axis=1)


def sum_paired(source, target):
    taps, channels = source.shape[1], source.shape[2]
    columns = taps // 3
    zeros = jnp.zeros((columns * channels, channels), jnp.bfloat16)
    for tap in range(taps):
        total = source[0, tap].astype(jnp.float32)
        total += source[1, tap].astype(jnp.float32)
        total += source[2, tap].astype(jnp.float32)
        total = total.astype(jnp.bfloat16)
        target[pl.ds(tap * channels, channels), 0:channels] = total
        target[pl.ds((tap + columns) * channels, channels), channels : 2 * channels] = total
    target[pl.ds(taps * channels, columns * channels), 0:channels] = zeros
    target[pl.ds(0, columns * channels), channels : 2 * channels] = zeros


def scale_offset(sums_ref, gain_ref, shift_ref, entries):
    sums = jnp.sum(sums_ref[...], axis=0)
    channels = sums.shape[1]
    per_group = channels // GROUPS
    sums = jnp.concatenate([sums, jnp.zeros((6, channels), jnp.float32)], axis=0)
    member = lax.broadcasted_iota(jnp.int32, sums.shape, 1) % per_group
    total = sums
    for step in range(1, per_group):
        total += jnp.where(member >= step, pltpu.roll(sums, step, 1), 0.0)
        total += jnp.where(member < per_group - step, pltpu.roll(sums, channels - step, 1), 0.0)
    total = total * (1.0 / (entries * per_group))
    mean = total[0:1]
    var = total[1:2] - mean * mean
    scale = gain_ref[...] * lax.rsqrt(var + 1e-06)
    return 0.5 * scale, 0.5 * (shift_ref[...] - mean * scale)


def store_taps(values, scale, offset, wide_ref, taps_ref, row):
    width, channels = values.shape
    half = values.astype(jnp.float32) * scale + offset
    act = half * jnp.tanh(half) + half
    wide_ref[row, 8 : 8 + width, :] = act
    wide_ref[row, 7:8, :] = act[0:1]
    wide_ref[row, 8 + width : 9 + width, :] = act[width - 1 : width]
    for tap in range(3):
        shifted = wide_ref[row, 7 + tap : 7 + tap + width, :]
        taps_ref[row, :, tap * channels : (tap + 1) * channels] = shifted.astype(jnp.bfloat16)


def window(taps_ref, row, count):
    _, width, lanes = taps_ref.shape
    parts = [
        taps_ref[row + tap : row + tap + count].reshape(count * width, lanes) for tap in range(3)
    ]
    return jnp.concatenate(parts, axis=1)


def product(rows, weight_ref):
    both = jnp.dot(rows, weight_ref[...], preferred_element_type=jnp.float32)
    half = both.shape[1] // 2
    return both[:, :half] + both[:, half:]


def first_kernel(
    count, sums_ref, own_ref, pair_ref, other_ref, weight_ref, bias_ref, gain_ref, shift_ref,
    bias_two_ref, gain_two_ref, shift_two_ref,
    hidden_ref, out_ref, next_ref, wide_ref, taps_ref, summed_ref, vectors_ref, sems,
):
    copies = [
        pltpu.make_async_copy(source, vectors_ref.at[i], sems.at[i])
        for i, source in enumerate((bias_two_ref, gain_two_ref, shift_two_ref))
    ]
    for copy in copies:
        copy.start()
    index = lax.axis_index("rows")
    rows, width, channels = own_ref.shape
    even = index % 2 == 0
    scale, offset = scale_offset(sums_ref, gain_ref, shift_ref, rows * width * count)
    sum_weight(weight_ref, summed_ref)

    def make(row):
        if row < 2:
            values = jnp.where(even, other_ref[row], pair_ref[row])
            values = jnp.where(index == 0, own_ref[0], values)
        elif row < rows + 2:
            values = own_ref[row - 2]
        else:
            values = jnp.where(even, pair_ref[row - rows - 2], other_ref[row - rows - 2])
            values = jnp.where(index == count - 1, own_ref[rows - 1], values)
        store_taps(values, scale, offset, wide_ref, taps_ref, row)

    total = jnp.zeros((8, channels), jnp.float32)
    square = jnp.zeros((8, channels), jnp.float32)
    for row in range(1, rows + 3):
        make(row)
    hidden = product(window(taps_ref, 1, rows), summed_ref) + bias_ref[...]
    hidden = hidden.astype(jnp.bfloat16)
    for row in range(rows):
        values = hidden[row * width : (row + 1) * width]
        hidden_ref[row + 1] = values
        total, square = add_sums(values.astype(jnp.float32), total, square)
    make(0)
    make(rows + 3)
    halo = jnp.concatenate([window(taps_ref, 0, 1), window(taps_ref, rows + 1, 1)], axis=0)
    halo = (product(halo, summed_ref) + bias_ref[...]).astype(jnp.bfloat16)
    hidden_ref[0] = halo[:width]
    hidden_ref[rows + 1] = halo[width:]
    store_sums(total, square, out_ref)
    for i in range(3):
        copies[i].wait()
        next_ref[pl.ds(i, 1), :] = vectors_ref[i]

    @pl.when(index == 0)
    def _():
        hidden_ref[0] = hidden_ref[1]

    @pl.when(index == count - 1)
    def _():
        hidden_ref[rows + 1] = hidden_ref[rows]


def second_kernel(
    count, sums_ref, hidden_ref, own_ref, weight_ref, params_ref,
    out_ref, wide_ref, taps_ref, summed_ref, done_ref, sems,
):
    rows, width, channels = own_ref.shape
    scale, offset = scale_offset(
        sums_ref, params_ref.at[1:2], params_ref.at[2:3], rows * width * count
    )
    sum_paired(weight_ref, summed_ref)
    copies = [
        pltpu.make_async_copy(done_ref.at[row], out_ref.at[row], sems.at[row])
        for row in range(rows)
    ]
    for row in range(2):
        store_taps(hidden_ref[row], scale, offset, wide_ref, taps_ref, row)
    for row in range(0, rows, 2):
        for i in range(2, 4):
            store_taps(hidden_ref[row + i], scale, offset, wide_ref, taps_ref, row + i)
        window = jnp.concatenate([taps_ref[row + tap] for tap in range(4)], axis=1)
        both = jnp.dot(window, summed_ref[...], preferred_element_type=jnp.float32)
        for i in range(2):
            branch = both[:, i * channels : (i + 1) * channels] + params_ref[0:1, :]
            values = own_ref[row + i].astype(jnp.float32) + branch
            done_ref[row + i] = values.astype(jnp.bfloat16)
            copies[row + i].start()
    for copy in copies:
        copy.wait()


def exchanged(sums):
    count = lax.axis_size("rows")
    ends_first = [i // 2 if i % 2 == 0 else count - 1 - i // 2 for i in range(count)]
    return lax.all_to_all(sums, "rows", 0, 0, axis_index_groups=[ends_first])


def body(
    latents, gain_one, shift_one, weight_one, bias_one, gain_two, shift_two, weight_two, bias_two
):
    count = lax.axis_size("rows")
    own = latents[0]
    rows, width, channels = own.shape
    sums_shape = jax.ShapeDtypeStruct((count, 2, channels), jnp.float32)
    taps = weight_one.shape[1] * weight_one.shape[2]
    slab_shape = jax.ShapeDtypeStruct((2, width, channels), jnp.bfloat16)

    def raw(weight):
        return weight.reshape(3, taps, channels, channels)

    swap_pair = [(i, i ^ 1) for i in range(count)]
    swap_other = [(i, i + 1 if i % 2 else i - 1) for i in range(1, count - 1)]

    sums, pair, other = pl.pallas_call(
        sums_kernel,
        out_shape=[sums_shape, slab_shape, slab_shape],
        in_specs=[VMEM],
        out_specs=[VMEM] * 3,
        compiler_params=PARAMS,
        name="sums",
        cost_estimate=pl.CostEstimate(
            flops=40000000000, bytes_accessed=10000000, transcendentals=0
        ),
    )(own)
    other = lax.ppermute(other, "rows", swap_other)
    pair = lax.ppermute(pair, "rows", swap_pair)
    sums = exchanged(sums)
    hidden, sums, params = pl.pallas_call(
        functools.partial(first_kernel, count),
        out_shape=[
            jax.ShapeDtypeStruct((rows + 2, width, channels), jnp.bfloat16),
            sums_shape,
            jax.ShapeDtypeStruct((8, channels), jnp.float32),
        ],
        in_specs=[VMEM] * 8 + [HBM] * 3,
        out_specs=[VMEM] * 3,
        scratch_shapes=[
            pltpu.VMEM((rows + 4, width + 16, channels), jnp.float32),
            pltpu.VMEM((rows + 4, width, 3 * channels), jnp.bfloat16),
            pltpu.VMEM((taps * channels, 2 * channels), jnp.bfloat16),
            pltpu.VMEM((3, 1, channels), jnp.float32),
            pltpu.SemaphoreType.DMA((3,)),
        ],
        compiler_params=PARAMS, name="first",
    )(
        sums,
        own,
        pair,
        other,
        raw(weight_one),
        *[vector.reshape(1, channels) for vector in (bias_one, gain_one, shift_one)],
        *[
            pltpu.with_memory_space_constraint(vector.reshape(1, channels), pltpu.HBM)
            for vector in (bias_two, gain_two, shift_two)
        ],
    )
    sums = exchanged(sums)
    decoded = pl.pallas_call(
        functools.partial(second_kernel, count),
        out_shape=jax.ShapeDtypeStruct(own.shape, jnp.bfloat16),
        in_specs=[VMEM] * 5,
        out_specs=ANY,
        scratch_shapes=[
            pltpu.VMEM((rows + 2, width + 16, channels), jnp.float32),
            pltpu.VMEM((rows + 2, width, 3 * channels), jnp.bfloat16),
            pltpu.VMEM((taps // 3 * 4 * channels, 2 * channels), jnp.bfloat16),
            pltpu.VMEM(own.shape, jnp.bfloat16),
            pltpu.SemaphoreType.DMA((rows,)),
        ],
        compiler_params=PARAMS, name="second",
    )(sums, hidden, own, raw(weight_two), params)
    return decoded[None]


def solution(mesh):
    return jax.shard_map(
        body,
        mesh=mesh,
        in_specs=(P("groups", "rows", None, None), P(), P(), P(), P(), P(), P(), P(), P()),
        out_specs=P("groups", "rows", None, None),
        check_vma=False,
    )
```

```python
import functools

import jax
import jax.numpy as jnp
from jax import lax
from jax.experimental import pallas as pl
from jax.experimental.pallas import tpu as pltpu
from jax.sharding import PartitionSpec as P

GROUPS = 32
HBM = pl.BlockSpec(memory_space=pltpu.HBM)
ANY = pl.BlockSpec(memory_space=pl.ANY)
VMEM = pl.BlockSpec(memory_space=pltpu.VMEM)
PARAMS = pltpu.CompilerParams(vmem_limit_bytes=24 * 1024 * 1024)


def store_sums(total, square, out_ref):
    total = jnp.sum(total, axis=0, keepdims=True)
    square = jnp.sum(square, axis=0, keepdims=True)
    both = jnp.concatenate([total, square], axis=0)
    out_ref[...] = jnp.broadcast_to(both[None], out_ref.shape)


def add_sums(values, total, square):
    width, channels = values.shape
    split = (width // 8, 8, channels)
    total += jnp.sum(values.reshape(split), axis=0)
    square += jnp.sum((values * values).reshape(split), axis=0)
    return total, square


def sums_kernel(own_ref, out_ref, pair_ref, other_ref):
    rows, _, channels = own_ref.shape
    even = lax.axis_index("rows") % 2 == 0
    for row in range(2):
        top = own_ref[row]
        bottom = own_ref[rows - 2 + row]
        pair_ref[row] = jnp.where(even, bottom, top)
        other_ref[row] = jnp.where(even, top, bottom)
    total = jnp.zeros((8, channels), jnp.float32)
    square = jnp.zeros((8, channels), jnp.float32)
    for row in range(rows):
        total, square = add_sums(own_ref[row].astype(jnp.float32), total, square)
    store_sums(total, square, out_ref)


def sum_weight(source, target):
    taps, channels = source.shape[1], source.shape[2]
    for tap in range(taps):
        total = source[0, tap].astype(jnp.float32)
        total += source[1, tap].astype(jnp.float32)
        total += source[2, tap].astype(jnp.float32)
        high = total.astype(jnp.bfloat16)
        low = (total - high.astype(jnp.float32)).astype(jnp.bfloat16)
        target[pl.ds(tap * channels, channels), :] = jnp.concatenate([high, low], axis=1)


def sum_paired(source, target):
    taps, channels = source.shape[1], source.shape[2]
    columns = taps // 3
    zeros = jnp.zeros((columns * channels, channels), jnp.bfloat16)
    for tap in range(taps):
        total = source[0, tap].astype(jnp.float32)
        total += source[1, tap].astype(jnp.float32)
        total += source[2, tap].astype(jnp.float32)
        total = total.astype(jnp.bfloat16)
        target[pl.ds(tap * channels, channels), 0:channels] = total
        target[pl.ds((tap + columns) * channels, channels), channels : 2 * channels] = total
    target[pl.ds(taps * channels, columns * channels), 0:channels] = zeros
    target[pl.ds(0, columns * channels), channels : 2 * channels] = zeros


def scale_offset(sums_ref, gain_ref, shift_ref, entries):
    sums = jnp.sum(sums_ref[...], axis=0)
    channels = sums.shape[1]
    per_group = channels // GROUPS
    sums = jnp.concatenate([sums, jnp.zeros((6, channels), jnp.float32)], axis=0)
    member = lax.broadcasted_iota(jnp.int32, sums.shape, 1) % per_group
    total = sums
    for step in range(1, per_group):
        total += jnp.where(member >= step, pltpu.roll(sums, step, 1), 0.0)
        total += jnp.where(member < per_group - step, pltpu.roll(sums, channels - step, 1), 0.0)
    total = total * (1.0 / (entries * per_group))
    mean = total[0:1]
    var = jnp.maximum(total[1:2] - mean * mean, 0.0)
    scale = gain_ref[...] * lax.rsqrt(var + 1e-06)
    return 0.5 * scale, 0.5 * (shift_ref[...] - mean * scale)


def store_taps(values, scale, offset, wide_ref, taps_ref, row):
    width, channels = values.shape
    half = values.astype(jnp.float32) * scale + offset
    act = half * jnp.tanh(half) + half
    wide_ref[row, 8 : 8 + width, :] = act
    wide_ref[row, 7:8, :] = act[0:1]
    wide_ref[row, 8 + width : 9 + width, :] = act[width - 1 : width]
    for tap in range(3):
        shifted = wide_ref[row, 7 + tap : 7 + tap + width, :]
        taps_ref[row, :, tap * channels : (tap + 1) * channels] = shifted.astype(jnp.bfloat16)


def conv_rows(taps_ref, row, count, weight_ref):
    _, width, lanes = taps_ref.shape
    window = jnp.concatenate(
        [taps_ref[row + tap : row + tap + count].reshape(count * width, lanes) for tap in range(3)],
        axis=1,
    )
    both = jnp.dot(window, weight_ref[...], preferred_element_type=jnp.float32)
    half = both.shape[1] // 2
    return both[:, :half] + both[:, half:]


def first_kernel(
    count, sums_ref, own_ref, pair_ref, other_ref, weight_ref, bias_ref, gain_ref, shift_ref,
    bias_two_ref, gain_two_ref, shift_two_ref,
    hidden_ref, out_ref, next_ref, wide_ref, taps_ref, summed_ref, vectors_ref, sems,
):
    copies = [
        pltpu.make_async_copy(source, vectors_ref.at[i], sems.at[i])
        for i, source in enumerate((bias_two_ref, gain_two_ref, shift_two_ref))
    ]
    for copy in copies:
        copy.start()
    index = lax.axis_index("rows")
    rows, width, channels = own_ref.shape
    even = index % 2 == 0
    scale, offset = scale_offset(sums_ref, gain_ref, shift_ref, rows * width * count)
    sum_weight(weight_ref, summed_ref)

    def make(row):
        if row < 2:
            values = jnp.where(even, other_ref[row], pair_ref[row])
            values = jnp.where(index == 0, own_ref[0], values)
        elif row < rows + 2:
            values = own_ref[row - 2]
        else:
            values = jnp.where(even, pair_ref[row - rows - 2], other_ref[row - rows - 2])
            values = jnp.where(index == count - 1, own_ref[rows - 1], values)
        store_taps(values, scale, offset, wide_ref, taps_ref, row)

    total = jnp.zeros((8, channels), jnp.float32)
    square = jnp.zeros((8, channels), jnp.float32)
    for row in range(rows + 4):
        make(row)
    hidden = conv_rows(taps_ref, 0, rows + 2, summed_ref) + bias_ref[...]
    hidden = hidden.astype(jnp.bfloat16)
    for row in range(rows + 2):
        values = hidden[row * width : (row + 1) * width]
        hidden_ref[row] = values
        if 0 < row <= rows:
            total, square = add_sums(values.astype(jnp.float32), total, square)
    store_sums(total, square, out_ref)
    for i in range(3):
        copies[i].wait()
        next_ref[pl.ds(i, 1), :] = vectors_ref[i]

    @pl.when(index == 0)
    def _():
        hidden_ref[0] = hidden_ref[1]

    @pl.when(index == count - 1)
    def _():
        hidden_ref[rows + 1] = hidden_ref[rows]


def second_kernel(
    count, sums_ref, hidden_ref, own_ref, weight_ref, params_ref,
    out_ref, wide_ref, taps_ref, summed_ref, done_ref, sems,
):
    rows, width, channels = own_ref.shape
    scale, offset = scale_offset(
        sums_ref, params_ref.at[1:2], params_ref.at[2:3], rows * width * count
    )
    sum_paired(weight_ref, summed_ref)
    copies = []
    for row in range(2):
        store_taps(hidden_ref[row], scale, offset, wide_ref, taps_ref, row)
    for row in range(0, rows, 2):
        for i in range(2, 4):
            store_taps(hidden_ref[row + i], scale, offset, wide_ref, taps_ref, row + i)
        parts = 2 if row == rows - 2 else 1
        for part in range(parts):
            size = width // parts
            columns = pl.ds(part * size, size)
            window = jnp.concatenate(
                [taps_ref[row + tap, columns, :] for tap in range(4)], axis=1
            )
            both = jnp.dot(window, summed_ref[...], preferred_element_type=jnp.float32)
            for i in range(2):
                branch = both[:, i * channels : (i + 1) * channels] + params_ref[0:1, :]
                values = own_ref[row + i, columns, :].astype(jnp.float32) + branch
                done_ref[row + i, columns, :] = values.astype(jnp.bfloat16)
                copies.append(
                    pltpu.make_async_copy(
                        done_ref.at[row + i, columns],
                        out_ref.at[row + i, columns],
                        sems.at[len(copies)],
                    )
                )
                copies[-1].start()
    for copy in copies:
        copy.wait()


def exchanged(sums):
    count = lax.axis_size("rows")
    ends_first = [i // 2 if i % 2 == 0 else count - 1 - i // 2 for i in range(count)]
    return lax.all_to_all(sums, "rows", 0, 0, axis_index_groups=[ends_first])


def body(
    latents, gain_one, shift_one, weight_one, bias_one, gain_two, shift_two, weight_two, bias_two
):
    count = lax.axis_size("rows")
    own = latents[0]
    rows, width, channels = own.shape
    sums_shape = jax.ShapeDtypeStruct((count, 2, channels), jnp.float32)
    taps = weight_one.shape[1] * weight_one.shape[2]
    slab_shape = jax.ShapeDtypeStruct((2, width, channels), jnp.bfloat16)

    def raw(weight):
        return weight.reshape(3, taps, channels, channels)

    swap_pair = [(i, i ^ 1) for i in range(count)]
    swap_other = [(i, i + 1 if i % 2 else i - 1) for i in range(1, count - 1)]

    sums, pair, other = pl.pallas_call(
        sums_kernel,
        out_shape=[sums_shape, slab_shape, slab_shape],
        in_specs=[VMEM],
        out_specs=[VMEM] * 3,
        compiler_params=PARAMS,
        name="sums",
        cost_estimate=pl.CostEstimate(
            flops=40000000000, bytes_accessed=10000000, transcendentals=0
        ),
    )(own)
    other = lax.ppermute(other, "rows", swap_other)
    pair = lax.ppermute(pair, "rows", swap_pair)
    sums = exchanged(sums)
    hidden, sums, params = pl.pallas_call(
        functools.partial(first_kernel, count),
        out_shape=[
            jax.ShapeDtypeStruct((rows + 2, width, channels), jnp.bfloat16),
            sums_shape,
            jax.ShapeDtypeStruct((8, channels), jnp.float32),
        ],
        in_specs=[VMEM] * 8 + [HBM] * 3,
        out_specs=[VMEM] * 3,
        scratch_shapes=[
            pltpu.VMEM((rows + 4, width + 16, channels), jnp.float32),
            pltpu.VMEM((rows + 4, width, 3 * channels), jnp.bfloat16),
            pltpu.VMEM((taps * channels, 2 * channels), jnp.bfloat16),
            pltpu.VMEM((3, 1, channels), jnp.float32),
            pltpu.SemaphoreType.DMA((3,)),
        ],
        compiler_params=PARAMS, name="first",
    )(
        sums,
        own,
        pair,
        other,
        raw(weight_one),
        *[vector.reshape(1, channels) for vector in (bias_one, gain_one, shift_one)],
        *[
            pltpu.with_memory_space_constraint(vector.reshape(1, channels), pltpu.HBM)
            for vector in (bias_two, gain_two, shift_two)
        ],
    )
    sums = exchanged(sums)
    decoded = pl.pallas_call(
        functools.partial(second_kernel, count),
        out_shape=jax.ShapeDtypeStruct(own.shape, jnp.bfloat16),
        in_specs=[VMEM] * 5,
        out_specs=ANY,
        scratch_shapes=[
            pltpu.VMEM((rows + 2, width + 16, channels), jnp.float32),
            pltpu.VMEM((rows + 2, width, 3 * channels), jnp.bfloat16),
            pltpu.VMEM((taps // 3 * 4 * channels, 2 * channels), jnp.bfloat16),
            pltpu.VMEM(own.shape, jnp.bfloat16),
            pltpu.SemaphoreType.DMA((rows + 2,)),
        ],
        compiler_params=PARAMS, name="second",
    )(sums, hidden, own, raw(weight_two), params)
    return decoded[None]


def solution(mesh):
    return jax.shard_map(
        body,
        mesh=mesh,
        in_specs=(P("groups", "rows", None, None), P(), P(), P(), P(), P(), P(), P(), P()),
        out_specs=P("groups", "rows", None, None),
        check_vma=False,
    )
```

```python
import functools

import jax
import jax.numpy as jnp
from jax import lax
from jax.experimental import pallas as pl
from jax.experimental.pallas import tpu as pltpu
from jax.sharding import PartitionSpec as P

GROUPS = 32
HBM = pl.BlockSpec(memory_space=pltpu.HBM)
ANY = pl.BlockSpec(memory_space=pl.ANY)
VMEM = pl.BlockSpec(memory_space=pltpu.VMEM)
PARAMS = pltpu.CompilerParams(vmem_limit_bytes=24 * 1024 * 1024)


def store_sums(total, square, out_ref):
    total = jnp.sum(total, axis=0, keepdims=True)
    square = jnp.sum(square, axis=0, keepdims=True)
    both = jnp.concatenate([total, square], axis=0)
    out_ref[...] = jnp.broadcast_to(both[None], out_ref.shape)


def add_sums(values, total, square):
    width, channels = values.shape
    split = (width // 8, 8, channels)
    total += jnp.sum(values.reshape(split), axis=0)
    square += jnp.sum((values * values).reshape(split), axis=0)
    return total, square


def sums_kernel(own_ref, out_ref, pair_ref, other_ref):
    rows, _, channels = own_ref.shape
    even = lax.axis_index("rows") % 2 == 0
    for row in range(2):
        top = own_ref[row]
        bottom = own_ref[rows - 2 + row]
        pair_ref[row] = jnp.where(even, bottom, top)
        other_ref[row] = jnp.where(even, top, bottom)
    total = jnp.zeros((8, channels), jnp.float32)
    square = jnp.zeros((8, channels), jnp.float32)
    for row in range(rows):
        total, square = add_sums(own_ref[row].astype(jnp.float32), total, square)
    store_sums(total, square, out_ref)


def sum_weight(source, target):
    taps, channels = source.shape[1], source.shape[2]
    for tap in range(taps):
        total = source[0, tap].astype(jnp.float32)
        total += source[1, tap].astype(jnp.float32)
        total += source[2, tap].astype(jnp.float32)
        high = total.astype(jnp.bfloat16)
        low = (total - high.astype(jnp.float32)).astype(jnp.bfloat16)
        target[pl.ds(tap * channels, channels), :] = jnp.concatenate([high, low], axis=1)


def sum_paired(source, target):
    taps, channels = source.shape[1], source.shape[2]
    columns = taps // 3
    zeros = jnp.zeros((columns * channels, channels), jnp.bfloat16)
    for tap in range(taps):
        total = source[0, tap].astype(jnp.float32)
        total += source[1, tap].astype(jnp.float32)
        total += source[2, tap].astype(jnp.float32)
        total = total.astype(jnp.bfloat16)
        target[pl.ds(tap * channels, channels), 0:channels] = total
        target[pl.ds((tap + columns) * channels, channels), channels : 2 * channels] = total
    target[pl.ds(taps * channels, columns * channels), 0:channels] = zeros
    target[pl.ds(0, columns * channels), channels : 2 * channels] = zeros


def scale_offset(sums_ref, gain_ref, shift_ref, entries):
    sums = jnp.sum(sums_ref[...], axis=0)
    channels = sums.shape[1]
    per_group = channels // GROUPS
    sums = jnp.concatenate([sums, jnp.zeros((6, channels), jnp.float32)], axis=0)
    member = lax.broadcasted_iota(jnp.int32, sums.shape, 1) % per_group
    total = sums
    for step in range(1, per_group):
        total += jnp.where(member >= step, pltpu.roll(sums, step, 1), 0.0)
        total += jnp.where(member < per_group - step, pltpu.roll(sums, channels - step, 1), 0.0)
    total = total * (1.0 / (entries * per_group))
    mean = total[0:1]
    var = jnp.maximum(total[1:2] - mean * mean, 0.0)
    scale = gain_ref[...] * lax.rsqrt(var + 1e-06)
    return 0.5 * scale, 0.5 * (shift_ref[...] - mean * scale)


def store_taps(values, scale, offset, wide_ref, taps_ref, row):
    width, channels = values.shape
    half = values.astype(jnp.float32) * scale + offset
    act = half * jnp.tanh(half) + half
    wide_ref[row, 8 : 8 + width, :] = act
    wide_ref[row, 7:8, :] = act[0:1]
    wide_ref[row, 8 + width : 9 + width, :] = act[width - 1 : width]
    for tap in range(3):
        shifted = wide_ref[row, 7 + tap : 7 + tap + width, :]
        taps_ref[row, :, tap * channels : (tap + 1) * channels] = shifted.astype(jnp.bfloat16)


def conv_rows(taps_ref, row, count, weight_ref):
    _, width, lanes = taps_ref.shape
    window = jnp.concatenate(
        [taps_ref[row + tap : row + tap + count].reshape(count * width, lanes) for tap in range(3)],
        axis=1,
    )
    both = jnp.dot(window, weight_ref[...], preferred_element_type=jnp.float32)
    half = both.shape[1] // 2
    return both[:, :half] + both[:, half:]


def first_kernel(
    count, sums_ref, own_ref, pair_ref, other_ref, weight_ref, bias_ref, gain_ref, shift_ref,
    bias_two_ref, gain_two_ref, shift_two_ref,
    hidden_ref, out_ref, next_ref, wide_ref, taps_ref, summed_ref, vectors_ref, sems,
):
    copies = [
        pltpu.make_async_copy(source, vectors_ref.at[i], sems.at[i])
        for i, source in enumerate((bias_two_ref, gain_two_ref, shift_two_ref))
    ]
    for copy in copies:
        copy.start()
    index = lax.axis_index("rows")
    rows, width, channels = own_ref.shape
    even = index % 2 == 0
    scale, offset = scale_offset(sums_ref, gain_ref, shift_ref, rows * width * count)
    sum_weight(weight_ref, summed_ref)

    def make(row):
        if row < 2:
            values = jnp.where(even, other_ref[row], pair_ref[row])
            values = jnp.where(index == 0, own_ref[0], values)
        elif row < rows + 2:
            values = own_ref[row - 2]
        else:
            values = jnp.where(even, pair_ref[row - rows - 2], other_ref[row - rows - 2])
            values = jnp.where(index == count - 1, own_ref[rows - 1], values)
        store_taps(values, scale, offset, wide_ref, taps_ref, row)

    total = jnp.zeros((8, channels), jnp.float32)
    square = jnp.zeros((8, channels), jnp.float32)
    for row in range(rows + 4):
        make(row)
    hidden = conv_rows(taps_ref, 0, rows + 2, summed_ref) + bias_ref[...]
    hidden = hidden.astype(jnp.bfloat16)
    for row in range(rows + 2):
        values = hidden[row * width : (row + 1) * width]
        hidden_ref[row] = values
        if 0 < row <= rows:
            total, square = add_sums(values.astype(jnp.float32), total, square)
    store_sums(total, square, out_ref)
    for i in range(3):
        copies[i].wait()
        next_ref[pl.ds(i, 1), :] = vectors_ref[i]

    @pl.when(index == 0)
    def _():
        hidden_ref[0] = hidden_ref[1]

    @pl.when(index == count - 1)
    def _():
        hidden_ref[rows + 1] = hidden_ref[rows]


def second_kernel(
    count, sums_ref, hidden_ref, own_ref, weight_ref, params_ref,
    out_ref, wide_ref, taps_ref, summed_ref, done_ref, sems,
):
    rows, width, channels = own_ref.shape
    scale, offset = scale_offset(
        sums_ref, params_ref.at[1:2], params_ref.at[2:3], rows * width * count
    )
    sum_paired(weight_ref, summed_ref)
    copies = []
    for row in range(2):
        store_taps(hidden_ref[row], scale, offset, wide_ref, taps_ref, row)
    for row in range(0, rows, 2):
        for i in range(2, 4):
            store_taps(hidden_ref[row + i], scale, offset, wide_ref, taps_ref, row + i)
        parts = 2 if row == rows - 2 else 1
        for part in range(parts):
            size = width // parts
            columns = pl.ds(part * size, size)
            window = jnp.concatenate(
                [taps_ref[row + tap, columns, :] for tap in range(4)], axis=1
            )
            both = jnp.dot(window, summed_ref[...], preferred_element_type=jnp.float32)
            for i in range(2):
                branch = both[:, i * channels : (i + 1) * channels] + params_ref[0:1, :]
                values = own_ref[row + i, columns, :].astype(jnp.float32) + branch
                done_ref[row + i, columns, :] = values.astype(jnp.bfloat16)
                copies.append(
                    pltpu.make_async_copy(
                        done_ref.at[row + i, columns],
                        out_ref.at[row + i, columns],
                        sems.at[len(copies)],
                    )
                )
                copies[-1].start()
    for copy in copies:
        copy.wait()


def exchanged(sums):
    count = lax.axis_size("rows")
    ends_first = [i // 2 if i % 2 == 0 else count - 1 - i // 2 for i in range(count)]
    return lax.all_to_all(sums, "rows", 0, 0, axis_index_groups=[ends_first])


def body(
    latents, gain_one, shift_one, weight_one, bias_one, gain_two, shift_two, weight_two, bias_two
):
    count = lax.axis_size("rows")
    own = latents[0]
    rows, width, channels = own.shape
    sums_shape = jax.ShapeDtypeStruct((count, 2, channels), jnp.float32)
    taps = weight_one.shape[1] * weight_one.shape[2]
    slab_shape = jax.ShapeDtypeStruct((2, width, channels), jnp.bfloat16)

    def raw(weight):
        return weight.reshape(3, taps, channels, channels)

    swap_pair = [(i, i ^ 1) for i in range(count)]
    swap_other = [(i, i + 1 if i % 2 else i - 1) for i in range(1, count - 1)]

    sums, pair, other = pl.pallas_call(
        sums_kernel,
        out_shape=[jax.ShapeDtypeStruct((1, 2, channels), jnp.float32), slab_shape, slab_shape],
        in_specs=[VMEM],
        out_specs=[VMEM] * 3,
        compiler_params=PARAMS,
        name="sums",
        cost_estimate=pl.CostEstimate(
            flops=40000000000, bytes_accessed=10000000, transcendentals=0
        ),
    )(own)
    partner = lax.ppermute(sums, "rows", swap_pair)
    pair = lax.ppermute(pair, "rows", swap_pair)
    other = lax.ppermute(other, "rows", swap_other)
    by_core = [list(range(core, count, 2)) for core in range(2)]
    sums = jnp.broadcast_to(sums + partner, (count // 2, 2, channels))
    sums = lax.all_to_all(sums, "rows", 0, 0, axis_index_groups=by_core)
    hidden, sums, params = pl.pallas_call(
        functools.partial(first_kernel, count),
        out_shape=[
            jax.ShapeDtypeStruct((rows + 2, width, channels), jnp.bfloat16),
            sums_shape,
            jax.ShapeDtypeStruct((8, channels), jnp.float32),
        ],
        in_specs=[VMEM] * 8 + [HBM] * 3,
        out_specs=[VMEM] * 3,
        scratch_shapes=[
            pltpu.VMEM((rows + 4, width + 16, channels), jnp.float32),
            pltpu.VMEM((rows + 4, width, 3 * channels), jnp.bfloat16),
            pltpu.VMEM((taps * channels, 2 * channels), jnp.bfloat16),
            pltpu.VMEM((3, 1, channels), jnp.float32),
            pltpu.SemaphoreType.DMA((3,)),
        ],
        compiler_params=PARAMS, name="first",
    )(
        sums,
        own,
        pair,
        other,
        raw(weight_one),
        *[vector.reshape(1, channels) for vector in (bias_one, gain_one, shift_one)],
        *[
            pltpu.with_memory_space_constraint(vector.reshape(1, channels), pltpu.HBM)
            for vector in (bias_two, gain_two, shift_two)
        ],
    )
    sums = exchanged(sums)
    decoded = pl.pallas_call(
        functools.partial(second_kernel, count),
        out_shape=jax.ShapeDtypeStruct(own.shape, jnp.bfloat16),
        in_specs=[VMEM] * 5,
        out_specs=ANY,
        scratch_shapes=[
            pltpu.VMEM((rows + 2, width + 16, channels), jnp.float32),
            pltpu.VMEM((rows + 2, width, 3 * channels), jnp.bfloat16),
            pltpu.VMEM((taps // 3 * 4 * channels, 2 * channels), jnp.bfloat16),
            pltpu.VMEM(own.shape, jnp.bfloat16),
            pltpu.SemaphoreType.DMA((rows + 2,)),
        ],
        compiler_params=PARAMS, name="second",
    )(sums, hidden, own, raw(weight_two), params)
    return decoded[None]


def solution(mesh):
    return jax.shard_map(
        body,
        mesh=mesh,
        in_specs=(P("groups", "rows", None, None), P(), P(), P(), P(), P(), P(), P(), P()),
        out_specs=P("groups", "rows", None, None),
        check_vma=False,
    )
```

```python
import functools

import jax
import jax.numpy as jnp
from jax import lax
from jax.experimental import pallas as pl
from jax.experimental.pallas import tpu as pltpu
from jax.sharding import PartitionSpec as P

GROUPS = 32
HBM = pl.BlockSpec(memory_space=pltpu.HBM)
ANY = pl.BlockSpec(memory_space=pl.ANY)
VMEM = pl.BlockSpec(memory_space=pltpu.VMEM)
PARAMS = pltpu.CompilerParams(vmem_limit_bytes=24 * 1024 * 1024)


def store_sums(total, square, out_ref):
    channels = total.shape[1]
    per_group = channels // GROUPS
    member = lax.broadcasted_iota(jnp.int32, (8, channels), 1) % per_group

    def grouped(part):
        part = jnp.broadcast_to(jnp.sum(part, axis=0, keepdims=True), (8, channels))
        result = part
        for step in range(1, per_group):
            result += jnp.where(member >= step, pltpu.roll(part, step, 1), 0.0)
            rolled = pltpu.roll(part, channels - step, 1)
            result += jnp.where(member < per_group - step, rolled, 0.0)
        return result

    row = jnp.where(member == 0, grouped(total), grouped(square))[0:1]
    out_ref[...] = jnp.broadcast_to(row[None], out_ref.shape)


def add_sums(values, total, square):
    width, channels = values.shape
    split = (width // 8, 8, channels)
    total += jnp.sum(values.reshape(split), axis=0)
    square += jnp.sum((values * values).reshape(split), axis=0)
    return total, square


def sums_kernel(own_ref, out_ref, pair_ref, other_ref):
    rows, _, channels = own_ref.shape
    even = lax.axis_index("rows") % 2 == 0
    for row in range(2):
        top = own_ref[row]
        bottom = own_ref[rows - 2 + row]
        pair_ref[row] = jnp.where(even, bottom, top)
        other_ref[row] = jnp.where(even, top, bottom)
    total = jnp.zeros((8, channels), jnp.float32)
    square = jnp.zeros((8, channels), jnp.float32)
    for row in range(rows):
        total, square = add_sums(own_ref[row].astype(jnp.float32), total, square)
    store_sums(total, square, out_ref)


def sum_weight(source, target):
    taps, channels = source.shape[1], source.shape[2]
    for tap in range(taps):
        total = source[0, tap].astype(jnp.float32)
        total += source[1, tap].astype(jnp.float32)
        total += source[2, tap].astype(jnp.float32)
        high = total.astype(jnp.bfloat16)
        low = (total - high.astype(jnp.float32)).astype(jnp.bfloat16)
        target[pl.ds(tap * channels, channels), :] = jnp.concatenate([high, low], axis=1)


def sum_paired(source, target):
    taps, channels = source.shape[1], source.shape[2]
    columns = taps // 3
    zeros = jnp.zeros((columns * channels, channels), jnp.bfloat16)
    for tap in range(taps):
        total = source[0, tap].astype(jnp.float32)
        total += source[1, tap].astype(jnp.float32)
        total += source[2, tap].astype(jnp.float32)
        total = total.astype(jnp.bfloat16)
        target[pl.ds(tap * channels, channels), 0:channels] = total
        target[pl.ds((tap + columns) * channels, channels), channels : 2 * channels] = total
    target[pl.ds(taps * channels, columns * channels), 0:channels] = zeros
    target[pl.ds(0, columns * channels), channels : 2 * channels] = zeros


def scale_offset(sums_ref, gain_ref, shift_ref, entries):
    sums = jnp.sum(sums_ref[...], axis=0)
    channels = sums.shape[1]
    per_group = channels // GROUPS
    sums = jnp.broadcast_to(sums, (8, channels)) * (1.0 / (entries * per_group))
    member = lax.broadcasted_iota(jnp.int32, sums.shape, 1) % per_group

    def spread(lane):
        part = jnp.where(member == lane, sums, 0.0)
        result = part
        for target in range(per_group):
            if target != lane:
                result += pltpu.roll(part, (target - lane) % channels, 1)
        return result

    mean = spread(0)
    var = jnp.maximum(spread(1) - mean * mean, 0.0)
    scale = gain_ref[...] * lax.rsqrt(var + 1e-06)
    return 0.5 * scale[0:1], (0.5 * (shift_ref[...] - mean * scale))[0:1]


def store_taps(values, scale, offset, wide_ref, taps_ref, row):
    width, channels = values.shape
    half = values.astype(jnp.float32) * scale + offset
    act = half * jnp.tanh(half) + half
    wide_ref[row, 8 : 8 + width, :] = act
    wide_ref[row, 7:8, :] = act[0:1]
    wide_ref[row, 8 + width : 9 + width, :] = act[width - 1 : width]
    for tap in range(3):
        shifted = wide_ref[row, 7 + tap : 7 + tap + width, :]
        taps_ref[row, :, tap * channels : (tap + 1) * channels] = shifted.astype(jnp.bfloat16)


def conv_rows(taps_ref, row, count, weight_ref):
    _, width, lanes = taps_ref.shape
    window = jnp.concatenate(
        [taps_ref[row + tap : row + tap + count].reshape(count * width, lanes) for tap in range(3)],
        axis=1,
    )
    both = jnp.dot(window, weight_ref[...], preferred_element_type=jnp.float32)
    half = both.shape[1] // 2
    return both[:, :half] + both[:, half:]


def first_kernel(
    count, sums_ref, own_ref, pair_ref, other_ref, weight_ref, bias_ref, gain_ref, shift_ref,
    bias_two_ref, gain_two_ref, shift_two_ref,
    hidden_ref, out_ref, next_ref, wide_ref, taps_ref, summed_ref, vectors_ref, sems,
):
    copies = [
        pltpu.make_async_copy(source, vectors_ref.at[i], sems.at[i])
        for i, source in enumerate((bias_two_ref, gain_two_ref, shift_two_ref))
    ]
    for copy in copies:
        copy.start()
    index = lax.axis_index("rows")
    rows, width, channels = own_ref.shape
    even = index % 2 == 0
    scale, offset = scale_offset(sums_ref, gain_ref, shift_ref, rows * width * count)
    sum_weight(weight_ref, summed_ref)

    def make(row):
        if row < 2:
            values = jnp.where(even, other_ref[row], pair_ref[row])
            values = jnp.where(index == 0, own_ref[0], values)
        elif row < rows + 2:
            values = own_ref[row - 2]
        else:
            values = jnp.where(even, pair_ref[row - rows - 2], other_ref[row - rows - 2])
            values = jnp.where(index == count - 1, own_ref[rows - 1], values)
        store_taps(values, scale, offset, wide_ref, taps_ref, row)

    total = jnp.zeros((8, channels), jnp.float32)
    square = jnp.zeros((8, channels), jnp.float32)
    for row in range(rows + 4):
        make(row)
    hidden = conv_rows(taps_ref, 0, rows + 2, summed_ref) + bias_ref[...]
    hidden = hidden.astype(jnp.bfloat16)
    for row in range(rows + 2):
        values = hidden[row * width : (row + 1) * width]
        hidden_ref[row] = values
        if 0 < row <= rows:
            total, square = add_sums(values.astype(jnp.float32), total, square)
    store_sums(total, square, out_ref)
    for i in range(3):
        copies[i].wait()
        next_ref[pl.ds(i, 1), :] = vectors_ref[i]

    @pl.when(index == 0)
    def _():
        hidden_ref[0] = hidden_ref[1]

    @pl.when(index == count - 1)
    def _():
        hidden_ref[rows + 1] = hidden_ref[rows]


def second_kernel(
    count, sums_ref, hidden_ref, own_ref, weight_ref, params_ref,
    out_ref, wide_ref, taps_ref, summed_ref, done_ref, sems,
):
    rows, width, channels = own_ref.shape
    scale, offset = scale_offset(
        sums_ref, params_ref.at[1:2], params_ref.at[2:3], rows * width * count
    )
    sum_paired(weight_ref, summed_ref)
    copies = []
    for row in range(2):
        store_taps(hidden_ref[row], scale, offset, wide_ref, taps_ref, row)
    for row in range(0, rows, 2):
        for i in range(2, 4):
            store_taps(hidden_ref[row + i], scale, offset, wide_ref, taps_ref, row + i)
        parts = 2 if row == rows - 2 else 1
        for part in range(parts):
            size = width // parts
            columns = pl.ds(part * size, size)
            window = jnp.concatenate(
                [taps_ref[row + tap, columns, :] for tap in range(4)], axis=1
            )
            both = jnp.dot(window, summed_ref[...], preferred_element_type=jnp.float32)
            for i in range(2):
                branch = both[:, i * channels : (i + 1) * channels] + params_ref[0:1, :]
                values = own_ref[row + i, columns, :].astype(jnp.float32) + branch
                done_ref[row + i, columns, :] = values.astype(jnp.bfloat16)
                copies.append(
                    pltpu.make_async_copy(
                        done_ref.at[row + i, columns],
                        out_ref.at[row + i, columns],
                        sems.at[len(copies)],
                    )
                )
                copies[-1].start()
    for copy in copies:
        copy.wait()


def exchanged(sums):
    count = lax.axis_size("rows")
    ends_first = [i // 2 if i % 2 == 0 else count - 1 - i // 2 for i in range(count)]
    return lax.all_to_all(sums, "rows", 0, 0, axis_index_groups=[ends_first])


def body(
    latents, gain_one, shift_one, weight_one, bias_one, gain_two, shift_two, weight_two, bias_two
):
    count = lax.axis_size("rows")
    own = latents[0]
    rows, width, channels = own.shape
    sums_shape = jax.ShapeDtypeStruct((count, 1, channels), jnp.float32)
    taps = weight_one.shape[1] * weight_one.shape[2]
    slab_shape = jax.ShapeDtypeStruct((2, width, channels), jnp.bfloat16)

    def raw(weight):
        return weight.reshape(3, taps, channels, channels)

    swap_pair = [(i, i ^ 1) for i in range(count)]
    swap_other = [(i, i + 1 if i % 2 else i - 1) for i in range(1, count - 1)]

    sums, pair, other = pl.pallas_call(
        sums_kernel,
        out_shape=[sums_shape, slab_shape, slab_shape],
        in_specs=[VMEM],
        out_specs=[VMEM] * 3,
        compiler_params=PARAMS,
        name="sums",
        cost_estimate=pl.CostEstimate(
            flops=40000000000, bytes_accessed=10000000, transcendentals=0
        ),
    )(own)
    other = lax.ppermute(other, "rows", swap_other)
    pair = lax.ppermute(pair, "rows", swap_pair)
    sums = exchanged(sums)
    hidden, sums, params = pl.pallas_call(
        functools.partial(first_kernel, count),
        out_shape=[
            jax.ShapeDtypeStruct((rows + 2, width, channels), jnp.bfloat16),
            sums_shape,
            jax.ShapeDtypeStruct((8, channels), jnp.float32),
        ],
        in_specs=[VMEM] * 8 + [HBM] * 3,
        out_specs=[VMEM] * 3,
        scratch_shapes=[
            pltpu.VMEM((rows + 4, width + 16, channels), jnp.float32),
            pltpu.VMEM((rows + 4, width, 3 * channels), jnp.bfloat16),
            pltpu.VMEM((taps * channels, 2 * channels), jnp.bfloat16),
            pltpu.VMEM((3, 1, channels), jnp.float32),
            pltpu.SemaphoreType.DMA((3,)),
        ],
        compiler_params=PARAMS, name="first",
    )(
        sums,
        own,
        pair,
        other,
        raw(weight_one),
        *[vector.reshape(1, channels) for vector in (bias_one, gain_one, shift_one)],
        *[
            pltpu.with_memory_space_constraint(vector.reshape(1, channels), pltpu.HBM)
            for vector in (bias_two, gain_two, shift_two)
        ],
    )
    sums = exchanged(sums)
    decoded = pl.pallas_call(
        functools.partial(second_kernel, count),
        out_shape=jax.ShapeDtypeStruct(own.shape, jnp.bfloat16),
        in_specs=[VMEM] * 5,
        out_specs=ANY,
        scratch_shapes=[
            pltpu.VMEM((rows + 2, width + 16, channels), jnp.float32),
            pltpu.VMEM((rows + 2, width, 3 * channels), jnp.bfloat16),
            pltpu.VMEM((taps // 3 * 4 * channels, 2 * channels), jnp.bfloat16),
            pltpu.VMEM(own.shape, jnp.bfloat16),
            pltpu.SemaphoreType.DMA((rows + 2,)),
        ],
        compiler_params=PARAMS, name="second",
    )(sums, hidden, own, raw(weight_two), params)
    return decoded[None]


def solution(mesh):
    return jax.shard_map(
        body,
        mesh=mesh,
        in_specs=(P("groups", "rows", None, None), P(), P(), P(), P(), P(), P(), P(), P()),
        out_specs=P("groups", "rows", None, None),
        check_vma=False,
    )
```

```python
import functools

import jax
import jax.numpy as jnp
from jax import lax
from jax.experimental import pallas as pl
from jax.experimental.pallas import tpu as pltpu
from jax.sharding import PartitionSpec as P

GROUPS = 32
HBM = pl.BlockSpec(memory_space=pltpu.HBM)
ANY = pl.BlockSpec(memory_space=pl.ANY)
VMEM = pl.BlockSpec(memory_space=pltpu.VMEM)
PARAMS = pltpu.CompilerParams(vmem_limit_bytes=24 * 1024 * 1024)


def store_sums(total, square, out_ref):
    channels = total.shape[1]
    per_group = channels // GROUPS
    member = lax.broadcasted_iota(jnp.int32, (8, channels), 1) % per_group

    def grouped(part):
        part = jnp.broadcast_to(jnp.sum(part, axis=0, keepdims=True), (8, channels))
        result = part
        for step in range(1, per_group):
            result += jnp.where(member >= step, pltpu.roll(part, step, 1), 0.0)
            rolled = pltpu.roll(part, channels - step, 1)
            result += jnp.where(member < per_group - step, rolled, 0.0)
        return result

    row = jnp.where(member == 0, grouped(total), grouped(square))[0:1]
    out_ref[...] = jnp.broadcast_to(row[None], out_ref.shape)


def add_sums(values, total, square):
    width, channels = values.shape
    split = (width // 8, 8, channels)
    total += jnp.sum(values.reshape(split), axis=0)
    square += jnp.sum((values * values).reshape(split), axis=0)
    return total, square


def sums_kernel(own_ref, out_ref, pair_ref, other_ref):
    rows, _, channels = own_ref.shape
    even = lax.axis_index("rows") % 2 == 0
    for row in range(2):
        top = own_ref[row]
        bottom = own_ref[rows - 2 + row]
        pair_ref[row] = jnp.where(even, bottom, top)
        other_ref[row] = jnp.where(even, top, bottom)
    total = jnp.zeros((8, channels), jnp.float32)
    square = jnp.zeros((8, channels), jnp.float32)
    for row in range(rows):
        total, square = add_sums(own_ref[row].astype(jnp.float32), total, square)
    store_sums(total, square, out_ref)


def sum_weight(source, target):
    taps, channels = source.shape[1], source.shape[2]
    for tap in range(taps):
        total = source[0, tap].astype(jnp.float32)
        total += source[1, tap].astype(jnp.float32)
        total += source[2, tap].astype(jnp.float32)
        high = total.astype(jnp.bfloat16)
        low = (total - high.astype(jnp.float32)).astype(jnp.bfloat16)
        target[pl.ds(tap * channels, channels), :] = jnp.concatenate([high, low], axis=1)


def scale_offset(sums_ref, gain_ref, shift_ref, entries):
    sums = jnp.sum(sums_ref[...], axis=0)
    channels = sums.shape[1]
    per_group = channels // GROUPS
    sums = jnp.broadcast_to(sums, (8, channels)) * (1.0 / (entries * per_group))
    member = lax.broadcasted_iota(jnp.int32, sums.shape, 1) % per_group

    def spread(lane):
        part = jnp.where(member == lane, sums, 0.0)
        result = part
        for target in range(per_group):
            if target != lane:
                result += pltpu.roll(part, (target - lane) % channels, 1)
        return result

    mean = spread(0)
    var = jnp.maximum(spread(1) - mean * mean, 0.0)
    scale = gain_ref[...] * lax.rsqrt(var + 1e-06)
    return 0.5 * scale[0:1], (0.5 * (shift_ref[...] - mean * scale))[0:1]


def store_taps(values, scale, offset, wide_ref, taps_ref, row):
    width, channels = values.shape
    half = values.astype(jnp.float32) * scale + offset
    act = half * jnp.tanh(half) + half
    wide_ref[row, 8 : 8 + width, :] = act
    wide_ref[row, 7:8, :] = act[0:1]
    wide_ref[row, 8 + width : 9 + width, :] = act[width - 1 : width]
    for tap in range(3):
        shifted = wide_ref[row, 7 + tap : 7 + tap + width, :]
        taps_ref[row, :, tap * channels : (tap + 1) * channels] = shifted.astype(jnp.bfloat16)


def conv_rows(taps_ref, row, count, weight_ref):
    _, width, lanes = taps_ref.shape
    window = jnp.concatenate(
        [taps_ref[row + tap : row + tap + count].reshape(count * width, lanes) for tap in range(3)],
        axis=1,
    )
    both = jnp.dot(window, weight_ref[...], preferred_element_type=jnp.float32)
    half = both.shape[1] // 2
    return both[:, :half] + both[:, half:]


def first_kernel(
    count, sums_ref, own_ref, pair_ref, other_ref, weight_ref, bias_ref, gain_ref, shift_ref,
    bias_two_ref, gain_two_ref, shift_two_ref,
    hidden_ref, out_ref, next_ref, wide_ref, taps_ref, summed_ref, vectors_ref, sems,
):
    copies = [
        pltpu.make_async_copy(source, vectors_ref.at[i], sems.at[i])
        for i, source in enumerate((bias_two_ref, gain_two_ref, shift_two_ref))
    ]
    for copy in copies:
        copy.start()
    index = lax.axis_index("rows")
    rows, width, channels = own_ref.shape
    even = index % 2 == 0
    scale, offset = scale_offset(sums_ref, gain_ref, shift_ref, rows * width * count)
    sum_weight(weight_ref, summed_ref)

    def make(row):
        if row < 2:
            values = jnp.where(even, other_ref[row], pair_ref[row])
            values = jnp.where(index == 0, own_ref[0], values)
        elif row < rows + 2:
            values = own_ref[row - 2]
        else:
            values = jnp.where(even, pair_ref[row - rows - 2], other_ref[row - rows - 2])
            values = jnp.where(index == count - 1, own_ref[rows - 1], values)
        store_taps(values, scale, offset, wide_ref, taps_ref, row)

    total = jnp.zeros((8, channels), jnp.float32)
    square = jnp.zeros((8, channels), jnp.float32)
    for row in range(rows + 4):
        make(row)
    hidden = conv_rows(taps_ref, 0, rows + 2, summed_ref) + bias_ref[...]
    hidden = hidden.astype(jnp.bfloat16)
    for row in range(rows + 2):
        values = hidden[row * width : (row + 1) * width]
        hidden_ref[row] = values
        if 0 < row <= rows:
            total, square = add_sums(values.astype(jnp.float32), total, square)
    store_sums(total, square, out_ref)
    for i in range(3):
        copies[i].wait()
        next_ref[pl.ds(i, 1), :] = vectors_ref[i]

    @pl.when(index == 0)
    def _():
        hidden_ref[0] = hidden_ref[1]

    @pl.when(index == count - 1)
    def _():
        hidden_ref[rows + 1] = hidden_ref[rows]


def second_kernel(
    count, sums_ref, hidden_ref, own_ref, weight_ref, params_ref,
    out_ref, wide_ref, taps_ref, summed_ref, done_ref, sems,
):
    rows, width, channels = own_ref.shape
    scale, offset = scale_offset(
        sums_ref, params_ref.at[1:2], params_ref.at[2:3], rows * width * count
    )
    sum_weight(weight_ref, summed_ref)
    copies = [
        pltpu.make_async_copy(done_ref.at[row], out_ref.at[row], sems.at[row])
        for row in range(rows)
    ]
    start = 0
    for count in (rows - 1, 1):
        for row in range(start + 2 if start else 0, start + count + 2):
            store_taps(hidden_ref[row], scale, offset, wide_ref, taps_ref, row)
        branch = conv_rows(taps_ref, start, count, summed_ref) + params_ref[0:1, :]
        for i in range(count):
            row = start + i
            values = own_ref[row].astype(jnp.float32) + branch[i * width : (i + 1) * width]
            done_ref[row] = values.astype(jnp.bfloat16)
            copies[row].start()
        start += count
    for copy in copies:
        copy.wait()


def exchanged(sums):
    count = lax.axis_size("rows")
    ends_first = [i // 2 if i % 2 == 0 else count - 1 - i // 2 for i in range(count)]
    return lax.all_to_all(sums, "rows", 0, 0, axis_index_groups=[ends_first])


def body(
    latents, gain_one, shift_one, weight_one, bias_one, gain_two, shift_two, weight_two, bias_two
):
    count = lax.axis_size("rows")
    own = latents[0]
    rows, width, channels = own.shape
    sums_shape = jax.ShapeDtypeStruct((count, 1, channels), jnp.float32)
    taps = weight_one.shape[1] * weight_one.shape[2]
    slab_shape = jax.ShapeDtypeStruct((2, width, channels), jnp.bfloat16)

    def raw(weight):
        return weight.reshape(3, taps, channels, channels)

    swap_pair = [(i, i ^ 1) for i in range(count)]
    swap_other = [(i, i + 1 if i % 2 else i - 1) for i in range(1, count - 1)]

    sums, pair, other = pl.pallas_call(
        sums_kernel,
        out_shape=[sums_shape, slab_shape, slab_shape],
        in_specs=[VMEM],
        out_specs=[VMEM] * 3,
        compiler_params=PARAMS,
        name="sums",
        cost_estimate=pl.CostEstimate(
            flops=40000000000, bytes_accessed=10000000, transcendentals=0
        ),
    )(own)
    other = lax.ppermute(other, "rows", swap_other)
    pair = lax.ppermute(pair, "rows", swap_pair)
    sums = exchanged(sums)
    hidden, sums, params = pl.pallas_call(
        functools.partial(first_kernel, count),
        out_shape=[
            jax.ShapeDtypeStruct((rows + 2, width, channels), jnp.bfloat16),
            sums_shape,
            jax.ShapeDtypeStruct((8, channels), jnp.float32),
        ],
        in_specs=[VMEM] * 8 + [HBM] * 3,
        out_specs=[VMEM] * 3,
        scratch_shapes=[
            pltpu.VMEM((rows + 4, width + 16, channels), jnp.float32),
            pltpu.VMEM((rows + 4, width, 3 * channels), jnp.bfloat16),
            pltpu.VMEM((taps * channels, 2 * channels), jnp.bfloat16),
            pltpu.VMEM((3, 1, channels), jnp.float32),
            pltpu.SemaphoreType.DMA((3,)),
        ],
        compiler_params=PARAMS, name="first",
    )(
        sums,
        own,
        pair,
        other,
        raw(weight_one),
        *[vector.reshape(1, channels) for vector in (bias_one, gain_one, shift_one)],
        *[
            pltpu.with_memory_space_constraint(vector.reshape(1, channels), pltpu.HBM)
            for vector in (bias_two, gain_two, shift_two)
        ],
    )
    sums = exchanged(sums)
    decoded = pl.pallas_call(
        functools.partial(second_kernel, count),
        out_shape=jax.ShapeDtypeStruct(own.shape, jnp.bfloat16),
        in_specs=[VMEM] * 5,
        out_specs=ANY,
        scratch_shapes=[
            pltpu.VMEM((rows + 2, width + 16, channels), jnp.float32),
            pltpu.VMEM((rows + 2, width, 3 * channels), jnp.bfloat16),
            pltpu.VMEM((taps * channels, 2 * channels), jnp.bfloat16),
            pltpu.VMEM(own.shape, jnp.bfloat16),
            pltpu.SemaphoreType.DMA((rows,)),
        ],
        compiler_params=PARAMS, name="second",
    )(sums, hidden, own, raw(weight_two), params)
    return decoded[None]


def solution(mesh):
    return jax.shard_map(
        body,
        mesh=mesh,
        in_specs=(P("groups", "rows", None, None), P(), P(), P(), P(), P(), P(), P(), P()),
        out_specs=P("groups", "rows", None, None),
        check_vma=False,
    )
```

```python
import functools

import jax
import jax.numpy as jnp
from jax import lax
from jax.experimental import pallas as pl
from jax.experimental.pallas import tpu as pltpu
from jax.sharding import PartitionSpec as P

GROUPS = 32
HBM = pl.BlockSpec(memory_space=pltpu.HBM)
ANY = pl.BlockSpec(memory_space=pl.ANY)
VMEM = pl.BlockSpec(memory_space=pltpu.VMEM)
PARAMS = pltpu.CompilerParams(vmem_limit_bytes=24 * 1024 * 1024)


def store_sums(total, square, out_ref):
    channels = total.shape[1]
    per_group = channels // GROUPS
    member = lax.broadcasted_iota(jnp.int32, (8, channels), 1) % per_group

    def grouped(part):
        part = jnp.broadcast_to(jnp.sum(part, axis=0, keepdims=True), (8, channels))
        result = part
        for step in range(1, per_group):
            result += jnp.where(member >= step, pltpu.roll(part, step, 1), 0.0)
            rolled = pltpu.roll(part, channels - step, 1)
            result += jnp.where(member < per_group - step, rolled, 0.0)
        return result

    row = jnp.where(member == 0, grouped(total), grouped(square))[0:1]
    out_ref[...] = jnp.broadcast_to(row[None], out_ref.shape)


def add_sums(values, total, square):
    width, channels = values.shape
    split = (width // 8, 8, channels)
    total += jnp.sum(values.reshape(split), axis=0)
    square += jnp.sum((values * values).reshape(split), axis=0)
    return total, square


def sums_kernel(own_ref, out_ref, pair_ref, other_ref):
    rows, _, channels = own_ref.shape
    even = lax.axis_index("rows") % 2 == 0
    for row in range(2):
        top = own_ref[row]
        bottom = own_ref[rows - 2 + row]
        pair_ref[row] = jnp.where(even, bottom, top)
        other_ref[row] = jnp.where(even, top, bottom)
    total = jnp.zeros((8, channels), jnp.float32)
    square = jnp.zeros((8, channels), jnp.float32)
    for row in range(rows):
        total, square = add_sums(own_ref[row].astype(jnp.float32), total, square)
    store_sums(total, square, out_ref)


def sum_weight(source, target):
    taps, channels = source.shape[1], source.shape[2]
    for tap in range(taps):
        total = source[0, tap].astype(jnp.float32)
        total += source[1, tap].astype(jnp.float32)
        total += source[2, tap].astype(jnp.float32)
        high = total.astype(jnp.bfloat16)
        low = (total - high.astype(jnp.float32)).astype(jnp.bfloat16)
        target[pl.ds(tap * channels, channels), :] = jnp.concatenate([high, low], axis=1)


def scale_offset(sums_ref, gain_ref, shift_ref, entries):
    sums = jnp.sum(sums_ref[...], axis=0)
    channels = sums.shape[1]
    per_group = channels // GROUPS
    sums = jnp.broadcast_to(sums, (8, channels)) * (1.0 / (entries * per_group))
    member = lax.broadcasted_iota(jnp.int32, sums.shape, 1) % per_group

    def spread(lane):
        part = jnp.where(member == lane, sums, 0.0)
        result = part
        for target in range(per_group):
            if target != lane:
                result += pltpu.roll(part, (target - lane) % channels, 1)
        return result

    mean = spread(0)
    var = jnp.maximum(spread(1) - mean * mean, 0.0)
    scale = gain_ref[...] * lax.rsqrt(var + 1e-06)
    return 0.5 * scale[0:1], (0.5 * (shift_ref[...] - mean * scale))[0:1]


def store_taps(values, scale, offset, wide_ref, taps_ref, row):
    width, channels = values.shape
    half = values.astype(jnp.float32) * scale + offset
    act = half * jnp.tanh(half) + half
    wide_ref[row, 8 : 8 + width, :] = act
    wide_ref[row, 7:8, :] = act[0:1]
    wide_ref[row, 8 + width : 9 + width, :] = act[width - 1 : width]
    for tap in range(3):
        shifted = wide_ref[row, 7 + tap : 7 + tap + width, :]
        taps_ref[row, :, tap * channels : (tap + 1) * channels] = shifted.astype(jnp.bfloat16)


def conv_rows(taps_ref, row, count, weight_ref):
    _, width, lanes = taps_ref.shape
    window = jnp.concatenate(
        [taps_ref[row + tap : row + tap + count].reshape(count * width, lanes) for tap in range(3)],
        axis=1,
    )
    both = jnp.dot(window, weight_ref[...], preferred_element_type=jnp.float32)
    half = both.shape[1] // 2
    return both[:, :half] + both[:, half:]


def first_kernel(
    count, sums_ref, own_ref, pair_ref, other_ref, weight_ref, bias_ref, gain_ref, shift_ref,
    bias_two_ref, gain_two_ref, shift_two_ref,
    hidden_ref, out_ref, next_ref, wide_ref, taps_ref, summed_ref, vectors_ref, sems,
):
    copies = [
        pltpu.make_async_copy(source, vectors_ref.at[i], sems.at[i])
        for i, source in enumerate((bias_two_ref, gain_two_ref, shift_two_ref))
    ]
    for copy in copies:
        copy.start()
    index = lax.axis_index("rows")
    rows, width, channels = own_ref.shape
    even = index % 2 == 0
    scale, offset = scale_offset(sums_ref, gain_ref, shift_ref, rows * width * count)
    sum_weight(weight_ref, summed_ref)

    def make(row):
        if row < 2:
            values = jnp.where(even, other_ref[row], pair_ref[row])
            values = jnp.where(index == 0, own_ref[0], values)
        elif row < rows + 2:
            values = own_ref[row - 2]
        else:
            values = jnp.where(even, pair_ref[row - rows - 2], other_ref[row - rows - 2])
            values = jnp.where(index == count - 1, own_ref[rows - 1], values)
        store_taps(values, scale, offset, wide_ref, taps_ref, row)

    total = jnp.zeros((8, channels), jnp.float32)
    square = jnp.zeros((8, channels), jnp.float32)
    for row in range(rows + 4):
        make(row)
    hidden = conv_rows(taps_ref, 0, rows + 2, summed_ref) + bias_ref[...]
    hidden = hidden.astype(jnp.bfloat16)
    for row in range(rows + 2):
        values = hidden[row * width : (row + 1) * width]
        hidden_ref[row] = values
        if 0 < row <= rows:
            total, square = add_sums(values.astype(jnp.float32), total, square)
    store_sums(total, square, out_ref)
    for i in range(3):
        copies[i].wait()
        next_ref[pl.ds(i, 1), :] = vectors_ref[i]

    @pl.when(index == 0)
    def _():
        hidden_ref[0] = hidden_ref[1]

    @pl.when(index == count - 1)
    def _():
        hidden_ref[rows + 1] = hidden_ref[rows]


def second_kernel(
    count, sums_ref, hidden_ref, own_ref, weight_ref, params_ref,
    out_ref, wide_ref, taps_ref, summed_ref, done_ref, sems,
):
    rows, width, channels = own_ref.shape
    scale, offset = scale_offset(
        sums_ref, params_ref.at[1:2], params_ref.at[2:3], rows * width * count
    )
    sum_weight(weight_ref, summed_ref)
    copies = [
        pltpu.make_async_copy(done_ref.at[row], out_ref.at[row], sems.at[row])
        for row in range(rows)
    ]
    for row in range(rows + 2):
        store_taps(hidden_ref[row], scale, offset, wide_ref, taps_ref, row)
    branch = conv_rows(taps_ref, 0, rows, summed_ref) + params_ref[0:1, :]
    for row in range(rows):
        values = own_ref[row].astype(jnp.float32) + branch[row * width : (row + 1) * width]
        done_ref[row] = values.astype(jnp.bfloat16)
        copies[row].start()
    for copy in copies:
        copy.wait()


def exchanged(sums):
    count = lax.axis_size("rows")
    ends_first = [i // 2 if i % 2 == 0 else count - 1 - i // 2 for i in range(count)]
    return lax.all_to_all(sums, "rows", 0, 0, axis_index_groups=[ends_first])


def body(
    latents, gain_one, shift_one, weight_one, bias_one, gain_two, shift_two, weight_two, bias_two
):
    count = lax.axis_size("rows")
    own = latents[0]
    rows, width, channels = own.shape
    sums_shape = jax.ShapeDtypeStruct((count, 1, channels), jnp.float32)
    taps = weight_one.shape[1] * weight_one.shape[2]
    slab_shape = jax.ShapeDtypeStruct((2, width, channels), jnp.bfloat16)

    def raw(weight):
        return weight.reshape(3, taps, channels, channels)

    swap_pair = [(i, i ^ 1) for i in range(count)]
    swap_other = [(i, i + 1 if i % 2 else i - 1) for i in range(1, count - 1)]

    sums, pair, other = pl.pallas_call(
        sums_kernel,
        out_shape=[sums_shape, slab_shape, slab_shape],
        in_specs=[VMEM],
        out_specs=[VMEM] * 3,
        compiler_params=PARAMS,
        name="sums",
        cost_estimate=pl.CostEstimate(
            flops=40000000000, bytes_accessed=10000000, transcendentals=0
        ),
    )(own)
    other = lax.ppermute(other, "rows", swap_other)
    pair = lax.ppermute(pair, "rows", swap_pair)
    sums = exchanged(sums)
    hidden, sums, params = pl.pallas_call(
        functools.partial(first_kernel, count),
        out_shape=[
            jax.ShapeDtypeStruct((rows + 2, width, channels), jnp.bfloat16),
            sums_shape,
            jax.ShapeDtypeStruct((8, channels), jnp.float32),
        ],
        in_specs=[VMEM] * 8 + [HBM] * 3,
        out_specs=[VMEM] * 3,
        scratch_shapes=[
            pltpu.VMEM((rows + 4, width + 16, channels), jnp.float32),
            pltpu.VMEM((rows + 4, width, 3 * channels), jnp.bfloat16),
            pltpu.VMEM((taps * channels, 2 * channels), jnp.bfloat16),
            pltpu.VMEM((3, 1, channels), jnp.float32),
            pltpu.SemaphoreType.DMA((3,)),
        ],
        compiler_params=PARAMS, name="first",
    )(
        sums,
        own,
        pair,
        other,
        raw(weight_one),
        *[vector.reshape(1, channels) for vector in (bias_one, gain_one, shift_one)],
        *[
            pltpu.with_memory_space_constraint(vector.reshape(1, channels), pltpu.HBM)
            for vector in (bias_two, gain_two, shift_two)
        ],
    )
    sums = exchanged(sums)
    decoded = pl.pallas_call(
        functools.partial(second_kernel, count),
        out_shape=jax.ShapeDtypeStruct(own.shape, jnp.bfloat16),
        in_specs=[VMEM] * 5,
        out_specs=ANY,
        scratch_shapes=[
            pltpu.VMEM((rows + 2, width + 16, channels), jnp.float32),
            pltpu.VMEM((rows + 2, width, 3 * channels), jnp.bfloat16),
            pltpu.VMEM((taps * channels, 2 * channels), jnp.bfloat16),
            pltpu.VMEM(own.shape, jnp.bfloat16),
            pltpu.SemaphoreType.DMA((rows,)),
        ],
        compiler_params=PARAMS, name="second",
    )(sums, hidden, own, raw(weight_two), params)
    return decoded[None]


def solution(mesh):
    return jax.shard_map(
        body,
        mesh=mesh,
        in_specs=(P("groups", "rows", None, None), P(), P(), P(), P(), P(), P(), P(), P()),
        out_specs=P("groups", "rows", None, None),
        check_vma=False,
    )
```

```python
import functools

import jax
import jax.numpy as jnp
from jax import lax
from jax.experimental import pallas as pl
from jax.experimental.pallas import tpu as pltpu
from jax.sharding import PartitionSpec as P

GROUPS = 32
HBM = pl.BlockSpec(memory_space=pltpu.HBM)
ANY = pl.BlockSpec(memory_space=pl.ANY)
VMEM = pl.BlockSpec(memory_space=pltpu.VMEM)
PARAMS = pltpu.CompilerParams(vmem_limit_bytes=24 * 1024 * 1024)


def store_sums(total, square, out_ref):
    channels = total.shape[1]
    per_group = channels // GROUPS
    member = lax.broadcasted_iota(jnp.int32, (8, channels), 1) % per_group

    def grouped(part):
        part = jnp.broadcast_to(jnp.sum(part, axis=0, keepdims=True), (8, channels))
        result = part
        for step in range(1, per_group):
            result += jnp.where(member >= step, pltpu.roll(part, step, 1), 0.0)
            rolled = pltpu.roll(part, channels - step, 1)
            result += jnp.where(member < per_group - step, rolled, 0.0)
        return result

    row = jnp.where(member == 0, grouped(total), grouped(square))[0:1]
    out_ref[...] = jnp.broadcast_to(row[None], out_ref.shape)


def add_sums(values, total, square):
    width, channels = values.shape
    split = (width // 8, 8, channels)
    total += jnp.sum(values.reshape(split), axis=0)
    square += jnp.sum((values * values).reshape(split), axis=0)
    return total, square


def sums_kernel(own_ref, out_ref, pair_ref, other_ref):
    rows, _, channels = own_ref.shape
    even = lax.axis_index("rows") % 2 == 0
    for row in range(2):
        top = own_ref[row]
        bottom = own_ref[rows - 2 + row]
        pair_ref[row] = jnp.where(even, bottom, top)
        other_ref[row] = jnp.where(even, top, bottom)
    total = jnp.zeros((8, channels), jnp.float32)
    square = jnp.zeros((8, channels), jnp.float32)
    for row in range(rows):
        total, square = add_sums(own_ref[row].astype(jnp.float32), total, square)
    store_sums(total, square, out_ref)


def sum_weight(source, target):
    taps, channels = source.shape[1], source.shape[2]
    for tap in range(taps):
        total = source[0, tap].astype(jnp.float32)
        total += source[1, tap].astype(jnp.float32)
        total += source[2, tap].astype(jnp.float32)
        high = total.astype(jnp.bfloat16)
        low = (total - high.astype(jnp.float32)).astype(jnp.bfloat16)
        target[pl.ds(tap * channels, channels), :] = jnp.concatenate([high, low], axis=1)


def scale_offset(sums, gain_ref, shift_ref, entries):
    channels = sums.shape[1]
    per_group = channels // GROUPS
    sums = jnp.broadcast_to(sums, (8, channels)) * (1.0 / (entries * per_group))
    member = lax.broadcasted_iota(jnp.int32, sums.shape, 1) % per_group

    def spread(lane):
        part = jnp.where(member == lane, sums, 0.0)
        result = part
        for target in range(per_group):
            if target != lane:
                result += pltpu.roll(part, (target - lane) % channels, 1)
        return result

    mean = spread(0)
    var = jnp.maximum(spread(1) - mean * mean, 0.0)
    scale = gain_ref[...] * lax.rsqrt(var + 1e-06)
    return 0.5 * scale[0:1], (0.5 * (shift_ref[...] - mean * scale))[0:1]


def store_taps(values, scale, offset, wide_ref, taps_ref, row):
    width, channels = values.shape
    half = values.astype(jnp.float32) * scale + offset
    act = half * jnp.tanh(half) + half
    wide_ref[row, 8 : 8 + width, :] = act
    wide_ref[row, 7:8, :] = act[0:1]
    wide_ref[row, 8 + width : 9 + width, :] = act[width - 1 : width]
    for tap in range(3):
        shifted = wide_ref[row, 7 + tap : 7 + tap + width, :]
        taps_ref[row, :, tap * channels : (tap + 1) * channels] = shifted.astype(jnp.bfloat16)


def conv_rows(taps_ref, row, count, weight_ref):
    _, width, lanes = taps_ref.shape
    window = jnp.concatenate(
        [taps_ref[row + tap : row + tap + count].reshape(count * width, lanes) for tap in range(3)],
        axis=1,
    )
    both = jnp.dot(window, weight_ref[...], preferred_element_type=jnp.float32)
    half = both.shape[1] // 2
    return both[:, :half] + both[:, half:]


def first_kernel(
    count, sums_ref, handed_ref, own_ref, pair_ref, other_ref, weight_ref, bias_ref, gain_ref, shift_ref,
    bias_two_ref, gain_two_ref, shift_two_ref,
    hidden_ref, out_ref, next_ref, wide_ref, taps_ref, summed_ref, vectors_ref, sems,
):
    copies = [
        pltpu.make_async_copy(source, vectors_ref.at[i], sems.at[i])
        for i, source in enumerate((bias_two_ref, gain_two_ref, shift_two_ref))
    ]
    for copy in copies:
        copy.start()
    index = lax.axis_index("rows")
    rows, width, channels = own_ref.shape
    even = index % 2 == 0
    sums = jnp.where(even, handed_ref[0], sums_ref[0])
    scale, offset = scale_offset(sums, gain_ref, shift_ref, rows * width * count)
    sum_weight(weight_ref, summed_ref)

    def make(row):
        if row < 2:
            values = jnp.where(even, other_ref[row], pair_ref[row])
            values = jnp.where(index == 0, own_ref[0], values)
        elif row < rows + 2:
            values = own_ref[row - 2]
        else:
            values = jnp.where(even, pair_ref[row - rows - 2], other_ref[row - rows - 2])
            values = jnp.where(index == count - 1, own_ref[rows - 1], values)
        store_taps(values, scale, offset, wide_ref, taps_ref, row)

    total = jnp.zeros((8, channels), jnp.float32)
    square = jnp.zeros((8, channels), jnp.float32)
    for row in range(rows + 4):
        make(row)
    hidden = conv_rows(taps_ref, 0, rows + 2, summed_ref) + bias_ref[...]
    hidden = hidden.astype(jnp.bfloat16)
    for row in range(rows + 2):
        values = hidden[row * width : (row + 1) * width]
        hidden_ref[row] = values
        if 0 < row <= rows:
            total, square = add_sums(values.astype(jnp.float32), total, square)
    store_sums(total, square, out_ref)
    for i in range(3):
        copies[i].wait()
        next_ref[pl.ds(i, 1), :] = vectors_ref[i]

    @pl.when(index == 0)
    def _():
        hidden_ref[0] = hidden_ref[1]

    @pl.when(index == count - 1)
    def _():
        hidden_ref[rows + 1] = hidden_ref[rows]


def second_kernel(
    count, sums_ref, hidden_ref, own_ref, weight_ref, params_ref,
    out_ref, wide_ref, taps_ref, summed_ref, done_ref, sems,
):
    rows, width, channels = own_ref.shape
    scale, offset = scale_offset(
        jnp.sum(sums_ref[...], axis=0), params_ref.at[1:2], params_ref.at[2:3], rows * width * count
    )
    sum_weight(weight_ref, summed_ref)
    copies = [
        pltpu.make_async_copy(done_ref.at[row], out_ref.at[row], sems.at[row])
        for row in range(rows)
    ]
    for row in range(rows + 2):
        store_taps(hidden_ref[row], scale, offset, wide_ref, taps_ref, row)
    branch = conv_rows(taps_ref, 0, rows, summed_ref) + params_ref[0:1, :]
    for row in range(rows):
        values = own_ref[row].astype(jnp.float32) + branch[row * width : (row + 1) * width]
        done_ref[row] = values.astype(jnp.bfloat16)
        copies[row].start()
    for copy in copies:
        copy.wait()


def exchanged(sums):
    count = lax.axis_size("rows")
    ends_first = [i // 2 if i % 2 == 0 else count - 1 - i // 2 for i in range(count)]
    return lax.all_to_all(sums, "rows", 0, 0, axis_index_groups=[ends_first])


def odd_core_sum(sums, count, swap_pair):
    if count & (count - 1):
        total = exchanged(jnp.broadcast_to(sums, (count,) + sums.shape[1:]))
        total = jnp.sum(total, axis=0, keepdims=True)
        return total, total
    total = sums + lax.ppermute(sums, "rows", swap_pair)
    step = 2
    while step < count:
        pairs = [(i, i ^ step) for i in range(1, count, 2)]
        total = total + lax.ppermute(total, "rows", pairs)
        step *= 2
    return total, lax.ppermute(total, "rows", [(i, i - 1) for i in range(1, count, 2)])


def body(
    latents, gain_one, shift_one, weight_one, bias_one, gain_two, shift_two, weight_two, bias_two
):
    count = lax.axis_size("rows")
    own = latents[0]
    rows, width, channels = own.shape
    sums_shape = jax.ShapeDtypeStruct((count, 1, channels), jnp.float32)
    taps = weight_one.shape[1] * weight_one.shape[2]
    slab_shape = jax.ShapeDtypeStruct((2, width, channels), jnp.bfloat16)

    def raw(weight):
        return weight.reshape(3, taps, channels, channels)

    swap_pair = [(i, i ^ 1) for i in range(count)]
    swap_other = [(i, i + 1 if i % 2 else i - 1) for i in range(1, count - 1)]

    sums, pair, other = pl.pallas_call(
        sums_kernel,
        out_shape=[jax.ShapeDtypeStruct((1, 1, channels), jnp.float32), slab_shape, slab_shape],
        in_specs=[VMEM],
        out_specs=[VMEM] * 3,
        compiler_params=PARAMS,
        name="sums",
        cost_estimate=pl.CostEstimate(
            flops=40000000000, bytes_accessed=10000000, transcendentals=0
        ),
    )(own)
    sums, handed = odd_core_sum(sums, count, swap_pair)
    pair = lax.ppermute(pair, "rows", swap_pair)
    other = lax.ppermute(other, "rows", swap_other)
    hidden, sums, params = pl.pallas_call(
        functools.partial(first_kernel, count),
        out_shape=[
            jax.ShapeDtypeStruct((rows + 2, width, channels), jnp.bfloat16),
            sums_shape,
            jax.ShapeDtypeStruct((8, channels), jnp.float32),
        ],
        in_specs=[VMEM] * 9 + [HBM] * 3,
        out_specs=[VMEM] * 3,
        scratch_shapes=[
            pltpu.VMEM((rows + 4, width + 16, channels), jnp.float32),
            pltpu.VMEM((rows + 4, width, 3 * channels), jnp.bfloat16),
            pltpu.VMEM((taps * channels, 2 * channels), jnp.bfloat16),
            pltpu.VMEM((3, 1, channels), jnp.float32),
            pltpu.SemaphoreType.DMA((3,)),
        ],
        compiler_params=PARAMS, name="first",
    )(
        sums,
        handed,
        own,
        pair,
        other,
        raw(weight_one),
        *[vector.reshape(1, channels) for vector in (bias_one, gain_one, shift_one)],
        *[
            pltpu.with_memory_space_constraint(vector.reshape(1, channels), pltpu.HBM)
            for vector in (bias_two, gain_two, shift_two)
        ],
    )
    sums = exchanged(sums)
    decoded = pl.pallas_call(
        functools.partial(second_kernel, count),
        out_shape=jax.ShapeDtypeStruct(own.shape, jnp.bfloat16),
        in_specs=[VMEM] * 5,
        out_specs=ANY,
        scratch_shapes=[
            pltpu.VMEM((rows + 2, width + 16, channels), jnp.float32),
            pltpu.VMEM((rows + 2, width, 3 * channels), jnp.bfloat16),
            pltpu.VMEM((taps * channels, 2 * channels), jnp.bfloat16),
            pltpu.VMEM(own.shape, jnp.bfloat16),
            pltpu.SemaphoreType.DMA((rows,)),
        ],
        compiler_params=PARAMS, name="second",
    )(sums, hidden, own, raw(weight_two), params)
    return decoded[None]


def solution(mesh):
    return jax.shard_map(
        body,
        mesh=mesh,
        in_specs=(P("groups", "rows", None, None), P(), P(), P(), P(), P(), P(), P(), P()),
        out_specs=P("groups", "rows", None, None),
        check_vma=False,
    )
```

```python
import functools

import jax
import jax.numpy as jnp
from jax import lax
from jax.experimental import pallas as pl
from jax.experimental.pallas import tpu as pltpu
from jax.sharding import PartitionSpec as P

GROUPS = 32
HBM = pl.BlockSpec(memory_space=pltpu.HBM)
ANY = pl.BlockSpec(memory_space=pl.ANY)
VMEM = pl.BlockSpec(memory_space=pltpu.VMEM)
PARAMS = pltpu.CompilerParams(vmem_limit_bytes=24 * 1024 * 1024)


def store_sums(total, square, out_ref):
    channels = total.shape[1]
    per_group = channels // GROUPS
    member = lax.broadcasted_iota(jnp.int32, (8, channels), 1) % per_group

    def grouped(part):
        part = jnp.broadcast_to(jnp.sum(part, axis=0, keepdims=True), (8, channels))
        result = part
        for step in range(1, per_group):
            result += jnp.where(member >= step, pltpu.roll(part, step, 1), 0.0)
            rolled = pltpu.roll(part, channels - step, 1)
            result += jnp.where(member < per_group - step, rolled, 0.0)
        return result

    row = jnp.where(member == 0, grouped(total), grouped(square))[0:1]
    out_ref[...] = jnp.broadcast_to(row[None], out_ref.shape)


def add_sums(values, total, square):
    width, channels = values.shape
    split = (width // 8, 8, channels)
    total += jnp.sum(values.reshape(split), axis=0)
    square += jnp.sum((values * values).reshape(split), axis=0)
    return total, square


def sums_kernel(own_ref, out_ref, pair_ref, other_ref):
    rows, _, channels = own_ref.shape
    even = lax.axis_index("rows") % 2 == 0
    for row in range(2):
        top = own_ref[row]
        bottom = own_ref[rows - 2 + row]
        pair_ref[row] = jnp.where(even, bottom, top)
        other_ref[row] = jnp.where(even, top, bottom)
    total = jnp.zeros((8, channels), jnp.float32)
    square = jnp.zeros((8, channels), jnp.float32)
    for row in range(rows):
        total, square = add_sums(own_ref[row].astype(jnp.float32), total, square)
    store_sums(total, square, out_ref)


def sum_weight(source, target):
    taps, channels = source.shape[1], source.shape[2]
    for tap in range(taps):
        total = source[0, tap].astype(jnp.float32)
        total += source[1, tap].astype(jnp.float32)
        total += source[2, tap].astype(jnp.float32)
        high = total.astype(jnp.bfloat16)
        low = (total - high.astype(jnp.float32)).astype(jnp.bfloat16)
        target[pl.ds(tap * channels, channels), :] = jnp.concatenate([high, low], axis=1)


def scale_offset(sums_ref, gain_ref, shift_ref, entries):
    sums = jnp.sum(sums_ref[...], axis=0)
    channels = sums.shape[1]
    per_group = channels // GROUPS
    sums = jnp.broadcast_to(sums, (8, channels)) * (1.0 / (entries * per_group))
    member = lax.broadcasted_iota(jnp.int32, sums.shape, 1) % per_group

    def spread(lane):
        part = jnp.where(member == lane, sums, 0.0)
        result = part
        for target in range(per_group):
            if target != lane:
                result += pltpu.roll(part, (target - lane) % channels, 1)
        return result

    mean = spread(0)
    var = jnp.maximum(spread(1) - mean * mean, 0.0)
    scale = gain_ref[...] * lax.rsqrt(var + 1e-06)
    return 0.5 * scale[0:1], (0.5 * (shift_ref[...] - mean * scale))[0:1]


def store_taps(values, scale, offset, wide_ref, taps_ref, row):
    width, channels = values.shape
    half = values.astype(jnp.float32) * scale + offset
    act = half * jnp.tanh(half) + half
    wide_ref[row, 8 : 8 + width, :] = act
    wide_ref[row, 7:8, :] = act[0:1]
    wide_ref[row, 8 + width : 9 + width, :] = act[width - 1 : width]
    for tap in range(3):
        shifted = act if tap == 1 else wide_ref[row, 7 + tap : 7 + tap + width, :]
        taps_ref[row, :, tap * channels : (tap + 1) * channels] = shifted.astype(jnp.bfloat16)


def conv_rows(taps_ref, row, count, weight_ref):
    _, width, lanes = taps_ref.shape
    window = jnp.concatenate(
        [taps_ref[row + tap : row + tap + count].reshape(count * width, lanes) for tap in range(3)],
        axis=1,
    )
    both = jnp.dot(window, weight_ref[...], preferred_element_type=jnp.float32)
    half = both.shape[1] // 2
    return both[:, :half] + both[:, half:]


def first_kernel(
    count, sums_ref, own_ref, pair_ref, other_ref, weight_ref, bias_ref, gain_ref, shift_ref,
    bias_two_ref, gain_two_ref, shift_two_ref,
    hidden_ref, out_ref, next_ref, wide_ref, taps_ref, summed_ref, vectors_ref, sems,
):
    copies = [
        pltpu.make_async_copy(source, vectors_ref.at[i], sems.at[i])
        for i, source in enumerate((bias_two_ref, gain_two_ref, shift_two_ref))
    ]
    for copy in copies:
        copy.start()
    index = lax.axis_index("rows")
    rows, width, channels = own_ref.shape
    even = index % 2 == 0
    scale, offset = scale_offset(sums_ref, gain_ref, shift_ref, rows * width * count)
    sum_weight(weight_ref, summed_ref)

    def make(row):
        if row < 2:
            values = jnp.where(even, other_ref[row], pair_ref[row])
            values = jnp.where(index == 0, own_ref[0], values)
        elif row < rows + 2:
            values = own_ref[row - 2]
        else:
            values = jnp.where(even, pair_ref[row - rows - 2], other_ref[row - rows - 2])
            values = jnp.where(index == count - 1, own_ref[rows - 1], values)
        store_taps(values, scale, offset, wide_ref, taps_ref, row)

    total = jnp.zeros((8, channels), jnp.float32)
    square = jnp.zeros((8, channels), jnp.float32)
    for row in range(rows + 4):
        make(row)
    hidden = conv_rows(taps_ref, 0, rows + 2, summed_ref) + bias_ref[...]
    hidden = hidden.astype(jnp.bfloat16)
    for row in range(rows + 2):
        values = hidden[row * width : (row + 1) * width]
        hidden_ref[row] = values
        if 0 < row <= rows:
            total, square = add_sums(values.astype(jnp.float32), total, square)
    store_sums(total, square, out_ref)
    for i in range(3):
        copies[i].wait()
        next_ref[pl.ds(i, 1), :] = vectors_ref[i]

    @pl.when(index == 0)
    def _():
        hidden_ref[0] = hidden_ref[1]

    @pl.when(index == count - 1)
    def _():
        hidden_ref[rows + 1] = hidden_ref[rows]


def second_kernel(
    count, sums_ref, hidden_ref, own_ref, weight_ref, params_ref,
    out_ref, wide_ref, taps_ref, summed_ref, done_ref, sems,
):
    rows, width, channels = own_ref.shape
    scale, offset = scale_offset(
        sums_ref, params_ref.at[1:2], params_ref.at[2:3], rows * width * count
    )
    sum_weight(weight_ref, summed_ref)
    copies = [
        pltpu.make_async_copy(done_ref.at[row], out_ref.at[row], sems.at[row])
        for row in range(rows)
    ]
    for row in range(rows + 2):
        store_taps(hidden_ref[row], scale, offset, wide_ref, taps_ref, row)
    branch = conv_rows(taps_ref, 0, rows, summed_ref) + params_ref[0:1, :]
    for row in range(rows):
        values = own_ref[row].astype(jnp.float32) + branch[row * width : (row + 1) * width]
        done_ref[row] = values.astype(jnp.bfloat16)
        copies[row].start()
    for copy in copies:
        copy.wait()


def exchanged(sums):
    count = lax.axis_size("rows")
    ends_first = [i // 2 if i % 2 == 0 else count - 1 - i // 2 for i in range(count)]
    return lax.all_to_all(sums, "rows", 0, 0, axis_index_groups=[ends_first])


def body(
    latents, gain_one, shift_one, weight_one, bias_one, gain_two, shift_two, weight_two, bias_two
):
    count = lax.axis_size("rows")
    own = latents[0]
    rows, width, channels = own.shape
    sums_shape = jax.ShapeDtypeStruct((count, 1, channels), jnp.float32)
    taps = weight_one.shape[1] * weight_one.shape[2]
    slab_shape = jax.ShapeDtypeStruct((2, width, channels), jnp.bfloat16)

    def raw(weight):
        return weight.reshape(3, taps, channels, channels)

    swap_pair = [(i, i ^ 1) for i in range(count)]
    swap_other = [(i, i + 1 if i % 2 else i - 1) for i in range(1, count - 1)]

    sums, pair, other = pl.pallas_call(
        sums_kernel,
        out_shape=[sums_shape, slab_shape, slab_shape],
        in_specs=[VMEM],
        out_specs=[VMEM] * 3,
        compiler_params=PARAMS,
        name="sums",
        cost_estimate=pl.CostEstimate(
            flops=40000000000, bytes_accessed=10000000, transcendentals=0
        ),
    )(own)
    other = lax.ppermute(other, "rows", swap_other)
    pair = lax.ppermute(pair, "rows", swap_pair)
    sums = exchanged(sums)
    hidden, sums, params = pl.pallas_call(
        functools.partial(first_kernel, count),
        out_shape=[
            jax.ShapeDtypeStruct((rows + 2, width, channels), jnp.bfloat16),
            sums_shape,
            jax.ShapeDtypeStruct((8, channels), jnp.float32),
        ],
        in_specs=[VMEM] * 8 + [HBM] * 3,
        out_specs=[VMEM] * 3,
        scratch_shapes=[
            pltpu.VMEM((rows + 4, width + 16, channels), jnp.float32),
            pltpu.VMEM((rows + 4, width, 3 * channels), jnp.bfloat16),
            pltpu.VMEM((taps * channels, 2 * channels), jnp.bfloat16),
            pltpu.VMEM((3, 1, channels), jnp.float32),
            pltpu.SemaphoreType.DMA((3,)),
        ],
        compiler_params=PARAMS, name="first",
    )(
        sums,
        own,
        pair,
        other,
        raw(weight_one),
        *[vector.reshape(1, channels) for vector in (bias_one, gain_one, shift_one)],
        *[
            pltpu.with_memory_space_constraint(vector.reshape(1, channels), pltpu.HBM)
            for vector in (bias_two, gain_two, shift_two)
        ],
    )
    sums = exchanged(sums)
    decoded = pl.pallas_call(
        functools.partial(second_kernel, count),
        out_shape=jax.ShapeDtypeStruct(own.shape, jnp.bfloat16),
        in_specs=[VMEM] * 5,
        out_specs=ANY,
        scratch_shapes=[
            pltpu.VMEM((rows + 2, width + 16, channels), jnp.float32),
            pltpu.VMEM((rows + 2, width, 3 * channels), jnp.bfloat16),
            pltpu.VMEM((taps * channels, 2 * channels), jnp.bfloat16),
            pltpu.VMEM(own.shape, jnp.bfloat16),
            pltpu.SemaphoreType.DMA((rows,)),
        ],
        compiler_params=PARAMS, name="second",
    )(sums, hidden, own, raw(weight_two), params)
    return decoded[None]


def solution(mesh):
    return jax.shard_map(
        body,
        mesh=mesh,
        in_specs=(P("groups", "rows", None, None), P(), P(), P(), P(), P(), P(), P(), P()),
        out_specs=P("groups", "rows", None, None),
        check_vma=False,
    )
```

```python
import functools

import jax
import jax.numpy as jnp
from jax import lax
from jax.experimental import pallas as pl
from jax.experimental.pallas import tpu as pltpu
from jax.sharding import PartitionSpec as P

GROUPS = 32
HBM = pl.BlockSpec(memory_space=pltpu.HBM)
ANY = pl.BlockSpec(memory_space=pl.ANY)
VMEM = pl.BlockSpec(memory_space=pltpu.VMEM)
PARAMS = pltpu.CompilerParams(vmem_limit_bytes=24 * 1024 * 1024)


def store_sums(total, square, out_ref):
    channels = total.shape[1]
    per_group = channels // GROUPS
    member = lax.broadcasted_iota(jnp.int32, (8, channels), 1) % per_group

    def grouped(part):
        part = jnp.broadcast_to(jnp.sum(part, axis=0, keepdims=True), (8, channels))
        result = part
        for step in range(1, per_group):
            result += jnp.where(member >= step, pltpu.roll(part, step, 1), 0.0)
            rolled = pltpu.roll(part, channels - step, 1)
            result += jnp.where(member < per_group - step, rolled, 0.0)
        return result

    row = jnp.where(member == 0, grouped(total), grouped(square))[0:1]
    out_ref[...] = jnp.broadcast_to(row[None], out_ref.shape)


def add_sums(values, total, square):
    width, channels = values.shape
    split = (width // 8, 8, channels)
    total += jnp.sum(values.reshape(split), axis=0)
    square += jnp.sum((values * values).reshape(split), axis=0)
    return total, square


def sums_kernel(own_ref, out_ref, pair_ref, other_ref):
    rows, _, channels = own_ref.shape
    even = lax.axis_index("rows") % 2 == 0
    pair_ref[0] = jnp.where(even, own_ref[rows - 1], own_ref[0])
    for row in range(2):
        other_ref[row] = jnp.where(even, own_ref[row], own_ref[rows - 2 + row])
    total = jnp.zeros((8, channels), jnp.float32)
    square = jnp.zeros((8, channels), jnp.float32)
    for row in range(rows):
        total, square = add_sums(own_ref[row].astype(jnp.float32), total, square)
    store_sums(total, square, out_ref)


def sum_weight(source, target):
    taps, channels = source.shape[1], source.shape[2]
    for tap in range(taps):
        total = source[0, tap].astype(jnp.float32)
        total += source[1, tap].astype(jnp.float32)
        total += source[2, tap].astype(jnp.float32)
        high = total.astype(jnp.bfloat16)
        low = (total - high.astype(jnp.float32)).astype(jnp.bfloat16)
        target[pl.ds(tap * channels, channels), :] = jnp.concatenate([high, low], axis=1)


def scale_offset(sums_ref, gain_ref, shift_ref, entries):
    sums = jnp.sum(sums_ref[...], axis=0)
    channels = sums.shape[1]
    per_group = channels // GROUPS
    sums = jnp.broadcast_to(sums, (8, channels)) * (1.0 / (entries * per_group))
    member = lax.broadcasted_iota(jnp.int32, sums.shape, 1) % per_group

    def spread(lane):
        part = jnp.where(member == lane, sums, 0.0)
        result = part
        for target in range(per_group):
            if target != lane:
                result += pltpu.roll(part, (target - lane) % channels, 1)
        return result

    mean = spread(0)
    var = jnp.maximum(spread(1) - mean * mean, 0.0)
    scale = gain_ref[...] * lax.rsqrt(var + 1e-06)
    return 0.5 * scale[0:1], (0.5 * (shift_ref[...] - mean * scale))[0:1]


def store_taps(values, scale, offset, wide_ref, taps_ref, slot, row=None):
    row = slot if row is None else row
    width, channels = values.shape
    half = values.astype(jnp.float32) * scale + offset
    act = half * jnp.tanh(half) + half
    wide_ref[slot, 8 : 8 + width, :] = act
    wide_ref[slot, 7:8, :] = act[0:1]
    wide_ref[slot, 8 + width : 9 + width, :] = act[width - 1 : width]
    for tap in range(3):
        shifted = wide_ref[slot, 7 + tap : 7 + tap + width, :]
        taps_ref[row, :, tap * channels : (tap + 1) * channels] = shifted.astype(jnp.bfloat16)


def window(taps_ref, row, count):
    _, width, lanes = taps_ref.shape
    parts = [
        taps_ref[pl.ds(row + tap, count)].reshape(count * width, lanes) for tap in range(3)
    ]
    return jnp.concatenate(parts, axis=1)


def product(rows, weight_ref):
    both = jnp.dot(rows, weight_ref[...], preferred_element_type=jnp.float32)
    half = both.shape[1] // 2
    return both[:, :half] + both[:, half:]


def first_kernel(
    count, sums_ref, own_ref, pair_ref, other_ref, weight_ref, bias_ref, gain_ref, shift_ref,
    bias_two_ref, gain_two_ref, shift_two_ref,
    hidden_ref, edge_ref, out_ref, next_ref, wide_ref, taps_ref, summed_ref, vectors_ref, sems,
):
    copies = [
        pltpu.make_async_copy(source, vectors_ref.at[i], sems.at[i])
        for i, source in enumerate((bias_two_ref, gain_two_ref, shift_two_ref))
    ]
    for copy in copies:
        copy.start()
    index = lax.axis_index("rows")
    rows, width, channels = own_ref.shape
    even = index % 2 == 0
    scale, offset = scale_offset(sums_ref, gain_ref, shift_ref, rows * width * count)
    sum_weight(weight_ref, summed_ref)

    def make(values, slot, row=None):
        store_taps(values, scale, offset, wide_ref, taps_ref, slot, row)

    for row in range(rows):
        make(own_ref[row], row + 2)
    make(pair_ref[0], 1, jnp.where(even, rows + 2, 1))
    border = jnp.logical_or(index == 0, index == count - 1)
    border_row = jnp.where(even, own_ref[0], own_ref[rows - 1])
    for row, slot in ((0, 0), (1, rows + 2)):
        values = jnp.where(border, border_row, other_ref[row])
        make(values, slot, jnp.where(even, row, rows + 2 + row))
    cross = window(taps_ref, jnp.where(even, 0, rows + 1), 1)
    windows = jnp.concatenate([window(taps_ref, 1, rows), cross], axis=0)
    hidden = (product(windows, summed_ref) + bias_ref[...]).astype(jnp.bfloat16)
    total = jnp.zeros((8, channels), jnp.float32)
    square = jnp.zeros((8, channels), jnp.float32)
    for row in range(rows + 1):
        values = hidden[row * width : (row + 1) * width]
        hidden_ref[row] = values
        if row < rows:
            total, square = add_sums(values.astype(jnp.float32), total, square)
    edge_ref[0] = jnp.where(even, hidden[(rows - 1) * width : rows * width], hidden[:width])
    store_sums(total, square, out_ref)
    for i in range(3):
        copies[i].wait()
        next_ref[pl.ds(i, 1), :] = vectors_ref[i]

    @pl.when(index == 0)
    def _():
        hidden_ref[rows] = hidden_ref[0]

    @pl.when(index == count - 1)
    def _():
        hidden_ref[rows] = hidden_ref[rows - 1]


def second_kernel(
    count, sums_ref, hidden_ref, edge_ref, own_ref, weight_ref, params_ref,
    out_ref, wide_ref, taps_ref, summed_ref, done_ref, sems,
):
    rows, width, channels = own_ref.shape
    scale, offset = scale_offset(
        sums_ref, params_ref.at[1:2], params_ref.at[2:3], rows * width * count
    )
    sum_weight(weight_ref, summed_ref)
    copies = [
        pltpu.make_async_copy(done_ref.at[row], out_ref.at[row], sems.at[row])
        for row in range(rows)
    ]
    even = lax.axis_index("rows") % 2 == 0
    ends = {
        0: jnp.where(even, hidden_ref[rows], edge_ref[0]),
        rows + 1: jnp.where(even, edge_ref[0], hidden_ref[rows]),
    }
    for row in range(rows + 2):
        values = ends[row] if row in ends else hidden_ref[row - 1]
        store_taps(values, scale, offset, wide_ref, taps_ref, row)
    branch = product(window(taps_ref, 0, rows), summed_ref) + params_ref[0:1, :]
    for row in range(rows):
        values = own_ref[row].astype(jnp.float32) + branch[row * width : (row + 1) * width]
        done_ref[row] = values.astype(jnp.bfloat16)
        copies[row].start()
    for copy in copies:
        copy.wait()


def exchanged(sums):
    count = lax.axis_size("rows")
    ends_first = [i // 2 if i % 2 == 0 else count - 1 - i // 2 for i in range(count)]
    return lax.all_to_all(sums, "rows", 0, 0, axis_index_groups=[ends_first])


def body(
    latents, gain_one, shift_one, weight_one, bias_one, gain_two, shift_two, weight_two, bias_two
):
    count = lax.axis_size("rows")
    own = latents[0]
    rows, width, channels = own.shape
    sums_shape = jax.ShapeDtypeStruct((count, 1, channels), jnp.float32)
    taps = weight_one.shape[1] * weight_one.shape[2]
    edge_shape = jax.ShapeDtypeStruct((1, width, channels), jnp.bfloat16)
    slab_shape = jax.ShapeDtypeStruct((2, width, channels), jnp.bfloat16)

    def raw(weight):
        return weight.reshape(3, taps, channels, channels)

    swap_pair = [(i, i ^ 1) for i in range(count)]
    swap_other = [(i, i + 1 if i % 2 else i - 1) for i in range(1, count - 1)]

    sums, pair, other = pl.pallas_call(
        sums_kernel,
        out_shape=[sums_shape, edge_shape, slab_shape],
        in_specs=[VMEM],
        out_specs=[VMEM] * 3,
        compiler_params=PARAMS,
        name="sums",
        cost_estimate=pl.CostEstimate(
            flops=40000000000, bytes_accessed=10000000, transcendentals=0
        ),
    )(own)
    other = lax.ppermute(other, "rows", swap_other)
    pair = lax.ppermute(pair, "rows", swap_pair)
    sums = exchanged(sums)
    hidden, edge, sums, params = pl.pallas_call(
        functools.partial(first_kernel, count),
        out_shape=[
            jax.ShapeDtypeStruct((rows + 1, width, channels), jnp.bfloat16),
            edge_shape,
            sums_shape,
            jax.ShapeDtypeStruct((8, channels), jnp.float32),
        ],
        in_specs=[VMEM] * 8 + [HBM] * 3,
        out_specs=[VMEM] * 4,
        scratch_shapes=[
            pltpu.VMEM((rows + 4, width + 16, channels), jnp.float32),
            pltpu.VMEM((rows + 4, width, 3 * channels), jnp.bfloat16),
            pltpu.VMEM((taps * channels, 2 * channels), jnp.bfloat16),
            pltpu.VMEM((3, 1, channels), jnp.float32),
            pltpu.SemaphoreType.DMA((3,)),
        ],
        compiler_params=PARAMS, name="first",
    )(
        sums,
        own,
        pair,
        other,
        raw(weight_one),
        *[vector.reshape(1, channels) for vector in (bias_one, gain_one, shift_one)],
        *[
            pltpu.with_memory_space_constraint(vector.reshape(1, channels), pltpu.HBM)
            for vector in (bias_two, gain_two, shift_two)
        ],
    )
    edge = lax.ppermute(edge, "rows", swap_pair)
    sums = exchanged(sums)
    decoded = pl.pallas_call(
        functools.partial(second_kernel, count),
        out_shape=jax.ShapeDtypeStruct(own.shape, jnp.bfloat16),
        in_specs=[VMEM] * 6,
        out_specs=ANY,
        scratch_shapes=[
            pltpu.VMEM((rows + 2, width + 16, channels), jnp.float32),
            pltpu.VMEM((rows + 2, width, 3 * channels), jnp.bfloat16),
            pltpu.VMEM((taps * channels, 2 * channels), jnp.bfloat16),
            pltpu.VMEM(own.shape, jnp.bfloat16),
            pltpu.SemaphoreType.DMA((rows,)),
        ],
        compiler_params=PARAMS, name="second",
    )(sums, hidden, edge, own, raw(weight_two), params)
    return decoded[None]


def solution(mesh):
    return jax.shard_map(
        body,
        mesh=mesh,
        in_specs=(P("groups", "rows", None, None), P(), P(), P(), P(), P(), P(), P(), P()),
        out_specs=P("groups", "rows", None, None),
        check_vma=False,
    )
```

```python
import functools

import jax
import jax.numpy as jnp
from jax import lax
from jax.experimental import pallas as pl
from jax.experimental.pallas import tpu as pltpu
from jax.sharding import PartitionSpec as P

GROUPS = 32
HBM = pl.BlockSpec(memory_space=pltpu.HBM)
ANY = pl.BlockSpec(memory_space=pl.ANY)
VMEM = pl.BlockSpec(memory_space=pltpu.VMEM)
PARAMS = pltpu.CompilerParams(vmem_limit_bytes=24 * 1024 * 1024)


def store_sums(total, square, out_ref):
    channels = total.shape[1]
    per_group = channels // GROUPS
    member = lax.broadcasted_iota(jnp.int32, (8, channels), 1) % per_group

    def grouped(part):
        part = jnp.broadcast_to(jnp.sum(part, axis=0, keepdims=True), (8, channels))
        result = part
        for step in range(1, per_group):
            result += jnp.where(member >= step, pltpu.roll(part, step, 1), 0.0)
            rolled = pltpu.roll(part, channels - step, 1)
            result += jnp.where(member < per_group - step, rolled, 0.0)
        return result

    row = jnp.where(member == 0, grouped(total), grouped(square))[0:1]
    out_ref[...] = jnp.broadcast_to(row[None], out_ref.shape)


def add_sums(values, total, square):
    width, channels = values.shape
    split = (width // 8, 8, channels)
    total += jnp.sum(values.reshape(split), axis=0)
    square += jnp.sum((values * values).reshape(split), axis=0)
    return total, square


def sums_kernel(own_ref, out_ref, pair_ref, other_ref):
    rows, _, channels = own_ref.shape
    even = lax.axis_index("rows") % 2 == 0
    pair_ref[0] = jnp.where(even, own_ref[rows - 1], own_ref[0])
    for row in range(2):
        other_ref[row] = jnp.where(even, own_ref[row], own_ref[rows - 2 + row])
    total = jnp.zeros((8, channels), jnp.float32)
    square = jnp.zeros((8, channels), jnp.float32)
    for row in range(rows):
        total, square = add_sums(own_ref[row].astype(jnp.float32), total, square)
    store_sums(total, square, out_ref)


def sum_weight(source, target):
    taps, channels = source.shape[1], source.shape[2]
    for tap in range(taps):
        total = source[0, tap].astype(jnp.float32)
        total += source[1, tap].astype(jnp.float32)
        total += source[2, tap].astype(jnp.float32)
        high = total.astype(jnp.bfloat16)
        low = (total - high.astype(jnp.float32)).astype(jnp.bfloat16)
        target[pl.ds(tap * channels, channels), :] = jnp.concatenate([high, low], axis=1)


def scale_offset(sums_ref, gain_ref, shift_ref, entries):
    sums = jnp.sum(sums_ref[...], axis=0)
    channels = sums.shape[1]
    per_group = channels // GROUPS
    sums = jnp.broadcast_to(sums, (8, channels)) * (1.0 / (entries * per_group))
    member = lax.broadcasted_iota(jnp.int32, sums.shape, 1) % per_group

    def spread(lane):
        part = jnp.where(member == lane, sums, 0.0)
        result = part
        for target in range(per_group):
            if target != lane:
                result += pltpu.roll(part, (target - lane) % channels, 1)
        return result

    mean = spread(0)
    var = jnp.maximum(spread(1) - mean * mean, 0.0)
    scale = gain_ref[...] * lax.rsqrt(var + 1e-06)
    return 0.5 * scale[0:1], (0.5 * (shift_ref[...] - mean * scale))[0:1]


def store_taps(values, scale, offset, wide_ref, taps_ref, row):
    width, channels = values.shape
    half = values.astype(jnp.float32) * scale + offset
    act = half * jnp.tanh(half) + half
    wide_ref[row, 8 : 8 + width, :] = act
    wide_ref[row, 7:8, :] = act[0:1]
    wide_ref[row, 8 + width : 9 + width, :] = act[width - 1 : width]
    for tap in range(3):
        shifted = wide_ref[row, 7 + tap : 7 + tap + width, :]
        taps_ref[row, :, tap * channels : (tap + 1) * channels] = shifted.astype(jnp.bfloat16)


def window(taps_ref, row, count):
    _, width, lanes = taps_ref.shape
    parts = [
        taps_ref[row + tap : row + tap + count].reshape(count * width, lanes) for tap in range(3)
    ]
    return jnp.concatenate(parts, axis=1)


def product(rows, weight_ref):
    both = jnp.dot(rows, weight_ref[...], preferred_element_type=jnp.float32)
    half = both.shape[1] // 2
    return both[:, :half] + both[:, half:]


def first_kernel(
    count, sums_ref, own_ref, pair_ref, other_ref, weight_ref, bias_ref, gain_ref, shift_ref,
    bias_two_ref, gain_two_ref, shift_two_ref,
    hidden_ref, edge_ref, out_ref, next_ref, wide_ref, taps_ref, summed_ref, vectors_ref, sems,
):
    copies = [
        pltpu.make_async_copy(source, vectors_ref.at[i], sems.at[i])
        for i, source in enumerate((bias_two_ref, gain_two_ref, shift_two_ref))
    ]
    for copy in copies:
        copy.start()
    index = lax.axis_index("rows")
    rows, width, channels = own_ref.shape
    even = index % 2 == 0
    scale, offset = scale_offset(sums_ref, gain_ref, shift_ref, rows * width * count)
    sum_weight(weight_ref, summed_ref)

    def make(values, slot):
        store_taps(values, scale, offset, wide_ref, taps_ref, slot)

    border = jnp.logical_or(index == 0, index == count - 1)
    border_row = jnp.where(even, own_ref[0], own_ref[rows - 1])
    outer = [jnp.where(border, border_row, other_ref[row]) for row in range(2)]
    make(jnp.where(even, outer[1], pair_ref[0]), 0)
    for row in range(rows):
        make(own_ref[row], row + 1)
    make(jnp.where(even, pair_ref[0], outer[0]), rows + 1)
    make(jnp.where(even, outer[0], own_ref[rows - 1]), rows + 2)
    make(jnp.where(even, outer[1], outer[0]), rows + 3)
    make(jnp.where(even, own_ref[0], outer[1]), rows + 4)
    cross = window(taps_ref, rows + 2, 1)
    windows = jnp.concatenate([window(taps_ref, 0, rows), cross], axis=0)
    hidden = (product(windows, summed_ref) + bias_ref[...]).astype(jnp.bfloat16)
    total = jnp.zeros((8, channels), jnp.float32)
    square = jnp.zeros((8, channels), jnp.float32)
    for row in range(rows + 1):
        values = hidden[row * width : (row + 1) * width]
        hidden_ref[row] = values
        if row < rows:
            total, square = add_sums(values.astype(jnp.float32), total, square)
    edge_ref[0] = jnp.where(even, hidden[(rows - 1) * width : rows * width], hidden[:width])
    store_sums(total, square, out_ref)
    for i in range(3):
        copies[i].wait()
        next_ref[pl.ds(i, 1), :] = vectors_ref[i]

    @pl.when(index == 0)
    def _():
        hidden_ref[rows] = hidden_ref[0]

    @pl.when(index == count - 1)
    def _():
        hidden_ref[rows] = hidden_ref[rows - 1]


def second_kernel(
    count, sums_ref, hidden_ref, edge_ref, own_ref, weight_ref, params_ref,
    out_ref, wide_ref, taps_ref, summed_ref, done_ref, sems,
):
    rows, width, channels = own_ref.shape
    scale, offset = scale_offset(
        sums_ref, params_ref.at[1:2], params_ref.at[2:3], rows * width * count
    )
    sum_weight(weight_ref, summed_ref)
    copies = [
        pltpu.make_async_copy(done_ref.at[row], out_ref.at[row], sems.at[row])
        for row in range(rows)
    ]
    even = lax.axis_index("rows") % 2 == 0
    ends = {
        0: jnp.where(even, hidden_ref[rows], edge_ref[0]),
        rows + 1: jnp.where(even, edge_ref[0], hidden_ref[rows]),
    }
    for row in range(rows + 2):
        values = ends[row] if row in ends else hidden_ref[row - 1]
        store_taps(values, scale, offset, wide_ref, taps_ref, row)
    branch = product(window(taps_ref, 0, rows), summed_ref) + params_ref[0:1, :]
    for row in range(rows):
        values = own_ref[row].astype(jnp.float32) + branch[row * width : (row + 1) * width]
        done_ref[row] = values.astype(jnp.bfloat16)
        copies[row].start()
    for copy in copies:
        copy.wait()


def exchanged(sums):
    count = lax.axis_size("rows")
    ends_first = [i // 2 if i % 2 == 0 else count - 1 - i // 2 for i in range(count)]
    return lax.all_to_all(sums, "rows", 0, 0, axis_index_groups=[ends_first])


def body(
    latents, gain_one, shift_one, weight_one, bias_one, gain_two, shift_two, weight_two, bias_two
):
    count = lax.axis_size("rows")
    own = latents[0]
    rows, width, channels = own.shape
    sums_shape = jax.ShapeDtypeStruct((count, 1, channels), jnp.float32)
    taps = weight_one.shape[1] * weight_one.shape[2]
    edge_shape = jax.ShapeDtypeStruct((1, width, channels), jnp.bfloat16)
    slab_shape = jax.ShapeDtypeStruct((2, width, channels), jnp.bfloat16)

    def raw(weight):
        return weight.reshape(3, taps, channels, channels)

    swap_pair = [(i, i ^ 1) for i in range(count)]
    swap_other = [(i, i + 1 if i % 2 else i - 1) for i in range(1, count - 1)]

    sums, pair, other = pl.pallas_call(
        sums_kernel,
        out_shape=[sums_shape, edge_shape, slab_shape],
        in_specs=[VMEM],
        out_specs=[VMEM] * 3,
        compiler_params=PARAMS,
        name="sums",
        cost_estimate=pl.CostEstimate(
            flops=40000000000, bytes_accessed=10000000, transcendentals=0
        ),
    )(own)
    other = lax.ppermute(other, "rows", swap_other)
    pair = lax.ppermute(pair, "rows", swap_pair)
    sums = exchanged(sums)
    hidden, edge, sums, params = pl.pallas_call(
        functools.partial(first_kernel, count),
        out_shape=[
            jax.ShapeDtypeStruct((rows + 1, width, channels), jnp.bfloat16),
            edge_shape,
            sums_shape,
            jax.ShapeDtypeStruct((8, channels), jnp.float32),
        ],
        in_specs=[VMEM] * 8 + [HBM] * 3,
        out_specs=[VMEM] * 4,
        scratch_shapes=[
            pltpu.VMEM((rows + 5, width + 16, channels), jnp.float32),
            pltpu.VMEM((rows + 5, width, 3 * channels), jnp.bfloat16),
            pltpu.VMEM((taps * channels, 2 * channels), jnp.bfloat16),
            pltpu.VMEM((3, 1, channels), jnp.float32),
            pltpu.SemaphoreType.DMA((3,)),
        ],
        compiler_params=PARAMS, name="first",
    )(
        sums,
        own,
        pair,
        other,
        raw(weight_one),
        *[vector.reshape(1, channels) for vector in (bias_one, gain_one, shift_one)],
        *[
            pltpu.with_memory_space_constraint(vector.reshape(1, channels), pltpu.HBM)
            for vector in (bias_two, gain_two, shift_two)
        ],
    )
    edge = lax.ppermute(edge, "rows", swap_pair)
    sums = exchanged(sums)
    decoded = pl.pallas_call(
        functools.partial(second_kernel, count),
        out_shape=jax.ShapeDtypeStruct(own.shape, jnp.bfloat16),
        in_specs=[VMEM] * 6,
        out_specs=ANY,
        scratch_shapes=[
            pltpu.VMEM((rows + 2, width + 16, channels), jnp.float32),
            pltpu.VMEM((rows + 2, width, 3 * channels), jnp.bfloat16),
            pltpu.VMEM((taps * channels, 2 * channels), jnp.bfloat16),
            pltpu.VMEM(own.shape, jnp.bfloat16),
            pltpu.SemaphoreType.DMA((rows,)),
        ],
        compiler_params=PARAMS, name="second",
    )(sums, hidden, edge, own, raw(weight_two), params)
    return decoded[None]


def solution(mesh):
    return jax.shard_map(
        body,
        mesh=mesh,
        in_specs=(P("groups", "rows", None, None), P(), P(), P(), P(), P(), P(), P(), P()),
        out_specs=P("groups", "rows", None, None),
        check_vma=False,
    )
```

```python
import functools

import jax
import jax.numpy as jnp
from jax import lax
from jax.experimental import pallas as pl
from jax.experimental.pallas import tpu as pltpu
from jax.sharding import PartitionSpec as P

GROUPS = 32
HBM = pl.BlockSpec(memory_space=pltpu.HBM)
ANY = pl.BlockSpec(memory_space=pl.ANY)
VMEM = pl.BlockSpec(memory_space=pltpu.VMEM)
PARAMS = pltpu.CompilerParams(vmem_limit_bytes=24 * 1024 * 1024)


def store_sums(total, square, out_ref):
    channels = total.shape[1]
    per_group = channels // GROUPS
    member = lax.broadcasted_iota(jnp.int32, (8, channels), 1) % per_group

    def grouped(part):
        part = jnp.broadcast_to(jnp.sum(part, axis=0, keepdims=True), (8, channels))
        result = part
        for step in range(1, per_group):
            result += jnp.where(member >= step, pltpu.roll(part, step, 1), 0.0)
            rolled = pltpu.roll(part, channels - step, 1)
            result += jnp.where(member < per_group - step, rolled, 0.0)
        return result

    row = jnp.where(member == 0, grouped(total), grouped(square))[0:1]
    out_ref[...] = jnp.broadcast_to(row[None], out_ref.shape)


def add_sums(values, total, square):
    width, channels = values.shape
    split = (width // 8, 8, channels)
    total += jnp.sum(values.reshape(split), axis=0)
    square += jnp.sum((values * values).reshape(split), axis=0)
    return total, square


def sums_kernel(own_ref, out_ref, pair_ref, other_ref):
    rows, _, channels = own_ref.shape
    even = lax.axis_index("rows") % 2 == 0
    pair_ref[0] = jnp.where(even, own_ref[rows - 1], own_ref[0])
    for row in range(2):
        other_ref[row] = jnp.where(even, own_ref[row], own_ref[rows - 2 + row])
    total = jnp.zeros((8, channels), jnp.float32)
    square = jnp.zeros((8, channels), jnp.float32)
    for row in range(rows):
        total, square = add_sums(own_ref[row].astype(jnp.float32), total, square)
    store_sums(total, square, out_ref)


def sum_weight(source, target):
    taps, channels = source.shape[1], source.shape[2]
    for tap in range(taps):
        total = source[0, tap].astype(jnp.float32)
        total += source[1, tap].astype(jnp.float32)
        total += source[2, tap].astype(jnp.float32)
        high = total.astype(jnp.bfloat16)
        low = (total - high.astype(jnp.float32)).astype(jnp.bfloat16)
        target[pl.ds(tap * channels, channels), :] = jnp.concatenate([high, low], axis=1)


def scale_offset(sums_ref, gain_ref, shift_ref, entries):
    sums = jnp.sum(sums_ref[...], axis=0)
    channels = sums.shape[1]
    per_group = channels // GROUPS
    sums = jnp.broadcast_to(sums, (8, channels)) * (1.0 / (entries * per_group))
    member = lax.broadcasted_iota(jnp.int32, sums.shape, 1) % per_group

    def spread(lane):
        part = jnp.where(member == lane, sums, 0.0)
        result = part
        for target in range(per_group):
            if target != lane:
                result += pltpu.roll(part, (target - lane) % channels, 1)
        return result

    mean = spread(0)
    var = jnp.maximum(spread(1) - mean * mean, 0.0)
    scale = gain_ref[...] * lax.rsqrt(var + 1e-06)
    return 0.5 * scale[0:1], (0.5 * (shift_ref[...] - mean * scale))[0:1]


def store_taps(values, scale, offset, wide_ref, taps_ref, row):
    width, channels = values.shape
    half = values.astype(jnp.float32) * scale + offset
    act = half * jnp.tanh(half) + half
    wide_ref[row, 8 : 8 + width, :] = act
    wide_ref[row, 7:8, :] = act[0:1]
    wide_ref[row, 8 + width : 9 + width, :] = act[width - 1 : width]
    for tap in range(3):
        shifted = wide_ref[row, 7 + tap : 7 + tap + width, :]
        taps_ref[row, :, tap * channels : (tap + 1) * channels] = shifted.astype(jnp.bfloat16)


def window(taps_ref, row, count):
    _, width, lanes = taps_ref.shape
    parts = [
        taps_ref[row + tap : row + tap + count].reshape(count * width, lanes) for tap in range(3)
    ]
    return jnp.concatenate(parts, axis=1)


def product(rows, weight_ref):
    both = jnp.dot(rows, weight_ref[...], preferred_element_type=jnp.float32)
    half = both.shape[1] // 2
    return both[:, :half] + both[:, half:]


def first_kernel(
    count, sums_ref, own_ref, pair_ref, other_ref, weight_ref, bias_ref, gain_ref, shift_ref,
    bias_two_ref, gain_two_ref, shift_two_ref,
    hidden_ref, edge_ref, out_ref, next_ref, wide_ref, taps_ref, summed_ref, vectors_ref, sems,
):
    copies = [
        pltpu.make_async_copy(source, vectors_ref.at[i], sems.at[i])
        for i, source in enumerate((bias_two_ref, gain_two_ref, shift_two_ref))
    ]
    for copy in copies:
        copy.start()
    index = lax.axis_index("rows")
    rows, width, channels = own_ref.shape
    even = index % 2 == 0
    scale, offset = scale_offset(sums_ref, gain_ref, shift_ref, rows * width * count)
    sum_weight(weight_ref, summed_ref)

    def make(values, slot):
        store_taps(values, scale, offset, wide_ref, taps_ref, slot)

    border = jnp.logical_or(index == 0, index == count - 1)
    border_row = jnp.where(even, own_ref[0], own_ref[rows - 1])
    outer = [jnp.where(border, border_row, other_ref[row]) for row in range(2)]
    make(jnp.where(even, outer[1], pair_ref[0]), 0)
    for row in range(rows):
        make(own_ref[row], row + 1)
    make(jnp.where(even, pair_ref[0], outer[0]), rows + 1)
    make(jnp.where(even, outer[0], own_ref[rows - 1]), rows + 2)
    make(jnp.where(even, outer[1], outer[0]), rows + 3)
    make(jnp.where(even, own_ref[0], outer[1]), rows + 4)
    total = jnp.zeros((8, channels), jnp.float32)
    square = jnp.zeros((8, channels), jnp.float32)
    hidden = product(window(taps_ref, 0, rows), summed_ref) + bias_ref[...]
    hidden = hidden.astype(jnp.bfloat16)
    for row in range(rows):
        values = hidden[row * width : (row + 1) * width]
        hidden_ref[row] = values
        total, square = add_sums(values.astype(jnp.float32), total, square)
    cross = product(window(taps_ref, rows + 2, 1), summed_ref) + bias_ref[...]
    hidden_ref[rows] = cross.astype(jnp.bfloat16)
    edge_ref[0] = jnp.where(even, hidden[(rows - 1) * width : rows * width], hidden[:width])
    store_sums(total, square, out_ref)
    for i in range(3):
        copies[i].wait()
        next_ref[pl.ds(i, 1), :] = vectors_ref[i]

    @pl.when(index == 0)
    def _():
        hidden_ref[rows] = hidden_ref[0]

    @pl.when(index == count - 1)
    def _():
        hidden_ref[rows] = hidden_ref[rows - 1]


def second_kernel(
    count, sums_ref, hidden_ref, edge_ref, own_ref, weight_ref, params_ref,
    out_ref, wide_ref, taps_ref, summed_ref, done_ref, sems,
):
    rows, width, channels = own_ref.shape
    scale, offset = scale_offset(
        sums_ref, params_ref.at[1:2], params_ref.at[2:3], rows * width * count
    )
    sum_weight(weight_ref, summed_ref)
    copies = [
        pltpu.make_async_copy(done_ref.at[row], out_ref.at[row], sems.at[row])
        for row in range(rows)
    ]
    even = lax.axis_index("rows") % 2 == 0
    ends = {
        0: jnp.where(even, hidden_ref[rows], edge_ref[0]),
        rows + 1: jnp.where(even, edge_ref[0], hidden_ref[rows]),
    }
    for row in range(rows + 2):
        values = ends[row] if row in ends else hidden_ref[row - 1]
        store_taps(values, scale, offset, wide_ref, taps_ref, row)
    branch = product(window(taps_ref, 0, rows), summed_ref) + params_ref[0:1, :]
    for row in range(rows):
        values = own_ref[row].astype(jnp.float32) + branch[row * width : (row + 1) * width]
        done_ref[row] = values.astype(jnp.bfloat16)
        copies[row].start()
    for copy in copies:
        copy.wait()


def exchanged(sums):
    count = lax.axis_size("rows")
    ends_first = [i // 2 if i % 2 == 0 else count - 1 - i // 2 for i in range(count)]
    return lax.all_to_all(sums, "rows", 0, 0, axis_index_groups=[ends_first])


def body(
    latents, gain_one, shift_one, weight_one, bias_one, gain_two, shift_two, weight_two, bias_two
):
    count = lax.axis_size("rows")
    own = latents[0]
    rows, width, channels = own.shape
    sums_shape = jax.ShapeDtypeStruct((count, 1, channels), jnp.float32)
    taps = weight_one.shape[1] * weight_one.shape[2]
    edge_shape = jax.ShapeDtypeStruct((1, width, channels), jnp.bfloat16)
    slab_shape = jax.ShapeDtypeStruct((2, width, channels), jnp.bfloat16)

    def raw(weight):
        return weight.reshape(3, taps, channels, channels)

    swap_pair = [(i, i ^ 1) for i in range(count)]
    swap_other = [(i, i + 1 if i % 2 else i - 1) for i in range(1, count - 1)]

    sums, pair, other = pl.pallas_call(
        sums_kernel,
        out_shape=[sums_shape, edge_shape, slab_shape],
        in_specs=[VMEM],
        out_specs=[VMEM] * 3,
        compiler_params=PARAMS,
        name="sums",
        cost_estimate=pl.CostEstimate(
            flops=40000000000, bytes_accessed=10000000, transcendentals=0
        ),
    )(own)
    other = lax.ppermute(other, "rows", swap_other)
    pair = lax.ppermute(pair, "rows", swap_pair)
    sums = exchanged(sums)
    hidden, edge, sums, params = pl.pallas_call(
        functools.partial(first_kernel, count),
        out_shape=[
            jax.ShapeDtypeStruct((rows + 1, width, channels), jnp.bfloat16),
            edge_shape,
            sums_shape,
            jax.ShapeDtypeStruct((8, channels), jnp.float32),
        ],
        in_specs=[VMEM] * 8 + [HBM] * 3,
        out_specs=[VMEM] * 4,
        scratch_shapes=[
            pltpu.VMEM((rows + 5, width + 16, channels), jnp.float32),
            pltpu.VMEM((rows + 5, width, 3 * channels), jnp.bfloat16),
            pltpu.VMEM((taps * channels, 2 * channels), jnp.bfloat16),
            pltpu.VMEM((3, 1, channels), jnp.float32),
            pltpu.SemaphoreType.DMA((3,)),
        ],
        compiler_params=PARAMS, name="first",
    )(
        sums,
        own,
        pair,
        other,
        raw(weight_one),
        *[vector.reshape(1, channels) for vector in (bias_one, gain_one, shift_one)],
        *[
            pltpu.with_memory_space_constraint(vector.reshape(1, channels), pltpu.HBM)
            for vector in (bias_two, gain_two, shift_two)
        ],
    )
    edge = lax.ppermute(edge, "rows", swap_pair)
    sums = exchanged(sums)
    decoded = pl.pallas_call(
        functools.partial(second_kernel, count),
        out_shape=jax.ShapeDtypeStruct(own.shape, jnp.bfloat16),
        in_specs=[VMEM] * 6,
        out_specs=ANY,
        scratch_shapes=[
            pltpu.VMEM((rows + 2, width + 16, channels), jnp.float32),
            pltpu.VMEM((rows + 2, width, 3 * channels), jnp.bfloat16),
            pltpu.VMEM((taps * channels, 2 * channels), jnp.bfloat16),
            pltpu.VMEM(own.shape, jnp.bfloat16),
            pltpu.SemaphoreType.DMA((rows,)),
        ],
        compiler_params=PARAMS, name="second",
    )(sums, hidden, edge, own, raw(weight_two), params)
    return decoded[None]


def solution(mesh):
    return jax.shard_map(
        body,
        mesh=mesh,
        in_specs=(P("groups", "rows", None, None), P(), P(), P(), P(), P(), P(), P(), P()),
        out_specs=P("groups", "rows", None, None),
        check_vma=False,
    )
```

```python
import functools

import jax
import jax.numpy as jnp
from jax import lax
from jax.experimental import pallas as pl
from jax.experimental.pallas import tpu as pltpu
from jax.sharding import PartitionSpec as P

GROUPS = 32
HBM = pl.BlockSpec(memory_space=pltpu.HBM)
ANY = pl.BlockSpec(memory_space=pl.ANY)
VMEM = pl.BlockSpec(memory_space=pltpu.VMEM)
PARAMS = pltpu.CompilerParams(vmem_limit_bytes=24 * 1024 * 1024)


def store_sums(total, square, out_ref):
    channels = total.shape[1]
    per_group = channels // GROUPS
    member = lax.broadcasted_iota(jnp.int32, (8, channels), 1) % per_group

    def grouped(part):
        part = jnp.broadcast_to(jnp.sum(part, axis=0, keepdims=True), (8, channels))
        result = part
        for step in range(1, per_group):
            result += jnp.where(member >= step, pltpu.roll(part, step, 1), 0.0)
            rolled = pltpu.roll(part, channels - step, 1)
            result += jnp.where(member < per_group - step, rolled, 0.0)
        return result

    row = jnp.where(member == 0, grouped(total), grouped(square))[0:1]
    out_ref[...] = jnp.broadcast_to(row[None], out_ref.shape)


def add_sums(values, total, square):
    width, channels = values.shape
    split = (width // 8, 8, channels)
    total += jnp.sum(values.reshape(split), axis=0)
    square += jnp.sum((values * values).reshape(split), axis=0)
    return total, square


def sums_kernel(own_ref, out_ref, pair_ref, other_ref):
    rows, _, channels = own_ref.shape
    even = lax.axis_index("rows") % 2 == 0
    pair_ref[0] = jnp.where(even, own_ref[rows - 1], own_ref[0])
    for row in range(2):
        other_ref[row] = jnp.where(even, own_ref[row], own_ref[rows - 2 + row])
    total = jnp.zeros((8, channels), jnp.float32)
    square = jnp.zeros((8, channels), jnp.float32)
    for row in range(rows):
        total, square = add_sums(own_ref[row].astype(jnp.float32), total, square)
    store_sums(total, square, out_ref)


def sum_weight(source, target):
    taps, channels = source.shape[1], source.shape[2]
    for tap in range(taps):
        total = source[0, tap].astype(jnp.float32)
        total += source[1, tap].astype(jnp.float32)
        total += source[2, tap].astype(jnp.float32)
        high = total.astype(jnp.bfloat16)
        low = (total - high.astype(jnp.float32)).astype(jnp.bfloat16)
        target[pl.ds(tap * channels, channels), :] = jnp.concatenate([high, low], axis=1)


def scale_offset(sums_ref, gain_ref, shift_ref, entries):
    sums = jnp.sum(sums_ref[...], axis=0)
    channels = sums.shape[1]
    per_group = channels // GROUPS
    sums = jnp.broadcast_to(sums, (8, channels)) * (1.0 / (entries * per_group))
    member = lax.broadcasted_iota(jnp.int32, sums.shape, 1) % per_group

    def spread(lane):
        part = jnp.where(member == lane, sums, 0.0)
        result = part
        for target in range(per_group):
            if target != lane:
                result += pltpu.roll(part, (target - lane) % channels, 1)
        return result

    mean = spread(0)
    var = jnp.maximum(spread(1) - mean * mean, 0.0)
    scale = gain_ref[...] * lax.rsqrt(var + 1e-06)
    return 0.5 * scale[0:1], (0.5 * (shift_ref[...] - mean * scale))[0:1]


def store_taps(values, scale, offset, wide_ref, taps_ref, row):
    width, channels = values.shape
    half = values.astype(jnp.float32) * scale + offset
    act = half * jnp.tanh(half) + half
    wide_ref[row, 8 : 8 + width, :] = act
    wide_ref[row, 7:8, :] = act[0:1]
    wide_ref[row, 8 + width : 9 + width, :] = act[width - 1 : width]
    for tap in range(3):
        shifted = wide_ref[row, 7 + tap : 7 + tap + width, :]
        taps_ref[row, :, tap * channels : (tap + 1) * channels] = shifted.astype(jnp.bfloat16)


def window(taps_ref, row, count):
    _, width, lanes = taps_ref.shape
    parts = [
        taps_ref[row + tap : row + tap + count].reshape(count * width, lanes) for tap in range(3)
    ]
    return jnp.concatenate(parts, axis=1)


def product(rows, weight_ref):
    both = jnp.dot(rows, weight_ref[...], preferred_element_type=jnp.float32)
    half = both.shape[1] // 2
    return both[:, :half] + both[:, half:]


def first_kernel(
    count, sums_ref, own_ref, pair_ref, other_ref, weight_ref, bias_ref, gain_ref, shift_ref,
    bias_two_ref, gain_two_ref, shift_two_ref,
    hidden_ref, edge_ref, out_ref, next_ref, wide_ref, taps_ref, summed_ref, vectors_ref, sems,
):
    copies = [
        pltpu.make_async_copy(source, vectors_ref.at[i], sems.at[i])
        for i, source in enumerate((bias_two_ref, gain_two_ref, shift_two_ref))
    ]
    index = lax.axis_index("rows")
    rows, width, channels = own_ref.shape
    even = index % 2 == 0
    scale, offset = scale_offset(sums_ref, gain_ref, shift_ref, rows * width * count)
    sum_weight(weight_ref, summed_ref)
    for copy in copies:
        copy.start()

    def make(values, slot):
        store_taps(values, scale, offset, wide_ref, taps_ref, slot)

    border = jnp.logical_or(index == 0, index == count - 1)
    border_row = jnp.where(even, own_ref[0], own_ref[rows - 1])
    outer = [jnp.where(border, border_row, other_ref[row]) for row in range(2)]
    make(jnp.where(even, outer[1], pair_ref[0]), 0)
    for row in range(rows):
        make(own_ref[row], row + 1)
    make(jnp.where(even, pair_ref[0], outer[0]), rows + 1)
    make(jnp.where(even, outer[0], own_ref[rows - 1]), rows + 2)
    make(jnp.where(even, outer[1], outer[0]), rows + 3)
    make(jnp.where(even, own_ref[0], outer[1]), rows + 4)
    total = jnp.zeros((8, channels), jnp.float32)
    square = jnp.zeros((8, channels), jnp.float32)
    hidden = product(window(taps_ref, 0, rows), summed_ref) + bias_ref[...]
    hidden = hidden.astype(jnp.bfloat16)
    for row in range(rows):
        values = hidden[row * width : (row + 1) * width]
        hidden_ref[row] = values
        total, square = add_sums(values.astype(jnp.float32), total, square)
    cross = product(window(taps_ref, rows + 2, 1), summed_ref) + bias_ref[...]
    hidden_ref[rows] = cross.astype(jnp.bfloat16)
    edge_ref[0] = jnp.where(even, hidden[(rows - 1) * width : rows * width], hidden[:width])
    store_sums(total, square, out_ref)
    for i in range(3):
        copies[i].wait()
        next_ref[pl.ds(i, 1), :] = vectors_ref[i]

    @pl.when(index == 0)
    def _():
        hidden_ref[rows] = hidden_ref[0]

    @pl.when(index == count - 1)
    def _():
        hidden_ref[rows] = hidden_ref[rows - 1]


def second_kernel(
    count, sums_ref, hidden_ref, edge_ref, own_ref, weight_ref, params_ref,
    out_ref, wide_ref, taps_ref, summed_ref, done_ref, sems,
):
    rows, width, channels = own_ref.shape
    scale, offset = scale_offset(
        sums_ref, params_ref.at[1:2], params_ref.at[2:3], rows * width * count
    )
    sum_weight(weight_ref, summed_ref)
    copies = [
        pltpu.make_async_copy(done_ref.at[row], out_ref.at[row], sems.at[row])
        for row in range(rows)
    ]
    even = lax.axis_index("rows") % 2 == 0
    ends = {
        0: jnp.where(even, hidden_ref[rows], edge_ref[0]),
        rows + 1: jnp.where(even, edge_ref[0], hidden_ref[rows]),
    }
    for row in range(rows + 2):
        values = ends[row] if row in ends else hidden_ref[row - 1]
        store_taps(values, scale, offset, wide_ref, taps_ref, row)
    branch = product(window(taps_ref, 0, rows), summed_ref) + params_ref[0:1, :]
    for row in range(rows):
        values = own_ref[row].astype(jnp.float32) + branch[row * width : (row + 1) * width]
        done_ref[row] = values.astype(jnp.bfloat16)
        copies[row].start()
    for copy in copies:
        copy.wait()


def exchanged(sums):
    count = lax.axis_size("rows")
    ends_first = [i // 2 if i % 2 == 0 else count - 1 - i // 2 for i in range(count)]
    return lax.all_to_all(sums, "rows", 0, 0, axis_index_groups=[ends_first])


def body(
    latents, gain_one, shift_one, weight_one, bias_one, gain_two, shift_two, weight_two, bias_two
):
    count = lax.axis_size("rows")
    own = latents[0]
    rows, width, channels = own.shape
    sums_shape = jax.ShapeDtypeStruct((count, 1, channels), jnp.float32)
    taps = weight_one.shape[1] * weight_one.shape[2]
    edge_shape = jax.ShapeDtypeStruct((1, width, channels), jnp.bfloat16)
    slab_shape = jax.ShapeDtypeStruct((2, width, channels), jnp.bfloat16)

    def raw(weight):
        return weight.reshape(3, taps, channels, channels)

    swap_pair = [(i, i ^ 1) for i in range(count)]
    swap_other = [(i, i + 1 if i % 2 else i - 1) for i in range(1, count - 1)]

    sums, pair, other = pl.pallas_call(
        sums_kernel,
        out_shape=[sums_shape, edge_shape, slab_shape],
        in_specs=[VMEM],
        out_specs=[VMEM] * 3,
        compiler_params=PARAMS,
        name="sums",
        cost_estimate=pl.CostEstimate(
            flops=40000000000, bytes_accessed=10000000, transcendentals=0
        ),
    )(own)
    other = lax.ppermute(other, "rows", swap_other)
    pair = lax.ppermute(pair, "rows", swap_pair)
    sums = exchanged(sums)
    hidden, edge, sums, params = pl.pallas_call(
        functools.partial(first_kernel, count),
        out_shape=[
            jax.ShapeDtypeStruct((rows + 1, width, channels), jnp.bfloat16),
            edge_shape,
            sums_shape,
            jax.ShapeDtypeStruct((8, channels), jnp.float32),
        ],
        in_specs=[VMEM] * 8 + [HBM] * 3,
        out_specs=[VMEM] * 4,
        scratch_shapes=[
            pltpu.VMEM((rows + 5, width + 16, channels), jnp.float32),
            pltpu.VMEM((rows + 5, width, 3 * channels), jnp.bfloat16),
            pltpu.VMEM((taps * channels, 2 * channels), jnp.bfloat16),
            pltpu.VMEM((3, 1, channels), jnp.float32),
            pltpu.SemaphoreType.DMA((3,)),
        ],
        compiler_params=PARAMS, name="first",
    )(
        sums,
        own,
        pair,
        other,
        raw(weight_one),
        *[vector.reshape(1, channels) for vector in (bias_one, gain_one, shift_one)],
        *[
            pltpu.with_memory_space_constraint(vector.reshape(1, channels), pltpu.HBM)
            for vector in (bias_two, gain_two, shift_two)
        ],
    )
    edge = lax.ppermute(edge, "rows", swap_pair)
    sums = exchanged(sums)
    decoded = pl.pallas_call(
        functools.partial(second_kernel, count),
        out_shape=jax.ShapeDtypeStruct(own.shape, jnp.bfloat16),
        in_specs=[VMEM] * 6,
        out_specs=ANY,
        scratch_shapes=[
            pltpu.VMEM((rows + 2, width + 16, channels), jnp.float32),
            pltpu.VMEM((rows + 2, width, 3 * channels), jnp.bfloat16),
            pltpu.VMEM((taps * channels, 2 * channels), jnp.bfloat16),
            pltpu.VMEM(own.shape, jnp.bfloat16),
            pltpu.SemaphoreType.DMA((rows,)),
        ],
        compiler_params=PARAMS, name="second",
    )(sums, hidden, edge, own, raw(weight_two), params)
    return decoded[None]


def solution(mesh):
    return jax.shard_map(
        body,
        mesh=mesh,
        in_specs=(P("groups", "rows", None, None), P(), P(), P(), P(), P(), P(), P(), P()),
        out_specs=P("groups", "rows", None, None),
        check_vma=False,
    )
```

```python
import functools

import jax
import jax.numpy as jnp
from jax import lax
from jax.experimental import pallas as pl
from jax.experimental.pallas import tpu as pltpu
from jax.sharding import PartitionSpec as P

GROUPS = 32
HBM = pl.BlockSpec(memory_space=pltpu.HBM)
ANY = pl.BlockSpec(memory_space=pl.ANY)
VMEM = pl.BlockSpec(memory_space=pltpu.VMEM)
PARAMS = pltpu.CompilerParams(vmem_limit_bytes=24 * 1024 * 1024)


def store_sums(total, square, out_ref):
    channels = total.shape[1]
    per_group = channels // GROUPS
    member = lax.broadcasted_iota(jnp.int32, (8, channels), 1) % per_group

    def grouped(part):
        part = jnp.broadcast_to(jnp.sum(part, axis=0, keepdims=True), (8, channels))
        result = part
        for step in range(1, per_group):
            result += jnp.where(member >= step, pltpu.roll(part, step, 1), 0.0)
            rolled = pltpu.roll(part, channels - step, 1)
            result += jnp.where(member < per_group - step, rolled, 0.0)
        return result

    row = jnp.where(member == 0, grouped(total), grouped(square))[0:1]
    out_ref[...] = jnp.broadcast_to(row[None], out_ref.shape)


def add_sums(values, total, square):
    width, channels = values.shape
    split = (width // 8, 8, channels)
    total += jnp.sum(values.reshape(split), axis=0)
    square += jnp.sum((values * values).reshape(split), axis=0)
    return total, square


def sums_kernel(own_ref, out_ref, pair_ref, other_ref):
    rows, _, channels = own_ref.shape
    even = lax.axis_index("rows") % 2 == 0
    pair_ref[0] = jnp.where(even, own_ref[rows - 1], own_ref[0])
    for row in range(2):
        other_ref[row] = jnp.where(even, own_ref[row], own_ref[rows - 2 + row])
    total = jnp.zeros((8, channels), jnp.float32)
    square = jnp.zeros((8, channels), jnp.float32)
    for row in range(rows):
        total, square = add_sums(own_ref[row].astype(jnp.float32), total, square)
    store_sums(total, square, out_ref)


def sum_weight(source, target):
    taps, channels = source.shape[1], source.shape[2]
    for tap in range(taps):
        total = source[0, tap].astype(jnp.float32)
        total += source[1, tap].astype(jnp.float32)
        total += source[2, tap].astype(jnp.float32)
        high = total.astype(jnp.bfloat16)
        low = (total - high.astype(jnp.float32)).astype(jnp.bfloat16)
        target[pl.ds(tap * channels, channels), :] = jnp.concatenate([high, low], axis=1)


def scale_offset(sums_ref, gain_ref, shift_ref, entries):
    sums = jnp.sum(sums_ref[...], axis=0)
    channels = sums.shape[1]
    per_group = channels // GROUPS
    sums = jnp.broadcast_to(sums, (8, channels)) * (1.0 / (entries * per_group))
    member = lax.broadcasted_iota(jnp.int32, sums.shape, 1) % per_group

    def spread(lane):
        part = jnp.where(member == lane, sums, 0.0)
        result = part
        for target in range(per_group):
            if target != lane:
                result += pltpu.roll(part, (target - lane) % channels, 1)
        return result

    mean = spread(0)
    var = jnp.maximum(spread(1) - mean * mean, 0.0)
    scale = gain_ref[...] * lax.rsqrt(var + 1e-06)
    return 0.5 * scale[0:1], (0.5 * (shift_ref[...] - mean * scale))[0:1]


def store_taps(values, scale, offset, wide_ref, taps_ref, row):
    width, channels = values.shape
    half = values.astype(jnp.float32) * scale + offset
    act = half * jnp.tanh(half) + half
    wide_ref[row, 8 : 8 + width, :] = act
    wide_ref[row, 7:8, :] = act[0:1]
    wide_ref[row, 8 + width : 9 + width, :] = act[width - 1 : width]
    for tap in range(3):
        shifted = wide_ref[row, 7 + tap : 7 + tap + width, :]
        taps_ref[row, :, tap * channels : (tap + 1) * channels] = shifted.astype(jnp.bfloat16)


def window(taps_ref, row, count):
    _, width, lanes = taps_ref.shape
    parts = [
        taps_ref[row + tap : row + tap + count].reshape(count * width, lanes) for tap in range(3)
    ]
    return jnp.concatenate(parts, axis=1)


def product(rows, weight_ref):
    both = jnp.dot(rows, weight_ref[...], preferred_element_type=jnp.float32)
    half = both.shape[1] // 2
    return both[:, :half] + both[:, half:]


def first_kernel(
    count, sums_ref, own_ref, pair_ref, other_ref, weight_ref, bias_ref, gain_ref, shift_ref,
    gain_two_ref, shift_two_ref,
    hidden_ref, edge_ref, out_ref, next_ref, wide_ref, taps_ref, summed_ref, vectors_ref, sems,
):
    copies = [
        pltpu.make_async_copy(source, vectors_ref.at[i], sems.at[i])
        for i, source in enumerate((gain_two_ref, shift_two_ref))
    ]
    for copy in copies:
        copy.start()
    index = lax.axis_index("rows")
    rows, width, channels = own_ref.shape
    even = index % 2 == 0
    scale, offset = scale_offset(sums_ref, gain_ref, shift_ref, rows * width * count)
    sum_weight(weight_ref, summed_ref)

    def make(values, slot):
        store_taps(values, scale, offset, wide_ref, taps_ref, slot)

    border = jnp.logical_or(index == 0, index == count - 1)
    border_row = jnp.where(even, own_ref[0], own_ref[rows - 1])
    outer = [jnp.where(border, border_row, other_ref[row]) for row in range(2)]
    make(jnp.where(even, outer[1], pair_ref[0]), 0)
    for row in range(rows):
        make(own_ref[row], row + 1)
    make(jnp.where(even, pair_ref[0], outer[0]), rows + 1)
    make(jnp.where(even, outer[0], own_ref[rows - 1]), rows + 2)
    make(jnp.where(even, outer[1], outer[0]), rows + 3)
    make(jnp.where(even, own_ref[0], outer[1]), rows + 4)
    total = jnp.zeros((8, channels), jnp.float32)
    square = jnp.zeros((8, channels), jnp.float32)
    hidden = product(window(taps_ref, 0, rows), summed_ref) + bias_ref[...]
    hidden = hidden.astype(jnp.bfloat16)
    for row in range(rows):
        values = hidden[row * width : (row + 1) * width]
        hidden_ref[row] = values
        total, square = add_sums(values.astype(jnp.float32), total, square)
    cross = product(window(taps_ref, rows + 2, 1), summed_ref) + bias_ref[...]
    hidden_ref[rows] = cross.astype(jnp.bfloat16)
    edge_ref[0] = jnp.where(even, hidden[(rows - 1) * width : rows * width], hidden[:width])
    store_sums(total, square, out_ref)
    for i in range(2):
        copies[i].wait()
        next_ref[pl.ds(i, 1), :] = vectors_ref[i]

    @pl.when(index == 0)
    def _():
        hidden_ref[rows] = hidden_ref[0]

    @pl.when(index == count - 1)
    def _():
        hidden_ref[rows] = hidden_ref[rows - 1]


def second_kernel(
    count, sums_ref, hidden_ref, edge_ref, own_ref, weight_ref, params_ref, bias_ref,
    out_ref, wide_ref, taps_ref, summed_ref, done_ref, sems, held_ref, bias_sem,
):
    rows, width, channels = own_ref.shape
    bias_copy = pltpu.make_async_copy(bias_ref, held_ref, bias_sem)
    bias_copy.start()
    scale, offset = scale_offset(
        sums_ref, params_ref.at[0:1], params_ref.at[1:2], rows * width * count
    )
    sum_weight(weight_ref, summed_ref)
    copies = [
        pltpu.make_async_copy(done_ref.at[row], out_ref.at[row], sems.at[row])
        for row in range(rows)
    ]
    even = lax.axis_index("rows") % 2 == 0
    ends = {
        0: jnp.where(even, hidden_ref[rows], edge_ref[0]),
        rows + 1: jnp.where(even, edge_ref[0], hidden_ref[rows]),
    }
    for row in range(rows + 2):
        values = ends[row] if row in ends else hidden_ref[row - 1]
        store_taps(values, scale, offset, wide_ref, taps_ref, row)
    branch = product(window(taps_ref, 0, rows), summed_ref)
    bias_copy.wait()
    branch += held_ref[...]
    for row in range(rows):
        values = own_ref[row].astype(jnp.float32) + branch[row * width : (row + 1) * width]
        done_ref[row] = values.astype(jnp.bfloat16)
        copies[row].start()
    for copy in copies:
        copy.wait()


def exchanged(sums):
    count = lax.axis_size("rows")
    ends_first = [i // 2 if i % 2 == 0 else count - 1 - i // 2 for i in range(count)]
    return lax.all_to_all(sums, "rows", 0, 0, axis_index_groups=[ends_first])


def body(
    latents, gain_one, shift_one, weight_one, bias_one, gain_two, shift_two, weight_two, bias_two
):
    count = lax.axis_size("rows")
    own = latents[0]
    rows, width, channels = own.shape
    sums_shape = jax.ShapeDtypeStruct((count, 1, channels), jnp.float32)
    taps = weight_one.shape[1] * weight_one.shape[2]
    edge_shape = jax.ShapeDtypeStruct((1, width, channels), jnp.bfloat16)
    slab_shape = jax.ShapeDtypeStruct((2, width, channels), jnp.bfloat16)

    def raw(weight):
        return weight.reshape(3, taps, channels, channels)

    swap_pair = [(i, i ^ 1) for i in range(count)]
    swap_other = [(i, i + 1 if i % 2 else i - 1) for i in range(1, count - 1)]

    sums, pair, other = pl.pallas_call(
        sums_kernel,
        out_shape=[sums_shape, edge_shape, slab_shape],
        in_specs=[VMEM],
        out_specs=[VMEM] * 3,
        compiler_params=PARAMS,
        name="sums",
        cost_estimate=pl.CostEstimate(
            flops=40000000000, bytes_accessed=10000000, transcendentals=0
        ),
    )(own)
    other = lax.ppermute(other, "rows", swap_other)
    pair = lax.ppermute(pair, "rows", swap_pair)
    sums = exchanged(sums)
    hidden, edge, sums, params = pl.pallas_call(
        functools.partial(first_kernel, count),
        out_shape=[
            jax.ShapeDtypeStruct((rows + 1, width, channels), jnp.bfloat16),
            edge_shape,
            sums_shape,
            jax.ShapeDtypeStruct((8, channels), jnp.float32),
        ],
        in_specs=[VMEM] * 8 + [HBM] * 2,
        out_specs=[VMEM] * 4,
        scratch_shapes=[
            pltpu.VMEM((rows + 5, width + 16, channels), jnp.float32),
            pltpu.VMEM((rows + 5, width, 3 * channels), jnp.bfloat16),
            pltpu.VMEM((taps * channels, 2 * channels), jnp.bfloat16),
            pltpu.VMEM((2, 1, channels), jnp.float32),
            pltpu.SemaphoreType.DMA((2,)),
        ],
        compiler_params=PARAMS, name="first",
    )(
        sums,
        own,
        pair,
        other,
        raw(weight_one),
        *[vector.reshape(1, channels) for vector in (bias_one, gain_one, shift_one)],
        *[
            pltpu.with_memory_space_constraint(vector.reshape(1, channels), pltpu.HBM)
            for vector in (gain_two, shift_two)
        ],
    )
    edge = lax.ppermute(edge, "rows", swap_pair)
    sums = exchanged(sums)
    decoded = pl.pallas_call(
        functools.partial(second_kernel, count),
        out_shape=jax.ShapeDtypeStruct(own.shape, jnp.bfloat16),
        in_specs=[VMEM] * 6 + [HBM],
        out_specs=ANY,
        scratch_shapes=[
            pltpu.VMEM((rows + 2, width + 16, channels), jnp.float32),
            pltpu.VMEM((rows + 2, width, 3 * channels), jnp.bfloat16),
            pltpu.VMEM((taps * channels, 2 * channels), jnp.bfloat16),
            pltpu.VMEM(own.shape, jnp.bfloat16),
            pltpu.SemaphoreType.DMA((rows,)),
            pltpu.VMEM((1, channels), jnp.float32),
            pltpu.SemaphoreType.DMA,
        ],
        compiler_params=PARAMS, name="second",
    )(
        sums,
        hidden,
        edge,
        own,
        raw(weight_two),
        params,
        pltpu.with_memory_space_constraint(bias_two.reshape(1, channels), pltpu.HBM),
    )
    return decoded[None]


def solution(mesh):
    return jax.shard_map(
        body,
        mesh=mesh,
        in_specs=(P("groups", "rows", None, None), P(), P(), P(), P(), P(), P(), P(), P()),
        out_specs=P("groups", "rows", None, None),
        check_vma=False,
    )
```

```python
import functools

import jax
import jax.numpy as jnp
from jax import lax
from jax.experimental import pallas as pl
from jax.experimental.pallas import tpu as pltpu
from jax.sharding import PartitionSpec as P

GROUPS = 32
HBM = pl.BlockSpec(memory_space=pltpu.HBM)
ANY = pl.BlockSpec(memory_space=pl.ANY)
VMEM = pl.BlockSpec(memory_space=pltpu.VMEM)
PARAMS = pltpu.CompilerParams(vmem_limit_bytes=24 * 1024 * 1024)


def store_sums(total, square, out_ref):
    channels = total.shape[1]
    per_group = channels // GROUPS
    member = lax.broadcasted_iota(jnp.int32, (8, channels), 1) % per_group

    def grouped(part):
        part = jnp.broadcast_to(jnp.sum(part, axis=0, keepdims=True), (8, channels))
        result = part
        for step in range(1, per_group):
            result += jnp.where(member >= step, pltpu.roll(part, step, 1), 0.0)
            rolled = pltpu.roll(part, channels - step, 1)
            result += jnp.where(member < per_group - step, rolled, 0.0)
        return result

    row = jnp.where(member == 0, grouped(total), grouped(square))[0:1]
    out_ref[...] = jnp.broadcast_to(row[None], out_ref.shape)


def add_sums(values, total, square):
    width, channels = values.shape
    split = (width // 8, 8, channels)
    total += jnp.sum(values.reshape(split), axis=0)
    square += jnp.sum((values * values).reshape(split), axis=0)
    return total, square


def sums_kernel(own_ref, out_ref, pair_ref, other_ref):
    rows, _, channels = own_ref.shape
    even = lax.axis_index("rows") % 2 == 0
    for row in range(2):
        top = own_ref[row]
        bottom = own_ref[rows - 2 + row]
        pair_ref[row] = jnp.where(even, bottom, top)
        other_ref[row] = jnp.where(even, top, bottom)
    total = jnp.zeros((8, channels), jnp.float32)
    square = jnp.zeros((8, channels), jnp.float32)
    for row in range(rows):
        total, square = add_sums(own_ref[row].astype(jnp.float32), total, square)
    store_sums(total, square, out_ref)


def sum_weight(source, target):
    taps, channels = source.shape[1], source.shape[2]
    for tap in range(taps):
        total = source[0, tap].astype(jnp.float32)
        total += source[1, tap].astype(jnp.float32)
        total += source[2, tap].astype(jnp.float32)
        high = total.astype(jnp.bfloat16)
        low = (total - high.astype(jnp.float32)).astype(jnp.bfloat16)
        target[pl.ds(tap * channels, channels), :] = jnp.concatenate([high, low], axis=1)


def scale_offset(sums_ref, gain_ref, shift_ref, entries):
    sums = jnp.sum(sums_ref[...], axis=0)
    channels = sums.shape[1]
    per_group = channels // GROUPS
    sums = jnp.broadcast_to(sums, (8, channels)) * (1.0 / (entries * per_group))
    member = lax.broadcasted_iota(jnp.int32, sums.shape, 1) % per_group

    def spread(lane):
        part = jnp.where(member == lane, sums, 0.0)
        result = part
        for target in range(per_group):
            if target != lane:
                result += pltpu.roll(part, (target - lane) % channels, 1)
        return result

    mean = spread(0)
    var = jnp.maximum(spread(1) - mean * mean, 0.0)
    scale = gain_ref[...] * lax.rsqrt(var + 1e-06)
    return 0.5 * scale[0:1], (0.5 * (shift_ref[...] - mean * scale))[0:1]


def store_taps(values, scale, offset, wide_ref, taps_ref, row):
    width, channels = values.shape
    half = values.astype(jnp.float32) * scale + offset
    act = half * jnp.tanh(half) + half
    wide_ref[row, 8 : 8 + width, :] = act
    wide_ref[row, 7:8, :] = act[0:1]
    wide_ref[row, 8 + width : 9 + width, :] = act[width - 1 : width]
    for tap in range(3):
        shifted = wide_ref[row, 7 + tap : 7 + tap + width, :]
        taps_ref[row, :, tap * channels : (tap + 1) * channels] = shifted.astype(jnp.bfloat16)


def conv_rows(taps_ref, row, count, weight_ref):
    _, width, lanes = taps_ref.shape
    window = jnp.concatenate(
        [taps_ref[row + tap : row + tap + count].reshape(count * width, lanes) for tap in range(3)],
        axis=1,
    )
    both = jnp.dot(window, weight_ref[...], preferred_element_type=jnp.float32)
    half = both.shape[1] // 2
    return both[:, :half] + both[:, half:]


def first_kernel(
    count, sums_ref, own_ref, pair_ref, other_ref, weight_ref, bias_ref, gain_ref, shift_ref,
    bias_two_ref, gain_two_ref, shift_two_ref,
    hidden_ref, out_ref, next_ref, wide_ref, taps_ref, summed_ref, vectors_ref, sems,
):
    copies = [
        pltpu.make_async_copy(source, vectors_ref.at[i], sems.at[i])
        for i, source in enumerate((bias_two_ref, gain_two_ref, shift_two_ref))
    ]
    for copy in copies:
        copy.start()
    index = lax.axis_index("rows")
    rows, width, channels = own_ref.shape
    even = index % 2 == 0
    scale, offset = scale_offset(sums_ref, gain_ref, shift_ref, rows * width * count)
    sum_weight(weight_ref, summed_ref)

    def make(row):
        if row < 2:
            values = jnp.where(even, other_ref[row], pair_ref[row])
            values = jnp.where(index == 0, own_ref[0], values)
        elif row < rows + 2:
            values = own_ref[row - 2]
        else:
            values = jnp.where(even, pair_ref[row - rows - 2], other_ref[row - rows - 2])
            values = jnp.where(index == count - 1, own_ref[rows - 1], values)
        store_taps(values, scale, offset, wide_ref, taps_ref, row)

    total = jnp.zeros((8, channels), jnp.float32)
    square = jnp.zeros((8, channels), jnp.float32)
    for row in range(rows + 4):
        make(row)
    hidden = conv_rows(taps_ref, 0, rows + 2, summed_ref) + bias_ref[...]
    hidden = hidden.astype(jnp.bfloat16)
    for row in range(rows + 2):
        values = hidden[row * width : (row + 1) * width]
        hidden_ref[row] = values
        if 0 < row <= rows:
            total, square = add_sums(values.astype(jnp.float32), total, square)
    store_sums(total, square, out_ref)
    for i in range(3):
        copies[i].wait()
        next_ref[pl.ds(i, 1), :] = vectors_ref[i]

    @pl.when(index == 0)
    def _():
        hidden_ref[0] = hidden_ref[1]

    @pl.when(index == count - 1)
    def _():
        hidden_ref[rows + 1] = hidden_ref[rows]


def second_kernel(
    count, sums_ref, hidden_ref, own_ref, weight_ref, params_ref,
    out_ref, wide_ref, taps_ref, summed_ref, done_ref, sems,
):
    rows, width, channels = own_ref.shape
    scale, offset = scale_offset(
        sums_ref, params_ref.at[1:2], params_ref.at[2:3], rows * width * count
    )
    sum_weight(weight_ref, summed_ref)
    copies = [
        pltpu.make_async_copy(done_ref.at[row], out_ref.at[row], sems.at[row])
        for row in range(rows)
    ]
    for row in range(rows + 2):
        store_taps(hidden_ref[row], scale, offset, wide_ref, taps_ref, row)
    branch = conv_rows(taps_ref, 0, rows, summed_ref) + params_ref[0:1, :]
    for row in range(rows):
        values = own_ref[row].astype(jnp.float32) + branch[row * width : (row + 1) * width]
        done_ref[row] = values.astype(jnp.bfloat16)
        copies[row].start()
    for copy in copies:
        copy.wait()


def exchanged(sums):
    count = lax.axis_size("rows")
    ends_first = [i // 2 if i % 2 == 0 else count - 1 - i // 2 for i in range(count)]
    return lax.all_to_all(sums, "rows", 0, 0, axis_index_groups=[ends_first])


def body(
    latents, gain_one, shift_one, weight_one, bias_one, gain_two, shift_two, weight_two, bias_two
):
    count = lax.axis_size("rows")
    own = latents[0]
    rows, width, channels = own.shape
    sums_shape = jax.ShapeDtypeStruct((count, 1, channels), jnp.float32)
    taps = weight_one.shape[1] * weight_one.shape[2]
    slab_shape = jax.ShapeDtypeStruct((2, width, channels), jnp.bfloat16)

    def raw(weight):
        return weight.reshape(3, taps, channels, channels)

    swap_pair = [(i, i ^ 1) for i in range(count)]
    swap_other = [(i, i + 1 if i % 2 else i - 1) for i in range(1, count - 1)]

    sums, pair, other = pl.pallas_call(
        sums_kernel,
        out_shape=[jax.ShapeDtypeStruct((1, 1, channels), jnp.float32), slab_shape, slab_shape],
        in_specs=[VMEM],
        out_specs=[VMEM] * 3,
        compiler_params=PARAMS,
        name="sums",
        cost_estimate=pl.CostEstimate(
            flops=40000000000, bytes_accessed=10000000, transcendentals=0
        ),
    )(own)
    partner = lax.ppermute(sums, "rows", swap_pair)
    pair = lax.ppermute(pair, "rows", swap_pair)
    other = lax.ppermute(other, "rows", swap_other)
    half = count // 2
    order = [i // 2 if i % 2 == 0 else half - 1 - i // 2 for i in range(half)]
    by_core = [[2 * chip + core for chip in order] for core in range(2)]
    sums = jnp.broadcast_to(sums + partner, (half, 1, channels))
    sums = lax.all_to_all(sums, "rows", 0, 0, axis_index_groups=by_core)
    hidden, sums, params = pl.pallas_call(
        functools.partial(first_kernel, count),
        out_shape=[
            jax.ShapeDtypeStruct((rows + 2, width, channels), jnp.bfloat16),
            sums_shape,
            jax.ShapeDtypeStruct((8, channels), jnp.float32),
        ],
        in_specs=[VMEM] * 8 + [HBM] * 3,
        out_specs=[VMEM] * 3,
        scratch_shapes=[
            pltpu.VMEM((rows + 4, width + 16, channels), jnp.float32),
            pltpu.VMEM((rows + 4, width, 3 * channels), jnp.bfloat16),
            pltpu.VMEM((taps * channels, 2 * channels), jnp.bfloat16),
            pltpu.VMEM((3, 1, channels), jnp.float32),
            pltpu.SemaphoreType.DMA((3,)),
        ],
        compiler_params=PARAMS, name="first",
    )(
        sums,
        own,
        pair,
        other,
        raw(weight_one),
        *[vector.reshape(1, channels) for vector in (bias_one, gain_one, shift_one)],
        *[
            pltpu.with_memory_space_constraint(vector.reshape(1, channels), pltpu.HBM)
            for vector in (bias_two, gain_two, shift_two)
        ],
    )
    sums = exchanged(sums)
    decoded = pl.pallas_call(
        functools.partial(second_kernel, count),
        out_shape=jax.ShapeDtypeStruct(own.shape, jnp.bfloat16),
        in_specs=[VMEM] * 5,
        out_specs=ANY,
        scratch_shapes=[
            pltpu.VMEM((rows + 2, width + 16, channels), jnp.float32),
            pltpu.VMEM((rows + 2, width, 3 * channels), jnp.bfloat16),
            pltpu.VMEM((taps * channels, 2 * channels), jnp.bfloat16),
            pltpu.VMEM(own.shape, jnp.bfloat16),
            pltpu.SemaphoreType.DMA((rows,)),
        ],
        compiler_params=PARAMS, name="second",
    )(sums, hidden, own, raw(weight_two), params)
    return decoded[None]


def solution(mesh):
    return jax.shard_map(
        body,
        mesh=mesh,
        in_specs=(P("groups", "rows", None, None), P(), P(), P(), P(), P(), P(), P(), P()),
        out_specs=P("groups", "rows", None, None),
        check_vma=False,
    )
```

```python
import functools

import jax
import jax.numpy as jnp
from jax import lax
from jax.experimental import pallas as pl
from jax.experimental.pallas import tpu as pltpu
from jax.sharding import PartitionSpec as P

GROUPS = 32
HBM = pl.BlockSpec(memory_space=pltpu.HBM)
ANY = pl.BlockSpec(memory_space=pl.ANY)
VMEM = pl.BlockSpec(memory_space=pltpu.VMEM)
PARAMS = pltpu.CompilerParams(vmem_limit_bytes=24 * 1024 * 1024)


def store_sums(total, square, out_ref):
    channels = total.shape[1]
    per_group = channels // GROUPS
    member = lax.broadcasted_iota(jnp.int32, (8, channels), 1) % per_group

    def grouped(part):
        part = jnp.broadcast_to(jnp.sum(part, axis=0, keepdims=True), (8, channels))
        result = part
        for step in range(1, per_group):
            result += jnp.where(member >= step, pltpu.roll(part, step, 1), 0.0)
            rolled = pltpu.roll(part, channels - step, 1)
            result += jnp.where(member < per_group - step, rolled, 0.0)
        return result

    row = jnp.where(member == 0, grouped(total), grouped(square))[0:1]
    out_ref[...] = jnp.broadcast_to(row[None], out_ref.shape)


def add_sums(values, total, square):
    width, channels = values.shape
    split = (width // 8, 8, channels)
    total += jnp.sum(values.reshape(split), axis=0)
    square += jnp.sum((values * values).reshape(split), axis=0)
    return total, square


def sums_kernel(own_ref, out_ref, pair_ref, other_ref):
    rows, _, channels = own_ref.shape
    even = lax.axis_index("rows") % 2 == 0
    for row in range(2):
        top = own_ref[row]
        bottom = own_ref[rows - 2 + row]
        pair_ref[row] = jnp.where(even, bottom, top)
        other_ref[row] = jnp.where(even, top, bottom)
    total = jnp.zeros((8, channels), jnp.float32)
    square = jnp.zeros((8, channels), jnp.float32)
    for row in range(rows):
        total, square = add_sums(own_ref[row].astype(jnp.float32), total, square)
    store_sums(total, square, out_ref)


def sum_weight(source, target):
    taps, channels = source.shape[1], source.shape[2]
    for tap in range(taps):
        total = source[0, tap].astype(jnp.float32)
        total += source[1, tap].astype(jnp.float32)
        total += source[2, tap].astype(jnp.float32)
        high = total.astype(jnp.bfloat16)
        low = (total - high.astype(jnp.float32)).astype(jnp.bfloat16)
        target[pl.ds(tap * channels, channels), :] = jnp.concatenate([high, low], axis=1)


def scale_offset(sums_ref, gain_ref, shift_ref, entries):
    sums = jnp.sum(sums_ref[...], axis=0)
    channels = sums.shape[1]
    per_group = channels // GROUPS
    sums = jnp.broadcast_to(sums, (8, channels)) * (1.0 / (entries * per_group))
    member = lax.broadcasted_iota(jnp.int32, sums.shape, 1) % per_group

    def spread(lane):
        part = jnp.where(member == lane, sums, 0.0)
        result = part
        for target in range(per_group):
            if target != lane:
                result += pltpu.roll(part, (target - lane) % channels, 1)
        return result

    mean = spread(0)
    var = jnp.maximum(spread(1) - mean * mean, 0.0)
    scale = gain_ref[...] * lax.rsqrt(var + 1e-06)
    return 0.5 * scale[0:1], (0.5 * (shift_ref[...] - mean * scale))[0:1]


def store_taps(values, scale, offset, wide_ref, taps_ref, row):
    width, channels = values.shape
    half = values.astype(jnp.float32) * scale + offset
    act = half * jnp.tanh(half) + half
    wide_ref[row, 8 : 8 + width, :] = act
    wide_ref[row, 7:8, :] = act[0:1]
    wide_ref[row, 8 + width : 9 + width, :] = act[width - 1 : width]
    for tap in range(3):
        shifted = wide_ref[row, 7 + tap : 7 + tap + width, :]
        taps_ref[row, :, tap * channels : (tap + 1) * channels] = shifted.astype(jnp.bfloat16)


def conv_rows(taps_ref, row, count, weight_ref):
    _, width, lanes = taps_ref.shape
    window = jnp.concatenate(
        [taps_ref[row + tap : row + tap + count].reshape(count * width, lanes) for tap in range(3)],
        axis=1,
    )
    both = jnp.dot(window, weight_ref[...], preferred_element_type=jnp.float32)
    half = both.shape[1] // 2
    return both[:, :half] + both[:, half:]


def first_kernel(
    count, sums_ref, own_ref, upper_ref, lower_ref, weight_ref, bias_ref, gain_ref, shift_ref,
    bias_two_ref, gain_two_ref, shift_two_ref,
    hidden_ref, out_ref, next_ref, wide_ref, taps_ref, summed_ref, vectors_ref, sems,
):
    copies = [
        pltpu.make_async_copy(source, vectors_ref.at[i], sems.at[i])
        for i, source in enumerate((bias_two_ref, gain_two_ref, shift_two_ref))
    ]
    for copy in copies:
        copy.start()
    index = lax.axis_index("rows")
    rows, width, channels = own_ref.shape
    scale, offset = scale_offset(sums_ref, gain_ref, shift_ref, rows * width * count)
    sum_weight(weight_ref, summed_ref)

    def make(row):
        if row < 2:
            values = upper_ref[row]
        elif row < rows + 2:
            values = own_ref[row - 2]
        else:
            values = lower_ref[row - rows - 2]
        store_taps(values, scale, offset, wide_ref, taps_ref, row)

    total = jnp.zeros((8, channels), jnp.float32)
    square = jnp.zeros((8, channels), jnp.float32)
    for row in range(rows + 4):
        make(row)
    hidden = conv_rows(taps_ref, 0, rows + 2, summed_ref) + bias_ref[...]
    hidden = hidden.astype(jnp.bfloat16)
    for row in range(rows + 2):
        values = hidden[row * width : (row + 1) * width]
        hidden_ref[row] = values
        if 0 < row <= rows:
            total, square = add_sums(values.astype(jnp.float32), total, square)
    store_sums(total, square, out_ref)
    for i in range(3):
        copies[i].wait()
        next_ref[pl.ds(i, 1), :] = vectors_ref[i]

    @pl.when(index == 0)
    def _():
        hidden_ref[0] = hidden_ref[1]

    @pl.when(index == count - 1)
    def _():
        hidden_ref[rows + 1] = hidden_ref[rows]


def second_kernel(
    count, sums_ref, hidden_ref, own_ref, weight_ref, params_ref,
    out_ref, wide_ref, taps_ref, summed_ref, done_ref, sems,
):
    rows, width, channels = own_ref.shape
    scale, offset = scale_offset(
        sums_ref, params_ref.at[1:2], params_ref.at[2:3], rows * width * count
    )
    sum_weight(weight_ref, summed_ref)
    copies = [
        pltpu.make_async_copy(done_ref.at[row], out_ref.at[row], sems.at[row])
        for row in range(rows)
    ]
    for row in range(rows + 2):
        store_taps(hidden_ref[row], scale, offset, wide_ref, taps_ref, row)
    branch = conv_rows(taps_ref, 0, rows, summed_ref) + params_ref[0:1, :]
    for row in range(rows):
        values = own_ref[row].astype(jnp.float32) + branch[row * width : (row + 1) * width]
        done_ref[row] = values.astype(jnp.bfloat16)
        copies[row].start()
    for copy in copies:
        copy.wait()


def exchanged(sums):
    count = lax.axis_size("rows")
    ends_first = [i // 2 if i % 2 == 0 else count - 1 - i // 2 for i in range(count)]
    return lax.all_to_all(sums, "rows", 0, 0, axis_index_groups=[ends_first])


def body(
    latents, gain_one, shift_one, weight_one, bias_one, gain_two, shift_two, weight_two, bias_two
):
    count = lax.axis_size("rows")
    own = latents[0]
    rows, width, channels = own.shape
    sums_shape = jax.ShapeDtypeStruct((count, 1, channels), jnp.float32)
    taps = weight_one.shape[1] * weight_one.shape[2]
    slab_shape = jax.ShapeDtypeStruct((2, width, channels), jnp.bfloat16)

    def raw(weight):
        return weight.reshape(3, taps, channels, channels)

    swap_pair = [(i, i ^ 1) for i in range(count)]
    swap_other = [(i, i + 1 if i % 2 else i - 1) for i in range(1, count - 1)]

    sums, pair, other = pl.pallas_call(
        sums_kernel,
        out_shape=[sums_shape, slab_shape, slab_shape],
        in_specs=[VMEM],
        out_specs=[VMEM] * 3,
        compiler_params=PARAMS,
        name="sums",
        cost_estimate=pl.CostEstimate(
            flops=40000000000, bytes_accessed=10000000, transcendentals=0
        ),
    )(own)
    other = lax.ppermute(other, "rows", swap_other)
    pair = lax.ppermute(pair, "rows", swap_pair)
    index = lax.axis_index("rows")
    even = index % 2 == 0
    upper = jnp.where(index == 0, own[:1], jnp.where(even, other, pair))
    lower = jnp.where(index == count - 1, own[-1:], jnp.where(even, pair, other))
    sums = exchanged(sums)
    hidden, sums, params = pl.pallas_call(
        functools.partial(first_kernel, count),
        out_shape=[
            jax.ShapeDtypeStruct((rows + 2, width, channels), jnp.bfloat16),
            sums_shape,
            jax.ShapeDtypeStruct((8, channels), jnp.float32),
        ],
        in_specs=[VMEM] * 8 + [HBM] * 3,
        out_specs=[VMEM] * 3,
        scratch_shapes=[
            pltpu.VMEM((rows + 4, width + 16, channels), jnp.float32),
            pltpu.VMEM((rows + 4, width, 3 * channels), jnp.bfloat16),
            pltpu.VMEM((taps * channels, 2 * channels), jnp.bfloat16),
            pltpu.VMEM((3, 1, channels), jnp.float32),
            pltpu.SemaphoreType.DMA((3,)),
        ],
        compiler_params=PARAMS, name="first",
    )(
        sums,
        own,
        upper,
        lower,
        raw(weight_one),
        *[vector.reshape(1, channels) for vector in (bias_one, gain_one, shift_one)],
        *[
            pltpu.with_memory_space_constraint(vector.reshape(1, channels), pltpu.HBM)
            for vector in (bias_two, gain_two, shift_two)
        ],
    )
    sums = exchanged(sums)
    decoded = pl.pallas_call(
        functools.partial(second_kernel, count),
        out_shape=jax.ShapeDtypeStruct(own.shape, jnp.bfloat16),
        in_specs=[VMEM] * 5,
        out_specs=ANY,
        scratch_shapes=[
            pltpu.VMEM((rows + 2, width + 16, channels), jnp.float32),
            pltpu.VMEM((rows + 2, width, 3 * channels), jnp.bfloat16),
            pltpu.VMEM((taps * channels, 2 * channels), jnp.bfloat16),
            pltpu.VMEM(own.shape, jnp.bfloat16),
            pltpu.SemaphoreType.DMA((rows,)),
        ],
        compiler_params=PARAMS, name="second",
    )(sums, hidden, own, raw(weight_two), params)
    return decoded[None]


def solution(mesh):
    return jax.shard_map(
        body,
        mesh=mesh,
        in_specs=(P("groups", "rows", None, None), P(), P(), P(), P(), P(), P(), P(), P()),
        out_specs=P("groups", "rows", None, None),
        check_vma=False,
    )
```

```python
import functools

import jax
import jax.numpy as jnp
from jax import lax
from jax.experimental import pallas as pl
from jax.experimental.pallas import tpu as pltpu
from jax.sharding import PartitionSpec as P

GROUPS = 32
HBM = pl.BlockSpec(memory_space=pltpu.HBM)
ANY = pl.BlockSpec(memory_space=pl.ANY)
VMEM = pl.BlockSpec(memory_space=pltpu.VMEM)
PARAMS = pltpu.CompilerParams(vmem_limit_bytes=24 * 1024 * 1024)


def store_sums(total, square, out_ref):
    channels = total.shape[1]
    per_group = channels // GROUPS
    member = lax.broadcasted_iota(jnp.int32, (8, channels), 1) % per_group

    def grouped(part):
        part = jnp.broadcast_to(jnp.sum(part, axis=0, keepdims=True), (8, channels))
        result = part
        for step in range(1, per_group):
            result += jnp.where(member >= step, pltpu.roll(part, step, 1), 0.0)
            rolled = pltpu.roll(part, channels - step, 1)
            result += jnp.where(member < per_group - step, rolled, 0.0)
        return result

    row = jnp.where(member < per_group // 2, grouped(total), grouped(square))[0:1]
    out_ref[...] = jnp.broadcast_to(row[None], out_ref.shape)


def add_sums(values, total, square):
    width, channels = values.shape
    split = (width // 8, 8, channels)
    total += jnp.sum(values.reshape(split), axis=0)
    square += jnp.sum((values * values).reshape(split), axis=0)
    return total, square


def sums_kernel(own_ref, out_ref, pair_ref, other_ref):
    rows, _, channels = own_ref.shape
    even = lax.axis_index("rows") % 2 == 0
    for row in range(2):
        top = own_ref[row]
        bottom = own_ref[rows - 2 + row]
        pair_ref[row] = jnp.where(even, bottom, top)
        other_ref[row] = jnp.where(even, top, bottom)
    total = jnp.zeros((8, channels), jnp.float32)
    square = jnp.zeros((8, channels), jnp.float32)
    for row in range(rows):
        total, square = add_sums(own_ref[row].astype(jnp.float32), total, square)
    store_sums(total, square, out_ref)


def sum_weight(source, target):
    taps, channels = source.shape[1], source.shape[2]
    for tap in range(taps):
        total = source[0, tap].astype(jnp.float32)
        total += source[1, tap].astype(jnp.float32)
        total += source[2, tap].astype(jnp.float32)
        high = total.astype(jnp.bfloat16)
        low = (total - high.astype(jnp.float32)).astype(jnp.bfloat16)
        target[pl.ds(tap * channels, channels), :] = jnp.concatenate([high, low], axis=1)


def scale_offset(sums_ref, gain_ref, shift_ref, entries):
    sums = jnp.sum(sums_ref[...], axis=0)
    channels = sums.shape[1]
    per_group = channels // GROUPS
    sums = jnp.broadcast_to(sums, (8, channels)) * (1.0 / (entries * per_group))
    member = lax.broadcasted_iota(jnp.int32, sums.shape, 1) % per_group

    half = per_group // 2
    mean = jnp.where(member < half, sums, pltpu.roll(sums, half, 1))
    mean_square = jnp.where(member < half, pltpu.roll(sums, channels - half, 1), sums)
    var = jnp.maximum(mean_square - mean * mean, 0.0)
    scale = gain_ref[...] * lax.rsqrt(var + 1e-06)
    return 0.5 * scale[0:1], (0.5 * (shift_ref[...] - mean * scale))[0:1]


def store_taps(values, scale, offset, wide_ref, taps_ref, row):
    width, channels = values.shape
    half = values.astype(jnp.float32) * scale + offset
    act = half * jnp.tanh(half) + half
    wide_ref[row, 8 : 8 + width, :] = act
    wide_ref[row, 7:8, :] = act[0:1]
    wide_ref[row, 8 + width : 9 + width, :] = act[width - 1 : width]
    for tap in range(3):
        shifted = wide_ref[row, 7 + tap : 7 + tap + width, :]
        taps_ref[row, :, tap * channels : (tap + 1) * channels] = shifted.astype(jnp.bfloat16)


def conv_rows(taps_ref, row, count, weight_ref):
    _, width, lanes = taps_ref.shape
    window = jnp.concatenate(
        [taps_ref[row + tap : row + tap + count].reshape(count * width, lanes) for tap in range(3)],
        axis=1,
    )
    both = jnp.dot(window, weight_ref[...], preferred_element_type=jnp.float32)
    half = both.shape[1] // 2
    return both[:, :half] + both[:, half:]


def first_kernel(
    count, sums_ref, own_ref, pair_ref, other_ref, weight_ref, bias_ref, gain_ref, shift_ref,
    bias_two_ref, gain_two_ref, shift_two_ref,
    hidden_ref, out_ref, next_ref, wide_ref, taps_ref, summed_ref, vectors_ref, sems,
):
    copies = [
        pltpu.make_async_copy(source, vectors_ref.at[i], sems.at[i])
        for i, source in enumerate((bias_two_ref, gain_two_ref, shift_two_ref))
    ]
    for copy in copies:
        copy.start()
    index = lax.axis_index("rows")
    rows, width, channels = own_ref.shape
    even = index % 2 == 0
    scale, offset = scale_offset(sums_ref, gain_ref, shift_ref, rows * width * count)
    sum_weight(weight_ref, summed_ref)

    def make(row):
        if row < 2:
            values = jnp.where(even, other_ref[row], pair_ref[row])
            values = jnp.where(index == 0, own_ref[0], values)
        elif row < rows + 2:
            values = own_ref[row - 2]
        else:
            values = jnp.where(even, pair_ref[row - rows - 2], other_ref[row - rows - 2])
            values = jnp.where(index == count - 1, own_ref[rows - 1], values)
        store_taps(values, scale, offset, wide_ref, taps_ref, row)

    total = jnp.zeros((8, channels), jnp.float32)
    square = jnp.zeros((8, channels), jnp.float32)
    for row in range(rows + 4):
        make(row)
    hidden = conv_rows(taps_ref, 0, rows + 2, summed_ref) + bias_ref[...]
    hidden = hidden.astype(jnp.bfloat16)
    for row in range(rows + 2):
        values = hidden[row * width : (row + 1) * width]
        hidden_ref[row] = values
        if 0 < row <= rows:
            total, square = add_sums(values.astype(jnp.float32), total, square)
    store_sums(total, square, out_ref)
    for i in range(3):
        copies[i].wait()
        next_ref[pl.ds(i, 1), :] = vectors_ref[i]

    @pl.when(index == 0)
    def _():
        hidden_ref[0] = hidden_ref[1]

    @pl.when(index == count - 1)
    def _():
        hidden_ref[rows + 1] = hidden_ref[rows]


def second_kernel(
    count, sums_ref, hidden_ref, own_ref, weight_ref, params_ref,
    out_ref, wide_ref, taps_ref, summed_ref, done_ref, sems,
):
    rows, width, channels = own_ref.shape
    scale, offset = scale_offset(
        sums_ref, params_ref.at[1:2], params_ref.at[2:3], rows * width * count
    )
    sum_weight(weight_ref, summed_ref)
    copies = [
        pltpu.make_async_copy(done_ref.at[row], out_ref.at[row], sems.at[row])
        for row in range(rows)
    ]
    for row in range(rows + 2):
        store_taps(hidden_ref[row], scale, offset, wide_ref, taps_ref, row)
    branch = conv_rows(taps_ref, 0, rows, summed_ref) + params_ref[0:1, :]
    for row in range(rows):
        values = own_ref[row].astype(jnp.float32) + branch[row * width : (row + 1) * width]
        done_ref[row] = values.astype(jnp.bfloat16)
        copies[row].start()
    for copy in copies:
        copy.wait()


def exchanged(sums):
    count = lax.axis_size("rows")
    ends_first = [i // 2 if i % 2 == 0 else count - 1 - i // 2 for i in range(count)]
    return lax.all_to_all(sums, "rows", 0, 0, axis_index_groups=[ends_first])


def body(
    latents, gain_one, shift_one, weight_one, bias_one, gain_two, shift_two, weight_two, bias_two
):
    count = lax.axis_size("rows")
    own = latents[0]
    rows, width, channels = own.shape
    sums_shape = jax.ShapeDtypeStruct((count, 1, channels), jnp.float32)
    taps = weight_one.shape[1] * weight_one.shape[2]
    slab_shape = jax.ShapeDtypeStruct((2, width, channels), jnp.bfloat16)

    def raw(weight):
        return weight.reshape(3, taps, channels, channels)

    swap_pair = [(i, i ^ 1) for i in range(count)]
    swap_other = [(i, i + 1 if i % 2 else i - 1) for i in range(1, count - 1)]

    sums, pair, other = pl.pallas_call(
        sums_kernel,
        out_shape=[sums_shape, slab_shape, slab_shape],
        in_specs=[VMEM],
        out_specs=[VMEM] * 3,
        compiler_params=PARAMS,
        name="sums",
        cost_estimate=pl.CostEstimate(
            flops=40000000000, bytes_accessed=10000000, transcendentals=0
        ),
    )(own)
    other = lax.ppermute(other, "rows", swap_other)
    pair = lax.ppermute(pair, "rows", swap_pair)
    sums = exchanged(sums)
    hidden, sums, params = pl.pallas_call(
        functools.partial(first_kernel, count),
        out_shape=[
            jax.ShapeDtypeStruct((rows + 2, width, channels), jnp.bfloat16),
            sums_shape,
            jax.ShapeDtypeStruct((8, channels), jnp.float32),
        ],
        in_specs=[VMEM] * 8 + [HBM] * 3,
        out_specs=[VMEM] * 3,
        scratch_shapes=[
            pltpu.VMEM((rows + 4, width + 16, channels), jnp.float32),
            pltpu.VMEM((rows + 4, width, 3 * channels), jnp.bfloat16),
            pltpu.VMEM((taps * channels, 2 * channels), jnp.bfloat16),
            pltpu.VMEM((3, 1, channels), jnp.float32),
            pltpu.SemaphoreType.DMA((3,)),
        ],
        compiler_params=PARAMS, name="first",
    )(
        sums,
        own,
        pair,
        other,
        raw(weight_one),
        *[vector.reshape(1, channels) for vector in (bias_one, gain_one, shift_one)],
        *[
            pltpu.with_memory_space_constraint(vector.reshape(1, channels), pltpu.HBM)
            for vector in (bias_two, gain_two, shift_two)
        ],
    )
    sums = exchanged(sums)
    decoded = pl.pallas_call(
        functools.partial(second_kernel, count),
        out_shape=jax.ShapeDtypeStruct(own.shape, jnp.bfloat16),
        in_specs=[VMEM] * 5,
        out_specs=ANY,
        scratch_shapes=[
            pltpu.VMEM((rows + 2, width + 16, channels), jnp.float32),
            pltpu.VMEM((rows + 2, width, 3 * channels), jnp.bfloat16),
            pltpu.VMEM((taps * channels, 2 * channels), jnp.bfloat16),
            pltpu.VMEM(own.shape, jnp.bfloat16),
            pltpu.SemaphoreType.DMA((rows,)),
        ],
        compiler_params=PARAMS, name="second",
    )(sums, hidden, own, raw(weight_two), params)
    return decoded[None]


def solution(mesh):
    return jax.shard_map(
        body,
        mesh=mesh,
        in_specs=(P("groups", "rows", None, None), P(), P(), P(), P(), P(), P(), P(), P()),
        out_specs=P("groups", "rows", None, None),
        check_vma=False,
    )
```

```python
import functools

import jax
import jax.numpy as jnp
from jax import lax
from jax.experimental import pallas as pl
from jax.experimental.pallas import tpu as pltpu
from jax.sharding import PartitionSpec as P

GROUPS = 32
HBM = pl.BlockSpec(memory_space=pltpu.HBM)
ANY = pl.BlockSpec(memory_space=pl.ANY)
VMEM = pl.BlockSpec(memory_space=pltpu.VMEM)
PARAMS = pltpu.CompilerParams(vmem_limit_bytes=24 * 1024 * 1024)


def store_sums(total, square, out_ref):
    channels = total.shape[1]
    per_group = channels // GROUPS
    member = lax.broadcasted_iota(jnp.int32, (8, channels), 1) % per_group

    def grouped(part):
        part = jnp.broadcast_to(jnp.sum(part, axis=0, keepdims=True), (8, channels))
        result = part
        for step in range(1, per_group):
            result += jnp.where(member >= step, pltpu.roll(part, step, 1), 0.0)
            rolled = pltpu.roll(part, channels - step, 1)
            result += jnp.where(member < per_group - step, rolled, 0.0)
        return result

    row = jnp.where(member == 0, grouped(total), grouped(square))[0:1]
    out_ref[...] = jnp.broadcast_to(row[None], out_ref.shape)


def add_sums(values, total, square):
    width, channels = values.shape
    split = (width // 8, 8, channels)
    total += jnp.sum(values.reshape(split), axis=0)
    square += jnp.sum((values * values).reshape(split), axis=0)
    return total, square


def sums_kernel(own_ref, out_ref, pair_ref, other_ref):
    rows, _, channels = own_ref.shape
    even = lax.axis_index("rows") % 2 == 0
    for row in range(2):
        top = own_ref[row]
        bottom = own_ref[rows - 2 + row]
        pair_ref[row] = jnp.where(even, bottom, top)
        other_ref[row] = jnp.where(even, top, bottom)
    total = jnp.zeros((8, channels), jnp.float32)
    square = jnp.zeros((8, channels), jnp.float32)
    for row in range(rows):
        total, square = add_sums(own_ref[row].astype(jnp.float32), total, square)
    store_sums(total, square, out_ref)


def sum_weight(source, target):
    taps, channels = source.shape[1], source.shape[2]
    for tap in range(taps):
        total = source[0, tap].astype(jnp.float32)
        total += source[1, tap].astype(jnp.float32)
        total += source[2, tap].astype(jnp.float32)
        high = total.astype(jnp.bfloat16)
        low = (total - high.astype(jnp.float32)).astype(jnp.bfloat16)
        target[pl.ds(tap * channels, channels), :] = jnp.concatenate([high, low], axis=1)


def scale_offset(sums_ref, gain_ref, shift_ref, entries):
    sums = jnp.sum(sums_ref[...], axis=0)
    channels = sums.shape[1]
    per_group = channels // GROUPS
    sums = jnp.broadcast_to(sums, (8, channels)) * (1.0 / (entries * per_group))
    member = lax.broadcasted_iota(jnp.int32, sums.shape, 1) % per_group

    def spread(lane):
        part = jnp.where(member == lane, sums, 0.0)
        result = part
        for target in range(per_group):
            if target != lane:
                result += pltpu.roll(part, (target - lane) % channels, 1)
        return result

    mean = spread(0)
    var = jnp.maximum(spread(1) - mean * mean, 0.0)
    scale = gain_ref[...] * lax.rsqrt(var + 1e-06)
    return 0.5 * scale[0:1], (0.5 * (shift_ref[...] - mean * scale))[0:1]


def store_taps(values, scale, offset, wide_ref, taps_ref, row):
    width, channels = values.shape
    half = values.astype(jnp.float32) * scale + offset
    act = half * jnp.tanh(half) + half
    wide_ref[row, 8 : 8 + width, :] = act
    wide_ref[row, 7:8, :] = act[0:1]
    wide_ref[row, 8 + width : 9 + width, :] = act[width - 1 : width]
    for tap in range(3):
        shifted = wide_ref[row, 7 + tap : 7 + tap + width, :]
        taps_ref[row, :, tap * channels : (tap + 1) * channels] = shifted.astype(jnp.bfloat16)


def conv_rows(taps_ref, row, count, weight_ref):
    _, width, lanes = taps_ref.shape
    window = jnp.concatenate(
        [taps_ref[row + tap : row + tap + count].reshape(count * width, lanes) for tap in range(3)],
        axis=1,
    )
    both = jnp.dot(window, weight_ref[...], preferred_element_type=jnp.float32)
    half = both.shape[1] // 2
    return both[:, :half] + both[:, half:]


def first_kernel(
    count, sums_ref, own_ref, pair_ref, other_ref, weight_ref, bias_ref, gain_ref, shift_ref,
    bias_two_ref, gain_two_ref, shift_two_ref,
    hidden_ref, out_ref, next_ref, wide_ref, taps_ref, summed_ref, vectors_ref, sems,
):
    copies = [
        pltpu.make_async_copy(source, vectors_ref.at[i], sems.at[i])
        for i, source in enumerate((bias_two_ref, gain_two_ref, shift_two_ref))
    ]
    for copy in copies:
        copy.start()
    index = lax.axis_index("rows")
    rows, width, channels = own_ref.shape
    even = index % 2 == 0
    scale, offset = scale_offset(sums_ref, gain_ref, shift_ref, rows * width * count)
    sum_weight(weight_ref, summed_ref)

    def make(row):
        if row < 2:
            values = jnp.where(even, other_ref[row], pair_ref[row])
            values = jnp.where(index == 0, own_ref[0], values)
        elif row < rows + 2:
            values = own_ref[row - 2]
        else:
            values = jnp.where(even, pair_ref[row - rows - 2], other_ref[row - rows - 2])
            values = jnp.where(index == count - 1, own_ref[rows - 1], values)
        store_taps(values, scale, offset, wide_ref, taps_ref, row)

    total = jnp.zeros((8, channels), jnp.float32)
    square = jnp.zeros((8, channels), jnp.float32)
    for row in range(rows + 4):
        make(row)
    hidden = conv_rows(taps_ref, 0, rows + 2, summed_ref) + bias_ref[...]
    hidden = hidden.astype(jnp.bfloat16)
    for row in range(rows + 2):
        values = hidden[row * width : (row + 1) * width]
        hidden_ref[row] = values
        if 0 < row <= rows:
            total, square = add_sums(values.astype(jnp.float32), total, square)
    store_sums(total, square, out_ref)
    for i in range(3):
        copies[i].wait()
        next_ref[pl.ds(i, 1), :] = vectors_ref[i]


def second_kernel(
    count, sums_ref, hidden_ref, own_ref, weight_ref, params_ref,
    out_ref, wide_ref, taps_ref, summed_ref, done_ref, sems,
):
    rows, width, channels = own_ref.shape
    scale, offset = scale_offset(
        sums_ref, params_ref.at[1:2], params_ref.at[2:3], rows * width * count
    )
    sum_weight(weight_ref, summed_ref)
    copies = [
        pltpu.make_async_copy(done_ref.at[row], out_ref.at[row], sems.at[row])
        for row in range(rows)
    ]
    index = lax.axis_index("rows")
    ends = {
        0: jnp.where(index == 0, hidden_ref[1], hidden_ref[0]),
        rows + 1: jnp.where(index == count - 1, hidden_ref[rows], hidden_ref[rows + 1]),
    }
    for row in range(rows + 2):
        values = ends[row] if row in ends else hidden_ref[row]
        store_taps(values, scale, offset, wide_ref, taps_ref, row)
    branch = conv_rows(taps_ref, 0, rows, summed_ref) + params_ref[0:1, :]
    for row in range(rows):
        values = own_ref[row].astype(jnp.float32) + branch[row * width : (row + 1) * width]
        done_ref[row] = values.astype(jnp.bfloat16)
        copies[row].start()
    for copy in copies:
        copy.wait()


def exchanged(sums):
    count = lax.axis_size("rows")
    ends_first = [i // 2 if i % 2 == 0 else count - 1 - i // 2 for i in range(count)]
    return lax.all_to_all(sums, "rows", 0, 0, axis_index_groups=[ends_first])


def body(
    latents, gain_one, shift_one, weight_one, bias_one, gain_two, shift_two, weight_two, bias_two
):
    count = lax.axis_size("rows")
    own = latents[0]
    rows, width, channels = own.shape
    sums_shape = jax.ShapeDtypeStruct((count, 1, channels), jnp.float32)
    taps = weight_one.shape[1] * weight_one.shape[2]
    slab_shape = jax.ShapeDtypeStruct((2, width, channels), jnp.bfloat16)

    def raw(weight):
        return weight.reshape(3, taps, channels, channels)

    swap_pair = [(i, i ^ 1) for i in range(count)]
    swap_other = [(i, i + 1 if i % 2 else i - 1) for i in range(1, count - 1)]

    sums, pair, other = pl.pallas_call(
        sums_kernel,
        out_shape=[sums_shape, slab_shape, slab_shape],
        in_specs=[VMEM],
        out_specs=[VMEM] * 3,
        compiler_params=PARAMS,
        name="sums",
        cost_estimate=pl.CostEstimate(
            flops=40000000000, bytes_accessed=10000000, transcendentals=0
        ),
    )(own)
    other = lax.ppermute(other, "rows", swap_other)
    pair = lax.ppermute(pair, "rows", swap_pair)
    sums = exchanged(sums)
    hidden, sums, params = pl.pallas_call(
        functools.partial(first_kernel, count),
        out_shape=[
            jax.ShapeDtypeStruct((rows + 2, width, channels), jnp.bfloat16),
            sums_shape,
            jax.ShapeDtypeStruct((8, channels), jnp.float32),
        ],
        in_specs=[VMEM] * 8 + [HBM] * 3,
        out_specs=[VMEM] * 3,
        scratch_shapes=[
            pltpu.VMEM((rows + 4, width + 16, channels), jnp.float32),
            pltpu.VMEM((rows + 4, width, 3 * channels), jnp.bfloat16),
            pltpu.VMEM((taps * channels, 2 * channels), jnp.bfloat16),
            pltpu.VMEM((3, 1, channels), jnp.float32),
            pltpu.SemaphoreType.DMA((3,)),
        ],
        compiler_params=PARAMS, name="first",
    )(
        sums,
        own,
        pair,
        other,
        raw(weight_one),
        *[vector.reshape(1, channels) for vector in (bias_one, gain_one, shift_one)],
        *[
            pltpu.with_memory_space_constraint(vector.reshape(1, channels), pltpu.HBM)
            for vector in (bias_two, gain_two, shift_two)
        ],
    )
    sums = exchanged(sums)
    decoded = pl.pallas_call(
        functools.partial(second_kernel, count),
        out_shape=jax.ShapeDtypeStruct(own.shape, jnp.bfloat16),
        in_specs=[VMEM] * 5,
        out_specs=ANY,
        scratch_shapes=[
            pltpu.VMEM((rows + 2, width + 16, channels), jnp.float32),
            pltpu.VMEM((rows + 2, width, 3 * channels), jnp.bfloat16),
            pltpu.VMEM((taps * channels, 2 * channels), jnp.bfloat16),
            pltpu.VMEM(own.shape, jnp.bfloat16),
            pltpu.SemaphoreType.DMA((rows,)),
        ],
        compiler_params=PARAMS, name="second",
    )(sums, hidden, own, raw(weight_two), params)
    return decoded[None]


def solution(mesh):
    return jax.shard_map(
        body,
        mesh=mesh,
        in_specs=(P("groups", "rows", None, None), P(), P(), P(), P(), P(), P(), P(), P()),
        out_specs=P("groups", "rows", None, None),
        check_vma=False,
    )
```

```python
import functools

import jax
import jax.numpy as jnp
from jax import lax
from jax.experimental import pallas as pl
from jax.experimental.pallas import tpu as pltpu
from jax.sharding import PartitionSpec as P

GROUPS = 32
HBM = pl.BlockSpec(memory_space=pltpu.HBM)
ANY = pl.BlockSpec(memory_space=pl.ANY)
VMEM = pl.BlockSpec(memory_space=pltpu.VMEM)
PARAMS = pltpu.CompilerParams(vmem_limit_bytes=24 * 1024 * 1024)


def store_sums(total, square, out_ref):
    channels = total.shape[1]
    per_group = channels // GROUPS
    member = lax.broadcasted_iota(jnp.int32, (8, channels), 1) % per_group

    def grouped(part):
        part = jnp.broadcast_to(jnp.sum(part, axis=0, keepdims=True), (8, channels))
        result = part
        for step in range(1, per_group):
            result += jnp.where(member >= step, pltpu.roll(part, step, 1), 0.0)
            rolled = pltpu.roll(part, channels - step, 1)
            result += jnp.where(member < per_group - step, rolled, 0.0)
        return result

    row = jnp.where(member == 0, grouped(total), grouped(square))[0:1]
    out_ref[...] = jnp.broadcast_to(row[None], out_ref.shape)


def add_sums(values, total, square):
    width, channels = values.shape
    split = (width // 8, 8, channels)
    total += jnp.sum(values.reshape(split), axis=0)
    square += jnp.sum((values * values).reshape(split), axis=0)
    return total, square


def sums_kernel(own_ref, out_ref, pair_ref, other_ref):
    rows, _, channels = own_ref.shape
    even = lax.axis_index("rows") % 2 == 0
    for row in range(2):
        top = own_ref[row]
        bottom = own_ref[rows - 2 + row]
        pair_ref[row] = jnp.where(even, bottom, top)
        other_ref[row] = jnp.where(even, top, bottom)
    total = jnp.zeros((8, channels), jnp.float32)
    square = jnp.zeros((8, channels), jnp.float32)
    for row in range(rows):
        total, square = add_sums(own_ref[row].astype(jnp.float32), total, square)
    store_sums(total, square, out_ref)


def sum_weight(source, target):
    taps, channels = source.shape[1], source.shape[2]
    for tap in range(taps):
        total = source[0, tap].astype(jnp.float32)
        total += source[1, tap].astype(jnp.float32)
        total += source[2, tap].astype(jnp.float32)
        high = total.astype(jnp.bfloat16)
        low = (total - high.astype(jnp.float32)).astype(jnp.bfloat16)
        target[pl.ds(tap * channels, channels), :] = jnp.concatenate([high, low], axis=1)


def scale_offset(sums_ref, gain_ref, shift_ref, entries):
    sums = jnp.sum(sums_ref[...], axis=0)
    channels = sums.shape[1]
    per_group = channels // GROUPS
    sums = jnp.broadcast_to(sums, (8, channels)) * (1.0 / (entries * per_group))
    member = lax.broadcasted_iota(jnp.int32, sums.shape, 1) % per_group

    def spread(lane):
        part = jnp.where(member == lane, sums, 0.0)
        result = part
        for target in range(per_group):
            if target != lane:
                result += pltpu.roll(part, (target - lane) % channels, 1)
        return result

    mean = spread(0)
    var = jnp.maximum(spread(1) - mean * mean, 0.0)
    scale = gain_ref[...] * lax.rsqrt(var + 1e-06)
    return 0.5 * scale[0:1], (0.5 * (shift_ref[...] - mean * scale))[0:1]


def store_taps(values, scale, offset, wide_ref, taps_ref, row):
    width, channels = values.shape
    half = values.astype(jnp.float32) * scale + offset
    act = half * jnp.tanh(half) + half
    wide_ref[row, 8 : 8 + width, :] = act
    wide_ref[row, 7:8, :] = act[0:1]
    wide_ref[row, 8 + width : 9 + width, :] = act[width - 1 : width]
    for tap in range(3):
        shifted = wide_ref[row, 7 + tap : 7 + tap + width, :]
        taps_ref[row, :, tap * channels : (tap + 1) * channels] = shifted.astype(jnp.bfloat16)


def conv_rows(taps_ref, row, count, weight_ref):
    _, width, lanes = taps_ref.shape
    window = jnp.concatenate(
        [taps_ref[row + tap : row + tap + count].reshape(count * width, lanes) for tap in range(3)],
        axis=1,
    )
    both = jnp.dot(window, weight_ref[...], preferred_element_type=jnp.float32)
    half = both.shape[1] // 2
    return both[:, :half] + both[:, half:]


def first_kernel(
    count, sums_ref, own_ref, pair_ref, other_ref, weight_ref, bias_ref, gain_ref, shift_ref,
    bias_two_ref, gain_two_ref, shift_two_ref, weight_two_ref,
    hidden_ref, out_ref, next_ref, two_ref, wide_ref, taps_ref, summed_ref, vectors_ref, sems,
):
    copies = [
        pltpu.make_async_copy(source, vectors_ref.at[i], sems.at[i])
        for i, source in enumerate((bias_two_ref, gain_two_ref, shift_two_ref))
    ]
    for copy in copies:
        copy.start()
    index = lax.axis_index("rows")
    rows, width, channels = own_ref.shape
    even = index % 2 == 0
    scale, offset = scale_offset(sums_ref, gain_ref, shift_ref, rows * width * count)
    sum_weight(weight_ref, summed_ref)

    def make(row):
        if row < 2:
            values = jnp.where(even, other_ref[row], pair_ref[row])
            values = jnp.where(index == 0, own_ref[0], values)
        elif row < rows + 2:
            values = own_ref[row - 2]
        else:
            values = jnp.where(even, pair_ref[row - rows - 2], other_ref[row - rows - 2])
            values = jnp.where(index == count - 1, own_ref[rows - 1], values)
        store_taps(values, scale, offset, wide_ref, taps_ref, row)

    total = jnp.zeros((8, channels), jnp.float32)
    square = jnp.zeros((8, channels), jnp.float32)
    for row in range(rows + 4):
        make(row)
    hidden = conv_rows(taps_ref, 0, rows + 2, summed_ref) + bias_ref[...]
    hidden = hidden.astype(jnp.bfloat16)
    for row in range(rows + 2):
        values = hidden[row * width : (row + 1) * width]
        hidden_ref[row] = values
        if 0 < row <= rows:
            total, square = add_sums(values.astype(jnp.float32), total, square)
    sum_weight(weight_two_ref, two_ref)
    store_sums(total, square, out_ref)
    for i in range(3):
        copies[i].wait()
        next_ref[pl.ds(i, 1), :] = vectors_ref[i]

    @pl.when(index == 0)
    def _():
        hidden_ref[0] = hidden_ref[1]

    @pl.when(index == count - 1)
    def _():
        hidden_ref[rows + 1] = hidden_ref[rows]


def second_kernel(
    count, sums_ref, hidden_ref, own_ref, weight_ref, params_ref,
    out_ref, wide_ref, taps_ref, done_ref, sems,
):
    rows, width, channels = own_ref.shape
    scale, offset = scale_offset(
        sums_ref, params_ref.at[1:2], params_ref.at[2:3], rows * width * count
    )
    copies = [
        pltpu.make_async_copy(done_ref.at[row], out_ref.at[row], sems.at[row])
        for row in range(rows)
    ]
    for row in range(rows + 2):
        store_taps(hidden_ref[row], scale, offset, wide_ref, taps_ref, row)
    branch = conv_rows(taps_ref, 0, rows, weight_ref) + params_ref[0:1, :]
    for row in range(rows):
        values = own_ref[row].astype(jnp.float32) + branch[row * width : (row + 1) * width]
        done_ref[row] = values.astype(jnp.bfloat16)
        copies[row].start()
    for copy in copies:
        copy.wait()


def exchanged(sums):
    count = lax.axis_size("rows")
    ends_first = [i // 2 if i % 2 == 0 else count - 1 - i // 2 for i in range(count)]
    return lax.all_to_all(sums, "rows", 0, 0, axis_index_groups=[ends_first])


def body(
    latents, gain_one, shift_one, weight_one, bias_one, gain_two, shift_two, weight_two, bias_two
):
    count = lax.axis_size("rows")
    own = latents[0]
    rows, width, channels = own.shape
    sums_shape = jax.ShapeDtypeStruct((count, 1, channels), jnp.float32)
    taps = weight_one.shape[1] * weight_one.shape[2]
    slab_shape = jax.ShapeDtypeStruct((2, width, channels), jnp.bfloat16)

    def raw(weight):
        return weight.reshape(3, taps, channels, channels)

    swap_pair = [(i, i ^ 1) for i in range(count)]
    swap_other = [(i, i + 1 if i % 2 else i - 1) for i in range(1, count - 1)]

    sums, pair, other = pl.pallas_call(
        sums_kernel,
        out_shape=[sums_shape, slab_shape, slab_shape],
        in_specs=[VMEM],
        out_specs=[VMEM] * 3,
        compiler_params=PARAMS,
        name="sums",
        cost_estimate=pl.CostEstimate(
            flops=40000000000, bytes_accessed=10000000, transcendentals=0
        ),
    )(own)
    other = lax.ppermute(other, "rows", swap_other)
    pair = lax.ppermute(pair, "rows", swap_pair)
    sums = exchanged(sums)
    hidden, sums, params, two = pl.pallas_call(
        functools.partial(first_kernel, count),
        out_shape=[
            jax.ShapeDtypeStruct((rows + 2, width, channels), jnp.bfloat16),
            sums_shape,
            jax.ShapeDtypeStruct((8, channels), jnp.float32),
            jax.ShapeDtypeStruct((taps * channels, 2 * channels), jnp.bfloat16),
        ],
        in_specs=[VMEM] * 8 + [HBM] * 3 + [VMEM],
        out_specs=[VMEM] * 4,
        scratch_shapes=[
            pltpu.VMEM((rows + 4, width + 16, channels), jnp.float32),
            pltpu.VMEM((rows + 4, width, 3 * channels), jnp.bfloat16),
            pltpu.VMEM((taps * channels, 2 * channels), jnp.bfloat16),
            pltpu.VMEM((3, 1, channels), jnp.float32),
            pltpu.SemaphoreType.DMA((3,)),
        ],
        compiler_params=PARAMS, name="first",
    )(
        sums,
        own,
        pair,
        other,
        raw(weight_one),
        *[vector.reshape(1, channels) for vector in (bias_one, gain_one, shift_one)],
        *[
            pltpu.with_memory_space_constraint(vector.reshape(1, channels), pltpu.HBM)
            for vector in (bias_two, gain_two, shift_two)
        ],
        raw(weight_two),
    )
    sums = exchanged(sums)
    decoded = pl.pallas_call(
        functools.partial(second_kernel, count),
        out_shape=jax.ShapeDtypeStruct(own.shape, jnp.bfloat16),
        in_specs=[VMEM] * 5,
        out_specs=ANY,
        scratch_shapes=[
            pltpu.VMEM((rows + 2, width + 16, channels), jnp.float32),
            pltpu.VMEM((rows + 2, width, 3 * channels), jnp.bfloat16),
            pltpu.VMEM(own.shape, jnp.bfloat16),
            pltpu.SemaphoreType.DMA((rows,)),
        ],
        compiler_params=PARAMS, name="second",
    )(sums, hidden, own, two, params)
    return decoded[None]


def solution(mesh):
    return jax.shard_map(
        body,
        mesh=mesh,
        in_specs=(P("groups", "rows", None, None), P(), P(), P(), P(), P(), P(), P(), P()),
        out_specs=P("groups", "rows", None, None),
        check_vma=False,
    )
```

```python
import functools

import jax
import jax.numpy as jnp
from jax import lax
from jax.experimental import pallas as pl
from jax.experimental.pallas import tpu as pltpu
from jax.sharding import PartitionSpec as P

GROUPS = 32
HBM = pl.BlockSpec(memory_space=pltpu.HBM)
ANY = pl.BlockSpec(memory_space=pl.ANY)
VMEM = pl.BlockSpec(memory_space=pltpu.VMEM)
PARAMS = pltpu.CompilerParams(vmem_limit_bytes=24 * 1024 * 1024)


def store_sums(total, square, out_ref):
    channels = total.shape[1]
    per_group = channels // GROUPS
    member = lax.broadcasted_iota(jnp.int32, (8, channels), 1) % per_group

    def grouped(part):
        part = jnp.broadcast_to(jnp.sum(part, axis=0, keepdims=True), (8, channels))
        result = part
        for step in range(1, per_group):
            result += jnp.where(member >= step, pltpu.roll(part, step, 1), 0.0)
            rolled = pltpu.roll(part, channels - step, 1)
            result += jnp.where(member < per_group - step, rolled, 0.0)
        return result

    row = jnp.where(member == 0, grouped(total), grouped(square))[0:1]
    out_ref[...] = jnp.broadcast_to(row[None], out_ref.shape)


def add_sums(values, total, square):
    width, channels = values.shape
    split = (width // 8, 8, channels)
    total += jnp.sum(values.reshape(split), axis=0)
    square += jnp.sum((values * values).reshape(split), axis=0)
    return total, square


def sums_kernel(own_ref, out_ref, pair_ref, other_ref):
    rows, _, channels = own_ref.shape
    even = lax.axis_index("rows") % 2 == 0
    for row in range(2):
        top = own_ref[row]
        bottom = own_ref[rows - 2 + row]
        pair_ref[row] = jnp.where(even, bottom, top)
        other_ref[row] = jnp.where(even, top, bottom)
    total = jnp.zeros((8, channels), jnp.float32)
    square = jnp.zeros((8, channels), jnp.float32)
    for row in range(rows):
        total, square = add_sums(own_ref[row].astype(jnp.float32), total, square)
    store_sums(total, square, out_ref)


def sum_weight(source, target):
    taps, channels = source.shape[1], source.shape[2]
    for tap in range(taps):
        total = source[0, tap].astype(jnp.float32)
        total += source[1, tap].astype(jnp.float32)
        total += source[2, tap].astype(jnp.float32)
        high = total.astype(jnp.bfloat16)
        low = (total - high.astype(jnp.float32)).astype(jnp.bfloat16)
        target[pl.ds(tap * channels, channels), :] = jnp.concatenate([high, low], axis=1)


def scale_offset(sums_ref, gain_ref, shift_ref, entries):
    sums = jnp.sum(sums_ref[...], axis=0)
    channels = sums.shape[1]
    per_group = channels // GROUPS
    sums = jnp.broadcast_to(sums, (8, channels)) * (1.0 / (entries * per_group))
    member = lax.broadcasted_iota(jnp.int32, sums.shape, 1) % per_group

    def spread(lane):
        part = jnp.where(member == lane, sums, 0.0)
        result = part
        for target in range(per_group):
            if target != lane:
                result += pltpu.roll(part, (target - lane) % channels, 1)
        return result

    mean = spread(0)
    var = jnp.maximum(spread(1) - mean * mean, 0.0)
    scale = gain_ref[...] * lax.rsqrt(var + 1e-06)
    return 0.5 * scale[0:1], (0.5 * (shift_ref[...] - mean * scale))[0:1]


def store_taps(values, scale, offset, wide_ref, taps_ref, row):
    width, channels = values.shape
    half = values.astype(jnp.float32) * scale + offset
    act = half * jnp.tanh(half) + half
    wide_ref[row, 8 : 8 + width, :] = act
    wide_ref[row, 7:8, :] = act[0:1]
    wide_ref[row, 8 + width : 9 + width, :] = act[width - 1 : width]
    for tap in range(3):
        shifted = wide_ref[row, 7 + tap : 7 + tap + width, :]
        taps_ref[row, :, tap * channels : (tap + 1) * channels] = shifted.astype(jnp.bfloat16)


def conv_rows(taps_ref, row, count, weight_ref):
    _, width, lanes = taps_ref.shape
    window = jnp.concatenate(
        [taps_ref[row + tap : row + tap + count].reshape(count * width, lanes) for tap in range(3)],
        axis=1,
    )
    both = jnp.dot(window, weight_ref[...], preferred_element_type=jnp.float32)
    half = both.shape[1] // 2
    return both[:, :half] + both[:, half:]


def first_kernel(
    count, sums_ref, own_ref, pair_ref, other_ref, weight_ref, bias_ref, gain_ref, shift_ref,
    bias_two_ref, gain_two_ref, shift_two_ref,
    hidden_ref, out_ref, next_ref, wide_ref, taps_ref, summed_ref, vectors_ref, sems,
):
    copies = [
        pltpu.make_async_copy(source, vectors_ref.at[i], sems.at[i])
        for i, source in enumerate((bias_two_ref, gain_two_ref, shift_two_ref))
    ]
    for copy in copies:
        copy.start()
    index = lax.axis_index("rows")
    rows, width, channels = own_ref.shape
    even = index % 2 == 0
    scale, offset = scale_offset(sums_ref, gain_ref, shift_ref, rows * width * count)
    sum_weight(weight_ref, summed_ref)

    def make(row):
        if row < 2:
            values = jnp.where(even, other_ref[row], pair_ref[row])
            values = jnp.where(index == 0, own_ref[0], values)
        elif row < rows + 2:
            values = own_ref[row - 2]
        else:
            values = jnp.where(even, pair_ref[row - rows - 2], other_ref[row - rows - 2])
            values = jnp.where(index == count - 1, own_ref[rows - 1], values)
        store_taps(values, scale, offset, wide_ref, taps_ref, row)

    total = jnp.zeros((8, channels), jnp.float32)
    square = jnp.zeros((8, channels), jnp.float32)
    for row in range(rows + 4):
        make(row)
    hidden = conv_rows(taps_ref, 0, rows + 2, summed_ref) + bias_ref[...]
    hidden = hidden.astype(jnp.bfloat16)
    for row in range(rows + 2):
        values = hidden[row * width : (row + 1) * width]
        hidden_ref[row] = values
        if 0 < row <= rows:
            total, square = add_sums(values.astype(jnp.float32), total, square)
    store_sums(total, square, out_ref)
    for i in range(3):
        copies[i].wait()
        next_ref[pl.ds(i, 1), :] = vectors_ref[i]

    @pl.when(index == 0)
    def _():
        hidden_ref[0] = hidden_ref[1]

    @pl.when(index == count - 1)
    def _():
        hidden_ref[rows + 1] = hidden_ref[rows]


def second_kernel(
    count, sums_ref, hidden_ref, own_ref, weight_ref, params_ref,
    out_ref, wide_ref, taps_ref, summed_ref, done_ref, sems,
):
    rows, width, channels = own_ref.shape
    scale, offset = scale_offset(
        sums_ref, params_ref.at[1:2], params_ref.at[2:3], rows * width * count
    )
    sum_weight(weight_ref, summed_ref)
    copies = [
        pltpu.make_async_copy(done_ref.at[row], out_ref.at[row], sems.at[row])
        for row in range(rows)
    ]
    for row in range(rows + 2):
        store_taps(hidden_ref[row], scale, offset, wide_ref, taps_ref, row)
    branch = conv_rows(taps_ref, 0, rows, summed_ref) + params_ref[0:1, :]
    for row in range(rows):
        values = own_ref[row].astype(jnp.float32) + branch[row * width : (row + 1) * width]
        done_ref[row] = values.astype(jnp.bfloat16)
        copies[row].start()
    for copy in copies:
        copy.wait()


def exchanged(sums):
    count = lax.axis_size("rows")
    ends_first = sorted(range(count), key=lambda i: (min(i // 2, (count - 1 - i) // 2), i))
    return lax.all_to_all(sums, "rows", 0, 0, axis_index_groups=[ends_first])


def body(
    latents, gain_one, shift_one, weight_one, bias_one, gain_two, shift_two, weight_two, bias_two
):
    count = lax.axis_size("rows")
    own = latents[0]
    rows, width, channels = own.shape
    sums_shape = jax.ShapeDtypeStruct((count, 1, channels), jnp.float32)
    taps = weight_one.shape[1] * weight_one.shape[2]
    slab_shape = jax.ShapeDtypeStruct((2, width, channels), jnp.bfloat16)

    def raw(weight):
        return weight.reshape(3, taps, channels, channels)

    swap_pair = [(i, i ^ 1) for i in range(count)]
    swap_other = [(i, i + 1 if i % 2 else i - 1) for i in range(1, count - 1)]

    sums, pair, other = pl.pallas_call(
        sums_kernel,
        out_shape=[sums_shape, slab_shape, slab_shape],
        in_specs=[VMEM],
        out_specs=[VMEM] * 3,
        compiler_params=PARAMS,
        name="sums",
        cost_estimate=pl.CostEstimate(
            flops=40000000000, bytes_accessed=10000000, transcendentals=0
        ),
    )(own)
    other = lax.ppermute(other, "rows", swap_other)
    pair = lax.ppermute(pair, "rows", swap_pair)
    sums = exchanged(sums)
    hidden, sums, params = pl.pallas_call(
        functools.partial(first_kernel, count),
        out_shape=[
            jax.ShapeDtypeStruct((rows + 2, width, channels), jnp.bfloat16),
            sums_shape,
            jax.ShapeDtypeStruct((8, channels), jnp.float32),
        ],
        in_specs=[VMEM] * 8 + [HBM] * 3,
        out_specs=[VMEM] * 3,
        scratch_shapes=[
            pltpu.VMEM((rows + 4, width + 16, channels), jnp.float32),
            pltpu.VMEM((rows + 4, width, 3 * channels), jnp.bfloat16),
            pltpu.VMEM((taps * channels, 2 * channels), jnp.bfloat16),
            pltpu.VMEM((3, 1, channels), jnp.float32),
            pltpu.SemaphoreType.DMA((3,)),
        ],
        compiler_params=PARAMS, name="first",
    )(
        sums,
        own,
        pair,
        other,
        raw(weight_one),
        *[vector.reshape(1, channels) for vector in (bias_one, gain_one, shift_one)],
        *[
            pltpu.with_memory_space_constraint(vector.reshape(1, channels), pltpu.HBM)
            for vector in (bias_two, gain_two, shift_two)
        ],
    )
    sums = exchanged(sums)
    decoded = pl.pallas_call(
        functools.partial(second_kernel, count),
        out_shape=jax.ShapeDtypeStruct(own.shape, jnp.bfloat16),
        in_specs=[VMEM] * 5,
        out_specs=ANY,
        scratch_shapes=[
            pltpu.VMEM((rows + 2, width + 16, channels), jnp.float32),
            pltpu.VMEM((rows + 2, width, 3 * channels), jnp.bfloat16),
            pltpu.VMEM((taps * channels, 2 * channels), jnp.bfloat16),
            pltpu.VMEM(own.shape, jnp.bfloat16),
            pltpu.SemaphoreType.DMA((rows,)),
        ],
        compiler_params=PARAMS, name="second",
    )(sums, hidden, own, raw(weight_two), params)
    return decoded[None]


def solution(mesh):
    return jax.shard_map(
        body,
        mesh=mesh,
        in_specs=(P("groups", "rows", None, None), P(), P(), P(), P(), P(), P(), P(), P()),
        out_specs=P("groups", "rows", None, None),
        check_vma=False,
    )
```
